32 devices in a mesh: seq: 8 (over y, x, core), tp: 4 (over z).
Axes of the slice: x: 2, y: 2, z: 4, core: 2. Of those that a mesh axis runs over, the one named last changes fastest.
Arguments:
- hidden_in: bfloat16 [6144, 2048], P('seq'), may hold values from -6 to 6
- gain_in: bfloat16 [2048], replicated, may hold values from 0.5 to 1.5
- w_input: bfloat16 [2048, 2048], P('seq', 'tp'), may hold values from -0.125 to 0.125
- w_forget: bfloat16 [2048, 2048], P('seq', 'tp'), may hold values from -0.125 to 0.125
- forget_bias: float32 [2048], replicated, may hold values from -1 to 11
- w_outgate: bfloat16 [2048, 2048], P('seq', 'tp'), may hold values from -0.125 to 0.125
- state_gain: bfloat16 [2048], replicated, may hold values from 0.5 to 1.5
- w_output: bfloat16 [2048, 2048], P('tp', 'seq'), may hold values from -0.125 to 0.125
- gain_mid: bfloat16 [2048], replicated, may hold values from 0.5 to 1.5
- w_gate: bfloat16 [2048, 5632], P('seq', 'tp'), may hold values from -0.125 to 0.125
- w_up: bfloat16 [2048, 5632], P('seq', 'tp'), may hold values from -0.125 to 0.125
- w_down: bfloat16 [5632, 2048], P('tp', 'seq'), may hold values from -0.078125 to 0.078125
- lengths: int32 [2], replicated, may hold values from 1152 to 4992, as said below
- layer_index: int32 [1], replicated, may hold values from 0 to 23
- cotangent: bfloat16 [6144, 2048], P('seq'), may hold values from -6 to 6
Outputs:
- block_out: bfloat16 [6144, 2048], P('seq', 'tp')
- grad_in: float32 [6144, 2048], P('seq', 'tp')
- grad_gain_in: float32 [2048], replicated
- grad_w_input: float32 [2048, 2048], P('seq', 'tp')
- grad_w_forget: float32 [2048, 2048], P('seq', 'tp')
- grad_forget_bias: float32 [2048], replicated
- grad_w_outgate: float32 [2048, 2048], P('seq', 'tp')
- grad_state_gain: float32 [2048], replicated
- grad_w_output: float32 [2048, 2048], P('tp', 'seq')
- grad_gain_mid: float32 [2048], replicated
- grad_w_gate: float32 [2048, 5632], P('seq', 'tp')
- grad_w_up: float32 [2048, 5632], P('seq', 'tp')
- grad_w_down: float32 [5632, 2048], P('tp', 'seq')
- rms_stats: float32 [3], replicated
The draws below stay inside these ranges and needn't reach their ends.
Inputs may be any that keep to these rules, and one draw needn't show every extreme that they name: The first sequence fills slots from 0, the second follows it directly, padding fills the rest; fewer than 384 slots are padding; lengths[1] lies from 1152 to 1535.
All inputs are finite; a program needn't handle non-finite values.
Results may differ from the reference program's by a relative error of at most 0.0081.
Values may be sent and summed in bfloat16 or wider, within the bound.
A program may use at most 256 MiB of HBM per device.

```python
import jax
import jax.numpy as jnp
from jax import lax

D = 2048
FF = 5632
LAYERS = 24
TOK_DEV = 768
TOKENS = 6144


def draw_lengths(key, part):
    first_key, second_key = jax.random.split(jax.random.fold_in(key, 17))
    second = jax.random.randint(first_key, (), 3 * TOK_DEV // 2, 2 * TOK_DEV, dtype=jnp.int32)
    padding = jax.random.randint(second_key, (), 0, TOK_DEV // 2, dtype=jnp.int32)
    first = TOKENS - second - padding
    return jnp.stack([first, second]).astype(jnp.int32)


def level_of(stream_key, extent, cuts, least, largest):
    factor_of = 1.0
    for position, shards_of in cuts:
        draws = jax.random.uniform(jax.random.fold_in(jax.random.fold_in(stream_key, 6), position), (shards_of,), jnp.float32, least / len(cuts), largest / len(cuts))
        factor_of = factor_of * jnp.repeat(jnp.exp(draws), extent[position] // shards_of).reshape((-1,) + (1,) * (len(extent) - 1 - position))
    return factor_of


def noise(stream_key, dims, spread, most, shards=(), kind=jnp.bfloat16):
    factor_of = level_of(stream_key, dims, shards, -0.22, 0.18) if shards else 1.0
    array = jax.random.normal(stream_key, dims, jnp.float32) * spread * factor_of
    return jnp.minimum(jnp.maximum(array, -most), most).astype(kind)


def setup_inputs(seed: int = 0) -> dict:
    key_of = jax.random.split(jax.random.key(seed), 16)
    hidden_in = noise(key_of[0], (TOKENS, D), 1.0, 6.0, ((0, 8),))
    gain_in = jnp.clip(1.0 + 0.1 * jax.random.normal(key_of[1], (D,), jnp.float32), 0.5, 1.5).astype(jnp.bfloat16)
    w_input = noise(key_of[2], (D, D), D ** -0.5, 0.125, ((0, 8), (1, 4)))
    w_forget = noise(key_of[3], (D, D), D ** -0.5, 0.125, ((0, 8), (1, 4)))
    forget_bias = jnp.clip(jax.random.uniform(key_of[4], (D,), jnp.float32, -1.0, 11.0), -1.0, 11.0)
    w_outgate = noise(key_of[5], (D, D), D ** -0.5, 0.125, ((0, 8), (1, 4)))
    state_gain = jnp.clip(1.0 + 0.1 * jax.random.normal(key_of[6], (D,), jnp.float32), 0.5, 1.5).astype(jnp.bfloat16)
    w_output = noise(key_of[7], (D, D), D ** -0.5, 0.125, ((0, 4), (1, 8)))
    gain_mid = jnp.clip(1.0 + 0.1 * jax.random.normal(key_of[8], (D,), jnp.float32), 0.5, 1.5).astype(jnp.bfloat16)
    w_gate = noise(key_of[9], (D, FF), D ** -0.5, 0.125, ((0, 8), (1, 4)))
    w_up = noise(key_of[10], (D, FF), D ** -0.5, 0.125, ((0, 8), (1, 4)))
    w_down = noise(key_of[11], (FF, D), FF ** -0.5, 0.078125, ((0, 4), (1, 8)))
    lengths = draw_lengths(jax.random.fold_in(key_of[15], 71), 0)
    layer_index = jax.random.randint(key_of[13], (1,), 0, LAYERS).astype(jnp.int32)
    cotangent = noise(key_of[14], (TOKENS, D), 1.0, 6.0, ((0, 8),))
    return dict(hidden_in=hidden_in, gain_in=gain_in, w_input=w_input, w_forget=w_forget, forget_bias=forget_bias, w_outgate=w_outgate, state_gain=state_gain, w_output=w_output, gain_mid=gain_mid, w_gate=w_gate, w_up=w_up, w_down=w_down, lengths=lengths, layer_index=layer_index, cotangent=cotangent)


norm_epsilon = 1e-06

@jax.custom_vjp
def low(v):
    return lax.optimization_barrier(v.astype(jnp.bfloat16)).astype(jnp.float32)

@jax.custom_vjp
def low_back(v):
    return v

def low_keep(v):
    return (low(v), None)

def low_pass(kept, grad):
    return (grad,)

def back_keep(v):
    return (v, None)

def back_low(kept, grad):
    return (low(grad),)
low.defvjp(low_keep, low_pass)
low_back.defvjp(back_keep, back_low)

def hdot(left, right):
    return jnp.dot(left, right, preferred_element_type=jnp.float32, precision=lax.Precision.HIGHEST)

def rms_scale(values):
    return lax.rsqrt(lax.optimization_barrier(jnp.mean(values * values, axis=-1, keepdims=True)) + norm_epsilon)

def reference(hidden_in, gain_in, w_input, w_forget, forget_bias, w_outgate, state_gain, w_output, gain_mid, w_gate, w_up, w_down, lengths, layer_index, cotangent):
    positions = jnp.arange(TOKENS, dtype=jnp.int32)
    total = lengths[0] + lengths[1]
    valid = (positions < total).astype(jnp.float32)[:, None]
    starts = ((positions == 0) | (positions == lengths[0])).astype(jnp.float32)[:, None]
    bound = layer_index[0].astype(jnp.float32) / LAYERS

    def forward(hidden, gain_one, weight_input, weight_forget, bias_forget, weight_outgate, gain_state, weight_output, gain_two, weight_gate, weight_up, weight_down):
        normed_in = low(hidden * rms_scale(hidden) * gain_one)
        input_pre = low_back(hdot(normed_in, weight_input))
        forget_pre = low_back(hdot(normed_in, weight_forget) + bias_forget)
        outgate_pre = low_back(hdot(normed_in, weight_outgate))
        forget_gate = bound + (1.0 - bound) * jax.nn.sigmoid(forget_pre)
        forget_eff = forget_gate * (1.0 - starts)
        drive = jax.nn.silu(input_pre) * (1.0 - forget_gate) * valid

        def advance(state, pair):
            state = pair[0] * state + pair[1]
            return (state, state)
        unused, states = lax.scan(jax.checkpoint(advance), jnp.zeros((D,), jnp.float32), (forget_eff, drive))
        gated_out = low(states * rms_scale(states) * gain_state * jax.nn.silu(outgate_pre))
        mixed = low_back(hdot(gated_out, weight_output))
        resid_mid = hidden + mixed
        normed_mid = low(resid_mid * rms_scale(resid_mid) * gain_two)
        gate_pre = low_back(hdot(normed_mid, weight_gate))
        up_pre = low_back(hdot(normed_mid, weight_up))
        hidden_glu = low(jax.nn.silu(gate_pre) * up_pre)
        glu_out = hdot(hidden_glu, weight_down)
        return (resid_mid + glu_out, (mixed, glu_out))
    floats = [a.astype(jnp.float32) for a in (hidden_in, gain_in, w_input, w_forget, forget_bias, w_outgate, state_gain, w_output, gain_mid, w_gate, w_up, w_down)]
    out_full, pullback, extras = jax.vjp(forward, *floats, has_aux=True)
    grads = pullback(cotangent.astype(jnp.float32))
    mixed, glu_out = extras
    sums = jnp.stack([jnp.sum(valid * mixed * mixed), jnp.sum(valid * glu_out * glu_out), jnp.sum(valid * out_full * out_full)])
    rms_stats = jnp.sqrt(sums / (total.astype(jnp.float32) * D))
    return (out_full.astype(jnp.bfloat16), grads[0], grads[1], grads[2], grads[3], grads[4], grads[5], grads[6], grads[7], grads[8], grads[9], grads[10], grads[11], rms_stats)
```

```python
import functools

import jax
import jax.numpy as jnp
from jax import lax
from jax.experimental import pallas as pl
from jax.experimental.pallas import tpu as pltpu
from jax.sharding import PartitionSpec as P

LAYERS = 24
EPS = 1e-06
MESH = pl.DeviceIdType.MESH
BF = jnp.bfloat16
F32 = jnp.float32
VM = pl.BlockSpec(memory_space=pltpu.VMEM)
HB = pl.BlockSpec(memory_space=pl.ANY)
LANE = 128
SEG = 8
CHUNKS = 8
VMEM_LIMIT = 60 * 1024 * 1024


def nn(left, right):
    return jnp.dot(left, right, preferred_element_type=F32)


def nt(left, right):
    return lax.dot_general(left, right, (((1,), (1,)), ((), ())), preferred_element_type=F32)


def tn(left, right):
    return lax.dot_general(left, right, (((0,), (0,)), ((), ())), preferred_element_type=F32)


def shape(dims, dtype):
    return jax.ShapeDtypeStruct(dims, dtype)


def get(ref, at):
    return jnp.concatenate([ref[g, at, :] for g in range(ref.shape[0])], axis=1)


def put(ref, at, values):
    for g in range(ref.shape[0]):
        ref[g, at, :] = values[:, g * LANE : (g + 1) * LANE]


def row_tile(rows):
    return rows // 3 if rows % 48 == 0 else rows


def greet_all(n, t, seq, tp):
    barrier = pltpu.get_barrier_semaphore()

    def along_seq(o, c):
        pl.semaphore_signal(barrier, inc=1, device_id=(lax.rem(seq + o, n), tp), device_id_type=MESH)
        return c

    def along_tp(o, c):
        pl.semaphore_signal(barrier, inc=1, device_id=(seq, lax.rem(tp + o, t)), device_id_type=MESH)
        return c

    lax.fori_loop(1, n, along_seq, 0)
    lax.fori_loop(1, t, along_tp, 0)
    pl.semaphore_wait(barrier, n - 1 + t - 1)


def greet_line(t, seq, tp):
    barrier = pltpu.get_barrier_semaphore()

    def along_tp(o, c):
        pl.semaphore_signal(barrier, inc=1, device_id=(seq, lax.rem(tp + o, t)), device_id_type=MESH)
        return c

    lax.fori_loop(1, t, along_tp, 0)
    pl.semaphore_wait(barrier, t - 1)


def spread(size, me, slots, send, recv, target):
    def copy(o, slot):
        return pltpu.make_async_remote_copy(
            src_ref=slots.at[slot],
            dst_ref=slots.at[slot],
            send_sem=send.at[o],
            recv_sem=recv.at[slot],
            device_id=target(lax.rem(me + o, size)),
            device_id_type=MESH,
        )

    def go(o, c):
        copy(o, me).start()
        return c

    def done(o, c):
        copy(o, lax.rem(me + o, size)).wait_recv()
        return c

    def sent(o, c):
        copy(o, me).wait_send()
        return c

    lax.fori_loop(1, size, go, 0)
    lax.fori_loop(1, size, done, 0)
    lax.fori_loop(1, size, sent, 0)


def row_sums(values):
    ones = jnp.ones((8, values.shape[1]), BF)
    high = values.astype(BF)
    rest = values - high.astype(F32)
    low = rest.astype(BF)
    return nt(ones, high) + nt(ones, low)


def sum_over_tp(part, t, seq, tp, slots, send, recv):
    slots[tp] = part
    spread(t, tp, slots, send, recv, lambda k: (seq, k))
    total = slots[0]
    for k in range(1, t):
        total = total + slots[k]
    return jnp.transpose(total)[:, :1]


def carry_over_seq(prod, state, n, seq, tp, slots, send, recv, backward):
    slots[seq] = jnp.concatenate([prod, state] + [jnp.zeros_like(prod)] * 6, axis=0)
    spread(n, seq, slots, send, recv, lambda k: (k, tp))

    def hop(i, total):
        j = n - 1 - i if backward else i
        block = slots[j]
        longer = block[1:2] + block[0:1] * total
        inside = (j > seq) if backward else (j < seq)
        return jnp.where(inside, longer, total)

    return lax.fori_loop(0, n, hop, jnp.zeros_like(prod))


def line_all_reduce(t, seq, tp, rows, chunks, partial, send, buf, sems, finish):
    s_in, s_out, r_buf = sems
    step = rows // chunks
    half = t // 2
    depth = jnp.where(tp < half, tp, t - 1 - tp)
    inner = jnp.where(tp < half, tp + 1, tp - 1)
    outer = jnp.where(tp < half, tp - 1, tp + 1)
    outer = jnp.where(depth > 0, outer, inner)
    middle = (depth == half - 1).astype(jnp.int32)

    def part_of(k):
        return pl.ds(pl.multiple_of(k * step, step), step)

    def inward(k, slot):
        return pltpu.make_async_remote_copy(
            src_ref=send.at[part_of(k)],
            dst_ref=buf.at[slot, part_of(k)],
            send_sem=s_in.at[k],
            recv_sem=r_buf.at[slot, k],
            device_id=(seq, inner),
            device_id_type=MESH,
        )

    def outward(k):
        return pltpu.make_async_remote_copy(
            src_ref=buf.at[1, part_of(k)],
            dst_ref=buf.at[1, part_of(k)],
            send_sem=s_out.at[k],
            recv_sem=r_buf.at[1, k],
            device_id=(seq, outer),
            device_id_type=MESH,
        )

    def first(k):
        part = partial(k)

        @pl.when(depth > 0)
        def _():
            inward(k, 0).wait_recv()
            send[part_of(k), :] = (part + buf[0, part_of(k), :].astype(F32)).astype(BF)

        @pl.when(depth == 0)
        def _():
            send[part_of(k), :] = part.astype(BF)

        inward(k, middle).start()

    def second(k):
        inward(k, 1).wait_recv()

        @pl.when(middle == 1)
        def _():
            both = send[part_of(k), :].astype(F32) + buf[1, part_of(k), :].astype(F32)
            buf[1, part_of(k), :] = both.astype(BF)

        @pl.when(depth > 0)
        def _():
            outward(k).start()

        finish(k)

    def both(k, c):
        @pl.when(k < chunks)
        def _():
            first(k)

        @pl.when(k > 0)
        def _():
            second(k - 1)

        return c

    lax.fori_loop(0, chunks + 1, both, 0)

    def drain(k, c):
        inward(k, middle).wait_send()

        @pl.when(depth > 0)
        def _():
            outward(k).wait_send()

        return c

    lax.fori_loop(0, chunks, drain, 0)


def line_reduce_scatter(t, seq, tp, rows, chunks, own, right, left, sems, finish):
    s_r, r_r, s_l, r_l = sems
    step = rows // chunks

    def part_of(k):
        return pl.ds(pl.multiple_of(k * step, step), step)

    def rightward(q, k):
        return pltpu.make_async_remote_copy(
            src_ref=own.at[q, part_of(k)],
            dst_ref=right.at[q, part_of(k)],
            send_sem=s_r.at[q, k],
            recv_sem=r_r.at[q, k],
            device_id=(seq, lax.rem(tp + 1, t)),
            device_id_type=MESH,
        )

    def leftward(q, k):
        return pltpu.make_async_remote_copy(
            src_ref=own.at[q, part_of(k)],
            dst_ref=left.at[q, part_of(k)],
            send_sem=s_l.at[q, k],
            recv_sem=r_l.at[q, k],
            device_id=(seq, lax.rem(tp + t - 1, t)),
            device_id_type=MESH,
        )

    def add(q, k, other):
        own[q, part_of(k), :] = (
            own[q, part_of(k), :].astype(F32) + other[q, part_of(k), :].astype(F32)
        ).astype(BF)

    def step_of(i, c):
        k = i // (t - 1)
        j = lax.rem(i, t - 1)

        @pl.when(t - 1 - j > tp)
        def _():
            q = t - 1 - j

            @pl.when(tp > 0)
            def _():
                rightward(q, k).wait_recv()
                add(q, k, right)

            rightward(q, k).start()

        @pl.when(j < tp)
        def _():
            @pl.when(tp < t - 1)
            def _():
                leftward(j, k).wait_recv()
                add(j, k, left)

            leftward(j, k).start()

        return c

    lax.fori_loop(0, chunks * (t - 1), step_of, 0)

    def last(k, c):
        @pl.when(tp == 0)
        def _():
            leftward(tp, k).wait_recv()
            finish(k, own[tp, part_of(k), :].astype(F32) + left[tp, part_of(k), :].astype(F32))

        @pl.when(tp == t - 1)
        def _():
            rightward(tp, k).wait_recv()
            finish(k, own[tp, part_of(k), :].astype(F32) + right[tp, part_of(k), :].astype(F32))

        @pl.when((tp > 0) & (tp < t - 1))
        def _():
            leftward(tp, k).wait_recv()
            rightward(tp, k).wait_recv()
            finish(
                k,
                own[tp, part_of(k), :].astype(F32)
                + left[tp, part_of(k), :].astype(F32)
                + right[tp, part_of(k), :].astype(F32),
            )

        return c

    lax.fori_loop(0, chunks, last, 0)

    def drain(i, c):
        k = i // (t - 1)
        j = lax.rem(i, t - 1)

        @pl.when(t - 1 - j > tp)
        def _():
            rightward(t - 1 - j, k).wait_send()

        @pl.when(j < tp)
        def _():
            leftward(j, k).wait_send()

        return c

    lax.fori_loop(0, chunks * (t - 1), drain, 0)


def mixer_forward(
    n, t, width,
    normed, x, w1, crow, gmid, valid, starts,
    ipre, fpre, opre, feff, states, gated, nmid, mixed, invst, invmid,
    prod, ssq, cslots, zslots, send, buf,
    cs, cr, zs, zr, s_in, s_out, r_buf,
):
    seq, tp = lax.axis_index("seq"), lax.axis_index("tp")
    greet_all(n, t, seq, tp)
    rows, depth = normed.shape
    chan = ipre.shape[1]
    tile = row_tile(rows)
    bias, sgain, bound = crow[0:1, :], crow[1:2, :], crow[2:3, :]

    def project(i, c):
        at = pl.ds(pl.multiple_of(i * tile, tile), tile)
        pre = nn(normed[at, :], w1[:, : 3 * chan])
        a = pre[:, :chan]
        f = pre[:, chan : 2 * chan] + bias
        ipre[at, :] = a
        fpre[at, :] = f
        opre[at, :] = pre[:, 2 * chan :]
        gate = bound + (1.0 - bound) * jax.nn.sigmoid(f)
        put(feff, at, gate * (1.0 - starts[at, :]))
        shifted = pl.ds(pl.multiple_of(i * tile + 8, 8), tile)
        put(states, shifted, a * jax.nn.sigmoid(a) * (1.0 - gate) * valid[at, :])
        return c

    lax.fori_loop(0, rows // tile, project, 0)
    put(feff, slice(rows, rows + 8), jnp.ones((8, chan), F32))

    length = rows // SEG

    def scan(i, c):
        p, h = c
        at, shifted = pl.ds(i, SEG, stride=length), pl.ds(i + 8, SEG, stride=length)
        f = get(feff, at)
        h = f * h + get(states, shifted)
        p = f * p
        put(states, shifted, h)
        put(prod, at, p)
        return p, h

    p, h = lax.fori_loop(
        0, length, scan, (jnp.ones((SEG, chan), F32), jnp.zeros((SEG, chan), F32))
    )
    block_p, block_h = p[0:1], h[0:1]
    for s in range(1, SEG):
        block_h = h[s : s + 1] + p[s : s + 1] * block_h
        block_p = p[s : s + 1] * block_p
    arriving = carry_over_seq(block_p, block_h, n, seq, tp, cslots, cs, cr, False)
    put(states, slice(0, 8), jnp.broadcast_to(arriving, (8, chan)))
    for s in range(SEG):
        at = slice(s * length, (s + 1) * length)
        shifted = slice(s * length + 8, (s + 1) * length + 8)
        whole = get(states, shifted) + get(prod, at) * arriving
        put(states, shifted, whole)
        ssq[at, :] = whole * whole
        arriving = h[s : s + 1] + p[s : s + 1] * arriving
    total = sum_over_tp(row_sums(ssq[...]), t, seq, tp, zslots, zs, zr)
    invst[...] = lax.rsqrt(total / width + EPS)

    def gating(i, c):
        at = pl.ds(pl.multiple_of(i * tile, tile), tile)
        shifted = pl.ds(pl.multiple_of(i * tile + 8, 8), tile)
        o = opre[at, :]
        gated[at, :] = (
            get(states, shifted) * invst[at, :] * sgain * (o * jax.nn.sigmoid(o))
        ).astype(BF)
        return c

    lax.fori_loop(0, rows // tile, gating, 0)

    step = rows // CHUNKS

    def partial(k):
        at = pl.ds(pl.multiple_of(k * step, step), step)
        return nt(gated[at, :], w1[:, 3 * chan :])

    def finish(k):
        at = pl.ds(pl.multiple_of(k * step, step), step)
        total = buf[1, at, :]
        mixed[at, :] = total
        resid = x[at, :].astype(F32) + total.astype(F32)
        inv = lax.rsqrt(jnp.mean(resid * resid, axis=-1, keepdims=True) + EPS)
        invmid[at, :] = inv
        nmid[at, :] = (resid * inv * gmid[...]).astype(BF)

    line_all_reduce(t, seq, tp, rows, CHUNKS, partial, send, buf, (s_in, s_out, r_buf), finish)


def feed_forward(
    nmid_h, cot_h, w2_h, gnm_h, glu_h, dw2_h,
    nmid, cot, wg, wu, wd, hid, gg, gu, gnm, glu, stage,
    s_w, s_a, s_o, s_d,
):
    rows, width = nmid.shape
    ff = wg.shape[1]
    tile = row_tile(rows)
    act_copies = [
        pltpu.make_async_copy(nmid_h, nmid, s_a.at[0]),
        pltpu.make_async_copy(cot_h, cot, s_a.at[1]),
    ]
    w_copies = [
        pltpu.make_async_copy(w2_h.at[:, pl.ds(j * ff, ff)], w, s_w.at[j])
        for j, w in enumerate((wg, wu, wd))
    ]
    for copy in (act_copies[0], w_copies[0], w_copies[1], act_copies[1], w_copies[2]):
        copy.start()
    for copy in (act_copies[0], w_copies[0], w_copies[1], act_copies[1], w_copies[2]):
        copy.wait()

    def out_copy(i, which):
        at = pl.ds(pl.multiple_of(i * tile, tile), tile)
        src, dst = ((gnm, gnm_h), (glu, glu_h))[which]
        return pltpu.make_async_copy(src.at[at], dst.at[at], s_o.at[which, i])

    def block(i, c):
        at = pl.ds(pl.multiple_of(i * tile, tile), tile)
        g = nn(nmid[at, :], wg[...])
        u = nn(nmid[at, :], wu[...])
        gh = nn(cot[at, :], wd[...])
        sig = jax.nn.sigmoid(g)
        act = g * sig
        hid[at, :] = (act * u).astype(BF)
        gg[at, :] = (gh * u * (sig * (1.0 + g * (1.0 - sig)))).astype(BF)
        gu[at, :] = (gh * act).astype(BF)
        gnm[at, :] = (nt(gg[at, :], wg[...]) + nt(gu[at, :], wu[...])).astype(BF)
        out_copy(i, 0).start()
        glu[at, :] = nt(hid[at, :], wd[...]).astype(BF)
        out_copy(i, 1).start()
        return c

    lax.fori_loop(0, rows // tile, block, 0)

    span = min(512, width)
    pieces = width // span

    def d_copy(i, slot):
        j = i // pieces
        r = lax.rem(i, pieces)
        return pltpu.make_async_copy(
            stage.at[slot],
            dw2_h.at[pl.ds(pl.multiple_of(r * span, span), span), pl.ds(pl.multiple_of(j * ff, LANE), ff)],
            s_d.at[slot],
        )

    for j, (left, right) in enumerate(((nmid, gg), (nmid, gu), (cot, hid))):

        def slab(r, c, j=j, left=left, right=right):
            i = j * pieces + r
            slot = lax.rem(i, 2)

            @pl.when(i >= 2)
            def _():
                d_copy(i - 2, slot).wait()

            at = pl.ds(pl.multiple_of(r * span, span), span)
            stage[slot] = tn(left[:, at], right[...]).astype(BF)
            d_copy(i, slot).start()
            return c

        lax.fori_loop(0, pieces, slab, 0)
    d_copy(3 * pieces - 2, (3 * pieces) % 2).wait()
    d_copy(3 * pieces - 1, (3 * pieces + 1) % 2).wait()

    def drain(i, c):
        out_copy(i, 0).wait()
        out_copy(i, 1).wait()
        return c

    lax.fori_loop(0, rows // tile, drain, 0)


def mid_backward(
    t, width,
    gnm_part, x, mixed, invmid, cot, gmid,
    gmix, gres, ggain,
    send, buf, wide, s_in, s_out, r_buf,
):
    seq, tp = lax.axis_index("seq"), lax.axis_index("tp")
    greet_line(t, seq, tp)
    rows = x.shape[0]
    chan = gres.shape[1]
    step = rows // CHUNKS
    ggain[...] = jnp.zeros_like(ggain)

    def partial(k):
        at = pl.ds(pl.multiple_of(k * step, step), step)
        return gnm_part[at, :].astype(F32)

    def finish(k):
        at = pl.ds(pl.multiple_of(k * step, step), step)
        g = buf[1, at, :].astype(F32)
        inv = invmid[at, :]
        hat = (x[at, :].astype(F32) + mixed[at, :].astype(F32)) * inv
        ggain[0:1, :] += jnp.sum(g * hat, axis=0, keepdims=True)
        e = g * gmid[...]
        mean = jnp.mean(e * hat, axis=-1, keepdims=True)
        out = cot[at, :].astype(F32) + inv * (e - hat * mean)
        wide[...] = out
        gmix[at, :] = out.astype(BF)
        gres[at, :] = wide[:, pl.ds(pl.multiple_of(tp * chan, LANE), chan)]

    line_all_reduce(t, seq, tp, rows, CHUNKS, partial, send, buf, (s_in, s_out, r_buf), finish)


def mixer_backward(
    n, t, width,
    gmix, normed, w1, gated, states, feff, ipre, fpre, opre, invst, valid, starts, crow,
    gni, dw1, vecs,
    grad, weighted, prod, inner, out3, cslots, zslots,
    cs, cr, zs, zr,
):
    seq, tp = lax.axis_index("seq"), lax.axis_index("tp")
    greet_all(n, t, seq, tp)
    rows = gmix.shape[0]
    chan = ipre.shape[1]
    tile = row_tile(rows)
    sgain, bound = crow[1:2, :], crow[2:3, :]
    vecs[...] = jnp.zeros_like(vecs)

    def gates(i, c):
        at = pl.ds(pl.multiple_of(i * tile, tile), tile)
        shifted = pl.ds(pl.multiple_of(i * tile + 8, 8), tile)
        g = nn(gmix[at, :], grad[...])
        hat = get(states, shifted) * invst[at, :]
        o = opre[at, :]
        sig = jax.nn.sigmoid(o)
        q = o * sig
        vecs[2:3, :] += jnp.sum(g * hat * q, axis=0, keepdims=True)
        out3[at, 2 * chan :] = (g * hat * sgain * (sig * (1.0 + o * (1.0 - sig)))).astype(BF)
        w = g * q * sgain
        put(weighted, at, w)
        inner[at, :] = w * hat
        return c

    grad[...] = w1[:, 3 * chan :]
    lax.fori_loop(0, rows // tile, gates, 0)
    dot = sum_over_tp(row_sums(inner[...]), t, seq, tp, zslots, zs, zr) / width
    inner[:, 0:1] = dot

    def leaving(i, c):
        at = pl.ds(pl.multiple_of(i * tile, tile), tile)
        shifted = pl.ds(pl.multiple_of(i * tile + 8, 8), tile)
        inv = invst[at, :]
        put(weighted, at, inv * (get(weighted, at) - get(states, shifted) * inv * inner[at, 0:1]))
        return c

    lax.fori_loop(0, rows // tile, leaving, 0)

    length = rows // SEG

    def scan(i, c):
        p, h = c
        r = length - 1 - i
        at = pl.ds(r, SEG, stride=length)
        f = get(feff, pl.ds(r + 1, SEG, stride=length))
        h = f * h + get(weighted, at)
        p = f * p
        put(weighted, at, h)
        put(prod, at, p)
        return p, h

    p, h = lax.fori_loop(
        0, length, scan, (jnp.ones((SEG, chan), F32), jnp.zeros((SEG, chan), F32))
    )
    block_p, block_h = p[SEG - 1 : SEG], h[SEG - 1 : SEG]
    for s in range(SEG - 2, -1, -1):
        block_h = h[s : s + 1] + p[s : s + 1] * block_h
        block_p = p[s : s + 1] * block_p
    first = get(feff, slice(0, 1))
    arriving = carry_over_seq(first * block_p, first * block_h, n, seq, tp, cslots, cs, cr, True)
    bias_sum = jnp.zeros((1, chan), F32)
    for s in range(SEG - 1, -1, -1):
        at = slice(s * length, (s + 1) * length)
        gs = get(weighted, at) + get(prod, at) * arriving
        arriving = h[s : s + 1] + p[s : s + 1] * arriving
        a = ipre[at, :]
        sa = jax.nn.sigmoid(a)
        act = a * sa
        sf = jax.nn.sigmoid(fpre[at, :])
        gate = bound + (1.0 - bound) * sf
        ok = valid[at, :]
        out3[at, :chan] = (gs * (1.0 - gate) * ok * (sa * (1.0 + a * (1.0 - sa)))).astype(BF)
        before = get(states, slice(s * length + 7, (s + 1) * length + 7))
        gate_grad = gs * before * (1.0 - starts[at, :]) - gs * act * ok
        gf = (gate_grad * (1.0 - bound) * sf * (1.0 - sf)).astype(BF)
        out3[at, chan : 2 * chan] = gf
        bias_sum = bias_sum + jnp.sum(gf.astype(F32), axis=0, keepdims=True)
    vecs[1:2, :] = bias_sum

    def spread_in(i, c):
        at = pl.ds(pl.multiple_of(i * tile, tile), tile)
        gni[at, :] = nt(out3[at, :], w1[:, : 3 * chan]).astype(BF)
        return c

    lax.fori_loop(0, rows // tile, spread_in, 0)

    span = 512

    def slab(r, c):
        at = pl.ds(pl.multiple_of(r * span, span), span)
        dw1[at, : 3 * chan] = tn(normed[:, at], out3[...]).astype(BF)
        dw1[at, 3 * chan :] = tn(gmix[:, at], gated[...]).astype(BF)
        return c

    lax.fori_loop(0, width // span, slab, 0)


def closing(
    n, t, width,
    glu_h, gni_h, x_h, mixed_h, gres, invin, valid, gain_in, vecs, ggain,
    out, gin, allvec,
    xc, mc, own_a, right_a, left_a, own_b, right_b, left_b, scaled, inner, zslots, vslots,
    s_x, s_own, sr_a, rr_a, sl_a, rl_a, sr_b, rr_b, sl_b, rl_b, zs, zr, vs, vr, ts, tr,
):
    seq, tp = lax.axis_index("seq"), lax.axis_index("tp")
    rows, chan = gres.shape
    mine = pl.ds(pl.multiple_of(tp * chan, LANE), chan)
    locals_ = [
        pltpu.make_async_copy(x_h.at[:, mine], xc, s_x.at[0]),
        pltpu.make_async_copy(mixed_h.at[:, mine], mc, s_x.at[1]),
    ]
    for q in range(t):
        locals_.append(pltpu.make_async_copy(glu_h.at[:, pl.ds(q * chan, chan)], own_a.at[q], s_own.at[0, q]))
        locals_.append(pltpu.make_async_copy(gni_h.at[:, pl.ds(q * chan, chan)], own_b.at[q], s_own.at[1, q]))
    for copy in locals_:
        copy.start()
    greet_all(n, t, seq, tp)
    for copy in locals_:
        copy.wait()
    half = CHUNKS // 2
    step = rows // half
    vslots[seq] = vecs[...]

    def finish_b(k, values):
        at = pl.ds(pl.multiple_of(k * step, step), step)
        hat = xc[at, :].astype(F32) * invin[at, :]
        s = values * gain_in[...]
        scaled[at, :] = s
        inner[at, :] = s * hat
        vslots[seq, 0:1, :] += jnp.sum(values * hat, axis=0, keepdims=True)

    def finish_a(k, values):
        at = pl.ds(pl.multiple_of(k * step, step), step)
        ok = valid[at, :]
        m = mc[at, :].astype(F32)
        full = xc[at, :].astype(F32) + m + values
        out[at, :] = full.astype(BF)
        vslots[seq, 4:5, :] += jnp.sum(ok * m * m, axis=0, keepdims=True)
        vslots[seq, 5:6, :] += jnp.sum(ok * values * values, axis=0, keepdims=True)
        vslots[seq, 6:7, :] += jnp.sum(ok * full * full, axis=0, keepdims=True)

    line_reduce_scatter(t, seq, tp, rows, half, own_b, right_b, left_b, (sr_b, rr_b, sl_b, rl_b), finish_b)
    line_reduce_scatter(t, seq, tp, rows, half, own_a, right_a, left_a, (sr_a, rr_a, sl_a, rl_a), finish_a)
    vslots[seq, 3:4, :] = ggain[0:1, :]
    dot = sum_over_tp(row_sums(inner[...]), t, seq, tp, zslots, zs, zr) / width
    gin[...] = gres[...] + invin[...] * (scaled[...] - xc[...].astype(F32) * invin[...] * dot)
    spread(n, seq, vslots, vs, vr, lambda k: (k, tp))
    total = vslots[0]
    for k in range(1, n):
        total = total + vslots[k]
    allvec[tp] = total
    spread(t, tp, allvec, ts, tr, lambda k: (seq, k))


DMA = pltpu.SemaphoreType.DMA


def params(collective=None, limit=VMEM_LIMIT):
    if collective is None:
        return pltpu.CompilerParams(vmem_limit_bytes=limit)
    return pltpu.CompilerParams(
        vmem_limit_bytes=limit, collective_id=collective, has_side_effects=True
    )


def line_sems(chunks):
    return [DMA((chunks,)), DMA((chunks,)), DMA((2, chunks))]


def on_device(
    n, t,
    hidden_in, gain_in, w_input, w_forget, forget_bias, w_outgate, state_gain, w_output,
    gain_mid, w_gate, w_up, w_down, lengths, layer_index, cotangent,
):
    rows, width = hidden_in.shape
    chan = w_input.shape[1]
    ff = w_gate.shape[1]
    ffp = -(-ff // LANE) * LANE
    tp = lax.axis_index("tp")
    offset = tp * chan

    def padded(w):
        return w if ffp == ff else jnp.pad(w, ((0, 0), (0, ffp - ff)))

    w1 = lax.all_gather(
        jnp.concatenate([w_input, w_forget, w_outgate, w_output.T], axis=1), "seq", axis=0, tiled=True
    )
    w2 = lax.all_gather(
        jnp.concatenate([padded(w_gate), padded(w_up), padded(w_down.T)], axis=1),
        "seq", axis=0, tiled=True,
    )

    positions = lax.axis_index("seq") * rows + jnp.arange(rows, dtype=jnp.int32)
    total = lengths[0] + lengths[1]
    valid = (positions < total).astype(F32)[:, None]
    starts = ((positions == 0) | (positions == lengths[0])).astype(F32)[:, None]
    bound = layer_index[0].astype(F32) / LAYERS
    inputs_f = hidden_in.astype(F32)
    inv_in = lax.rsqrt(jnp.mean(inputs_f * inputs_f, axis=-1, keepdims=True) + EPS)
    normed_in = (inputs_f * inv_in * gain_in.astype(F32)).astype(BF)

    def cols(vector):
        return lax.dynamic_slice_in_dim(vector, offset, chan, 0).astype(F32)

    crow = jnp.concatenate(
        [
            cols(forget_bias)[None],
            cols(state_gain)[None],
            jnp.broadcast_to(bound, (1, chan)),
            jnp.zeros((5, chan), F32),
        ],
        axis=0,
    )
    gmid = gain_mid.astype(F32)[None]
    plane = shape((rows, chan), F32)
    column = shape((rows, 1), F32)

    def groups(more=0):
        return shape((chan // LANE, rows + more, LANE), F32)

    wide16 = shape((rows, width), BF)

    ipre, fpre, opre, feff, states, gated, nmid, mixed, invst, invmid = pl.pallas_call(
        functools.partial(mixer_forward, n, t, width),
        out_shape=[
            plane, plane, plane,
            groups(8), groups(8),
            shape((rows, chan), BF), wide16, wide16, column, column,
        ],
        in_specs=[VM] * 7,
        out_specs=[VM] * 10,
        scratch_shapes=[
            pltpu.VMEM(groups().shape, F32),
            pltpu.VMEM((rows, chan), F32),
            pltpu.VMEM((n, 8, chan), F32),
            pltpu.VMEM((t, 8, rows), F32),
            pltpu.VMEM((rows, width), BF),
            pltpu.VMEM((2, rows, width), BF),
            DMA((n,)), DMA((n,)), DMA((t,)), DMA((t,)),
            *line_sems(CHUNKS),
        ],
        compiler_params=params(1),
        name="mixer_forward",
    )(normed_in, hidden_in, w1, crow, gmid, valid, starts)

    gnm_part, glu_part, dw2 = pl.pallas_call(
        feed_forward,
        out_shape=[wide16, wide16, shape((width, 3 * ffp), BF)],
        in_specs=[HB] * 3,
        out_specs=[HB] * 3,
        scratch_shapes=[
            pltpu.VMEM((rows, width), BF),
            pltpu.VMEM((rows, width), BF),
            pltpu.VMEM((width, ffp), BF),
            pltpu.VMEM((width, ffp), BF),
            pltpu.VMEM((width, ffp), BF),
            pltpu.VMEM((rows, ffp), BF),
            pltpu.VMEM((rows, ffp), BF),
            pltpu.VMEM((rows, ffp), BF),
            pltpu.VMEM((rows, width), BF),
            pltpu.VMEM((rows, width), BF),
            pltpu.VMEM((2, min(512, width), ffp), BF),
            DMA((3,)), DMA((2,)), DMA((2, rows // row_tile(rows))), DMA((2,)),
        ],
        compiler_params=params(),
        cost_estimate=pl.CostEstimate(
            flops=18 * rows * width * ffp, bytes_accessed=50_000_000, transcendentals=0
        ),
        name="feed_forward",
    )(nmid, cotangent, w2)

    sums2 = lax.psum_scatter(dw2, "seq", scatter_dimension=0, tiled=True)

    gmix, gres, ggain = pl.pallas_call(
        functools.partial(mid_backward, t, width),
        out_shape=[wide16, plane, shape((8, width), F32)],
        in_specs=[VM] * 6,
        out_specs=[VM] * 3,
        scratch_shapes=[
            pltpu.VMEM((rows, width), BF),
            pltpu.VMEM((2, rows, width), BF),
            pltpu.VMEM((rows // CHUNKS, width), F32),
            *line_sems(CHUNKS),
        ],
        compiler_params=params(2),
        name="mid_backward",
    )(gnm_part, hidden_in, mixed, invmid, cotangent, gmid)

    gni_part, dw1, vecs = pl.pallas_call(
        functools.partial(mixer_backward, n, t, width),
        out_shape=[wide16, shape((width, 4 * chan), BF), shape((8, chan), F32)],
        in_specs=[VM] * 13,
        out_specs=[VM] * 3,
        scratch_shapes=[
            pltpu.VMEM((width, chan), BF),
            pltpu.VMEM(groups().shape, F32),
            pltpu.VMEM(groups().shape, F32),
            pltpu.VMEM((rows, chan), F32),
            pltpu.VMEM((rows, 3 * chan), BF),
            pltpu.VMEM((n, 8, chan), F32),
            pltpu.VMEM((t, 8, rows), F32),
            DMA((n,)), DMA((n,)), DMA((t,)), DMA((t,)),
        ],
        compiler_params=params(3),
        name="mixer_backward",
    )(gmix, normed_in, w1, gated, states, feff, ipre, fpre, opre, invst, valid, starts, crow)

    sums1 = lax.psum_scatter(dw1, "seq", scatter_dimension=0, tiled=True)

    half = CHUNKS // 2
    shard_sems = [DMA((t, half))] * 4
    shard_bufs = [pltpu.VMEM((t, rows, chan), BF)] * 3
    ggain_cols = lax.dynamic_slice_in_dim(ggain, offset, chan, 1)
    block_out, grad_in, allvec = pl.pallas_call(
        functools.partial(closing, n, t, width),
        out_shape=[shape((rows, chan), BF), plane, shape((t, 8, chan), F32)],
        in_specs=[HB] * 4 + [VM] * 6,
        out_specs=[VM] * 3,
        scratch_shapes=[
            pltpu.VMEM((rows, chan), BF),
            pltpu.VMEM((rows, chan), BF),
            *shard_bufs,
            *shard_bufs,
            pltpu.VMEM((rows, chan), F32),
            pltpu.VMEM((rows, chan), F32),
            pltpu.VMEM((t, 8, rows), F32),
            pltpu.VMEM((n, 8, chan), F32),
            DMA((2,)), DMA((2, t)),
            *shard_sems,
            *shard_sems,
            DMA((t,)), DMA((t,)), DMA((n,)), DMA((n,)), DMA((t,)), DMA((t,)),
        ],
        compiler_params=params(4),
        name="closing",
    )(
        glu_part, gni_part, hidden_in, mixed, gres, inv_in, valid,
        cols(gain_in)[None], vecs, ggain_cols,
    )

    def vector(r):
        return allvec[:, r, :].reshape(width)

    squares = jnp.stack([jnp.sum(allvec[:, r, :]) for r in (4, 5, 6)])
    rms_stats = jnp.sqrt(squares / (total.astype(F32) * width))

    def piece(sums, j, size):
        return sums[:, j : j + size].astype(F32)

    return (
        block_out,
        grad_in,
        vector(0),
        piece(sums1, 0, chan),
        piece(sums1, chan, chan),
        vector(1),
        piece(sums1, 2 * chan, chan),
        vector(2),
        piece(sums1, 3 * chan, chan).T,
        vector(3),
        piece(sums2, 0, ff),
        piece(sums2, ffp, ff),
        piece(sums2, 2 * ffp, ff).T,
        rms_stats,
    )


def solution(mesh):
    weight, turned = P("seq", "tp"), P("tp", "seq")
    in_specs = (
        P("seq", None), P(), weight, weight, P(), weight, P(), turned, P(), weight, weight, turned,
        P(), P(), P("seq", None),
    )
    out_specs = (
        weight, weight, P(), weight, weight, P(), weight, P(), turned, P(), weight, weight, turned, P(),
    )
    body = functools.partial(on_device, mesh.shape["seq"], mesh.shape["tp"])
    return jax.shard_map(
        body, mesh=mesh, in_specs=in_specs, out_specs=out_specs, check_vma=False
    )
```

```python
import functools

import jax
import jax.numpy as jnp
from jax import lax
from jax.experimental import pallas as pl
from jax.experimental.pallas import tpu as pltpu
from jax.sharding import PartitionSpec as P

LAYERS = 24
EPS = 1e-06
MESH = pl.DeviceIdType.MESH
DMA = pltpu.SemaphoreType.DMA
BF = jnp.bfloat16
F32 = jnp.float32
VM = pl.BlockSpec(memory_space=pltpu.VMEM)
HB = pl.BlockSpec(memory_space=pl.ANY)
LANE = 128
SEG = 8
CHUNKS = 16
SHARD_CHUNKS = 4
ROUND_TRIP = 3
VMEM_LIMIT = 60 * 1024 * 1024


def nn(left, right):
    return jnp.dot(left, right, preferred_element_type=F32)


def nt(left, right):
    return lax.dot_general(left, right, (((1,), (1,)), ((), ())), preferred_element_type=F32)


def tn(left, right):
    return lax.dot_general(left, right, (((0,), (0,)), ((), ())), preferred_element_type=F32)


def shape(dims, dtype):
    return jax.ShapeDtypeStruct(dims, dtype)


def get(ref, at):
    return jnp.concatenate([ref[g, at, :] for g in range(ref.shape[0])], axis=1)


def put(ref, at, values):
    for g in range(ref.shape[0]):
        ref[g, at, :] = values[:, g * LANE : (g + 1) * LANE]


def put_shards(ref, at, values):
    k = ref.shape[2]
    for q in range(ref.shape[0]):
        ref[q, at, :] = values[:, q * k : (q + 1) * k]


def put_blocks(ref, h, values):
    for core in range(2):
        for half in range(2):
            first = (core * 2 + half) * h
            ref[core, half] = values[first : first + h].astype(ref.dtype)


def row_tile(rows):
    return rows // 3 if rows % 48 == 0 else rows


def greet_all(n, t, seq, tp):
    barrier = pltpu.get_barrier_semaphore()

    def along_seq(o, c):
        pl.semaphore_signal(barrier, inc=1, device_id=(lax.rem(seq + o, n), tp), device_id_type=MESH)
        return c

    def along_tp(o, c):
        pl.semaphore_signal(barrier, inc=1, device_id=(seq, lax.rem(tp + o, t)), device_id_type=MESH)
        return c

    lax.fori_loop(1, n, along_seq, 0)
    lax.fori_loop(1, t, along_tp, 0)
    pl.semaphore_wait(barrier, n - 1 + t - 1)


def greet_line(t, seq, tp):
    barrier = pltpu.get_barrier_semaphore()

    def along_tp(o, c):
        pl.semaphore_signal(barrier, inc=1, device_id=(seq, lax.rem(tp + o, t)), device_id_type=MESH)
        return c

    lax.fori_loop(1, t, along_tp, 0)
    pl.semaphore_wait(barrier, t - 1)


def spread(size, me, slots, send, recv, target):
    def copy(o, slot):
        return pltpu.make_async_remote_copy(
            src_ref=slots.at[slot],
            dst_ref=slots.at[slot],
            send_sem=send.at[o],
            recv_sem=recv.at[slot],
            device_id=target(lax.rem(me + o, size)),
            device_id_type=MESH,
        )

    def go(o, c):
        copy(o, me).start()
        return c

    def done(o, c):
        copy(o, lax.rem(me + o, size)).wait_recv()
        return c

    def sent(o, c):
        copy(o, me).wait_send()
        return c

    lax.fori_loop(1, size, go, 0)
    lax.fori_loop(1, size, done, 0)
    lax.fori_loop(1, size, sent, 0)


def row_sums(values):
    ones = jnp.ones((8, values.shape[1]), BF)
    high = values.astype(BF)
    rest = values - high.astype(F32)
    low = rest.astype(BF)
    return nt(ones, high) + nt(ones, low)


def sum_over_tp(part, t, seq, tp, slots, send, recv):
    slots[tp] = part
    spread(t, tp, slots, send, recv, lambda k: (seq, k))
    total = slots[0]
    for k in range(1, t):
        total = total + slots[k]
    return jnp.transpose(total)[:, :1]


def carry_over_seq(prod, state, n, seq, tp, slots, send, recv, backward):
    slots[seq] = jnp.concatenate([prod, state] + [jnp.zeros_like(prod)] * 6, axis=0)
    spread(n, seq, slots, send, recv, lambda k: (k, tp))

    def hop(i, total):
        j = n - 1 - i if backward else i
        block = slots[j]
        longer = block[1:2] + block[0:1] * total
        inside = (j > seq) if backward else (j < seq)
        return jnp.where(inside, longer, total)

    return lax.fori_loop(0, n, hop, jnp.zeros_like(prod))


def line_all_reduce(t, seq, tp, rows, chunks, partial, send, buf, sems, finish, beside=None):
    s_in, s_out, r_buf = sems
    step = rows // chunks
    half = t // 2
    depth = jnp.where(tp < half, tp, t - 1 - tp)
    inner = jnp.where(tp < half, tp + 1, tp - 1)
    outer = jnp.where(tp < half, tp - 1, tp + 1)
    outer = jnp.where(depth > 0, outer, inner)
    middle = (depth == half - 1).astype(jnp.int32)

    def part_of(k):
        return pl.ds(pl.multiple_of(k * step, step), step)

    def inward(k, slot):
        return pltpu.make_async_remote_copy(
            src_ref=send.at[part_of(k)],
            dst_ref=buf.at[slot, part_of(k)],
            send_sem=s_in.at[k],
            recv_sem=r_buf.at[slot, k],
            device_id=(seq, inner),
            device_id_type=MESH,
        )

    def outward(k):
        return pltpu.make_async_remote_copy(
            src_ref=buf.at[1, part_of(k)],
            dst_ref=buf.at[1, part_of(k)],
            send_sem=s_out.at[k],
            recv_sem=r_buf.at[1, k],
            device_id=(seq, outer),
            device_id_type=MESH,
        )

    def first(k):
        part = partial(k)

        @pl.when(depth > 0)
        def _():
            inward(k, 0).wait_recv()
            send[part_of(k), :] = (part + buf[0, part_of(k), :].astype(F32)).astype(BF)

        @pl.when(depth == 0)
        def _():
            send[part_of(k), :] = part.astype(BF)

        inward(k, middle).start()

    def second(k):
        inward(k, 1).wait_recv()

        @pl.when(middle == 1)
        def _():
            both = send[part_of(k), :].astype(F32) + buf[1, part_of(k), :].astype(F32)
            buf[1, part_of(k), :] = both.astype(BF)

        @pl.when(depth > 0)
        def _():
            outward(k).start()

        finish(k)

    lag = 1 + ROUND_TRIP * (half - 1 - depth)

    def both(k, c):
        @pl.when(k < chunks)
        def _():
            first(k)

        @pl.when((k >= lag) & (k - lag < chunks))
        def _():
            second(k - lag)

        if beside is not None:
            beside(k)
        return c

    lax.fori_loop(0, chunks + 1 + ROUND_TRIP * (half - 1), both, 0)

    def drain(k, c):
        inward(k, middle).wait_send()

        @pl.when(depth > 0)
        def _():
            outward(k).wait_send()

        return c

    lax.fori_loop(0, chunks, drain, 0)


def line_reduce_scatter(t, seq, tp, own, inbox, sems, finish):
    s_r, r_r, s_l, r_l = sems
    rows = own.shape[1]
    chunks = SHARD_CHUNKS
    step = rows // chunks

    def part_of(k):
        return pl.ds(pl.multiple_of(k * step, step), step)

    def rightward(q, k):
        return pltpu.make_async_remote_copy(
            src_ref=own.at[q, part_of(k)],
            dst_ref=inbox.at[q + 1, part_of(k)],
            send_sem=s_r.at[q, k],
            recv_sem=r_r.at[q, k],
            device_id=(seq, lax.rem(tp + 1, t)),
            device_id_type=MESH,
        )

    def leftward(q, k):
        return pltpu.make_async_remote_copy(
            src_ref=own.at[q, part_of(k)],
            dst_ref=inbox.at[q, part_of(k)],
            send_sem=s_l.at[q, k],
            recv_sem=r_l.at[q, k],
            device_id=(seq, lax.rem(tp + t - 1, t)),
            device_id_type=MESH,
        )

    def add(q, k, slot):
        own[q, part_of(k), :] = (
            own[q, part_of(k), :].astype(F32) + inbox[slot, part_of(k), :].astype(F32)
        ).astype(BF)

    def step_of(i):
        k = i // (t - 1)
        j = lax.rem(i, t - 1)

        @pl.when(t - 1 - j > tp)
        def _():
            q = t - 1 - j

            @pl.when(tp > 0)
            def _():
                rightward(q, k).wait_recv()
                add(q, k, q + 1)

            rightward(q, k).start()

        @pl.when(j < tp)
        def _():
            @pl.when(tp < t - 1)
            def _():
                leftward(j, k).wait_recv()
                add(j, k, j)

            leftward(j, k).start()

    def last(k):
        @pl.when(tp == 0)
        def _():
            leftward(tp, k).wait_recv()
            finish(k, own[tp, part_of(k), :].astype(F32) + inbox[tp, part_of(k), :].astype(F32))

        @pl.when(tp == t - 1)
        def _():
            rightward(tp, k).wait_recv()
            finish(k, own[tp, part_of(k), :].astype(F32) + inbox[tp + 1, part_of(k), :].astype(F32))

        @pl.when((tp > 0) & (tp < t - 1))
        def _():
            leftward(tp, k).wait_recv()
            rightward(tp, k).wait_recv()
            finish(
                k,
                own[tp, part_of(k), :].astype(F32)
                + inbox[tp, part_of(k), :].astype(F32)
                + inbox[tp + 1, part_of(k), :].astype(F32),
            )

    def drain():
        def sent(i, c):
            k = i // (t - 1)
            j = lax.rem(i, t - 1)

            @pl.when(t - 1 - j > tp)
            def _():
                rightward(t - 1 - j, k).wait_send()

            @pl.when(j < tp)
            def _():
                leftward(j, k).wait_send()

            return c

        lax.fori_loop(0, chunks * (t - 1), sent, 0)

    return chunks * (t - 1), step_of, last, drain


def chip_grid(n):
    chips = n // 2
    b = max(k for k in range(1, chips + 1) if chips % k == 0 and k * k <= chips)
    return chips // b, b


def grid_buffers(n, width, pieces, cols):
    ga, gb = chip_grid(n)
    h = width // n // 2
    pa, pb = max(ga - 1, 1), max(gb - 1, 1)
    return [
        pltpu.VMEM((pieces, 2, ga, gb, h, cols), BF),
        pltpu.VMEM((pieces, 2, ga, gb, h, cols), BF),
        pltpu.VMEM((pieces, pb, ga, h, cols), BF),
        pltpu.VMEM((pieces, pa, gb, h, cols), BF),
        pltpu.VMEM((pieces, pa, h, cols), BF),
        pltpu.VMEM((pieces, pb, h, cols), BF),
        DMA((pieces,)), DMA((pieces,)), DMA((pieces,)),
        DMA((2, pieces, pb)), DMA((2, pieces, pa)), DMA((2, pieces, pa)), DMA((2, pieces, pb)),
    ]


def grid_reduce(n, seq, tp, terms, pieces, cols, bufs, out):
    acc, first, far_b, far_a, near_a, near_b, s_own, s_f, r_f, m_fb, m_fa, m_na, m_nb = bufs
    ga, gb = chip_grid(n)
    core = lax.rem(seq, 2)
    a, b = seq // 2 // gb, lax.rem(seq // 2, gb)

    def device(a_, b_, core_):
        return ((a_ * gb + b_) * 2 + core_, tp)

    def columns(j):
        return pl.ds(j * cols, cols)

    def load(j):
        return pltpu.make_async_copy(
            terms.at[core, :, :, :, :, columns(j)], acc.at[j], s_own.at[j]
        )

    def swap(j):
        return pltpu.make_async_remote_copy(
            src_ref=terms.at[1 - core, :, :, :, :, columns(j)],
            dst_ref=first.at[j],
            send_sem=s_f.at[j],
            recv_sem=r_f.at[j],
            device_id=device(a, b, 1 - core),
            device_id_type=MESH,
        )

    def remote(src, dst, sems, j, o, target):
        return pltpu.make_async_remote_copy(
            src_ref=src,
            dst_ref=dst,
            send_sem=sems.at[0, j, o],
            recv_sem=sems.at[1, j, o],
            device_id=target,
            device_id_type=MESH,
        )

    def far(j):
        copies = []
        for o in range(1, gb):
            to = lax.rem(b + o, gb)
            copies.append(
                remote(acc.at[j, 0, :, to], far_b.at[j, o - 1], m_fb, j, o - 1, device(a, to, core))
            )
        for o in range(1, ga):
            to = lax.rem(a + o, ga)
            copies.append(
                remote(acc.at[j, 1, to], far_a.at[j, o - 1], m_fa, j, o - 1, device(to, b, core))
            )
        return copies

    def near(j):
        copies = []
        for o in range(1, ga):
            to = lax.rem(a + o, ga)
            copies.append(
                remote(acc.at[j, 0, to, b], near_a.at[j, o - 1], m_na, j, o - 1, device(to, b, core))
            )
        for o in range(1, gb):
            to = lax.rem(b + o, gb)
            copies.append(
                remote(acc.at[j, 1, a, to], near_b.at[j, o - 1], m_nb, j, o - 1, device(a, to, core))
            )
        return copies

    def start(j):
        load(j).start()
        swap(j).start()

    def stage1(j):
        load(j).wait()
        swap(j).wait_recv()

        def chip(i, c):
            x, y = i // gb, lax.rem(i, gb)
            for half in range(2):
                acc[j, half, x, y] = (
                    acc[j, half, x, y].astype(F32) + first[j, half, x, y].astype(F32)
                ).astype(BF)
            return c

        lax.fori_loop(0, ga * gb, chip, 0)
        for copy in far(j):
            copy.start()

    def stage2(j):
        for copy in far(j):
            copy.wait_recv()

        def along_a(x, c):
            total = acc[j, 0, x, b].astype(F32)
            for o in range(1, gb):
                total = total + far_b[j, o - 1, x].astype(F32)
            acc[j, 0, x, b] = total.astype(BF)
            return c

        def along_b(y, c):
            total = acc[j, 1, a, y].astype(F32)
            for o in range(1, ga):
                total = total + far_a[j, o - 1, y].astype(F32)
            acc[j, 1, a, y] = total.astype(BF)
            return c

        lax.fori_loop(0, ga, along_a, 0)
        lax.fori_loop(0, gb, along_b, 0)
        for copy in near(j):
            copy.start()

    def stage3(j):
        for copy in near(j):
            copy.wait_recv()
        total = acc[j, 0, a, b].astype(F32)
        for o in range(1, ga):
            total = total + near_a[j, o - 1].astype(F32)
        out(j, 0, total)
        total = acc[j, 1, a, b].astype(F32)
        for o in range(1, gb):
            total = total + near_b[j, o - 1].astype(F32)
        out(j, 1, total)

    def drain():
        for j in range(pieces):
            swap(j).wait_send()
            for copy in far(j) + near(j):
                copy.wait_send()

    return start, stage1, stage2, stage3, drain


def mixer_forward(
    n, t, width,
    normed, x, w1, crow, gmid, valid, starts,
    ipre, fpre, opre, feff, states, gated, nmid, mixed, invst, invmid,
    prod, ssq, part, cslots, zslots, send, buf,
    cs, cr, zs, zr, s_in, s_out, r_buf,
):
    seq, tp = lax.axis_index("seq"), lax.axis_index("tp")
    greet_all(n, t, seq, tp)
    rows, depth = normed.shape
    chan = ipre.shape[1]
    tile = row_tile(rows)
    bias, sgain, bound = crow[0:1, :], crow[1:2, :], crow[2:3, :]

    def project(i, c):
        at = pl.ds(pl.multiple_of(i * tile, tile), tile)
        pre = nn(normed[at, :], w1[:, : 3 * chan])
        a = pre[:, :chan]
        f = pre[:, chan : 2 * chan] + bias
        ipre[at, :] = a
        fpre[at, :] = f
        opre[at, :] = pre[:, 2 * chan :]
        gate = bound + (1.0 - bound) * jax.nn.sigmoid(f)
        put(feff, at, gate * (1.0 - starts[at, :]))
        shifted = pl.ds(pl.multiple_of(i * tile + 8, 8), tile)
        put(states, shifted, a * jax.nn.sigmoid(a) * (1.0 - gate) * valid[at, :])
        return c

    lax.fori_loop(0, rows // tile, project, 0)
    put(feff, slice(rows, rows + 8), jnp.ones((8, chan), F32))

    length = rows // SEG

    def scan(i, c):
        p, h = c
        at, shifted = pl.ds(i, SEG, stride=length), pl.ds(i + 8, SEG, stride=length)
        f = get(feff, at)
        h = f * h + get(states, shifted)
        p = f * p
        put(states, shifted, h)
        put(prod, at, p)
        return p, h

    p, h = lax.fori_loop(
        0, length, scan, (jnp.ones((SEG, chan), F32), jnp.zeros((SEG, chan), F32))
    )
    block_p, block_h = p[0:1], h[0:1]
    for s in range(1, SEG):
        block_h = h[s : s + 1] + p[s : s + 1] * block_h
        block_p = p[s : s + 1] * block_p
    arriving = carry_over_seq(block_p, block_h, n, seq, tp, cslots, cs, cr, False)
    put(states, slice(0, 8), jnp.broadcast_to(arriving, (8, chan)))
    for s in range(SEG):
        at = slice(s * length, (s + 1) * length)
        shifted = slice(s * length + 8, (s + 1) * length + 8)
        whole = get(states, shifted) + get(prod, at) * arriving
        put(states, shifted, whole)
        ssq[at, :] = whole * whole
        arriving = h[s : s + 1] + p[s : s + 1] * arriving
    total = sum_over_tp(row_sums(ssq[...]), t, seq, tp, zslots, zs, zr)
    invst[...] = lax.rsqrt(total / width + EPS)

    def gating(i, c):
        at = pl.ds(pl.multiple_of(i * tile, tile), tile)
        shifted = pl.ds(pl.multiple_of(i * tile + 8, 8), tile)
        o = opre[at, :]
        gated[at, :] = (
            get(states, shifted) * invst[at, :] * sgain * (o * jax.nn.sigmoid(o))
        ).astype(BF)
        return c

    lax.fori_loop(0, rows // tile, gating, 0)

    step = rows // CHUNKS

    group = part.shape[0] // step

    def partial(k):
        @pl.when(lax.rem(k, group) == 0)
        def _():
            big = pl.ds(pl.multiple_of(k * step, step), step * group)
            part[...] = nt(gated[big, :], w1[:, 3 * chan :])

        return part[pl.ds(pl.multiple_of(lax.rem(k, group) * step, step), step), :]

    def finish(k):
        at = pl.ds(pl.multiple_of(k * step, step), step)
        total = buf[1, at, :]
        mixed[at, :] = total
        resid = x[at, :].astype(F32) + total.astype(F32)
        inv = lax.rsqrt(jnp.mean(resid * resid, axis=-1, keepdims=True) + EPS)
        invmid[at, :] = inv
        nmid[at, :] = (resid * inv * gmid[...]).astype(BF)

    line_all_reduce(t, seq, tp, rows, CHUNKS, partial, send, buf, (s_in, s_out, r_buf), finish)


def feed_forward(
    nmid_h, cot_h, w2_h, gnm_h, glu_h, dw2_h,
    nmid, cot, wg, wu, wd, hid, gg, gu, gnm, glu, stage,
    s_w, s_a, s_o, s_d,
):
    rows, width = nmid.shape
    ff = wg.shape[1]
    tile = row_tile(rows)
    act_copies = [
        pltpu.make_async_copy(nmid_h, nmid, s_a.at[0]),
        pltpu.make_async_copy(cot_h, cot, s_a.at[1]),
    ]
    w_copies = [
        pltpu.make_async_copy(w2_h.at[:, pl.ds(j * ff, ff)], w, s_w.at[j])
        for j, w in enumerate((wg, wu, wd))
    ]
    for copy in (act_copies[0], w_copies[0], w_copies[1], act_copies[1], w_copies[2]):
        copy.start()
    for copy in (act_copies[0], w_copies[0], w_copies[1], act_copies[1], w_copies[2]):
        copy.wait()

    def out_copy(i, which):
        at = pl.ds(pl.multiple_of(i * tile, tile), tile)
        if which == 0:
            return pltpu.make_async_copy(gnm.at[at], gnm_h.at[at], s_o.at[0, i])
        return pltpu.make_async_copy(glu.at[:, at], glu_h.at[:, at], s_o.at[1, i])

    def block(i, c):
        at = pl.ds(pl.multiple_of(i * tile, tile), tile)
        g = nn(nmid[at, :], wg[...])
        u = nn(nmid[at, :], wu[...])
        gh = nn(cot[at, :], wd[...])
        sig = jax.nn.sigmoid(g)
        act = g * sig
        hid[at, :] = (act * u).astype(BF)
        gg[at, :] = (gh * u * (sig * (1.0 + g * (1.0 - sig)))).astype(BF)
        gu[at, :] = (gh * act).astype(BF)
        gnm[at, :] = (nt(gg[at, :], wg[...]) + nt(gu[at, :], wu[...])).astype(BF)
        out_copy(i, 0).start()
        put_shards(glu, at, nt(hid[at, :], wd[...]).astype(BF))
        out_copy(i, 1).start()
        return c

    lax.fori_loop(0, rows // tile, block, 0)

    ga, gb, h = dw2_h.shape[2:5]
    span = 4 * h
    pieces = ga * gb

    def d_copy(i, slot):
        j = i // pieces
        r = lax.rem(i, pieces)
        return pltpu.make_async_copy(
            stage.at[slot],
            dw2_h.at[:, :, r // gb, lax.rem(r, gb), :, pl.ds(pl.multiple_of(j * ff, LANE), ff)],
            s_d.at[slot],
        )

    for j, (left, right) in enumerate(((nmid, gg), (nmid, gu), (cot, hid))):

        def slab(r, c, j=j, left=left, right=right):
            i = j * pieces + r
            slot = lax.rem(i, 2)

            @pl.when(i >= 2)
            def _():
                d_copy(i - 2, slot).wait()

            at = pl.ds(pl.multiple_of(r * span, span), span)
            put_blocks(stage.at[slot], h, tn(left[:, at], right[...]))
            d_copy(i, slot).start()
            return c

        lax.fori_loop(0, pieces, slab, 0)
    d_copy(3 * pieces - 2, (3 * pieces) % 2).wait()
    d_copy(3 * pieces - 1, (3 * pieces + 1) % 2).wait()

    def drain(i, c):
        out_copy(i, 0).wait()
        out_copy(i, 1).wait()
        return c

    lax.fori_loop(0, rows // tile, drain, 0)


def mid_backward(
    n, t, width,
    gnm_h, dw2_h, x, mixed, invmid, cot, gmid,
    gmix, gres, ggain, sums,
    send, buf, wide, s_g, s_in, s_out, r_buf, *bufs,
):
    seq, tp = lax.axis_index("seq"), lax.axis_index("tp")
    load = pltpu.make_async_copy(gnm_h, send, s_g)
    load.start()
    greet_all(n, t, seq, tp)
    rows = x.shape[0]
    chan = gres.shape[1]
    step = rows // CHUNKS
    pieces, shard, cols = sums.shape
    ggain[...] = jnp.zeros_like(ggain)

    def out(j, half, values):
        sums[j, half * (shard // 2) : (half + 1) * (shard // 2), :] = values

    start, stage1, stage2, stage3, drain = grid_reduce(n, seq, tp, dw2_h, pieces, cols, bufs, out)
    start(0)
    load.wait()

    def partial(k):
        at = pl.ds(pl.multiple_of(k * step, step), step)
        return send[at, :].astype(F32)

    def finish(k):
        at = pl.ds(pl.multiple_of(k * step, step), step)
        g = buf[1, at, :].astype(F32)
        inv = invmid[at, :]
        hat = (x[at, :].astype(F32) + mixed[at, :].astype(F32)) * inv
        ggain[0:1, :] += jnp.sum(g * hat, axis=0, keepdims=True)
        e = g * gmid[...]
        mean = jnp.mean(e * hat, axis=-1, keepdims=True)
        out = cot[at, :].astype(F32) + inv * (e - hat * mean)
        wide[...] = out
        gmix[at, :] = out.astype(BF)
        gres[at, :] = wide[:, pl.ds(pl.multiple_of(tp * chan, LANE), chan)]

    turns = [
        (1, lambda: (stage1(0), start(1))),
        (4, lambda: (stage1(1), start(2))),
        (5, lambda: stage2(0)),
        (8, lambda: stage1(2)),
        (9, lambda: stage3(0)),
        (10, lambda: stage2(1)),
        (13, lambda: stage3(1)),
        (14, lambda: stage2(2)),
        (16, lambda: stage3(2)),
    ]

    def beside(k):
        for turn, work in turns:

            @pl.when(k == turn)
            def _(work=work):
                work()

    line_all_reduce(
        t, seq, tp, rows, CHUNKS, partial, send, buf, (s_in, s_out, r_buf), finish, beside
    )
    drain()


def mixer_backward(
    n, t, width,
    glu_h, x_h, mixed_h,
    gmix, normed, w1, gated, states, feff, ipre, fpre, opre, invst, valid, starts, crow,
    gni_h, dw1_h, vecs, out,
    weighted, prod, inner, out3, cslots, zslots, xc, mc, own, inbox, gni, stage,
    cs, cr, zs, zr, s_x, sr, rr, sl, rl, s_o, s_d,
):
    seq, tp = lax.axis_index("seq"), lax.axis_index("tp")
    rows = gmix.shape[0]
    chan = ipre.shape[1]
    mine = pl.ds(pl.multiple_of(tp * chan, LANE), chan)
    fetches = [
        pltpu.make_async_copy(glu_h, own, s_x.at[0]),
        pltpu.make_async_copy(x_h.at[:, mine], xc, s_x.at[1]),
        pltpu.make_async_copy(mixed_h.at[:, mine], mc, s_x.at[2]),
    ]
    for copy in fetches:
        copy.start()
    greet_all(n, t, seq, tp)
    tile = row_tile(rows)
    sgain, bound = crow[1:2, :], crow[2:3, :]
    vecs[...] = jnp.zeros_like(vecs)
    for copy in fetches:
        copy.wait()
    step = rows // SHARD_CHUNKS

    def finish(k, values):
        at = pl.ds(pl.multiple_of(k * step, step), step)
        ok = valid[at, :]
        m = mc[at, :].astype(F32)
        full = xc[at, :].astype(F32) + m + values
        out[at, :] = full.astype(BF)
        vecs[4:5, :] += jnp.sum(ok * m * m, axis=0, keepdims=True)
        vecs[5:6, :] += jnp.sum(ok * values * values, axis=0, keepdims=True)
        vecs[6:7, :] += jnp.sum(ok * full * full, axis=0, keepdims=True)

    steps, step_of, last, drain = line_reduce_scatter(t, seq, tp, own, inbox, (sr, rr, sl, rl), finish)

    def pump(slot):
        def one(i, c):
            step_of(i)
            return c

        lax.fori_loop(slot * steps // 12, (slot + 1) * steps // 12, one, 0)

    def gates(i, c):
        at = pl.ds(pl.multiple_of(i * tile, tile), tile)
        shifted = pl.ds(pl.multiple_of(i * tile + 8, 8), tile)
        pump(i)
        g = nn(gmix[at, :], w1[:, 3 * chan :])
        hat = get(states, shifted) * invst[at, :]
        o = opre[at, :]
        sig = jax.nn.sigmoid(o)
        q = o * sig
        vecs[2:3, :] += jnp.sum(g * hat * q, axis=0, keepdims=True)
        out3[at, 2 * chan :] = (g * hat * sgain * (sig * (1.0 + o * (1.0 - sig)))).astype(BF)
        w = g * q * sgain
        put(weighted, at, w)
        inner[at, :] = w * hat
        return c

    lax.fori_loop(0, rows // tile, gates, 0)
    dot = sum_over_tp(row_sums(inner[...]), t, seq, tp, zslots, zs, zr) / width
    inner[:, 0:1] = dot
    pump(rows // tile)

    def leaving(i, c):
        at = pl.ds(pl.multiple_of(i * tile, tile), tile)
        shifted = pl.ds(pl.multiple_of(i * tile + 8, 8), tile)
        inv = invst[at, :]
        put(weighted, at, inv * (get(weighted, at) - get(states, shifted) * inv * inner[at, 0:1]))
        return c

    lax.fori_loop(0, rows // tile, leaving, 0)

    length = rows // SEG

    def scan(i, c):
        p, h = c
        r = length - 1 - i
        at = pl.ds(r, SEG, stride=length)
        f = get(feff, pl.ds(r + 1, SEG, stride=length))
        h = f * h + get(weighted, at)
        p = f * p
        put(weighted, at, h)
        put(prod, at, p)
        return p, h

    p, h = lax.fori_loop(
        0, length, scan, (jnp.ones((SEG, chan), F32), jnp.zeros((SEG, chan), F32))
    )
    block_p, block_h = p[SEG - 1 : SEG], h[SEG - 1 : SEG]
    for s in range(SEG - 2, -1, -1):
        block_h = h[s : s + 1] + p[s : s + 1] * block_h
        block_p = p[s : s + 1] * block_p
    pump(rows // tile + 1)
    first = get(feff, slice(0, 1))
    arriving = carry_over_seq(first * block_p, first * block_h, n, seq, tp, cslots, cs, cr, True)
    bias_sum = jnp.zeros((1, chan), F32)
    for s in range(SEG - 1, -1, -1):
        at = slice(s * length, (s + 1) * length)
        gs = get(weighted, at) + get(prod, at) * arriving
        arriving = h[s : s + 1] + p[s : s + 1] * arriving
        a = ipre[at, :]
        sa = jax.nn.sigmoid(a)
        act = a * sa
        sf = jax.nn.sigmoid(fpre[at, :])
        gate = bound + (1.0 - bound) * sf
        ok = valid[at, :]
        out3[at, :chan] = (gs * (1.0 - gate) * ok * (sa * (1.0 + a * (1.0 - sa)))).astype(BF)
        before = get(states, slice(s * length + 7, (s + 1) * length + 7))
        gate_grad = gs * before * (1.0 - starts[at, :]) - gs * act * ok
        gf = (gate_grad * (1.0 - bound) * sf * (1.0 - sf)).astype(BF)
        out3[at, chan : 2 * chan] = gf
        bias_sum = bias_sum + jnp.sum(gf.astype(F32), axis=0, keepdims=True)
        if s % 2 == 0:
            pump(rows // tile + 5 - s // 2)
    vecs[1:2, :] = bias_sum

    def gni_copy(i):
        at = pl.ds(pl.multiple_of(i * tile, tile), tile)
        return pltpu.make_async_copy(gni.at[:, at], gni_h.at[:, at], s_o.at[i])

    def spread_in(i, c):
        at = pl.ds(pl.multiple_of(i * tile, tile), tile)
        put_shards(gni, at, nt(out3[at, :], w1[:, : 3 * chan]).astype(BF))
        gni_copy(i).start()
        pump(12 - rows // tile + i)
        return c

    lax.fori_loop(0, rows // tile, spread_in, 0)

    ga, gb, h = dw1_h.shape[2:5]
    span = 4 * h

    def d_copy(r, slot):
        return pltpu.make_async_copy(
            stage.at[slot], dw1_h.at[:, :, r // gb, lax.rem(r, gb)], s_d.at[slot]
        )

    def slab(r, c):
        slot = lax.rem(r, 2)

        @pl.when(r >= 2)
        def _():
            d_copy(r - 2, slot).wait()

        at = pl.ds(pl.multiple_of(r * span, span), span)
        put_blocks(stage.at[slot, :, :, :, pl.ds(0, 3 * chan)], h, tn(normed[:, at], out3[...]))
        put_blocks(stage.at[slot, :, :, :, pl.ds(3 * chan, chan)], h, tn(gmix[:, at], gated[...]))
        d_copy(r, slot).start()
        return c

    lax.fori_loop(0, ga * gb, slab, 0)

    def ending(k, c):
        last(k)
        return c

    lax.fori_loop(0, SHARD_CHUNKS, ending, 0)
    for r in range(max(ga * gb - 2, 0), ga * gb):
        d_copy(r, r % 2).wait()

    def stored(i, c):
        gni_copy(i).wait()
        return c

    lax.fori_loop(0, rows // tile, stored, 0)
    drain()


def closing(
    n, t, width,
    gni_h, dw1_h, xc, gres, invin, gain_in, vecs, ggain,
    gin, allvec, sums,
    own, inbox, scaled, inner, zslots, vslots,
    s_own, sr, rr, sl, rl, zs, zr, vs, vr, ts, tr, *bufs,
):
    seq, tp = lax.axis_index("seq"), lax.axis_index("tp")
    rows, chan = gres.shape
    fetch = pltpu.make_async_copy(gni_h, own, s_own)
    fetch.start()
    greet_all(n, t, seq, tp)
    pieces, shard, cols = sums.shape

    def out(j, half, values):
        sums[j, half * (shard // 2) : (half + 1) * (shard // 2), :] = values

    start, stage1, stage2, stage3, drain_grid = grid_reduce(
        n, seq, tp, dw1_h, pieces, cols, bufs, out
    )
    start(0)
    start(1)
    fetch.wait()
    step = rows // SHARD_CHUNKS
    vslots[seq] = vecs[...]
    vslots[seq, 3:4, :] = ggain[0:1, :]

    def finish(k, values):
        at = pl.ds(pl.multiple_of(k * step, step), step)
        hat = xc[at, :].astype(F32) * invin[at, :]
        s = values * gain_in[...]
        scaled[at, :] = s
        inner[at, :] = s * hat
        vslots[seq, 0:1, :] += jnp.sum(values * hat, axis=0, keepdims=True)

    steps, step_of, last, drain = line_reduce_scatter(t, seq, tp, own, inbox, (sr, rr, sl, rl), finish)
    turns = [
        (2, lambda: stage1(0)),
        (4, lambda: stage1(1)),
        (6, lambda: stage2(0)),
        (9, lambda: stage3(0)),
        (10, lambda: stage2(1)),
        (11, lambda: stage3(1)),
    ]

    def turn_of(slot, c):
        def one(i, c):
            step_of(i)
            return c

        lax.fori_loop(slot * steps // 12, (slot + 1) * steps // 12, one, 0)
        for turn, work in turns:

            @pl.when(slot == turn)
            def _(work=work):
                work()

        return c

    lax.fori_loop(0, 12, turn_of, 0)

    def ending(k, c):
        last(k)
        return c

    lax.fori_loop(0, SHARD_CHUNKS, ending, 0)
    dot = sum_over_tp(row_sums(inner[...]), t, seq, tp, zslots, zs, zr) / width
    gin[...] = gres[...] + invin[...] * (scaled[...] - xc[...].astype(F32) * invin[...] * dot)
    spread(n, seq, vslots, vs, vr, lambda k: (k, tp))
    total = vslots[0]
    for k in range(1, n):
        total = total + vslots[k]
    allvec[tp] = total
    spread(t, tp, allvec, ts, tr, lambda k: (seq, k))
    drain()
    drain_grid()


def params(collective=None, limit=VMEM_LIMIT):
    if collective is None:
        return pltpu.CompilerParams(vmem_limit_bytes=limit)
    return pltpu.CompilerParams(
        vmem_limit_bytes=limit, collective_id=collective, has_side_effects=True
    )


def line_sems(chunks):
    return [DMA((chunks,)), DMA((chunks,)), DMA((2, chunks))]


def on_device(
    n, t,
    hidden_in, gain_in, w_input, w_forget, forget_bias, w_outgate, state_gain, w_output,
    gain_mid, w_gate, w_up, w_down, lengths, layer_index, cotangent,
):
    rows, width = hidden_in.shape
    chan = w_input.shape[1]
    ff = w_gate.shape[1]
    ffp = -(-ff // LANE) * LANE
    tp = lax.axis_index("tp")
    offset = tp * chan

    def padded(w):
        return w if ffp == ff else jnp.pad(w, ((0, 0), (0, ffp - ff)))

    w1 = lax.all_gather(
        jnp.concatenate([w_input, w_forget, w_outgate, w_output.T], axis=1), "seq", axis=0, tiled=True
    )
    w2 = lax.all_gather(
        jnp.concatenate([padded(w_gate), padded(w_up), padded(w_down.T)], axis=1),
        "seq", axis=0, tiled=True,
    )

    positions = lax.axis_index("seq") * rows + jnp.arange(rows, dtype=jnp.int32)
    total = lengths[0] + lengths[1]
    valid = (positions < total).astype(F32)[:, None]
    starts = ((positions == 0) | (positions == lengths[0])).astype(F32)[:, None]
    bound = layer_index[0].astype(F32) / LAYERS
    inputs_f = hidden_in.astype(F32)
    inv_in = lax.rsqrt(jnp.mean(inputs_f * inputs_f, axis=-1, keepdims=True) + EPS)
    normed_in = (inputs_f * inv_in * gain_in.astype(F32)).astype(BF)

    def cols(vector):
        return lax.dynamic_slice_in_dim(vector, offset, chan, 0).astype(F32)

    crow = jnp.concatenate(
        [
            cols(forget_bias)[None],
            cols(state_gain)[None],
            jnp.broadcast_to(bound, (1, chan)),
            jnp.zeros((5, chan), F32),
        ],
        axis=0,
    )
    gmid = gain_mid.astype(F32)[None]
    plane = shape((rows, chan), F32)
    column = shape((rows, 1), F32)
    ga, gb = chip_grid(n)
    h = width // n // 2
    shards16 = shape((t, rows, chan), BF)

    def groups(more=0):
        return shape((chan // LANE, rows + more, LANE), F32)

    wide16 = shape((rows, width), BF)

    ipre, fpre, opre, feff, states, gated, nmid, mixed, invst, invmid = pl.pallas_call(
        functools.partial(mixer_forward, n, t, width),
        out_shape=[
            plane, plane, plane,
            groups(8), groups(8),
            shape((rows, chan), BF), wide16, wide16, column, column,
        ],
        in_specs=[VM] * 7,
        out_specs=[VM] * 10,
        scratch_shapes=[
            pltpu.VMEM(groups().shape, F32),
            pltpu.VMEM((rows, chan), F32),
            pltpu.VMEM((rows // CHUNKS * 4, width), F32),
            pltpu.VMEM((n, 8, chan), F32),
            pltpu.VMEM((t, 8, rows), F32),
            pltpu.VMEM((rows, width), BF),
            pltpu.VMEM((2, rows, width), BF),
            DMA((n,)), DMA((n,)), DMA((t,)), DMA((t,)),
            *line_sems(CHUNKS),
        ],
        compiler_params=params(1),
        name="mixer_forward",
    )(normed_in, hidden_in, w1, crow, gmid, valid, starts)

    gnm_part, glu_part, dw2 = pl.pallas_call(
        feed_forward,
        out_shape=[wide16, shards16, shape((2, 2, ga, gb, h, 3 * ffp), BF)],
        in_specs=[HB] * 3,
        out_specs=[HB] * 3,
        scratch_shapes=[
            pltpu.VMEM((rows, width), BF),
            pltpu.VMEM((rows, width), BF),
            pltpu.VMEM((width, ffp), BF),
            pltpu.VMEM((width, ffp), BF),
            pltpu.VMEM((width, ffp), BF),
            pltpu.VMEM((rows, ffp), BF),
            pltpu.VMEM((rows, ffp), BF),
            pltpu.VMEM((rows, ffp), BF),
            pltpu.VMEM((rows, width), BF),
            pltpu.VMEM((t, rows, chan), BF),
            pltpu.VMEM((2, 2, 2, h, ffp), BF),
            DMA((3,)), DMA((2,)), DMA((2, rows // row_tile(rows))), DMA((2,)),
        ],
        compiler_params=params(),
        cost_estimate=pl.CostEstimate(
            flops=18 * rows * width * ffp, bytes_accessed=50_000_000, transcendentals=0
        ),
        name="feed_forward",
    )(nmid, cotangent, w2)

    gmix, gres, ggain, sums2 = pl.pallas_call(
        functools.partial(mid_backward, n, t, width),
        out_shape=[wide16, plane, shape((8, width), F32), shape((3, 2 * h, ffp), F32)],
        in_specs=[HB] * 2 + [VM] * 5,
        out_specs=[VM] * 4,
        scratch_shapes=[
            pltpu.VMEM((rows, width), BF),
            pltpu.VMEM((2, rows, width), BF),
            pltpu.VMEM((rows // CHUNKS, width), F32),
            DMA,
            *line_sems(CHUNKS),
            *grid_buffers(n, width, 3, ffp),
        ],
        compiler_params=params(2),
        name="mid_backward",
    )(gnm_part, dw2, hidden_in, mixed, invmid, cotangent, gmid)

    shard_sems = [DMA((t, SHARD_CHUNKS))] * 4
    shard_bufs = [pltpu.VMEM((t, rows, chan), BF), pltpu.VMEM((t + 1, rows, chan), BF)]
    gni_part, dw1, vecs, block_out = pl.pallas_call(
        functools.partial(mixer_backward, n, t, width),
        out_shape=[
            shards16, shape((2, 2, ga, gb, h, 4 * chan), BF), shape((8, chan), F32),
            shape((rows, chan), BF),
        ],
        in_specs=[HB] * 3 + [VM] * 13,
        out_specs=[HB] * 2 + [VM] * 2,
        scratch_shapes=[
            pltpu.VMEM(groups().shape, F32),
            pltpu.VMEM(groups().shape, F32),
            pltpu.VMEM((rows, chan), F32),
            pltpu.VMEM((rows, 3 * chan), BF),
            pltpu.VMEM((n, 8, chan), F32),
            pltpu.VMEM((t, 8, rows), F32),
            pltpu.VMEM((rows, chan), BF),
            pltpu.VMEM((rows, chan), BF),
            *shard_bufs,
            pltpu.VMEM((t, rows, chan), BF),
            pltpu.VMEM((2, 2, 2, h, 4 * chan), BF),
            DMA((n,)), DMA((n,)), DMA((t,)), DMA((t,)), DMA((3,)),
            *shard_sems,
            DMA((rows // row_tile(rows),)), DMA((2,)),
        ],
        compiler_params=params(3),
        name="mixer_backward",
    )(
        glu_part, hidden_in, mixed,
        gmix, normed_in, w1, gated, states, feff, ipre, fpre, opre, invst, valid, starts, crow,
    )

    ggain_cols = lax.dynamic_slice_in_dim(ggain, offset, chan, 1)
    x_cols = lax.dynamic_slice_in_dim(hidden_in, offset, chan, 1)
    grad_in, allvec, sums1 = pl.pallas_call(
        functools.partial(closing, n, t, width),
        out_shape=[plane, shape((t, 8, chan), F32), shape((2, 2 * h, 2 * chan), F32)],
        in_specs=[HB] * 2 + [VM] * 6,
        out_specs=[VM] * 3,
        scratch_shapes=[
            *shard_bufs,
            pltpu.VMEM((rows, chan), F32),
            pltpu.VMEM((rows, chan), F32),
            pltpu.VMEM((t, 8, rows), F32),
            pltpu.VMEM((n, 8, chan), F32),
            DMA,
            *shard_sems,
            DMA((t,)), DMA((t,)), DMA((n,)), DMA((n,)), DMA((t,)), DMA((t,)),
            *grid_buffers(n, width, 2, 2 * chan),
        ],
        compiler_params=params(4),
        name="closing",
    )(
        gni_part, dw1, x_cols, gres, inv_in, cols(gain_in)[None], vecs, ggain_cols,
    )

    def vector(r):
        return allvec[:, r, :].reshape(width)

    squares = jnp.stack([jnp.sum(allvec[:, r, :]) for r in (4, 5, 6)])
    rms_stats = jnp.sqrt(squares / (total.astype(F32) * width))

    return (
        block_out,
        grad_in,
        vector(0),
        sums1[0, :, :chan],
        sums1[0, :, chan:],
        vector(1),
        sums1[1, :, :chan],
        vector(2),
        sums1[1, :, chan:].T,
        vector(3),
        sums2[0, :, :ff],
        sums2[1, :, :ff],
        sums2[2, :, :ff].T,
        rms_stats,
    )


def solution(mesh):
    weight, turned = P("seq", "tp"), P("tp", "seq")
    in_specs = (
        P("seq", None), P(), weight, weight, P(), weight, P(), turned, P(), weight, weight, turned,
        P(), P(), P("seq", None),
    )
    out_specs = (
        weight, weight, P(), weight, weight, P(), weight, P(), turned, P(), weight, weight, turned, P(),
    )
    body = functools.partial(on_device, mesh.shape["seq"], mesh.shape["tp"])
    return jax.shard_map(
        body, mesh=mesh, in_specs=in_specs, out_specs=out_specs, check_vma=False
    )
```

```python
import functools

import jax
import jax.numpy as jnp
from jax import lax
from jax.experimental import pallas as pl
from jax.experimental.pallas import tpu as pltpu
from jax.sharding import PartitionSpec as P

LAYERS = 24
EPS = 1e-06
MESH = pl.DeviceIdType.MESH
DMA = pltpu.SemaphoreType.DMA
BF = jnp.bfloat16
F32 = jnp.float32
VM = pl.BlockSpec(memory_space=pltpu.VMEM)
HB = pl.BlockSpec(memory_space=pl.ANY)
LANE = 128
SEG = 8
CHUNKS = 16
SHARD_CHUNKS = 4
HOP_LAG = 2
ROUND_TRIP = 3
VMEM_LIMIT = 60 * 1024 * 1024


def nn(left, right):
    return jnp.dot(left, right, preferred_element_type=F32)


def nt(left, right):
    return lax.dot_general(left, right, (((1,), (1,)), ((), ())), preferred_element_type=F32)


def tn(left, right):
    return lax.dot_general(left, right, (((0,), (0,)), ((), ())), preferred_element_type=F32)


def shape(dims, dtype):
    return jax.ShapeDtypeStruct(dims, dtype)


def get(ref, at):
    return jnp.concatenate([ref[g, at, :] for g in range(ref.shape[0])], axis=1)


def put(ref, at, values):
    for g in range(ref.shape[0]):
        ref[g, at, :] = values[:, g * LANE : (g + 1) * LANE]


def put_shards(ref, at, values):
    k = ref.shape[2]
    for q in range(ref.shape[0]):
        ref[q, at, :] = values[:, q * k : (q + 1) * k]


def put_blocks(ref, h, values):
    for core in range(2):
        for half in range(2):
            first = (core * 2 + half) * h
            ref[core, half] = values[first : first + h].astype(ref.dtype)


def row_tile(rows):
    return rows // 3 if rows % 48 == 0 else rows


def greet_all(n, t, seq, tp):
    barrier = pltpu.get_barrier_semaphore()

    def along_seq(o, c):
        pl.semaphore_signal(barrier, inc=1, device_id=(lax.rem(seq + o, n), tp), device_id_type=MESH)
        return c

    def along_tp(o, c):
        pl.semaphore_signal(barrier, inc=1, device_id=(seq, lax.rem(tp + o, t)), device_id_type=MESH)
        return c

    lax.fori_loop(1, n, along_seq, 0)
    lax.fori_loop(1, t, along_tp, 0)
    pl.semaphore_wait(barrier, n - 1 + t - 1)


def greet_line(t, seq, tp):
    barrier = pltpu.get_barrier_semaphore()

    def along_tp(o, c):
        pl.semaphore_signal(barrier, inc=1, device_id=(seq, lax.rem(tp + o, t)), device_id_type=MESH)
        return c

    lax.fori_loop(1, t, along_tp, 0)
    pl.semaphore_wait(barrier, t - 1)


def spread(size, me, slots, send, recv, target):
    def copy(o, slot):
        return pltpu.make_async_remote_copy(
            src_ref=slots.at[slot],
            dst_ref=slots.at[slot],
            send_sem=send.at[o],
            recv_sem=recv.at[slot],
            device_id=target(lax.rem(me + o, size)),
            device_id_type=MESH,
        )

    def one(o, c):
        copy(o, me).start()
        return c

    def arrived(o, c):
        copy(o, lax.rem(me + o, size)).wait_recv()
        return c

    def sent(o, c):
        copy(o, me).wait_send()
        return c

    def go():
        lax.fori_loop(1, size, one, 0)

    def done():
        lax.fori_loop(1, size, arrived, 0)
        lax.fori_loop(1, size, sent, 0)

    return go, done


def row_sums(values):
    ones = jnp.ones((8, values.shape[1]), BF)
    high = values.astype(BF)
    rest = values - high.astype(F32)
    low = rest.astype(BF)
    return nt(ones, high) + nt(ones, low)


def sum_over_tp(part, t, seq, tp, slots, send, recv, between=None):
    slots[tp] = part
    go, done = spread(t, tp, slots, send, recv, lambda k: (seq, k))
    go()
    if between is not None:
        between()
    done()
    total = slots[0]
    for k in range(1, t):
        total = total + slots[k]
    return jnp.transpose(total)[:, :1]


def carry_over_seq(prod, state, n, seq, tp, slots, send, recv, backward, between=None):
    slots[seq] = jnp.concatenate([prod, state] + [jnp.zeros_like(prod)] * 6, axis=0)
    go, done = spread(n, seq, slots, send, recv, lambda k: (k, tp))
    go()
    if between is not None:
        between()
    done()

    def hop(i, total):
        j = n - 1 - i if backward else i
        block = slots[j]
        longer = block[1:2] + block[0:1] * total
        inside = (j > seq) if backward else (j < seq)
        return jnp.where(inside, longer, total)

    return lax.fori_loop(0, n, hop, jnp.zeros_like(prod))


def line_all_reduce(t, seq, tp, rows, chunks, partial, send, buf, sems, finish, beside=None):
    s_in, s_out, r_buf = sems
    step = rows // chunks
    half = t // 2
    depth = jnp.where(tp < half, tp, t - 1 - tp)
    inner = jnp.where(tp < half, tp + 1, tp - 1)
    outer = jnp.where(tp < half, tp - 1, tp + 1)
    outer = jnp.where(depth > 0, outer, inner)
    middle = (depth == half - 1).astype(jnp.int32)

    def part_of(k):
        return pl.ds(pl.multiple_of(k * step, step), step)

    def inward(k, slot):
        return pltpu.make_async_remote_copy(
            src_ref=send.at[part_of(k)],
            dst_ref=buf.at[slot, part_of(k)],
            send_sem=s_in.at[k],
            recv_sem=r_buf.at[slot, k],
            device_id=(seq, inner),
            device_id_type=MESH,
        )

    def outward(k):
        return pltpu.make_async_remote_copy(
            src_ref=buf.at[1, part_of(k)],
            dst_ref=buf.at[1, part_of(k)],
            send_sem=s_out.at[k],
            recv_sem=r_buf.at[1, k],
            device_id=(seq, outer),
            device_id_type=MESH,
        )

    def first(k):
        part = partial(k)

        @pl.when(depth > 0)
        def _():
            inward(k, 0).wait_recv()
            send[part_of(k), :] = (part + buf[0, part_of(k), :].astype(F32)).astype(BF)

        @pl.when(depth == 0)
        def _():
            send[part_of(k), :] = part.astype(BF)

        inward(k, middle).start()

    def second(k):
        inward(k, 1).wait_recv()

        @pl.when(middle == 1)
        def _():
            both = send[part_of(k), :].astype(F32) + buf[1, part_of(k), :].astype(F32)
            buf[1, part_of(k), :] = both.astype(BF)

        @pl.when(depth > 0)
        def _():
            outward(k).start()

        finish(k)

    lag = 1 + ROUND_TRIP * (half - 1 - depth)

    def both(k, c):
        @pl.when(k < chunks)
        def _():
            first(k)

        @pl.when((k >= lag) & (k - lag < chunks))
        def _():
            second(k - lag)

        if beside is not None:
            beside(k)
        return c

    lax.fori_loop(0, chunks + 1 + ROUND_TRIP * (half - 1), both, 0)

    def drain(k, c):
        inward(k, middle).wait_send()

        @pl.when(depth > 0)
        def _():
            outward(k).wait_send()

        return c

    lax.fori_loop(0, chunks, drain, 0)


def line_reduce_scatter(t, seq, tp, own, inbox, sems, finish):
    s_r, r_r, s_l, r_l = sems
    rows = own.shape[1]
    chunks = SHARD_CHUNKS
    step = rows // chunks
    count = chunks * (t - 1)

    def part_of(k):
        return pl.ds(pl.multiple_of(k * step, step), step)

    def rightward(q, k):
        return pltpu.make_async_remote_copy(
            src_ref=own.at[q, part_of(k)],
            dst_ref=inbox.at[q + 1, part_of(k)],
            send_sem=s_r.at[q, k],
            recv_sem=r_r.at[q, k],
            device_id=(seq, lax.rem(tp + 1, t)),
            device_id_type=MESH,
        )

    def leftward(q, k):
        return pltpu.make_async_remote_copy(
            src_ref=own.at[q, part_of(k)],
            dst_ref=inbox.at[q, part_of(k)],
            send_sem=s_l.at[q, k],
            recv_sem=r_l.at[q, k],
            device_id=(seq, lax.rem(tp + t - 1, t)),
            device_id_type=MESH,
        )

    def add(q, k, slot):
        own[q, part_of(k), :] = (
            own[q, part_of(k), :].astype(F32) + inbox[slot, part_of(k), :].astype(F32)
        ).astype(BF)

    def right_turn(i):
        k, j = i // (t - 1), lax.rem(i, t - 1)
        q = t - 1 - j

        @pl.when((i >= 0) & (i < count) & (q > tp))
        def _():
            @pl.when(tp > 0)
            def _():
                rightward(q, k).wait_recv()
                add(q, k, q + 1)

            rightward(q, k).start()

    def left_turn(i):
        k, q = i // (t - 1), lax.rem(i, t - 1)

        @pl.when((i >= 0) & (i < count) & (q < tp))
        def _():
            @pl.when(tp < t - 1)
            def _():
                leftward(q, k).wait_recv()
                add(q, k, q)

            leftward(q, k).start()

    def turn(i):
        right_turn(i - HOP_LAG * tp)
        left_turn(i - HOP_LAG * (t - 1 - tp))

    def last(k):
        @pl.when(tp == 0)
        def _():
            leftward(tp, k).wait_recv()
            finish(k, own[tp, part_of(k), :].astype(F32) + inbox[tp, part_of(k), :].astype(F32))

        @pl.when(tp == t - 1)
        def _():
            rightward(tp, k).wait_recv()
            finish(k, own[tp, part_of(k), :].astype(F32) + inbox[tp + 1, part_of(k), :].astype(F32))

        @pl.when((tp > 0) & (tp < t - 1))
        def _():
            leftward(tp, k).wait_recv()
            rightward(tp, k).wait_recv()
            finish(
                k,
                own[tp, part_of(k), :].astype(F32)
                + inbox[tp, part_of(k), :].astype(F32)
                + inbox[tp + 1, part_of(k), :].astype(F32),
            )

    def drain():
        def sent(i, c):
            k = i // (t - 1)
            j = lax.rem(i, t - 1)

            @pl.when(t - 1 - j > tp)
            def _():
                rightward(t - 1 - j, k).wait_send()

            @pl.when(j < tp)
            def _():
                leftward(j, k).wait_send()

            return c

        lax.fori_loop(0, count, sent, 0)

    return count + HOP_LAG * (t - 2), turn, last, drain


def chip_grid(n):
    chips = n // 2
    b = max(k for k in range(1, chips + 1) if chips % k == 0 and k * k <= chips)
    return chips // b, b


def grid_buffers(n, width, pieces, cols):
    ga, gb = chip_grid(n)
    h = width // n // 2
    pa, pb = max(ga - 1, 1), max(gb - 1, 1)
    return [
        pltpu.VMEM((pieces, 2, ga, gb, h, cols), BF),
        pltpu.VMEM((pieces, 2, ga, gb, h, cols), BF),
        pltpu.VMEM((pieces, pb, ga, h, cols), BF),
        pltpu.VMEM((pieces, pa, gb, h, cols), BF),
        pltpu.VMEM((pieces, pa, h, cols), BF),
        pltpu.VMEM((pieces, pb, h, cols), BF),
        DMA((pieces,)), DMA((pieces,)), DMA((pieces,)),
        DMA((2, pieces, pb)), DMA((2, pieces, pa)), DMA((2, pieces, pa)), DMA((2, pieces, pb)),
    ]


def grid_reduce(n, seq, tp, terms, pieces, cols, bufs, out):
    acc, first, far_b, far_a, near_a, near_b, s_own, s_f, r_f, m_fb, m_fa, m_na, m_nb = bufs
    ga, gb = chip_grid(n)
    core = lax.rem(seq, 2)
    a, b = seq // 2 // gb, lax.rem(seq // 2, gb)

    def device(a_, b_, core_):
        return ((a_ * gb + b_) * 2 + core_, tp)

    def columns(j):
        return pl.ds(j * cols, cols)

    def load(j):
        return pltpu.make_async_copy(
            terms.at[core, :, :, :, :, columns(j)], acc.at[j], s_own.at[j]
        )

    def swap(j):
        return pltpu.make_async_remote_copy(
            src_ref=terms.at[1 - core, :, :, :, :, columns(j)],
            dst_ref=first.at[j],
            send_sem=s_f.at[j],
            recv_sem=r_f.at[j],
            device_id=device(a, b, 1 - core),
            device_id_type=MESH,
        )

    def remote(src, dst, sems, j, o, target):
        return pltpu.make_async_remote_copy(
            src_ref=src,
            dst_ref=dst,
            send_sem=sems.at[0, j, o],
            recv_sem=sems.at[1, j, o],
            device_id=target,
            device_id_type=MESH,
        )

    def far(j):
        copies = []
        for o in range(1, gb):
            to = lax.rem(b + o, gb)
            copies.append(
                remote(acc.at[j, 0, :, to], far_b.at[j, o - 1], m_fb, j, o - 1, device(a, to, core))
            )
        for o in range(1, ga):
            to = lax.rem(a + o, ga)
            copies.append(
                remote(acc.at[j, 1, to], far_a.at[j, o - 1], m_fa, j, o - 1, device(to, b, core))
            )
        return copies

    def near(j):
        copies = []
        for o in range(1, ga):
            to = lax.rem(a + o, ga)
            copies.append(
                remote(acc.at[j, 0, to, b], near_a.at[j, o - 1], m_na, j, o - 1, device(to, b, core))
            )
        for o in range(1, gb):
            to = lax.rem(b + o, gb)
            copies.append(
                remote(acc.at[j, 1, a, to], near_b.at[j, o - 1], m_nb, j, o - 1, device(a, to, core))
            )
        return copies

    def start(j):
        load(j).start()
        swap(j).start()

    def stage1(j):
        load(j).wait()
        swap(j).wait_recv()

        def chip(i, c):
            x, y = i // gb, lax.rem(i, gb)
            for half in range(2):
                acc[j, half, x, y] = (
                    acc[j, half, x, y].astype(F32) + first[j, half, x, y].astype(F32)
                ).astype(BF)
            return c

        lax.fori_loop(0, ga * gb, chip, 0)
        for copy in far(j):
            copy.start()

    def stage2(j):
        for copy in far(j):
            copy.wait_recv()

        def along_a(x, c):
            total = acc[j, 0, x, b].astype(F32)
            for o in range(1, gb):
                total = total + far_b[j, o - 1, x].astype(F32)
            acc[j, 0, x, b] = total.astype(BF)
            return c

        def along_b(y, c):
            total = acc[j, 1, a, y].astype(F32)
            for o in range(1, ga):
                total = total + far_a[j, o - 1, y].astype(F32)
            acc[j, 1, a, y] = total.astype(BF)
            return c

        lax.fori_loop(0, ga, along_a, 0)
        lax.fori_loop(0, gb, along_b, 0)
        for copy in near(j):
            copy.start()

    def stage3(j):
        for copy in near(j):
            copy.wait_recv()
        total = acc[j, 0, a, b].astype(F32)
        for o in range(1, ga):
            total = total + near_a[j, o - 1].astype(F32)
        out(j, 0, total)
        total = acc[j, 1, a, b].astype(F32)
        for o in range(1, gb):
            total = total + near_b[j, o - 1].astype(F32)
        out(j, 1, total)

    def drain():
        for j in range(pieces):
            swap(j).wait_send()
            for copy in far(j) + near(j):
                copy.wait_send()

    return start, stage1, stage2, stage3, drain


def gather_sems(n, pieces):
    ga, gb = chip_grid(n)
    pa, pb = max(ga - 1, 1), max(gb - 1, 1)
    return [
        DMA((pieces,)), DMA((2, pieces, ga * gb)),
        DMA((2, pieces, pb)), DMA((2, pieces, pa)), DMA((2, pieces, gb, pa)), DMA((2, pieces, ga, pb)),
    ]


def grid_gather(n, seq, tp, j, src, dst, sems):
    s_local, m_core, m_fb, m_fa, m_na, m_nb = sems
    ga, gb = chip_grid(n)
    shard = src.shape[0]
    h = shard // 2
    core = lax.rem(seq, 2)
    a, b = seq // 2 // gb, lax.rem(seq // 2, gb)

    def device(a_, b_, core_):
        return ((a_ * gb + b_) * 2 + core_, tp)

    def block(x, y, core_, half, count):
        return pl.ds(pl.multiple_of(((x * gb + y) * 2 + core_) * shard + half * h, h), count)

    def remote(from_, rows, sem, index, target):
        return pltpu.make_async_remote_copy(
            src_ref=from_,
            dst_ref=dst.at[rows],
            send_sem=sem.at[(0, j) + index],
            recv_sem=sem.at[(1, j) + index],
            device_id=target,
            device_id_type=MESH,
        )

    def own(half):
        return src.at[pl.ds(half * h, h)]

    def far(incoming):
        copies = []
        for o in range(1, gb):
            to, of = lax.rem(b + o, gb), lax.rem(b + gb - o, gb)
            rows = block(a, of if incoming else b, core, 0, h)
            copies.append(remote(own(0), rows, m_fb, (o - 1,), device(a, to, core)))
        for o in range(1, ga):
            to, of = lax.rem(a + o, ga), lax.rem(a + ga - o, ga)
            rows = block(of if incoming else a, b, core, 1, h)
            copies.append(remote(own(1), rows, m_fa, (o - 1,), device(to, b, core)))
        return copies

    def near(incoming, first, least):
        copies = []
        for i in range(0 if first else 1, gb if least else 1):
            y = lax.rem(b + gb - i, gb)
            for o in range(1, ga):
                to, of = lax.rem(a + o, ga), lax.rem(a + ga - o, ga)
                rows = block(of if incoming else a, y, core, 0, h)
                from_ = own(0) if i == 0 or incoming else dst.at[rows]
                copies.append(remote(from_, rows, m_na, (i, o - 1), device(to, b, core)))
        for i in range(0 if first else 1, ga if least else 1):
            x = lax.rem(a + ga - i, ga)
            for o in range(1, gb):
                to, of = lax.rem(b + o, gb), lax.rem(b + gb - o, gb)
                rows = block(x, of if incoming else b, core, 1, h)
                from_ = own(1) if i == 0 or incoming else dst.at[rows]
                copies.append(remote(from_, rows, m_nb, (i, o - 1), device(a, to, core)))
        return copies

    def across(incoming, first, others):
        copies = []
        for i in range(ga):
            for k in range(gb):
                mine = i == 0 and k == 0
                if (mine and not first) or (not mine and not others):
                    continue
                x, y = lax.rem(a + i, ga), lax.rem(b + k, gb)
                rows = block(x, y, 1 - core if incoming else core, 0, shard)
                from_ = src if mine or incoming else dst.at[rows]
                copies.append(remote(from_, rows, m_core, (i * gb + k,), device(a, b, 1 - core)))
        return copies

    def local():
        return pltpu.make_async_copy(src, dst.at[block(a, b, core, 0, shard)], s_local.at[j])

    def start():
        for copy in far(False) + near(False, True, False) + across(False, True, False):
            copy.start()
        local().start()

    def relay():
        for copy in far(True):
            copy.wait_recv()
        for copy in near(False, False, True):
            copy.start()

    def share():
        for copy in near(True, True, True):
            copy.wait_recv()
        for copy in across(False, False, True):
            copy.start()

    def arrive():
        for copy in across(True, True, True):
            copy.wait_recv()
        local().wait()

    def drain():
        for copy in far(False) + near(False, True, True) + across(False, True, True):
            copy.wait_send()

    return start, relay, share, arrive, drain


def masks(lens, first, count):
    at = first + lax.broadcasted_iota(jnp.int32, (count, 1), 0)
    valid = (at < lens[0] + lens[1]).astype(F32)
    starts = ((at == 0) | (at == lens[0])).astype(F32)
    return valid, starts


def mixer_forward(
    n, t, width,
    lens, x_h, wi_h, wf_h, wo_h, wx_h, wg_h, wu_h, wd_h, consts,
    ipre_h, fpre_h, opre_h, feff_h, states_h, gated_h, normed_h, nmid_h, mixed_h, w1_h, w2_h,
    invst, invmid, invin,
    x, normed, ipre, fpre, opre, feff, states, gated, nmid, w1, prod, ssq, part, cslots, zslots, send, buf,
    s_x, s_st, s_w, s_n, s_m, cs, cr, zs, zr, s_in, s_out, r_buf, *sems,
):
    seq, tp = lax.axis_index("seq"), lax.axis_index("tp")
    load = pltpu.make_async_copy(x_h, x, s_x)
    load.start()
    sems1, sems2 = sems[:6], sems[6:]
    one = [
        grid_gather(n, seq, tp, j, src, w1.at[j], sems1)
        for j, src in enumerate((wi_h, wf_h, wo_h, wx_h))
    ]
    two = [
        grid_gather(n, seq, tp, j, src, w2_h.at[j], sems2)
        for j, src in enumerate((wg_h, wu_h, wd_h))
    ]
    START, RELAY, SHARE, ARRIVE, DRAIN = range(5)
    greet_all(n, t, seq, tp)
    one[0][START]()
    rows, depth = normed.shape
    chan = ipre.shape[1]
    tile = row_tile(rows)
    mine = pl.ds(pl.multiple_of(tp * chan, LANE), chan)
    bias, sgain, bound = consts[0:1, mine], consts[1:2, mine], consts[2:3, mine]

    def stores():
        pairs = (
            (ipre, ipre_h), (fpre, fpre_h), (opre, opre_h), (feff, feff_h), (states, states_h),
            (gated, gated_h), (normed, normed_h),
        )
        return [pltpu.make_async_copy(v, o, s_st.at[i]) for i, (v, o) in enumerate(pairs)]

    def keep(j):
        return pltpu.make_async_copy(w1.at[j], w1_h.at[j], s_w.at[j])

    load.wait()

    def norm(i, c):
        at = pl.ds(pl.multiple_of(i * tile, tile), tile)
        v = x[at, :].astype(F32)
        inv = lax.rsqrt(jnp.mean(v * v, axis=-1, keepdims=True) + EPS)
        invin[at, :] = inv
        normed[at, :] = (v * inv * consts[4:5, :]).astype(BF)
        return c

    lax.fori_loop(0, rows // tile, norm, 0)
    one[0][RELAY]()
    one[1][START]()
    one[0][SHARE]()
    one[1][RELAY]()
    one[2][START]()
    one[0][ARRIVE]()
    keep(0).start()

    def first(i, c):
        at = pl.ds(pl.multiple_of(i * tile, tile), tile)
        ipre[at, :] = nn(normed[at, :], w1[0])
        return c

    lax.fori_loop(0, rows // tile, first, 0)
    one[1][SHARE]()
    one[2][RELAY]()
    one[3][START]()
    one[1][ARRIVE]()
    keep(1).start()

    def second(i, c):
        at = pl.ds(pl.multiple_of(i * tile, tile), tile)
        f = nn(normed[at, :], w1[1]) + bias
        fpre[at, :] = f
        valid, starts = masks(lens, seq * rows + i * tile, tile)
        gate = bound + (1.0 - bound) * jax.nn.sigmoid(f)
        put(feff, at, gate * (1.0 - starts))
        shifted = pl.ds(pl.multiple_of(i * tile + 8, 8), tile)
        v = ipre[at, :]
        put(states, shifted, v * jax.nn.sigmoid(v) * (1.0 - gate) * valid)
        return c

    lax.fori_loop(0, rows // tile, second, 0)
    put(feff, slice(rows, rows + 8), jnp.ones((8, chan), F32))

    length = rows // SEG

    def scan(i, c):
        p, h = c
        at, shifted = pl.ds(i, SEG, stride=length), pl.ds(i + 8, SEG, stride=length)
        f = get(feff, at)
        h = f * h + get(states, shifted)
        p = f * p
        put(states, shifted, h)
        put(prod, at, p)
        return p, h

    p, h = lax.fori_loop(
        0, length, scan, (jnp.ones((SEG, chan), F32), jnp.zeros((SEG, chan), F32))
    )
    block_p, block_h = p[0:1], h[0:1]
    for s in range(1, SEG):
        block_h = h[s : s + 1] + p[s : s + 1] * block_h
        block_p = p[s : s + 1] * block_p

    def travel():
        one[2][SHARE]()
        one[3][RELAY]()
        two[0][START]()

    arriving = carry_over_seq(block_p, block_h, n, seq, tp, cslots, cs, cr, False, travel)
    put(states, slice(0, 8), jnp.broadcast_to(arriving, (8, chan)))
    for s in range(SEG):
        at = slice(s * length, (s + 1) * length)
        shifted = slice(s * length + 8, (s + 1) * length + 8)
        whole = get(states, shifted) + get(prod, at) * arriving
        put(states, shifted, whole)
        ssq[at, :] = whole * whole
        arriving = h[s : s + 1] + p[s : s + 1] * arriving

    def outgate():
        one[3][SHARE]()
        one[2][ARRIVE]()
        keep(2).start()

        def third(i, c):
            at = pl.ds(pl.multiple_of(i * tile, tile), tile)
            opre[at, :] = nn(normed[at, :], w1[2])
            return c

        lax.fori_loop(0, rows // tile, third, 0)

    total = sum_over_tp(row_sums(ssq[...]), t, seq, tp, zslots, zs, zr, outgate)
    invst[...] = lax.rsqrt(total / width + EPS)

    def gating(i, c):
        at = pl.ds(pl.multiple_of(i * tile, tile), tile)
        shifted = pl.ds(pl.multiple_of(i * tile + 8, 8), tile)
        o = opre[at, :]
        gated[at, :] = (
            get(states, shifted) * invst[at, :] * sgain * (o * jax.nn.sigmoid(o))
        ).astype(BF)
        return c

    lax.fori_loop(0, rows // tile, gating, 0)
    one[3][ARRIVE]()
    keep(3).start()
    for copy in stores():
        copy.start()

    step = rows // CHUNKS
    group = part.shape[0] // step

    def partial(k):
        @pl.when(lax.rem(k, group) == 0)
        def _():
            big = pl.ds(pl.multiple_of(k * step, step), step * group)
            part[...] = nt(gated[big, :], w1[3])

        return part[pl.ds(pl.multiple_of(lax.rem(k, group) * step, step), step), :]

    def store_n(k):
        at = pl.ds(pl.multiple_of(k * step, step), step)
        return pltpu.make_async_copy(nmid.at[at], nmid_h.at[at], s_n.at[k])

    def store_m(k):
        at = pl.ds(pl.multiple_of(k * step, step), step)
        return pltpu.make_async_copy(buf.at[1, at], mixed_h.at[at], s_m.at[k])

    def finish(k):
        at = pl.ds(pl.multiple_of(k * step, step), step)
        store_m(k).start()
        resid = x[at, :].astype(F32) + buf[1, at, :].astype(F32)
        inv = lax.rsqrt(jnp.mean(resid * resid, axis=-1, keepdims=True) + EPS)
        invmid[at, :] = inv
        nmid[at, :] = (resid * inv * consts[3:4, :]).astype(BF)
        store_n(k).start()

    turns = [
        (2, lambda: (two[0][RELAY](), two[1][START]())),
        (4, lambda: two[0][SHARE]()),
        (7, lambda: (two[1][RELAY](), two[2][START]())),
        (9, lambda: two[1][SHARE]()),
        (13, lambda: two[2][RELAY]()),
        (16, lambda: two[2][SHARE]()),
    ]

    def beside(k):
        for turn, work in turns:

            @pl.when(k == turn)
            def _(work=work):
                work()

    line_all_reduce(
        t, seq, tp, rows, CHUNKS, partial, send, buf, (s_in, s_out, r_buf), finish, beside
    )
    for g in two:
        g[ARRIVE]()
    for g in one + two:
        g[DRAIN]()
    for copy in stores():
        copy.wait()
    for j in range(4):
        keep(j).wait()

    def stored(k, c):
        store_n(k).wait()
        store_m(k).wait()
        return c

    lax.fori_loop(0, CHUNKS, stored, 0)


def feed_forward(
    nmid_h, cot_h, w2_h, gnm_h, glu_h, dw2_h,
    nmid, cot, wg, wu, wd, hid, gg, gu, gnm, glu, stage,
    s_w, s_a, s_o, s_d,
):
    rows, width = nmid.shape
    ff = wg.shape[1]
    tile = row_tile(rows)
    act_copies = [
        pltpu.make_async_copy(nmid_h, nmid, s_a.at[0]),
        pltpu.make_async_copy(cot_h, cot, s_a.at[1]),
    ]
    w_copies = [
        pltpu.make_async_copy(w2_h.at[j], w, s_w.at[j])
        for j, w in enumerate((wg, wu, wd))
    ]
    for copy in (act_copies[0], w_copies[0], w_copies[1], act_copies[1], w_copies[2]):
        copy.start()
    act_copies[0].wait()
    w_copies[0].wait()

    def out_copy(i, which):
        at = pl.ds(pl.multiple_of(i * tile, tile), tile)
        if which == 0:
            return pltpu.make_async_copy(gnm.at[at], gnm_h.at[at], s_o.at[0, i])
        return pltpu.make_async_copy(glu.at[:, at], glu_h.at[:, at], s_o.at[1, i])

    def block(i, c):
        at = pl.ds(pl.multiple_of(i * tile, tile), tile)
        g = nn(nmid[at, :], wg[...])

        @pl.when(i == 0)
        def _():
            w_copies[1].wait()
            act_copies[1].wait()
            w_copies[2].wait()

        u = nn(nmid[at, :], wu[...])
        gh = nn(cot[at, :], wd[...])
        sig = jax.nn.sigmoid(g)
        act = g * sig
        hid[at, :] = (act * u).astype(BF)
        gg[at, :] = (gh * u * (sig * (1.0 + g * (1.0 - sig)))).astype(BF)
        gu[at, :] = (gh * act).astype(BF)
        gnm[at, :] = (nt(gg[at, :], wg[...]) + nt(gu[at, :], wu[...])).astype(BF)
        out_copy(i, 0).start()
        put_shards(glu, at, nt(hid[at, :], wd[...]).astype(BF))
        out_copy(i, 1).start()
        return c

    lax.fori_loop(0, rows // tile, block, 0)

    ga, gb, h = dw2_h.shape[2:5]
    span = 4 * h
    pieces = ga * gb

    def d_copy(i, slot):
        j = i // pieces
        r = lax.rem(i, pieces)
        return pltpu.make_async_copy(
            stage.at[slot],
            dw2_h.at[:, :, r // gb, lax.rem(r, gb), :, pl.ds(pl.multiple_of(j * ff, LANE), ff)],
            s_d.at[slot],
        )

    for j, (left, right) in enumerate(((nmid, gg), (nmid, gu), (cot, hid))):

        def slab(r, c, j=j, left=left, right=right):
            i = j * pieces + r
            slot = lax.rem(i, 2)

            @pl.when(i >= 2)
            def _():
                d_copy(i - 2, slot).wait()

            at = pl.ds(pl.multiple_of(r * span, span), span)
            put_blocks(stage.at[slot], h, tn(left[:, at], right[...]))
            d_copy(i, slot).start()
            return c

        lax.fori_loop(0, pieces, slab, 0)
    d_copy(3 * pieces - 2, (3 * pieces) % 2).wait()
    d_copy(3 * pieces - 1, (3 * pieces + 1) % 2).wait()

    def drain(i, c):
        out_copy(i, 0).wait()
        out_copy(i, 1).wait()
        return c

    lax.fori_loop(0, rows // tile, drain, 0)


def mid_backward(
    n, t, width,
    gnm_h, dw2_h, x_h, mixed_h, cot_h, invmid, consts,
    gmix_h, gres_h, ggain, sums_h,
    x, mixed, cot, gmix, gres, sums, send, buf, wide, s_g, s_x, s_o, s_s, s_in, s_out, r_buf, *bufs,
):
    seq, tp = lax.axis_index("seq"), lax.axis_index("tp")
    load = pltpu.make_async_copy(gnm_h, send, s_g)
    load.start()
    fetches = [
        pltpu.make_async_copy(src, dst, s_x.at[i])
        for i, (src, dst) in enumerate(((x_h, x), (mixed_h, mixed), (cot_h, cot)))
    ]
    greet_all(n, t, seq, tp)
    rows = x.shape[0]
    chan = gres.shape[1]
    step = rows // CHUNKS
    pieces, shard, cols = sums.shape
    ggain[...] = jnp.zeros_like(ggain)

    def out(j, half, values):
        sums[j, half * (shard // 2) : (half + 1) * (shard // 2), :] = values

    start, stage1, stage2, stage3, drain = grid_reduce(n, seq, tp, dw2_h, pieces, cols, bufs, out)
    load.wait()
    start(0)
    for copy in fetches:
        copy.start()

    def summed(j):
        return pltpu.make_async_copy(sums.at[j], sums_h.at[j], s_s.at[j])

    def stored(k):
        at = pl.ds(pl.multiple_of(k * step, step), step)
        return (
            pltpu.make_async_copy(gmix.at[at], gmix_h.at[at], s_o.at[0, k]),
            pltpu.make_async_copy(gres.at[at], gres_h.at[at], s_o.at[1, k]),
        )

    def partial(k):
        at = pl.ds(pl.multiple_of(k * step, step), step)
        return send[at, :].astype(F32)

    def finish(k):
        @pl.when(k == 0)
        def _():
            for copy in fetches:
                copy.wait()

        at = pl.ds(pl.multiple_of(k * step, step), step)
        g = buf[1, at, :].astype(F32)
        inv = invmid[at, :]
        hat = (x[at, :].astype(F32) + mixed[at, :].astype(F32)) * inv
        ggain[0:1, :] += jnp.sum(g * hat, axis=0, keepdims=True)
        e = g * consts[3:4, :]
        mean = jnp.mean(e * hat, axis=-1, keepdims=True)
        result = cot[at, :].astype(F32) + inv * (e - hat * mean)
        wide[...] = result
        gmix[at, :] = result.astype(BF)
        gres[at, :] = wide[:, pl.ds(pl.multiple_of(tp * chan, LANE), chan)]
        for copy in stored(k):
            copy.start()

    turns = [
        (1, lambda: (stage1(0), start(1))),
        (4, lambda: (stage1(1), start(2))),
        (5, lambda: stage2(0)),
        (8, lambda: stage1(2)),
        (9, lambda: (stage3(0), summed(0).start())),
        (10, lambda: stage2(1)),
        (13, lambda: (stage3(1), summed(1).start())),
        (14, lambda: stage2(2)),
        (17, lambda: (stage3(2), summed(2).start())),
    ]

    def beside(k):
        for turn, work in turns:

            @pl.when(k == turn)
            def _(work=work):
                work()

    line_all_reduce(
        t, seq, tp, rows, CHUNKS, partial, send, buf, (s_in, s_out, r_buf), finish, beside
    )
    drain()
    for j in range(pieces):
        summed(j).wait()

    def ended(k, c):
        for copy in stored(k):
            copy.wait()
        return c

    lax.fori_loop(0, CHUNKS, ended, 0)


def mixer_backward(
    n, t, width,
    lens, glu_h, x_h, mixed_h, gmix_h, normed_h, w1_h, gated_h, states_h, feff_h, ipre_h, fpre_h, opre_h,
    invst, consts,
    gni_h, dw1_h, vecs, out,
    gmix, normed, w1, gated, states, feff, ipre, fpre, opre,
    weighted, prod, inner, out3, cslots, zslots, xc, mc, own, inbox, gni, stage,
    s_f, cs, cr, zs, zr, s_x, sr, rr, sl, rl, s_o, s_d,
):
    seq, tp = lax.axis_index("seq"), lax.axis_index("tp")
    rows = gmix.shape[0]
    chan = ipre.shape[1]
    mine = pl.ds(pl.multiple_of(tp * chan, LANE), chan)
    fetches = [
        pltpu.make_async_copy(glu_h, own, s_x.at[0]),
        pltpu.make_async_copy(x_h.at[:, mine], xc, s_x.at[1]),
        pltpu.make_async_copy(mixed_h.at[:, mine], mc, s_x.at[2]),
    ]
    pairs = [
        (gmix_h, gmix),
        (w1_h.at[3], w1.at[:, pl.ds(3 * chan, chan)]),
        (states_h, states), (opre_h, opre), (feff_h, feff), (ipre_h, ipre), (fpre_h, fpre),
    ] + [(w1_h.at[j], w1.at[:, pl.ds(j * chan, chan)]) for j in range(3)] + [
        (normed_h, normed), (gated_h, gated),
    ]
    inputs = [pltpu.make_async_copy(src, dst, s_f.at[i]) for i, (src, dst) in enumerate(pairs)]
    fetches[0].start()
    for copy in inputs[:4]:
        copy.start()
    greet_all(n, t, seq, tp)
    for copy in fetches[1:] + inputs[4:]:
        copy.start()
    tile = row_tile(rows)
    sgain, bound = consts[1:2, mine], consts[2:3, mine]
    vecs[...] = jnp.zeros_like(vecs)
    step = rows // SHARD_CHUNKS

    def finish(k, values):
        at = pl.ds(pl.multiple_of(k * step, step), step)
        ok, _ = masks(lens, seq * rows + k * step, step)
        m = mc[at, :].astype(F32)
        full = xc[at, :].astype(F32) + m + values
        out[at, :] = full.astype(BF)
        vecs[4:5, :] += jnp.sum(ok * m * m, axis=0, keepdims=True)
        vecs[5:6, :] += jnp.sum(ok * values * values, axis=0, keepdims=True)
        vecs[6:7, :] += jnp.sum(ok * full * full, axis=0, keepdims=True)

    turns, turn, last, drain = line_reduce_scatter(t, seq, tp, own, inbox, (sr, rr, sl, rl), finish)
    slots = 20

    def pump(slot):
        def one(i, c):
            turn(i)
            return c

        lax.fori_loop(slot * turns // slots, (slot + 1) * turns // slots, one, 0)

    fetches[0].wait()
    for copy in inputs[:4]:
        copy.wait()

    def gates(i, c):
        pump(i)
        at = pl.ds(pl.multiple_of(i * tile, tile), tile)
        shifted = pl.ds(pl.multiple_of(i * tile + 8, 8), tile)
        g = nn(gmix[at, :], w1[:, 3 * chan :])
        hat = get(states, shifted) * invst[at, :]
        o = opre[at, :]
        sig = jax.nn.sigmoid(o)
        q = o * sig
        vecs[2:3, :] += jnp.sum(g * hat * q, axis=0, keepdims=True)
        out3[at, 2 * chan :] = (g * hat * sgain * (sig * (1.0 + o * (1.0 - sig)))).astype(BF)
        w = g * q * sgain
        put(weighted, at, w)
        inner[at, :] = w * hat
        return c

    lax.fori_loop(0, 3, gates, 0)
    dot = sum_over_tp(row_sums(inner[...]), t, seq, tp, zslots, zs, zr, lambda: pump(3)) / width
    inner[:, 0:1] = dot

    def leaving(i, c):
        at = pl.ds(pl.multiple_of(i * tile, tile), tile)
        shifted = pl.ds(pl.multiple_of(i * tile + 8, 8), tile)
        inv = invst[at, :]
        put(weighted, at, inv * (get(weighted, at) - get(states, shifted) * inv * inner[at, 0:1]))
        return c

    lax.fori_loop(0, 3, leaving, 0)
    inputs[4].wait()

    length = rows // SEG

    def scan(i, c):
        p, h = c
        r = length - 1 - i
        at = pl.ds(r, SEG, stride=length)
        f = get(feff, pl.ds(r + 1, SEG, stride=length))
        h = f * h + get(weighted, at)
        p = f * p
        put(weighted, at, h)
        put(prod, at, p)
        return p, h

    p, h = lax.fori_loop(
        0, length, scan, (jnp.ones((SEG, chan), F32), jnp.zeros((SEG, chan), F32))
    )
    block_p, block_h = p[SEG - 1 : SEG], h[SEG - 1 : SEG]
    for s in range(SEG - 2, -1, -1):
        block_h = h[s : s + 1] + p[s : s + 1] * block_h
        block_p = p[s : s + 1] * block_p
    first = get(feff, slice(0, 1))
    arriving = carry_over_seq(
        first * block_p, first * block_h, n, seq, tp, cslots, cs, cr, True, lambda: pump(4)
    )
    inputs[5].wait()
    inputs[6].wait()
    bias_sum = jnp.zeros((1, chan), F32)
    for s in range(SEG - 1, -1, -1):
        pump(12 - s)
        at = slice(s * length, (s + 1) * length)
        gs = get(weighted, at) + get(prod, at) * arriving
        arriving = h[s : s + 1] + p[s : s + 1] * arriving
        a = ipre[at, :]
        sa = jax.nn.sigmoid(a)
        act = a * sa
        sf = jax.nn.sigmoid(fpre[at, :])
        gate = bound + (1.0 - bound) * sf
        ok, starts = masks(lens, seq * rows + s * length, length)
        out3[at, :chan] = (gs * (1.0 - gate) * ok * (sa * (1.0 + a * (1.0 - sa)))).astype(BF)
        before = get(states, slice(s * length + 7, (s + 1) * length + 7))
        gate_grad = gs * before * (1.0 - starts) - gs * act * ok
        gf = (gate_grad * (1.0 - bound) * sf * (1.0 - sf)).astype(BF)
        out3[at, chan : 2 * chan] = gf
        bias_sum = bias_sum + jnp.sum(gf.astype(F32), axis=0, keepdims=True)
    vecs[1:2, :] = bias_sum

    def gni_copy(i):
        at = pl.ds(pl.multiple_of(i * tile, tile), tile)
        return pltpu.make_async_copy(gni.at[:, at], gni_h.at[:, at], s_o.at[i])

    for copy in inputs[7:]:
        copy.wait()

    def spread_in(i, c):
        at = pl.ds(pl.multiple_of(i * tile, tile), tile)
        put_shards(gni, at, nt(out3[at, :], w1[:, : 3 * chan]).astype(BF))
        gni_copy(i).start()
        pump(13 + i)
        return c

    lax.fori_loop(0, 3, spread_in, 0)

    ga, gb, h = dw1_h.shape[2:5]
    span = 4 * h

    def d_copy(r, slot):
        return pltpu.make_async_copy(
            stage.at[slot], dw1_h.at[:, :, r // gb, lax.rem(r, gb)], s_d.at[slot]
        )

    def slab(r, c):
        slot = lax.rem(r, 2)

        @pl.when(r >= 2)
        def _():
            d_copy(r - 2, slot).wait()

        at = pl.ds(pl.multiple_of(r * span, span), span)
        put_blocks(stage.at[slot, :, :, :, pl.ds(0, 3 * chan)], h, tn(normed[:, at], out3[...]))
        put_blocks(stage.at[slot, :, :, :, pl.ds(3 * chan, chan)], h, tn(gmix[:, at], gated[...]))
        d_copy(r, slot).start()

        @pl.when(r < 4)
        def _():
            pump(16 + r)

        return c

    lax.fori_loop(0, ga * gb, slab, 0)
    for r in range(ga * gb, 4):
        pump(16 + r)
    for copy in fetches[1:]:
        copy.wait()

    def ending(k, c):
        last(k)
        return c

    lax.fori_loop(0, SHARD_CHUNKS, ending, 0)
    for r in range(max(ga * gb - 2, 0), ga * gb):
        d_copy(r, r % 2).wait()

    def stored(i, c):
        gni_copy(i).wait()
        return c

    lax.fori_loop(0, 3, stored, 0)
    drain()


def closing(
    n, t, width,
    gni_h, dw1_h, x_h, gres_h, invin, consts, vecs, ggain,
    gin, allvec, sums,
    xc, gres, own, inbox, scaled, inner, zslots, vslots,
    s_own, s_x, sr, rr, sl, rl, zs, zr, vs, vr, ts, tr, *bufs,
):
    seq, tp = lax.axis_index("seq"), lax.axis_index("tp")
    rows, chan = gres.shape
    mine = pl.ds(pl.multiple_of(tp * chan, LANE), chan)
    fetch = pltpu.make_async_copy(gni_h, own, s_own)
    fetches = [
        pltpu.make_async_copy(x_h.at[:, mine], xc, s_x.at[0]),
        pltpu.make_async_copy(gres_h, gres, s_x.at[1]),
    ]
    fetch.start()
    greet_all(n, t, seq, tp)
    pieces, shard, cols = sums.shape

    def out(j, half, values):
        sums[j, half * (shard // 2) : (half + 1) * (shard // 2), :] = values

    start, stage1, stage2, stage3, drain_grid = grid_reduce(
        n, seq, tp, dw1_h, pieces, cols, bufs, out
    )
    fetch.wait()
    start(0)
    for copy in fetches:
        copy.start()
    step = rows // SHARD_CHUNKS
    gain_in = consts[4:5, mine]
    vslots[seq] = vecs[...]
    vslots[seq, 3:4, :] = ggain[0:1, mine]

    def finish(k, values):
        at = pl.ds(pl.multiple_of(k * step, step), step)
        hat = xc[at, :].astype(F32) * invin[at, :]
        s = values * gain_in
        scaled[at, :] = s
        inner[at, :] = s * hat
        vslots[seq, 0:1, :] += jnp.sum(values * hat, axis=0, keepdims=True)

    turns, turn, last, drain = line_reduce_scatter(t, seq, tp, own, inbox, (sr, rr, sl, rl), finish)
    works = [
        (2, lambda: (stage1(0), start(1))),
        (5, lambda: stage1(1)),
        (6, lambda: stage2(0)),
        (9, lambda: stage3(0)),
        (10, lambda: stage2(1)),
        (13, lambda: stage3(1)),
    ]
    slots = 16

    def turn_of(slot, c):
        def one(i, c):
            turn(i)
            return c

        lax.fori_loop(slot * turns // slots, (slot + 1) * turns // slots, one, 0)
        for when, work in works:

            @pl.when(slot == when)
            def _(work=work):
                work()

        return c

    lax.fori_loop(0, slots, turn_of, 0)
    for copy in fetches:
        copy.wait()

    def ending(k, c):
        last(k)
        return c

    lax.fori_loop(0, SHARD_CHUNKS, ending, 0)
    go_v, done_v = spread(n, seq, vslots, vs, vr, lambda k: (k, tp))
    dot = sum_over_tp(row_sums(inner[...]), t, seq, tp, zslots, zs, zr, go_v) / width
    done_v()
    total = vslots[0]
    for k in range(1, n):
        total = total + vslots[k]
    allvec[tp] = total
    go_t, done_t = spread(t, tp, allvec, ts, tr, lambda k: (seq, k))
    go_t()
    gin[...] = gres[...] + invin[...] * (scaled[...] - xc[...].astype(F32) * invin[...] * dot)
    done_t()
    drain()
    drain_grid()


def params(collective=None, limit=VMEM_LIMIT):
    if collective is None:
        return pltpu.CompilerParams(vmem_limit_bytes=limit)
    return pltpu.CompilerParams(
        vmem_limit_bytes=limit, collective_id=collective, has_side_effects=True
    )


def line_sems(chunks):
    return [DMA((chunks,)), DMA((chunks,)), DMA((2, chunks))]


def on_device(
    n, t,
    hidden_in, gain_in, w_input, w_forget, forget_bias, w_outgate, state_gain, w_output,
    gain_mid, w_gate, w_up, w_down, lengths, layer_index, cotangent,
):
    rows, width = hidden_in.shape
    chan = w_input.shape[1]
    ff = w_gate.shape[1]
    ffp = -(-ff // LANE) * LANE

    def padded(w):
        return w if ffp == ff else jnp.pad(w, ((0, 0), (0, ffp - ff)))

    total = lengths[0] + lengths[1]
    bound = layer_index[0].astype(F32) / LAYERS
    consts = jnp.stack(
        [
            forget_bias,
            state_gain.astype(F32),
            jnp.broadcast_to(bound, (width,)),
            gain_mid.astype(F32),
            gain_in.astype(F32),
        ]
        + [jnp.zeros((width,), F32)] * 3
    )
    plane = shape((rows, chan), F32)
    plane16 = shape((rows, chan), BF)
    column = shape((rows, 1), F32)
    wide16 = shape((rows, width), BF)
    shards16 = shape((t, rows, chan), BF)
    ga, gb = chip_grid(n)
    h = width // n // 2

    def groups(more=0):
        return shape((chan // LANE, rows + more, LANE), F32)

    def vm(*arrays):
        return [pltpu.VMEM(a.shape, a.dtype) for a in arrays]

    SM = pl.BlockSpec(memory_space=pltpu.SMEM)
    w1s, w2s = shape((4, width, chan), BF), shape((3, width, ffp), BF)
    zslot, vslot = pltpu.VMEM((t, 8, rows), F32), pltpu.VMEM((n, 8, chan), F32)
    small = [DMA((n,)), DMA((n,)), DMA((t,)), DMA((t,))]
    saved = [plane, plane, plane, groups(8), groups(8), plane16, wide16]

    (
        ipre, fpre, opre, feff, states, gated, normed_in, nmid, mixed, w1, w2, invst, invmid, inv_in,
    ) = pl.pallas_call(
        functools.partial(mixer_forward, n, t, width),
        out_shape=saved + [wide16, wide16, w1s, w2s, column, column, column],
        in_specs=[SM] + [HB] * 8 + [VM],
        out_specs=[HB] * 11 + [VM] * 3,
        scratch_shapes=[
            *vm(wide16, wide16, plane, plane, plane, groups(8), groups(8), plane16, wide16, w1s),
            *vm(groups(), plane),
            pltpu.VMEM((rows // CHUNKS * 4, width), F32),
            vslot,
            zslot,
            pltpu.VMEM((rows, width), BF),
            pltpu.VMEM((2, rows, width), BF),
            DMA, DMA((7,)), DMA((4,)), DMA((CHUNKS,)), DMA((CHUNKS,)),
            *small,
            *line_sems(CHUNKS),
            *gather_sems(n, 4),
            *gather_sems(n, 3),
        ],
        compiler_params=params(1),
        name="mixer_forward",
    )(
        lengths, hidden_in, w_input, w_forget, w_outgate, w_output.T,
        padded(w_gate), padded(w_up), padded(w_down.T), consts,
    )

    gnm_part, glu_part, dw2 = pl.pallas_call(
        feed_forward,
        out_shape=[wide16, shards16, shape((2, 2, ga, gb, h, 3 * ffp), BF)],
        in_specs=[HB] * 3,
        out_specs=[HB] * 3,
        scratch_shapes=[
            *vm(wide16, wide16),
            *[pltpu.VMEM((width, ffp), BF)] * 3,
            *[pltpu.VMEM((rows, ffp), BF)] * 3,
            *vm(wide16, shards16),
            pltpu.VMEM((2, 2, 2, h, ffp), BF),
            DMA((3,)), DMA((2,)), DMA((2, 3)), DMA((2,)),
        ],
        compiler_params=params(),
        name="feed_forward",
    )(nmid, cotangent, w2)

    sums2s = shape((3, 2 * h, ffp), F32)
    gmix, gres, ggain, sums2 = pl.pallas_call(
        functools.partial(mid_backward, n, t, width),
        out_shape=[wide16, plane, shape((8, width), F32), sums2s],
        in_specs=[HB] * 5 + [VM] * 2,
        out_specs=[HB] * 2 + [VM, HB],
        scratch_shapes=[
            *vm(wide16, wide16, wide16, wide16, plane, sums2s, wide16),
            pltpu.VMEM((2, rows, width), BF),
            pltpu.VMEM((rows // CHUNKS, width), F32),
            DMA, DMA((3,)), DMA((2, CHUNKS)), DMA((3,)),
            *line_sems(CHUNKS),
            *grid_buffers(n, width, 3, ffp),
        ],
        compiler_params=params(2),
        name="mid_backward",
    )(gnm_part, dw2, hidden_in, mixed, cotangent, invmid, consts)

    shard_sems = [DMA((t, SHARD_CHUNKS))] * 4
    shard_bufs = [pltpu.VMEM((t, rows, chan), BF), pltpu.VMEM((t + 1, rows, chan), BF)]
    gni_part, dw1, vecs, block_out = pl.pallas_call(
        functools.partial(mixer_backward, n, t, width),
        out_shape=[
            shards16, shape((2, 2, ga, gb, h, 4 * chan), BF), shape((8, chan), F32), plane16,
        ],
        in_specs=[SM] + [HB] * 12 + [VM] * 2,
        out_specs=[HB] * 2 + [VM] * 2,
        scratch_shapes=[
            *vm(wide16, wide16),
            pltpu.VMEM((width, 4 * chan), BF),
            *vm(plane16, groups(8), groups(8), plane, plane, plane),
            *vm(groups(), groups(), plane, shape((rows, 3 * chan), BF)),
            vslot,
            zslot,
            *vm(plane16, plane16),
            *shard_bufs,
            *vm(shards16),
            pltpu.VMEM((2, 2, 2, h, 4 * chan), BF),
            DMA((12,)),
            *small,
            DMA((3,)),
            *shard_sems,
            DMA((3,)), DMA((2,)),
        ],
        compiler_params=params(3),
        name="mixer_backward",
    )(
        lengths, glu_part, hidden_in, mixed, gmix, normed_in, w1, gated, states, feff, ipre, fpre, opre,
        invst, consts,
    )

    grad_in, allvec, sums1 = pl.pallas_call(
        functools.partial(closing, n, t, width),
        out_shape=[plane, shape((t, 8, chan), F32), shape((2, 2 * h, 2 * chan), F32)],
        in_specs=[HB] * 4 + [VM] * 4,
        out_specs=[VM] * 3,
        scratch_shapes=[
            *vm(plane16, plane),
            *shard_bufs,
            *vm(plane, plane),
            zslot,
            vslot,
            DMA, DMA((2,)),
            *shard_sems,
            DMA((t,)), DMA((t,)), DMA((n,)), DMA((n,)), DMA((t,)), DMA((t,)),
            *grid_buffers(n, width, 2, 2 * chan),
        ],
        compiler_params=params(4),
        name="closing",
    )(gni_part, dw1, hidden_in, gres, inv_in, consts, vecs, ggain)

    def vector(r):
        return allvec[:, r, :].reshape(width)

    squares = jnp.stack([jnp.sum(allvec[:, r, :]) for r in (4, 5, 6)])
    rms_stats = jnp.sqrt(squares / (total.astype(F32) * width))

    return (
        block_out,
        grad_in,
        vector(0),
        sums1[0, :, :chan],
        sums1[0, :, chan:],
        vector(1),
        sums1[1, :, :chan],
        vector(2),
        sums1[1, :, chan:].T,
        vector(3),
        sums2[0, :, :ff],
        sums2[1, :, :ff],
        sums2[2, :, :ff].T,
        rms_stats,
    )


def solution(mesh):
    weight, turned = P("seq", "tp"), P("tp", "seq")
    in_specs = (
        P("seq", None), P(), weight, weight, P(), weight, P(), turned, P(), weight, weight, turned,
        P(), P(), P("seq", None),
    )
    out_specs = (
        weight, weight, P(), weight, weight, P(), weight, P(), turned, P(), weight, weight, turned, P(),
    )
    body = functools.partial(on_device, mesh.shape["seq"], mesh.shape["tp"])
    return jax.shard_map(
        body, mesh=mesh, in_specs=in_specs, out_specs=out_specs, check_vma=False
    )
```

```python
import functools

import jax
import jax.numpy as jnp
from jax import lax
from jax.experimental import pallas as pl
from jax.experimental.pallas import tpu as pltpu
from jax.sharding import PartitionSpec as P

LAYERS = 24
EPS = 1e-06
MESH = pl.DeviceIdType.MESH
DMA = pltpu.SemaphoreType.DMA
BF = jnp.bfloat16
F32 = jnp.float32
VM = pl.BlockSpec(memory_space=pltpu.VMEM)
HB = pl.BlockSpec(memory_space=pl.ANY)
LANE = 128
SEG = 8
TILES = 4
K2_LAGS = (2, 2, 3)
CHUNKS = 16
SHARD_CHUNKS = 4
HOP_LAG = 2
VMEM_LIMIT = 60 * 1024 * 1024


def nn(left, right):
    return jnp.dot(left, right, preferred_element_type=F32)


def nt(left, right):
    return lax.dot_general(left, right, (((1,), (1,)), ((), ())), preferred_element_type=F32)


def tn(left, right):
    return lax.dot_general(left, right, (((0,), (0,)), ((), ())), preferred_element_type=F32)


def shape(dims, dtype):
    return jax.ShapeDtypeStruct(dims, dtype)


def get(ref, at):
    return jnp.concatenate([ref[g, at, :] for g in range(ref.shape[0])], axis=1)


def put(ref, at, values):
    for g in range(ref.shape[0]):
        ref[g, at, :] = values[:, g * LANE : (g + 1) * LANE]


def put_shards(ref, at, values):
    k = ref.shape[2]
    for q in range(ref.shape[0]):
        ref[q, at, :] = values[:, q * k : (q + 1) * k]


def row_tile(rows):
    return rows // 3 if rows % 48 == 0 else rows


def greet_all(n, t, seq, tp):
    barrier = pltpu.get_barrier_semaphore()

    def along_seq(o, c):
        pl.semaphore_signal(barrier, inc=1, device_id=(lax.rem(seq + o, n), tp), device_id_type=MESH)
        return c

    def along_tp(o, c):
        pl.semaphore_signal(barrier, inc=1, device_id=(seq, lax.rem(tp + o, t)), device_id_type=MESH)
        return c

    lax.fori_loop(1, n, along_seq, 0)
    lax.fori_loop(1, t, along_tp, 0)
    pl.semaphore_wait(barrier, n - 1 + t - 1)


def greet_line(t, seq, tp):
    barrier = pltpu.get_barrier_semaphore()

    def along_tp(o, c):
        pl.semaphore_signal(barrier, inc=1, device_id=(seq, lax.rem(tp + o, t)), device_id_type=MESH)
        return c

    lax.fori_loop(1, t, along_tp, 0)
    pl.semaphore_wait(barrier, t - 1)


def spread(size, me, slots, send, recv, target):
    def copy(o, slot):
        return pltpu.make_async_remote_copy(
            src_ref=slots.at[slot],
            dst_ref=slots.at[slot],
            send_sem=send.at[o],
            recv_sem=recv.at[slot],
            device_id=target(lax.rem(me + o, size)),
            device_id_type=MESH,
        )

    def one(o, c):
        copy(o, me).start()
        return c

    def arrived(o, c):
        copy(o, lax.rem(me + o, size)).wait_recv()
        return c

    def sent(o, c):
        copy(o, me).wait_send()
        return c

    def go():
        lax.fori_loop(1, size, one, 0)

    def done():
        lax.fori_loop(1, size, arrived, 0)
        lax.fori_loop(1, size, sent, 0)

    return go, done


def row_sums(values):
    ones = jnp.ones((8, values.shape[1]), BF)
    high = values.astype(BF)
    rest = values - high.astype(F32)
    low = rest.astype(BF)
    return nt(ones, high) + nt(ones, low)


def sum_over_tp(part, t, seq, tp, slots, send, recv, between=None):
    slots[tp] = part
    go, done = spread(t, tp, slots, send, recv, lambda k: (seq, k))
    go()
    if between is not None:
        between()
    done()
    total = slots[0]
    for k in range(1, t):
        total = total + slots[k]
    return jnp.transpose(total)[:, :1]


def carry_over_seq(prod, state, n, seq, tp, slots, send, recv, backward, between=None):
    slots[seq] = jnp.concatenate([prod, state] + [jnp.zeros_like(prod)] * 6, axis=0)
    go, done = spread(n, seq, slots, send, recv, lambda k: (k, tp))
    go()
    if between is not None:
        between()
    done()

    def hop(i, total):
        j = n - 1 - i if backward else i
        block = slots[j]
        longer = block[1:2] + block[0:1] * total
        inside = (j > seq) if backward else (j < seq)
        return jnp.where(inside, longer, total)

    return lax.fori_loop(0, n, hop, jnp.zeros_like(prod))


def line_all_reduce(t, seq, tp, rows, chunks, partial, send, buf, sems, finish, lags):
    s_in, s_out, r_buf = sems
    step = rows // chunks
    half = t // 2
    depth = jnp.where(tp < half, tp, t - 1 - tp)
    inner = jnp.where(tp < half, tp + 1, tp - 1)
    outer = jnp.where(tp < half, tp - 1, tp + 1)
    outer = jnp.where(depth > 0, outer, inner)
    middle = (depth == half - 1).astype(jnp.int32)
    lag_in, lag_turn, lag_out = lags
    lag_first = lag_in * depth
    lag_second = lag_in * (half - 1) + lag_turn + lag_out * (half - 1 - depth)

    def part_of(k):
        return pl.ds(pl.multiple_of(k * step, step), step)

    def inward(k, slot):
        return pltpu.make_async_remote_copy(
            src_ref=send.at[part_of(k)],
            dst_ref=buf.at[slot, part_of(k)],
            send_sem=s_in.at[k],
            recv_sem=r_buf.at[slot, k],
            device_id=(seq, inner),
            device_id_type=MESH,
        )

    def outward(k):
        return pltpu.make_async_remote_copy(
            src_ref=buf.at[1, part_of(k)],
            dst_ref=buf.at[1, part_of(k)],
            send_sem=s_out.at[k],
            recv_sem=r_buf.at[1, k],
            device_id=(seq, outer),
            device_id_type=MESH,
        )

    def first(k):
        part = None if partial is None else partial(k)

        @pl.when(depth > 0)
        def _():
            inward(k, 0).wait_recv()
            mine = send[part_of(k), :].astype(F32) if part is None else part
            send[part_of(k), :] = (mine + buf[0, part_of(k), :].astype(F32)).astype(BF)

        if part is not None:

            @pl.when(depth == 0)
            def _():
                send[part_of(k), :] = part.astype(BF)

        inward(k, middle).start()

    def second(k):
        inward(k, 1).wait_recv()

        @pl.when(middle == 1)
        def _():
            both = send[part_of(k), :].astype(F32) + buf[1, part_of(k), :].astype(F32)
            buf[1, part_of(k), :] = both.astype(BF)

        @pl.when(depth > 0)
        def _():
            outward(k).start()

        finish(k)

    def turn(i):
        @pl.when((i >= lag_first) & (i - lag_first < chunks))
        def _():
            first(i - lag_first)

        @pl.when((i >= lag_second) & (i - lag_second < chunks))
        def _():
            second(i - lag_second)

    def drain():
        def sent(k, c):
            inward(k, middle).wait_send()

            @pl.when(depth > 0)
            def _():
                outward(k).wait_send()

            return c

        lax.fori_loop(0, chunks, sent, 0)

    return chunks + lag_in * (half - 1) + lag_turn + lag_out * (half - 1), turn, drain


def line_reduce_scatter(t, seq, tp, own, inbox, sems, finish):
    s_r, r_r, s_l, r_l = sems
    rows = own.shape[1]
    chunks = SHARD_CHUNKS
    step = rows // chunks
    count = chunks * (t - 1)

    def part_of(k):
        return pl.ds(pl.multiple_of(k * step, step), step)

    def rightward(q, k):
        return pltpu.make_async_remote_copy(
            src_ref=own.at[q, part_of(k)],
            dst_ref=inbox.at[q + 1, part_of(k)],
            send_sem=s_r.at[q, k],
            recv_sem=r_r.at[q, k],
            device_id=(seq, lax.rem(tp + 1, t)),
            device_id_type=MESH,
        )

    def leftward(q, k):
        return pltpu.make_async_remote_copy(
            src_ref=own.at[q, part_of(k)],
            dst_ref=inbox.at[q, part_of(k)],
            send_sem=s_l.at[q, k],
            recv_sem=r_l.at[q, k],
            device_id=(seq, lax.rem(tp + t - 1, t)),
            device_id_type=MESH,
        )

    def add(q, k, slot):
        own[q, part_of(k), :] = (
            own[q, part_of(k), :].astype(F32) + inbox[slot, part_of(k), :].astype(F32)
        ).astype(BF)

    def right_turn(i):
        k, j = i // (t - 1), lax.rem(i, t - 1)
        q = t - 1 - j

        @pl.when((i >= 0) & (i < count) & (q > tp))
        def _():
            @pl.when(tp > 0)
            def _():
                rightward(q, k).wait_recv()
                add(q, k, q + 1)

            rightward(q, k).start()

    def left_turn(i):
        k, q = i // (t - 1), lax.rem(i, t - 1)

        @pl.when((i >= 0) & (i < count) & (q < tp))
        def _():
            @pl.when(tp < t - 1)
            def _():
                leftward(q, k).wait_recv()
                add(q, k, q)

            leftward(q, k).start()

    def turn(i):
        right_turn(i - HOP_LAG * tp)
        left_turn(i - HOP_LAG * (t - 1 - tp))

    def last(k):
        @pl.when(tp == 0)
        def _():
            leftward(tp, k).wait_recv()
            finish(k, own[tp, part_of(k), :].astype(F32) + inbox[tp, part_of(k), :].astype(F32))

        @pl.when(tp == t - 1)
        def _():
            rightward(tp, k).wait_recv()
            finish(k, own[tp, part_of(k), :].astype(F32) + inbox[tp + 1, part_of(k), :].astype(F32))

        @pl.when((tp > 0) & (tp < t - 1))
        def _():
            leftward(tp, k).wait_recv()
            rightward(tp, k).wait_recv()
            finish(
                k,
                own[tp, part_of(k), :].astype(F32)
                + inbox[tp, part_of(k), :].astype(F32)
                + inbox[tp + 1, part_of(k), :].astype(F32),
            )

    def drain():
        def sent(i, c):
            k = i // (t - 1)
            j = lax.rem(i, t - 1)

            @pl.when(t - 1 - j > tp)
            def _():
                rightward(t - 1 - j, k).wait_send()

            @pl.when(j < tp)
            def _():
                leftward(j, k).wait_send()

            return c

        lax.fori_loop(0, count, sent, 0)

    return count + HOP_LAG * (t - 2), turn, last, drain


def chip_grid(n):
    chips = n // 2
    b = max(k for k in range(1, chips + 1) if chips % k == 0 and k * k <= chips)
    return chips // b, b


def grid_buffers(n, width, pieces, cols):
    ga, gb = chip_grid(n)
    h = width // n // 2
    pa, pb = max(ga - 1, 1), max(gb - 1, 1)
    return [
        pltpu.VMEM((pieces, pb, ga, h, cols), BF),
        pltpu.VMEM((pieces, pa, gb, h, cols), BF),
        pltpu.VMEM((pieces, pa, h, cols), BF),
        pltpu.VMEM((pieces, pb, h, cols), BF),
        DMA((2, pieces, pb, ga)), DMA((2, pieces, pa, gb)), DMA((2, pieces, pa)), DMA((2, pieces, pb)),
    ]


def add_cores(acc, first):
    part = 64

    def one(i, c):
        at = pl.ds(pl.multiple_of(i * part, part), part)
        acc[at, :] = (acc[at, :].astype(F32) + first[at, :].astype(F32)).astype(BF)
        return c

    lax.fori_loop(0, acc.shape[0] // part, one, 0)


def grid_reduce(n, seq, tp, j, acc, bufs, out):
    far_b, far_a, near_a, near_b, m_fb, m_fa, m_na, m_nb = bufs
    ga, gb = chip_grid(n)
    core = lax.rem(seq, 2)
    a, b = seq // 2 // gb, lax.rem(seq // 2, gb)
    h = near_a.shape[2]

    def device(a_, b_):
        return ((a_ * gb + b_) * 2 + core, tp)

    def block(half, x, y):
        return pl.ds(pl.multiple_of(((x * gb + y) * 2 + half) * h, h), h)

    def remote(rows, dst, sems, index, target):
        return pltpu.make_async_remote_copy(
            src_ref=acc.at[rows],
            dst_ref=dst,
            send_sem=sems.at[(0, j) + index],
            recv_sem=sems.at[(1, j) + index],
            device_id=target,
            device_id_type=MESH,
        )

    def first_way():
        copies = []
        for o in range(1, gb):
            to = lax.rem(b + o, gb)
            for x in range(ga):
                dst = far_b.at[j, o - 1, x]
                copies.append(remote(block(0, x, to), dst, m_fb, (o - 1, x), device(a, to)))
        for o in range(1, ga):
            to = lax.rem(a + o, ga)
            for y in range(gb):
                dst = far_a.at[j, o - 1, y]
                copies.append(remote(block(1, to, y), dst, m_fa, (o - 1, y), device(to, b)))
        return copies

    def second_way():
        copies = []
        for o in range(1, ga):
            to = lax.rem(a + o, ga)
            copies.append(
                remote(block(0, to, b), near_a.at[j, o - 1], m_na, (o - 1,), device(to, b))
            )
        for o in range(1, gb):
            to = lax.rem(b + o, gb)
            copies.append(
                remote(block(1, a, to), near_b.at[j, o - 1], m_nb, (o - 1,), device(a, to))
            )
        return copies

    def far():
        for copy in first_way():
            copy.start()

    def middle():
        for copy in first_way():
            copy.wait_recv()

        def along_a(x, c):
            total = acc[block(0, x, b), :].astype(F32)
            for o in range(1, gb):
                total = total + far_b[j, o - 1, x].astype(F32)
            acc[block(0, x, b), :] = total.astype(BF)
            return c

        def along_b(y, c):
            total = acc[block(1, a, y), :].astype(F32)
            for o in range(1, ga):
                total = total + far_a[j, o - 1, y].astype(F32)
            acc[block(1, a, y), :] = total.astype(BF)
            return c

        lax.fori_loop(0, ga, along_a, 0)
        lax.fori_loop(0, gb, along_b, 0)
        for copy in second_way():
            copy.start()

    def near():
        for copy in second_way():
            copy.wait_recv()
        total = acc[block(0, a, b), :].astype(F32)
        for o in range(1, ga):
            total = total + near_a[j, o - 1].astype(F32)
        out(0, total)
        total = acc[block(1, a, b), :].astype(F32)
        for o in range(1, gb):
            total = total + near_b[j, o - 1].astype(F32)
        out(1, total)

    def drain():
        for copy in first_way() + second_way():
            copy.wait_send()

    return far, middle, near, drain


def gather_sems(n, pieces):
    ga, gb = chip_grid(n)
    pa, pb = max(ga - 1, 1), max(gb - 1, 1)
    return [
        DMA((pieces,)), DMA((2, pieces, ga * gb)),
        DMA((2, pieces, pb)), DMA((2, pieces, pa)), DMA((2, pieces, gb, pa)), DMA((2, pieces, ga, pb)),
    ]


def grid_gather(n, seq, tp, j, src, dst, sems):
    s_local, m_core, m_fb, m_fa, m_na, m_nb = sems
    ga, gb = chip_grid(n)
    shard = src.shape[0]
    h = shard // 2
    core = lax.rem(seq, 2)
    a, b = seq // 2 // gb, lax.rem(seq // 2, gb)

    def device(a_, b_, core_):
        return ((a_ * gb + b_) * 2 + core_, tp)

    def block(x, y, core_, half, count):
        return pl.ds(pl.multiple_of(((x * gb + y) * 2 + core_) * shard + half * h, h), count)

    def remote(from_, rows, sem, index, target):
        return pltpu.make_async_remote_copy(
            src_ref=from_,
            dst_ref=dst.at[rows],
            send_sem=sem.at[(0, j) + index],
            recv_sem=sem.at[(1, j) + index],
            device_id=target,
            device_id_type=MESH,
        )

    def own(half):
        return src.at[pl.ds(half * h, h)]

    def far(incoming):
        copies = []
        for o in range(1, gb):
            to, of = lax.rem(b + o, gb), lax.rem(b + gb - o, gb)
            rows = block(a, of if incoming else b, core, 0, h)
            copies.append(remote(own(0), rows, m_fb, (o - 1,), device(a, to, core)))
        for o in range(1, ga):
            to, of = lax.rem(a + o, ga), lax.rem(a + ga - o, ga)
            rows = block(of if incoming else a, b, core, 1, h)
            copies.append(remote(own(1), rows, m_fa, (o - 1,), device(to, b, core)))
        return copies

    def near(incoming, first, least):
        copies = []
        for i in range(0 if first else 1, gb if least else 1):
            y = lax.rem(b + gb - i, gb)
            for o in range(1, ga):
                to, of = lax.rem(a + o, ga), lax.rem(a + ga - o, ga)
                rows = block(of if incoming else a, y, core, 0, h)
                from_ = own(0) if i == 0 or incoming else dst.at[rows]
                copies.append(remote(from_, rows, m_na, (i, o - 1), device(to, b, core)))
        for i in range(0 if first else 1, ga if least else 1):
            x = lax.rem(a + ga - i, ga)
            for o in range(1, gb):
                to, of = lax.rem(b + o, gb), lax.rem(b + gb - o, gb)
                rows = block(x, of if incoming else b, core, 1, h)
                from_ = own(1) if i == 0 or incoming else dst.at[rows]
                copies.append(remote(from_, rows, m_nb, (i, o - 1), device(a, to, core)))
        return copies

    def across(incoming, first, others):
        copies = []
        for i in range(ga):
            for k in range(gb):
                mine = i == 0 and k == 0
                if (mine and not first) or (not mine and not others):
                    continue
                x, y = lax.rem(a + i, ga), lax.rem(b + k, gb)
                rows = block(x, y, 1 - core if incoming else core, 0, shard)
                from_ = src if mine or incoming else dst.at[rows]
                copies.append(remote(from_, rows, m_core, (i * gb + k,), device(a, b, 1 - core)))
        return copies

    def local():
        return pltpu.make_async_copy(src, dst.at[block(a, b, core, 0, shard)], s_local.at[j])

    def start():
        for copy in far(False) + near(False, True, False) + across(False, True, False):
            copy.start()
        local().start()

    def relay():
        for copy in far(True):
            copy.wait_recv()
        for copy in near(False, False, True):
            copy.start()

    def share():
        for copy in near(True, True, True):
            copy.wait_recv()
        for copy in across(False, False, True):
            copy.start()

    def arrive():
        for copy in across(True, True, True):
            copy.wait_recv()
        local().wait()

    def drain():
        for copy in far(False) + near(False, True, True) + across(False, True, True):
            copy.wait_send()

    return start, relay, share, arrive, drain


def loop_with(first, last, body, works):
    def one(i, c):
        body(i)
        for when, work in works:

            @pl.when(i == when)
            def _(work=work):
                work()

        return c

    lax.fori_loop(first, last, one, 0)


def masks(lens, first, count):
    at = first + lax.broadcasted_iota(jnp.int32, (count, 1), 0)
    valid = (at < lens[0] + lens[1]).astype(F32)
    starts = ((at == 0) | (at == lens[0])).astype(F32)
    return valid, starts


def mixer_forward(
    n, t, width,
    lens, x_h, wi_h, wf_h, wo_h, wx_h, wg_h, wu_h, wd_h, consts,
    ipre_h, fpre_h, opre_h, feff_h, states_h, gated_h, normed_h, nmid_h, mixed_h, w1_h, w2_h,
    invst, invmid, invin,
    x, normed, ipre, fpre, opre, feff, states, gated, nmid, w1, prod, ssq, part, cslots, zslots, send, buf,
    s_x, s_st, s_w, s_n, s_m, cs, cr, zs, zr, s_in, s_out, r_buf, *sems,
):
    seq, tp = lax.axis_index("seq"), lax.axis_index("tp")
    load = pltpu.make_async_copy(x_h, x, s_x)
    load.start()
    sems1, sems2 = sems[:6], sems[6:]
    one = [
        grid_gather(n, seq, tp, j, src, w1.at[j], sems1)
        for j, src in enumerate((wi_h, wf_h, wo_h, wx_h))
    ]
    two = [
        grid_gather(n, seq, tp, j, src, w2_h.at[j], sems2)
        for j, src in enumerate((wg_h, wu_h, wd_h))
    ]
    START, RELAY, SHARE, ARRIVE, DRAIN = range(5)
    greet_all(n, t, seq, tp)
    one[0][START]()
    rows, depth = normed.shape
    chan = ipre.shape[1]
    tile = row_tile(rows)
    mine = pl.ds(pl.multiple_of(tp * chan, LANE), chan)
    bias, sgain, bound = consts[0:1, mine], consts[1:2, mine], consts[2:3, mine]

    def stores():
        pairs = (
            (ipre, ipre_h), (fpre, fpre_h), (opre, opre_h), (feff, feff_h), (states, states_h),
            (gated, gated_h), (normed, normed_h),
        )
        return [pltpu.make_async_copy(v, o, s_st.at[i]) for i, (v, o) in enumerate(pairs)]

    def keep(j):
        return pltpu.make_async_copy(w1.at[j], w1_h.at[j], s_w.at[j])

    load.wait()

    def norm(i, c):
        at = pl.ds(pl.multiple_of(i * tile, tile), tile)
        v = x[at, :].astype(F32)
        inv = lax.rsqrt(jnp.mean(v * v, axis=-1, keepdims=True) + EPS)
        invin[at, :] = inv
        normed[at, :] = (v * inv * consts[4:5, :]).astype(BF)
        return c

    lax.fori_loop(0, rows // tile, norm, 0)
    one[0][RELAY]()
    one[1][START]()
    one[0][SHARE]()
    one[1][RELAY]()
    one[2][START]()
    one[0][ARRIVE]()
    keep(0).start()

    def first(i, c):
        at = pl.ds(pl.multiple_of(i * tile, tile), tile)
        ipre[at, :] = nn(normed[at, :], w1[0])
        return c

    lax.fori_loop(0, rows // tile, first, 0)
    one[1][SHARE]()
    one[2][RELAY]()
    one[3][START]()
    one[1][ARRIVE]()
    keep(1).start()

    def second(i, c):
        at = pl.ds(pl.multiple_of(i * tile, tile), tile)
        f = nn(normed[at, :], w1[1]) + bias
        fpre[at, :] = f
        valid, starts = masks(lens, seq * rows + i * tile, tile)
        gate = bound + (1.0 - bound) * jax.nn.sigmoid(f)
        put(feff, at, gate * (1.0 - starts))
        shifted = pl.ds(pl.multiple_of(i * tile + 8, 8), tile)
        v = ipre[at, :]
        put(states, shifted, v * jax.nn.sigmoid(v) * (1.0 - gate) * valid)
        return c

    lax.fori_loop(0, rows // tile, second, 0)
    put(feff, slice(rows, rows + 8), jnp.ones((8, chan), F32))

    length = rows // SEG

    def scan(i, c):
        p, h = c
        at, shifted = pl.ds(i, SEG, stride=length), pl.ds(i + 8, SEG, stride=length)
        f = get(feff, at)
        h = f * h + get(states, shifted)
        p = f * p
        put(states, shifted, h)
        put(prod, at, p)
        return p, h

    p, h = lax.fori_loop(
        0, length, scan, (jnp.ones((SEG, chan), F32), jnp.zeros((SEG, chan), F32))
    )
    block_p, block_h = p[0:1], h[0:1]
    for s in range(1, SEG):
        block_h = h[s : s + 1] + p[s : s + 1] * block_h
        block_p = p[s : s + 1] * block_p

    def travel():
        one[2][SHARE]()
        one[3][RELAY]()
        two[0][START]()

    arriving = carry_over_seq(block_p, block_h, n, seq, tp, cslots, cs, cr, False, travel)
    put(states, slice(0, 8), jnp.broadcast_to(arriving, (8, chan)))
    for s in range(SEG):
        at = slice(s * length, (s + 1) * length)
        shifted = slice(s * length + 8, (s + 1) * length + 8)
        whole = get(states, shifted) + get(prod, at) * arriving
        put(states, shifted, whole)
        ssq[at, :] = whole * whole
        arriving = h[s : s + 1] + p[s : s + 1] * arriving

    def outgate():
        one[3][SHARE]()
        one[2][ARRIVE]()
        keep(2).start()

        def third(i, c):
            at = pl.ds(pl.multiple_of(i * tile, tile), tile)
            opre[at, :] = nn(normed[at, :], w1[2])
            return c

        lax.fori_loop(0, rows // tile, third, 0)

    total = sum_over_tp(row_sums(ssq[...]), t, seq, tp, zslots, zs, zr, outgate)
    invst[...] = lax.rsqrt(total / width + EPS)

    def gating(i, c):
        at = pl.ds(pl.multiple_of(i * tile, tile), tile)
        shifted = pl.ds(pl.multiple_of(i * tile + 8, 8), tile)
        o = opre[at, :]
        gated[at, :] = (
            get(states, shifted) * invst[at, :] * sgain * (o * jax.nn.sigmoid(o))
        ).astype(BF)
        return c

    lax.fori_loop(0, rows // tile, gating, 0)
    one[3][ARRIVE]()
    keep(3).start()
    for copy in stores():
        copy.start()

    step = rows // CHUNKS
    group = part.shape[0] // step

    def partial(k):
        @pl.when(lax.rem(k, group) == 0)
        def _():
            big = pl.ds(pl.multiple_of(k * step, step), step * group)
            part[...] = nt(gated[big, :], w1[3])

        return part[pl.ds(pl.multiple_of(lax.rem(k, group) * step, step), step), :]

    def store_n(k):
        at = pl.ds(pl.multiple_of(k * step, step), step)
        return pltpu.make_async_copy(nmid.at[at], nmid_h.at[at], s_n.at[k])

    def store_m(k):
        at = pl.ds(pl.multiple_of(k * step, step), step)
        return pltpu.make_async_copy(buf.at[1, at], mixed_h.at[at], s_m.at[k])

    def finish(k):
        at = pl.ds(pl.multiple_of(k * step, step), step)
        store_m(k).start()
        resid = x[at, :].astype(F32) + buf[1, at, :].astype(F32)
        inv = lax.rsqrt(jnp.mean(resid * resid, axis=-1, keepdims=True) + EPS)
        invmid[at, :] = inv
        nmid[at, :] = (resid * inv * consts[3:4, :]).astype(BF)
        store_n(k).start()

    turns = [
        (2, lambda: (two[0][RELAY](), two[1][START]())),
        (4, lambda: two[0][SHARE]()),
        (7, lambda: (two[1][RELAY](), two[2][START]())),
        (9, lambda: two[1][SHARE]()),
        (13, lambda: two[2][RELAY]()),
        (16, lambda: two[2][SHARE]()),
    ]

    count, turn, drain = line_all_reduce(
        t, seq, tp, rows, CHUNKS, partial, send, buf, (s_in, s_out, r_buf), finish, (0, 1, 3)
    )
    loop_with(0, count, turn, turns)
    drain()
    for g in two:
        g[ARRIVE]()
    for g in one + two:
        g[DRAIN]()
    for copy in stores():
        copy.wait()
    for j in range(4):
        keep(j).wait()

    def stored(k, c):
        store_n(k).wait()
        store_m(k).wait()
        return c

    lax.fori_loop(0, CHUNKS, stored, 0)


def feed_forward(
    n, t, width,
    nmid_h, cot_h, w2_h, x_h, mixed_h, invmid, consts,
    gmix_h, gres_h, glu_h, ggain, sums_h, down_h,
    nmid, cot, pool, hid, gg, gu, glu, xs, ms, gmix, gres, wide, sums, stage, send, buf,
    s_a, s_w, s_x, s_o, s_g, s_s, s_d, m_core, ready, s_in, s_out, r_buf, *bufs,
):
    seq, tp = lax.axis_index("seq"), lax.axis_index("tp")
    core = lax.rem(seq, 2)
    sibling = (seq + 1 - 2 * core, tp)
    act_copies = [
        pltpu.make_async_copy(nmid_h, nmid, s_a.at[0]),
        pltpu.make_async_copy(cot_h, cot, s_a.at[1]),
    ]
    w_copies = [pltpu.make_async_copy(w2_h.at[j], pool.at[j], s_w.at[j]) for j in range(3)]
    act_copies[0].start()
    w_copies[0].start()
    greet_all(n, t, seq, tp)
    for copy in (w_copies[1], act_copies[1], w_copies[2]):
        copy.start()
    rows, chan = nmid.shape[0], gres.shape[2]
    step = rows // CHUNKS
    tile = rows // TILES
    ggain[...] = jnp.zeros_like(ggain)

    def fetch(k):
        at, slot = pl.ds(pl.multiple_of(k * step, step), step), lax.rem(k, 2)
        return (
            pltpu.make_async_copy(x_h.at[at], xs.at[slot], s_x.at[0, slot]),
            pltpu.make_async_copy(mixed_h.at[at], ms.at[slot], s_x.at[1, slot]),
        )

    def stored(k):
        at, slot = pl.ds(pl.multiple_of(k * step, step), step), lax.rem(k, 2)
        return (
            pltpu.make_async_copy(gmix.at[slot], gmix_h.at[at], s_o.at[0, slot]),
            pltpu.make_async_copy(gres.at[slot], gres_h.at[at], s_o.at[1, slot]),
        )

    for copy in fetch(0):
        copy.start()

    def finish(k):
        for copy in fetch(k):
            copy.wait()

        @pl.when(k + 1 < CHUNKS)
        def _():
            for copy in fetch(k + 1):
                copy.start()

        @pl.when(k >= 2)
        def _():
            for copy in stored(k - 2):
                copy.wait()

        at, slot = pl.ds(pl.multiple_of(k * step, step), step), lax.rem(k, 2)
        g = buf[1, at, :].astype(F32)
        inv = invmid[at, :]
        hat = (xs[slot].astype(F32) + ms[slot].astype(F32)) * inv
        ggain[0:1, :] += jnp.sum(g * hat, axis=0, keepdims=True)
        e = g * consts[3:4, :]
        mean = jnp.mean(e * hat, axis=-1, keepdims=True)
        result = cot[at, :].astype(F32) + inv * (e - hat * mean)
        wide[...] = result
        gmix[slot] = result.astype(BF)
        gres[slot] = wide[:, pl.ds(pl.multiple_of(tp * chan, LANE), chan)]
        for copy in stored(k):
            copy.start()

    count, turn, drain = line_all_reduce(
        t, seq, tp, rows, CHUNKS, None, send, buf, (s_in, s_out, r_buf), finish, K2_LAGS
    )

    act_copies[0].wait()
    w_copies[0].wait()
    per = 2

    def block(i, c):
        at = pl.ds(pl.multiple_of(i * tile, tile), tile)
        g = nn(nmid[at, :], pool[0])

        @pl.when(i == 0)
        def _():
            w_copies[1].wait()
            act_copies[1].wait()
            w_copies[2].wait()

        u = nn(nmid[at, :], pool[1])
        gh = nn(cot[at, :], pool[2])
        sig = jax.nn.sigmoid(g)
        act = g * sig
        hid[at, :] = (act * u).astype(BF)
        gg[at, :] = (gh * u * (sig * (1.0 + g * (1.0 - sig)))).astype(BF)
        gu[at, :] = (gh * act).astype(BF)

        @pl.when(i > 0)
        def _():
            turn((i - 1) * per)

        send[at, :] = (nt(gg[at, :], pool[0]) + nt(gu[at, :], pool[1])).astype(BF)

        @pl.when(i > 0)
        def _():
            turn((i - 1) * per + 1)

        return c

    lax.fori_loop(0, TILES, block, 0)
    done = (TILES - 1) * per

    ga, gb = chip_grid(n)
    chips = ga * gb
    shard = width // n
    half_pool = pl.ds(0, width // 2)
    other_half = pl.ds(width // 2, width // 2)

    def give(i):
        j, r = i // chips, lax.rem(i, chips)
        return pltpu.make_async_remote_copy(
            src_ref=stage.at[lax.rem(i, 2), 1 - core],
            dst_ref=pool.at[j, pl.ds(pl.multiple_of(width // 2 + r * shard, shard), shard)],
            send_sem=s_g.at[lax.rem(i, 2)],
            recv_sem=m_core.at[i],
            device_id=sibling,
            device_id_type=MESH,
        )

    def gradient(j, left, right, first_turn, turns):
        pl.semaphore_signal(ready, inc=1, device_id=sibling, device_id_type=MESH)
        pl.semaphore_wait(ready, 1)

        def slab(r, c):
            i = j * chips + r
            slot = lax.rem(i, 2)

            @pl.when(i >= 2)
            def _():
                give(i - 2).wait_send()

            at = pl.ds(pl.multiple_of(r * 2 * shard, 2 * shard), 2 * shard)
            values = tn(left[:, at], right[...]).astype(BF)
            for k in range(2):
                stage[slot, k] = values[k * shard : (k + 1) * shard]
            give(i).start()
            pool[j, pl.ds(pl.multiple_of(r * shard, shard), shard), :] = stage[slot, core]
            loop_with(first_turn + r * turns // chips, first_turn + (r + 1) * turns // chips, turn, ())
            return c

        lax.fori_loop(0, chips, slab, 0)

    def cores(j):
        def arrived(r, c):
            give(j * chips + r).wait_recv()
            return c

        lax.fori_loop(0, chips, arrived, 0)
        add_cores(pool.at[j, half_pool], pool.at[j, other_half])

    def summed(j):
        return pltpu.make_async_copy(sums, sums_h.at[j], s_s.at[j])

    def out(half, values):
        sums[half * (shard // 2) : (half + 1) * (shard // 2), :] = values

    reduces = [
        grid_reduce(n, seq, tp, j, pool.at[j, half_pool], bufs, out) for j in range(2)
    ]
    gradient(0, nmid, gg, done, 2)
    cores(0)
    reduces[0][0]()
    gradient(1, nmid, gu, done + 2, 2)
    cores(1)
    reduces[1][0]()

    def glu_copy(i):
        at, slot = pl.ds(pl.multiple_of(i * tile, tile), tile), lax.rem(i, 2)
        return pltpu.make_async_copy(glu.at[slot], glu_h.at[:, at], s_d.at[slot])

    def forward(i, c):
        @pl.when(i >= 2)
        def _():
            glu_copy(i - 2).wait()

        at, slot = pl.ds(pl.multiple_of(i * tile, tile), tile), lax.rem(i, 2)
        values = nt(hid[at, :], pool[2]).astype(BF)
        for q in range(t):
            glu[slot, q] = values[:, q * chan : (q + 1) * chan]
        glu_copy(i).start()

        @pl.when(lax.rem(i, 2) == 1)
        def _():
            turn(done + 4 + i // 2)

        return c

    lax.fori_loop(0, TILES, forward, 0)
    glu_copy(TILES - 2).wait()
    glu_copy(TILES - 1).wait()
    reduces[0][1]()
    gradient(2, cot, hid, done + 4 + TILES // 2, 2)
    cores(2)
    down = pltpu.make_async_copy(pool.at[2, half_pool], down_h, s_s.at[2])
    down.start()

    def second_sum():
        summed(0).wait()
        reduces[1][2]()
        summed(1).start()

    now = done + 6 + TILES // 2
    loop_with(
        now,
        count,
        turn,
        (
            (now + 1, lambda: (reduces[0][2](), summed(0).start())),
            (now + 2, lambda: reduces[1][1]()),
            (now + 5, second_sum),
        ),
    )
    drain()
    for r in reduces:
        r[3]()
    give(3 * chips - 2).wait_send()
    give(3 * chips - 1).wait_send()
    summed(1).wait()
    down.wait()
    for k in (CHUNKS - 2, CHUNKS - 1):
        for copy in stored(k):
            copy.wait()


def mixer_backward(
    n, t, width,
    lens, glu_h, x_h, mixed_h, gmix_h, normed_h, w1_h, gated_h, states_h, feff_h, ipre_h, fpre_h, opre_h,
    down_h, invst, consts,
    gni_h, dw1_h, vecs, out, sums,
    acc, gmix, normed, w1, gated, states, feff, ipre, fpre, opre,
    weighted, prod, inner, out3, cslots, zslots, xc, mc, own, inbox, gni, stage,
    s_f, cs, cr, zs, zr, s_x, sr, rr, sl, rl, s_o, s_d, s_acc, *bufs,
):
    seq, tp = lax.axis_index("seq"), lax.axis_index("tp")
    down = pltpu.make_async_copy(down_h, acc, s_acc)
    down.start()
    rows = gmix.shape[0]
    chan = ipre.shape[1]
    mine = pl.ds(pl.multiple_of(tp * chan, LANE), chan)
    fetches = [
        pltpu.make_async_copy(glu_h, own, s_x.at[0]),
        pltpu.make_async_copy(x_h.at[:, mine], xc, s_x.at[1]),
        pltpu.make_async_copy(mixed_h.at[:, mine], mc, s_x.at[2]),
    ]
    pairs = [
        (gmix_h, gmix),
        (w1_h.at[3], w1.at[:, pl.ds(3 * chan, chan)]),
        (states_h, states), (opre_h, opre), (feff_h, feff), (ipre_h, ipre), (fpre_h, fpre),
    ] + [(w1_h.at[j], w1.at[:, pl.ds(j * chan, chan)]) for j in range(3)] + [
        (normed_h, normed), (gated_h, gated),
    ]
    inputs = [pltpu.make_async_copy(src, dst, s_f.at[i]) for i, (src, dst) in enumerate(pairs)]
    fetches[0].start()
    for copy in inputs[:4]:
        copy.start()
    greet_all(n, t, seq, tp)
    for copy in fetches[1:] + inputs[4:]:
        copy.start()

    def down_out(half, values):
        size = sums.shape[0] // 2
        sums[half * size : (half + 1) * size, :] = values

    far, middle, near, drain_grid = grid_reduce(n, seq, tp, 0, acc, bufs, down_out)
    down.wait()
    far()
    tile = row_tile(rows)
    sgain, bound = consts[1:2, mine], consts[2:3, mine]
    vecs[...] = jnp.zeros_like(vecs)
    step = rows // SHARD_CHUNKS

    def finish(k, values):
        at = pl.ds(pl.multiple_of(k * step, step), step)
        ok, _ = masks(lens, seq * rows + k * step, step)
        m = mc[at, :].astype(F32)
        full = xc[at, :].astype(F32) + m + values
        out[at, :] = full.astype(BF)
        vecs[4:5, :] += jnp.sum(ok * m * m, axis=0, keepdims=True)
        vecs[5:6, :] += jnp.sum(ok * values * values, axis=0, keepdims=True)
        vecs[6:7, :] += jnp.sum(ok * full * full, axis=0, keepdims=True)

    turns, turn, last, drain = line_reduce_scatter(t, seq, tp, own, inbox, (sr, rr, sl, rl), finish)
    slots = 20

    def pump(slot):
        def one(i, c):
            turn(i)
            return c

        lax.fori_loop(slot * turns // slots, (slot + 1) * turns // slots, one, 0)

    fetches[0].wait()
    for copy in inputs[:4]:
        copy.wait()

    def gates(i, c):
        pump(i)
        at = pl.ds(pl.multiple_of(i * tile, tile), tile)
        shifted = pl.ds(pl.multiple_of(i * tile + 8, 8), tile)
        g = nn(gmix[at, :], w1[:, 3 * chan :])
        hat = get(states, shifted) * invst[at, :]
        o = opre[at, :]
        sig = jax.nn.sigmoid(o)
        q = o * sig
        vecs[2:3, :] += jnp.sum(g * hat * q, axis=0, keepdims=True)
        out3[at, 2 * chan :] = (g * hat * sgain * (sig * (1.0 + o * (1.0 - sig)))).astype(BF)
        w = g * q * sgain
        put(weighted, at, w)
        inner[at, :] = w * hat
        return c

    lax.fori_loop(0, 3, gates, 0)
    dot = sum_over_tp(row_sums(inner[...]), t, seq, tp, zslots, zs, zr, lambda: pump(3)) / width
    inner[:, 0:1] = dot

    def leaving(i, c):
        at = pl.ds(pl.multiple_of(i * tile, tile), tile)
        shifted = pl.ds(pl.multiple_of(i * tile + 8, 8), tile)
        inv = invst[at, :]
        put(weighted, at, inv * (get(weighted, at) - get(states, shifted) * inv * inner[at, 0:1]))
        return c

    lax.fori_loop(0, 3, leaving, 0)
    inputs[4].wait()

    length = rows // SEG

    def scan(i, c):
        p, h = c
        r = length - 1 - i
        at = pl.ds(r, SEG, stride=length)
        f = get(feff, pl.ds(r + 1, SEG, stride=length))
        h = f * h + get(weighted, at)
        p = f * p
        put(weighted, at, h)
        put(prod, at, p)
        return p, h

    p, h = lax.fori_loop(
        0, length, scan, (jnp.ones((SEG, chan), F32), jnp.zeros((SEG, chan), F32))
    )
    block_p, block_h = p[SEG - 1 : SEG], h[SEG - 1 : SEG]
    for s in range(SEG - 2, -1, -1):
        block_h = h[s : s + 1] + p[s : s + 1] * block_h
        block_p = p[s : s + 1] * block_p
    first = get(feff, slice(0, 1))
    arriving = carry_over_seq(
        first * block_p, first * block_h, n, seq, tp, cslots, cs, cr, True, lambda: pump(4)
    )
    inputs[5].wait()
    inputs[6].wait()
    middle()
    bias_sum = jnp.zeros((1, chan), F32)
    for s in range(SEG - 1, -1, -1):
        pump(12 - s)
        at = slice(s * length, (s + 1) * length)
        gs = get(weighted, at) + get(prod, at) * arriving
        arriving = h[s : s + 1] + p[s : s + 1] * arriving
        a = ipre[at, :]
        sa = jax.nn.sigmoid(a)
        act = a * sa
        sf = jax.nn.sigmoid(fpre[at, :])
        gate = bound + (1.0 - bound) * sf
        ok, starts = masks(lens, seq * rows + s * length, length)
        out3[at, :chan] = (gs * (1.0 - gate) * ok * (sa * (1.0 + a * (1.0 - sa)))).astype(BF)
        before = get(states, slice(s * length + 7, (s + 1) * length + 7))
        gate_grad = gs * before * (1.0 - starts) - gs * act * ok
        gf = (gate_grad * (1.0 - bound) * sf * (1.0 - sf)).astype(BF)
        out3[at, chan : 2 * chan] = gf
        bias_sum = bias_sum + jnp.sum(gf.astype(F32), axis=0, keepdims=True)
    vecs[1:2, :] = bias_sum

    def gni_copy(i):
        at = pl.ds(pl.multiple_of(i * tile, tile), tile)
        return pltpu.make_async_copy(gni.at[:, at], gni_h.at[:, at], s_o.at[i])

    for copy in inputs[7:]:
        copy.wait()

    def spread_in(i, c):
        at = pl.ds(pl.multiple_of(i * tile, tile), tile)
        put_shards(gni, at, nt(out3[at, :], w1[:, : 3 * chan]).astype(BF))
        gni_copy(i).start()
        pump(13 + i)
        return c

    lax.fori_loop(0, 3, spread_in, 0)

    near()
    shard = width // n
    chips = n // 2

    def d_copy(r, slot):
        at = pl.ds(pl.multiple_of(r * shard, shard), shard)
        return pltpu.make_async_copy(stage.at[slot], dw1_h.at[:, at], s_d.at[slot])

    def keep(slot, first, values):
        for k in range(2):
            stage[slot, k, :, first : first + values.shape[1]] = values[k * shard : (k + 1) * shard]

    def slab(r, c):
        slot = lax.rem(r, 2)

        @pl.when(r >= 2)
        def _():
            d_copy(r - 2, slot).wait()

        at = pl.ds(pl.multiple_of(r * 2 * shard, 2 * shard), 2 * shard)
        keep(slot, 0, tn(normed[:, at], out3[...]).astype(BF))
        keep(slot, 3 * chan, tn(gmix[:, at], gated[...]).astype(BF))
        d_copy(r, slot).start()

        @pl.when(r < 4)
        def _():
            pump(16 + r)

        return c

    lax.fori_loop(0, chips, slab, 0)
    for r in range(chips, 4):
        pump(16 + r)
    for copy in fetches[1:]:
        copy.wait()

    def ending(k, c):
        last(k)
        return c

    lax.fori_loop(0, SHARD_CHUNKS, ending, 0)
    for r in range(max(chips - 2, 0), chips):
        d_copy(r, r % 2).wait()

    def stored(i, c):
        gni_copy(i).wait()
        return c

    lax.fori_loop(0, 3, stored, 0)
    drain()
    drain_grid()


def closing(
    n, t, width,
    gni_h, dw1_h, x_h, gres_h, invin, consts, vecs, ggain,
    gin, allvec, sums,
    acc, other, xc, gres, own, inbox, scaled, inner, zslots, vslots,
    s_acc, m_core, s_own, s_x, sr, rr, sl, rl, zs, zr, vs, vr, ts, tr, *bufs,
):
    seq, tp = lax.axis_index("seq"), lax.axis_index("tp")
    rows, chan = gres.shape
    mine = pl.ds(pl.multiple_of(tp * chan, LANE), chan)
    fetch = pltpu.make_async_copy(gni_h, own, s_own)
    fetches = [
        pltpu.make_async_copy(x_h.at[:, mine], xc, s_x.at[0]),
        pltpu.make_async_copy(gres_h, gres, s_x.at[1]),
    ]
    fetch.start()
    greet_all(n, t, seq, tp)
    pieces, shard, cols = sums.shape

    core = lax.rem(seq, 2)

    def load(j):
        return pltpu.make_async_copy(
            dw1_h.at[core, :, pl.ds(j * cols, cols)], acc.at[j], s_acc.at[j]
        )

    def swap(j):
        return pltpu.make_async_remote_copy(
            src_ref=dw1_h.at[1 - core, :, pl.ds(j * cols, cols)],
            dst_ref=other.at[j],
            send_sem=m_core.at[0, j],
            recv_sem=m_core.at[1, j],
            device_id=(seq + 1 - 2 * core, tp),
            device_id_type=MESH,
        )

    def start(j):
        load(j).start()
        swap(j).start()

    reduces = []
    for j in range(pieces):

        def out(half, values, j=j):
            sums[j, half * (shard // 2) : (half + 1) * (shard // 2), :] = values

        reduces.append(grid_reduce(n, seq, tp, j, acc.at[j], bufs, out))

    def stage1(j):
        load(j).wait()
        swap(j).wait_recv()
        add_cores(acc.at[j], other.at[j])
        reduces[j][0]()

    def stage2(j):
        reduces[j][1]()

    def stage3(j):
        reduces[j][2]()

    fetch.wait()
    start(0)
    for copy in fetches:
        copy.start()
    step = rows // SHARD_CHUNKS
    gain_in = consts[4:5, mine]
    vslots[seq] = vecs[...]
    vslots[seq, 3:4, :] = ggain[0:1, mine]

    def finish(k, values):
        at = pl.ds(pl.multiple_of(k * step, step), step)
        hat = xc[at, :].astype(F32) * invin[at, :]
        s = values * gain_in
        scaled[at, :] = s
        inner[at, :] = s * hat
        vslots[seq, 0:1, :] += jnp.sum(values * hat, axis=0, keepdims=True)

    turns, turn, last, drain = line_reduce_scatter(t, seq, tp, own, inbox, (sr, rr, sl, rl), finish)
    works = [
        (2, lambda: (stage1(0), start(1))),
        (5, lambda: stage1(1)),
        (6, lambda: stage2(0)),
        (9, lambda: stage3(0)),
        (10, lambda: stage2(1)),
        (13, lambda: stage3(1)),
    ]
    slots = 16

    def turn_of(slot):
        def one(i, c):
            turn(i)
            return c

        lax.fori_loop(slot * turns // slots, (slot + 1) * turns // slots, one, 0)

    loop_with(0, slots, turn_of, works)
    for copy in fetches:
        copy.wait()

    def ending(k, c):
        last(k)
        return c

    lax.fori_loop(0, SHARD_CHUNKS, ending, 0)
    go_v, done_v = spread(n, seq, vslots, vs, vr, lambda k: (k, tp))
    dot = sum_over_tp(row_sums(inner[...]), t, seq, tp, zslots, zs, zr, go_v) / width
    done_v()
    total = vslots[0]
    for k in range(1, n):
        total = total + vslots[k]
    allvec[tp] = total
    go_t, done_t = spread(t, tp, allvec, ts, tr, lambda k: (seq, k))
    go_t()
    gin[...] = gres[...] + invin[...] * (scaled[...] - xc[...].astype(F32) * invin[...] * dot)
    done_t()
    drain()
    for j in range(pieces):
        swap(j).wait_send()
        reduces[j][3]()


def params(collective=None, limit=VMEM_LIMIT):
    if collective is None:
        return pltpu.CompilerParams(vmem_limit_bytes=limit)
    return pltpu.CompilerParams(
        vmem_limit_bytes=limit, collective_id=collective, has_side_effects=True
    )


def line_sems(chunks):
    return [DMA((chunks,)), DMA((chunks,)), DMA((2, chunks))]


def on_device(
    n, t,
    hidden_in, gain_in, w_input, w_forget, forget_bias, w_outgate, state_gain, w_output,
    gain_mid, w_gate, w_up, w_down, lengths, layer_index, cotangent,
):
    rows, width = hidden_in.shape
    chan = w_input.shape[1]
    ff = w_gate.shape[1]
    ffp = -(-ff // LANE) * LANE

    def padded(w):
        return w if ffp == ff else jnp.pad(w, ((0, 0), (0, ffp - ff)))

    total = lengths[0] + lengths[1]
    bound = layer_index[0].astype(F32) / LAYERS
    consts = jnp.stack(
        [
            forget_bias,
            state_gain.astype(F32),
            jnp.broadcast_to(bound, (width,)),
            gain_mid.astype(F32),
            gain_in.astype(F32),
        ]
        + [jnp.zeros((width,), F32)] * 3
    )
    plane = shape((rows, chan), F32)
    plane16 = shape((rows, chan), BF)
    column = shape((rows, 1), F32)
    wide16 = shape((rows, width), BF)
    shards16 = shape((t, rows, chan), BF)

    def groups(more=0):
        return shape((chan // LANE, rows + more, LANE), F32)

    def vm(*arrays):
        return [pltpu.VMEM(a.shape, a.dtype) for a in arrays]

    SM = pl.BlockSpec(memory_space=pltpu.SMEM)
    w1s, w2s = shape((4, width, chan), BF), shape((3, width, ffp), BF)
    zslot, vslot = pltpu.VMEM((t, 8, rows), F32), pltpu.VMEM((n, 8, chan), F32)
    small = [DMA((n,)), DMA((n,)), DMA((t,)), DMA((t,))]
    saved = [plane, plane, plane, groups(8), groups(8), plane16, wide16]

    (
        ipre, fpre, opre, feff, states, gated, normed_in, nmid, mixed, w1, w2, invst, invmid, inv_in,
    ) = pl.pallas_call(
        functools.partial(mixer_forward, n, t, width),
        out_shape=saved + [wide16, wide16, w1s, w2s, column, column, column],
        in_specs=[SM] + [HB] * 8 + [VM],
        out_specs=[HB] * 11 + [VM] * 3,
        scratch_shapes=[
            *vm(wide16, wide16, plane, plane, plane, groups(8), groups(8), plane16, wide16, w1s),
            *vm(groups(), plane),
            pltpu.VMEM((rows // CHUNKS * 4, width), F32),
            vslot,
            zslot,
            pltpu.VMEM((rows, width), BF),
            pltpu.VMEM((2, rows, width), BF),
            DMA, DMA((7,)), DMA((4,)), DMA((CHUNKS,)), DMA((CHUNKS,)),
            *small,
            *line_sems(CHUNKS),
            *gather_sems(n, 4),
            *gather_sems(n, 3),
        ],
        compiler_params=params(1),
        name="mixer_forward",
    )(
        lengths, hidden_in, w_input, w_forget, w_outgate, w_output.T,
        padded(w_gate), padded(w_up), padded(w_down.T), consts,
    )

    shard, chips, tile, step = width // n, n // 2, rows // TILES, rows // CHUNKS
    piece = shape((shard, ffp), F32)
    ffs = shape((rows, ffp), BF)
    gmix, gres, glu_part, ggain, sums2, down = pl.pallas_call(
        functools.partial(feed_forward, n, t, width),
        out_shape=[
            wide16, plane, shards16, shape((8, width), F32), shape((2, shard, ffp), F32),
            shape((width // 2, ffp), BF),
        ],
        in_specs=[HB] * 5 + [VM] * 2,
        out_specs=[HB] * 3 + [VM] + [HB] * 2,
        scratch_shapes=[
            *vm(wide16, wide16, w2s, ffs, ffs, ffs),
            pltpu.VMEM((2, t, tile, chan), BF),
            pltpu.VMEM((2, step, width), BF),
            pltpu.VMEM((2, step, width), BF),
            pltpu.VMEM((2, step, width), BF),
            pltpu.VMEM((2, step, chan), F32),
            pltpu.VMEM((step, width), F32),
            *vm(piece),
            pltpu.VMEM((2, 2, shard, ffp), BF),
            *vm(wide16),
            pltpu.VMEM((2, rows, width), BF),
            DMA((2,)), DMA((3,)), DMA((2, 2)), DMA((2, 2)), DMA((2,)), DMA((3,)), DMA((2,)),
            DMA((3 * chips,)),
            pltpu.SemaphoreType.REGULAR,
            *line_sems(CHUNKS),
            *grid_buffers(n, width, 2, ffp),
        ],
        compiler_params=params(2),
        name="feed_forward",
    )(nmid, cotangent, w2, hidden_in, mixed, invmid, consts)

    shard_sems = [DMA((t, SHARD_CHUNKS))] * 4
    shard_bufs = [pltpu.VMEM((t, rows, chan), BF), pltpu.VMEM((t + 1, rows, chan), BF)]
    gni_part, dw1, vecs, block_out, sum_down = pl.pallas_call(
        functools.partial(mixer_backward, n, t, width),
        out_shape=[
            shards16, shape((2, width // 2, 4 * chan), BF), shape((8, chan), F32), plane16, piece,
        ],
        in_specs=[SM] + [HB] * 13 + [VM] * 2,
        out_specs=[HB] * 2 + [VM] * 3,
        scratch_shapes=[
            pltpu.VMEM((width // 2, ffp), BF),
            *vm(wide16, wide16),
            pltpu.VMEM((width, 4 * chan), BF),
            *vm(plane16, groups(8), groups(8), plane, plane, plane),
            *vm(groups(), groups(), plane, shape((rows, 3 * chan), BF)),
            vslot,
            zslot,
            *vm(plane16, plane16),
            *shard_bufs,
            *vm(shards16),
            pltpu.VMEM((2, 2, shard, 4 * chan), BF),
            DMA((12,)),
            *small,
            DMA((3,)),
            *shard_sems,
            DMA((3,)), DMA((2,)), DMA,
            *grid_buffers(n, width, 1, ffp),
        ],
        compiler_params=params(3),
        name="mixer_backward",
    )(
        lengths, glu_part, hidden_in, mixed, gmix, normed_in, w1, gated, states, feff, ipre, fpre, opre,
        down, invst, consts,
    )

    grad_in, allvec, sums1 = pl.pallas_call(
        functools.partial(closing, n, t, width),
        out_shape=[plane, shape((t, 8, chan), F32), shape((2, shard, 2 * chan), F32)],
        in_specs=[HB] * 4 + [VM] * 4,
        out_specs=[VM] * 3,
        scratch_shapes=[
            pltpu.VMEM((2, width // 2, 2 * chan), BF),
            pltpu.VMEM((2, width // 2, 2 * chan), BF),
            *vm(plane16, plane),
            *shard_bufs,
            *vm(plane, plane),
            zslot,
            vslot,
            DMA((2,)), DMA((2, 2)), DMA, DMA((2,)),
            *shard_sems,
            DMA((t,)), DMA((t,)), DMA((n,)), DMA((n,)), DMA((t,)), DMA((t,)),
            *grid_buffers(n, width, 2, 2 * chan),
        ],
        compiler_params=params(4),
        name="closing",
    )(gni_part, dw1, hidden_in, gres, inv_in, consts, vecs, ggain)

    def vector(r):
        return allvec[:, r, :].reshape(width)

    squares = jnp.stack([jnp.sum(allvec[:, r, :]) for r in (4, 5, 6)])
    rms_stats = jnp.sqrt(squares / (total.astype(F32) * width))

    return (
        block_out,
        grad_in,
        vector(0),
        sums1[0, :, :chan],
        sums1[0, :, chan:],
        vector(1),
        sums1[1, :, :chan],
        vector(2),
        sums1[1, :, chan:].T,
        vector(3),
        sums2[0, :, :ff],
        sums2[1, :, :ff],
        sum_down[:, :ff].T,
        rms_stats,
    )


def solution(mesh):
    weight, turned = P("seq", "tp"), P("tp", "seq")
    in_specs = (
        P("seq", None), P(), weight, weight, P(), weight, P(), turned, P(), weight, weight, turned,
        P(), P(), P("seq", None),
    )
    out_specs = (
        weight, weight, P(), weight, weight, P(), weight, P(), turned, P(), weight, weight, turned, P(),
    )
    body = functools.partial(on_device, mesh.shape["seq"], mesh.shape["tp"])
    return jax.shard_map(
        body, mesh=mesh, in_specs=in_specs, out_specs=out_specs, check_vma=False
    )
```

```python
import functools

import jax
import jax.numpy as jnp
from jax import lax
from jax.experimental import pallas as pl
from jax.experimental.pallas import tpu as pltpu
from jax.sharding import PartitionSpec as P

LAYERS = 24
EPS = 1e-06
MESH = pl.DeviceIdType.MESH
DMA = pltpu.SemaphoreType.DMA
BF = jnp.bfloat16
F32 = jnp.float32
VM = pl.BlockSpec(memory_space=pltpu.VMEM)
HB = pl.BlockSpec(memory_space=pl.ANY)
LANE = 128
SEG = 8
TILES = 4
K2_LAGS = (1, 2, 3)
CHUNKS = 16
SHARD_CHUNKS = 4
HOP_LAG = 2
VMEM_LIMIT = 60 * 1024 * 1024


def nn(left, right):
    return jnp.dot(left, right, preferred_element_type=F32)


def nt(left, right):
    return lax.dot_general(left, right, (((1,), (1,)), ((), ())), preferred_element_type=F32)


def tn(left, right):
    return lax.dot_general(left, right, (((0,), (0,)), ((), ())), preferred_element_type=F32)


def shape(dims, dtype):
    return jax.ShapeDtypeStruct(dims, dtype)


def get(ref, at):
    return jnp.concatenate([ref[g, at, :] for g in range(ref.shape[0])], axis=1)


def put(ref, at, values):
    for g in range(ref.shape[0]):
        ref[g, at, :] = values[:, g * LANE : (g + 1) * LANE]


def put_shards(ref, at, values):
    k = ref.shape[2]
    for q in range(ref.shape[0]):
        ref[q, at, :] = values[:, q * k : (q + 1) * k]


def row_tile(rows):
    return rows // 3 if rows % 48 == 0 else rows


def greet_all(n, t, seq, tp):
    barrier = pltpu.get_barrier_semaphore()

    def along_seq(o, c):
        pl.semaphore_signal(barrier, inc=1, device_id=(lax.rem(seq + o, n), tp), device_id_type=MESH)
        return c

    def along_tp(o, c):
        pl.semaphore_signal(barrier, inc=1, device_id=(seq, lax.rem(tp + o, t)), device_id_type=MESH)
        return c

    lax.fori_loop(1, n, along_seq, 0)
    lax.fori_loop(1, t, along_tp, 0)
    pl.semaphore_wait(barrier, n - 1 + t - 1)


def greet_line(t, seq, tp):
    barrier = pltpu.get_barrier_semaphore()

    def along_tp(o, c):
        pl.semaphore_signal(barrier, inc=1, device_id=(seq, lax.rem(tp + o, t)), device_id_type=MESH)
        return c

    lax.fori_loop(1, t, along_tp, 0)
    pl.semaphore_wait(barrier, t - 1)


def spread(size, me, slots, send, recv, target):
    def copy(o, slot):
        return pltpu.make_async_remote_copy(
            src_ref=slots.at[slot],
            dst_ref=slots.at[slot],
            send_sem=send.at[o],
            recv_sem=recv.at[slot],
            device_id=target(lax.rem(me + o, size)),
            device_id_type=MESH,
        )

    def one(o, c):
        copy(o, me).start()
        return c

    def arrived(o, c):
        copy(o, lax.rem(me + o, size)).wait_recv()
        return c

    def sent(o, c):
        copy(o, me).wait_send()
        return c

    def go():
        lax.fori_loop(1, size, one, 0)

    def done():
        lax.fori_loop(1, size, arrived, 0)
        lax.fori_loop(1, size, sent, 0)

    return go, done


def row_sums(values):
    ones = jnp.ones((8, values.shape[1]), BF)
    high = values.astype(BF)
    rest = values - high.astype(F32)
    low = rest.astype(BF)
    return nt(ones, high) + nt(ones, low)


def sum_over_tp(part, t, seq, tp, slots, send, recv, between=None):
    slots[tp] = part
    go, done = spread(t, tp, slots, send, recv, lambda k: (seq, k))
    go()
    if between is not None:
        between()
    done()
    total = slots[0]
    for k in range(1, t):
        total = total + slots[k]
    return jnp.transpose(total)[:, :1]


def carry_over_seq(prod, state, n, seq, tp, slots, send, recv, backward, between=None):
    slots[seq] = jnp.concatenate([prod, state] + [jnp.zeros_like(prod)] * 6, axis=0)
    go, done = spread(n, seq, slots, send, recv, lambda k: (k, tp))
    go()
    if between is not None:
        between()
    done()

    def hop(i, total):
        j = n - 1 - i if backward else i
        block = slots[j]
        longer = block[1:2] + block[0:1] * total
        inside = (j > seq) if backward else (j < seq)
        return jnp.where(inside, longer, total)

    return lax.fori_loop(0, n, hop, jnp.zeros_like(prod))


def line_all_reduce(t, seq, tp, rows, chunks, partial, send, buf, sems, finish, lags):
    s_in, s_out, r_buf = sems
    step = rows // chunks
    half = t // 2
    depth = jnp.where(tp < half, tp, t - 1 - tp)
    inner = jnp.where(tp < half, tp + 1, tp - 1)
    outer = jnp.where(tp < half, tp - 1, tp + 1)
    outer = jnp.where(depth > 0, outer, inner)
    middle = (depth == half - 1).astype(jnp.int32)
    lag_in, lag_turn, lag_out = lags
    lag_first = lag_in * depth
    lag_second = lag_in * (half - 1) + lag_turn + lag_out * (half - 1 - depth)

    def part_of(k):
        return pl.ds(pl.multiple_of(k * step, step), step)

    def inward(k, slot):
        return pltpu.make_async_remote_copy(
            src_ref=send.at[part_of(k)],
            dst_ref=buf.at[slot, part_of(k)],
            send_sem=s_in.at[k],
            recv_sem=r_buf.at[slot, k],
            device_id=(seq, inner),
            device_id_type=MESH,
        )

    def outward(k):
        return pltpu.make_async_remote_copy(
            src_ref=buf.at[1, part_of(k)],
            dst_ref=buf.at[1, part_of(k)],
            send_sem=s_out.at[k],
            recv_sem=r_buf.at[1, k],
            device_id=(seq, outer),
            device_id_type=MESH,
        )

    def first(k):
        part = None if partial is None else partial(k)

        @pl.when(depth > 0)
        def _():
            inward(k, 0).wait_recv()
            mine = send[part_of(k), :].astype(F32) if part is None else part
            send[part_of(k), :] = (mine + buf[0, part_of(k), :].astype(F32)).astype(BF)

        if part is not None:

            @pl.when(depth == 0)
            def _():
                send[part_of(k), :] = part.astype(BF)

        inward(k, middle).start()

    def second(k):
        inward(k, 1).wait_recv()

        @pl.when(middle == 1)
        def _():
            both = send[part_of(k), :].astype(F32) + buf[1, part_of(k), :].astype(F32)
            buf[1, part_of(k), :] = both.astype(BF)

        @pl.when(depth > 0)
        def _():
            outward(k).start()

        finish(k)

    def turn(i):
        @pl.when((i >= lag_first) & (i - lag_first < chunks))
        def _():
            first(i - lag_first)

        @pl.when((i >= lag_second) & (i - lag_second < chunks))
        def _():
            second(i - lag_second)

    def drain():
        def sent(k, c):
            inward(k, middle).wait_send()

            @pl.when(depth > 0)
            def _():
                outward(k).wait_send()

            return c

        lax.fori_loop(0, chunks, sent, 0)

    return chunks + lag_in * (half - 1) + lag_turn + lag_out * (half - 1), turn, drain


def line_reduce_scatter(t, seq, tp, own, inbox, sems, finish):
    s_r, r_r, s_l, r_l = sems
    rows = own.shape[1]
    chunks = SHARD_CHUNKS
    step = rows // chunks
    count = chunks * (t - 1)

    def part_of(k):
        return pl.ds(pl.multiple_of(k * step, step), step)

    def rightward(q, k):
        return pltpu.make_async_remote_copy(
            src_ref=own.at[q, part_of(k)],
            dst_ref=inbox.at[q + 1, part_of(k)],
            send_sem=s_r.at[q, k],
            recv_sem=r_r.at[q, k],
            device_id=(seq, lax.rem(tp + 1, t)),
            device_id_type=MESH,
        )

    def leftward(q, k):
        return pltpu.make_async_remote_copy(
            src_ref=own.at[q, part_of(k)],
            dst_ref=inbox.at[q, part_of(k)],
            send_sem=s_l.at[q, k],
            recv_sem=r_l.at[q, k],
            device_id=(seq, lax.rem(tp + t - 1, t)),
            device_id_type=MESH,
        )

    def add(q, k, slot):
        own[q, part_of(k), :] = (
            own[q, part_of(k), :].astype(F32) + inbox[slot, part_of(k), :].astype(F32)
        ).astype(BF)

    def right_turn(i):
        k, j = i // (t - 1), lax.rem(i, t - 1)
        q = t - 1 - j

        @pl.when((i >= 0) & (i < count) & (q > tp))
        def _():
            @pl.when(tp > 0)
            def _():
                rightward(q, k).wait_recv()
                add(q, k, q + 1)

            rightward(q, k).start()

    def left_turn(i):
        k, q = i // (t - 1), lax.rem(i, t - 1)

        @pl.when((i >= 0) & (i < count) & (q < tp))
        def _():
            @pl.when(tp < t - 1)
            def _():
                leftward(q, k).wait_recv()
                add(q, k, q)

            leftward(q, k).start()

    def turn(i):
        right_turn(i - HOP_LAG * tp)
        left_turn(i - HOP_LAG * (t - 1 - tp))

    def last(k):
        @pl.when(tp == 0)
        def _():
            leftward(tp, k).wait_recv()
            finish(k, own[tp, part_of(k), :].astype(F32) + inbox[tp, part_of(k), :].astype(F32))

        @pl.when(tp == t - 1)
        def _():
            rightward(tp, k).wait_recv()
            finish(k, own[tp, part_of(k), :].astype(F32) + inbox[tp + 1, part_of(k), :].astype(F32))

        @pl.when((tp > 0) & (tp < t - 1))
        def _():
            leftward(tp, k).wait_recv()
            rightward(tp, k).wait_recv()
            finish(
                k,
                own[tp, part_of(k), :].astype(F32)
                + inbox[tp, part_of(k), :].astype(F32)
                + inbox[tp + 1, part_of(k), :].astype(F32),
            )

    def drain():
        def sent(i, c):
            k = i // (t - 1)
            j = lax.rem(i, t - 1)

            @pl.when(t - 1 - j > tp)
            def _():
                rightward(t - 1 - j, k).wait_send()

            @pl.when(j < tp)
            def _():
                leftward(j, k).wait_send()

            return c

        lax.fori_loop(0, count, sent, 0)

    return count + HOP_LAG * (t - 2), turn, last, drain


def chip_grid(n):
    chips = n // 2
    b = max(k for k in range(1, chips + 1) if chips % k == 0 and k * k <= chips)
    return chips // b, b


def grid_buffers(n, width, pieces, cols):
    ga, gb = chip_grid(n)
    h = width // n // 2
    pa, pb = max(ga - 1, 1), max(gb - 1, 1)
    return [
        pltpu.VMEM((pieces, pb, ga, h, cols), BF),
        pltpu.VMEM((pieces, pa, gb, h, cols), BF),
        pltpu.VMEM((pieces, pa, h, cols), BF),
        pltpu.VMEM((pieces, pb, h, cols), BF),
        DMA((2, pieces, pb, ga)), DMA((2, pieces, pa, gb)), DMA((2, pieces, pa)), DMA((2, pieces, pb)),
    ]


def add_cores(acc, first):
    part = 64

    def one(i, c):
        at = pl.ds(pl.multiple_of(i * part, part), part)
        acc[at, :] = (acc[at, :].astype(F32) + first[at, :].astype(F32)).astype(BF)
        return c

    lax.fori_loop(0, acc.shape[0] // part, one, 0)


def grid_reduce(n, seq, tp, j, acc, bufs, out):
    far_b, far_a, near_a, near_b, m_fb, m_fa, m_na, m_nb = bufs
    ga, gb = chip_grid(n)
    core = lax.rem(seq, 2)
    a, b = seq // 2 // gb, lax.rem(seq // 2, gb)
    h = near_a.shape[2]

    def device(a_, b_):
        return ((a_ * gb + b_) * 2 + core, tp)

    def block(half, x, y):
        return pl.ds(pl.multiple_of(((x * gb + y) * 2 + half) * h, h), h)

    def remote(rows, dst, sems, index, target):
        return pltpu.make_async_remote_copy(
            src_ref=acc.at[rows],
            dst_ref=dst,
            send_sem=sems.at[(0, j) + index],
            recv_sem=sems.at[(1, j) + index],
            device_id=target,
            device_id_type=MESH,
        )

    def first_way():
        copies = []
        for o in range(1, gb):
            to = lax.rem(b + o, gb)
            for x in range(ga):
                dst = far_b.at[j, o - 1, x]
                copies.append(remote(block(0, x, to), dst, m_fb, (o - 1, x), device(a, to)))
        for o in range(1, ga):
            to = lax.rem(a + o, ga)
            for y in range(gb):
                dst = far_a.at[j, o - 1, y]
                copies.append(remote(block(1, to, y), dst, m_fa, (o - 1, y), device(to, b)))
        return copies

    def second_way():
        copies = []
        for o in range(1, ga):
            to = lax.rem(a + o, ga)
            copies.append(
                remote(block(0, to, b), near_a.at[j, o - 1], m_na, (o - 1,), device(to, b))
            )
        for o in range(1, gb):
            to = lax.rem(b + o, gb)
            copies.append(
                remote(block(1, a, to), near_b.at[j, o - 1], m_nb, (o - 1,), device(a, to))
            )
        return copies

    def far():
        for copy in first_way():
            copy.start()

    def middle():
        for copy in first_way():
            copy.wait_recv()

        def along_a(x, c):
            total = acc[block(0, x, b), :].astype(F32)
            for o in range(1, gb):
                total = total + far_b[j, o - 1, x].astype(F32)
            acc[block(0, x, b), :] = total.astype(BF)
            return c

        def along_b(y, c):
            total = acc[block(1, a, y), :].astype(F32)
            for o in range(1, ga):
                total = total + far_a[j, o - 1, y].astype(F32)
            acc[block(1, a, y), :] = total.astype(BF)
            return c

        lax.fori_loop(0, ga, along_a, 0)
        lax.fori_loop(0, gb, along_b, 0)
        for copy in second_way():
            copy.start()

    def near():
        for copy in second_way():
            copy.wait_recv()
        total = acc[block(0, a, b), :].astype(F32)
        for o in range(1, ga):
            total = total + near_a[j, o - 1].astype(F32)
        out(0, total)
        total = acc[block(1, a, b), :].astype(F32)
        for o in range(1, gb):
            total = total + near_b[j, o - 1].astype(F32)
        out(1, total)

    def drain():
        for copy in first_way() + second_way():
            copy.wait_send()

    return far, middle, near, drain


def gather_sems(n, pieces):
    ga, gb = chip_grid(n)
    pa, pb = max(ga - 1, 1), max(gb - 1, 1)
    return [
        DMA((pieces,)), DMA((2, pieces, ga * gb)),
        DMA((2, pieces, pb)), DMA((2, pieces, pa)), DMA((2, pieces, gb, pa)), DMA((2, pieces, ga, pb)),
    ]


def grid_gather(n, seq, tp, j, src, dst, sems):
    s_local, m_core, m_fb, m_fa, m_na, m_nb = sems
    ga, gb = chip_grid(n)
    shard = src.shape[0]
    h = shard // 2
    core = lax.rem(seq, 2)
    a, b = seq // 2 // gb, lax.rem(seq // 2, gb)

    def device(a_, b_, core_):
        return ((a_ * gb + b_) * 2 + core_, tp)

    def block(x, y, core_, half, count):
        return pl.ds(pl.multiple_of(((x * gb + y) * 2 + core_) * shard + half * h, h), count)

    def remote(from_, rows, sem, index, target):
        return pltpu.make_async_remote_copy(
            src_ref=from_,
            dst_ref=dst.at[rows],
            send_sem=sem.at[(0, j) + index],
            recv_sem=sem.at[(1, j) + index],
            device_id=target,
            device_id_type=MESH,
        )

    def own(half):
        return src.at[pl.ds(half * h, h)]

    def far(incoming):
        copies = []
        for o in range(1, gb):
            to, of = lax.rem(b + o, gb), lax.rem(b + gb - o, gb)
            rows = block(a, of if incoming else b, core, 0, h)
            copies.append(remote(own(0), rows, m_fb, (o - 1,), device(a, to, core)))
        for o in range(1, ga):
            to, of = lax.rem(a + o, ga), lax.rem(a + ga - o, ga)
            rows = block(of if incoming else a, b, core, 1, h)
            copies.append(remote(own(1), rows, m_fa, (o - 1,), device(to, b, core)))
        return copies

    def near(incoming, first, least):
        copies = []
        for i in range(0 if first else 1, gb if least else 1):
            y = lax.rem(b + gb - i, gb)
            for o in range(1, ga):
                to, of = lax.rem(a + o, ga), lax.rem(a + ga - o, ga)
                rows = block(of if incoming else a, y, core, 0, h)
                from_ = own(0) if i == 0 or incoming else dst.at[rows]
                copies.append(remote(from_, rows, m_na, (i, o - 1), device(to, b, core)))
        for i in range(0 if first else 1, ga if least else 1):
            x = lax.rem(a + ga - i, ga)
            for o in range(1, gb):
                to, of = lax.rem(b + o, gb), lax.rem(b + gb - o, gb)
                rows = block(x, of if incoming else b, core, 1, h)
                from_ = own(1) if i == 0 or incoming else dst.at[rows]
                copies.append(remote(from_, rows, m_nb, (i, o - 1), device(a, to, core)))
        return copies

    def across(incoming, first, others):
        copies = []
        for i in range(ga):
            for k in range(gb):
                mine = i == 0 and k == 0
                if (mine and not first) or (not mine and not others):
                    continue
                x, y = lax.rem(a + i, ga), lax.rem(b + k, gb)
                rows = block(x, y, 1 - core if incoming else core, 0, shard)
                from_ = src if mine or incoming else dst.at[rows]
                copies.append(remote(from_, rows, m_core, (i * gb + k,), device(a, b, 1 - core)))
        return copies

    def local():
        return pltpu.make_async_copy(src, dst.at[block(a, b, core, 0, shard)], s_local.at[j])

    def start():
        for copy in far(False) + near(False, True, False) + across(False, True, False):
            copy.start()
        local().start()

    def relay():
        for copy in far(True):
            copy.wait_recv()
        for copy in near(False, False, True):
            copy.start()

    def share():
        for copy in near(True, True, True):
            copy.wait_recv()
        for copy in across(False, False, True):
            copy.start()

    def arrive():
        for copy in across(True, True, True):
            copy.wait_recv()
        local().wait()

    def drain():
        for copy in far(False) + near(False, True, True) + across(False, True, True):
            copy.wait_send()

    return start, relay, share, arrive, drain


def loop_with(first, last, body, works):
    def one(i, c):
        body(i)
        for when, work in works:

            @pl.when(i == when)
            def _(work=work):
                work()

        return c

    lax.fori_loop(first, last, one, 0)


def masks(lens, first, count):
    at = first + lax.broadcasted_iota(jnp.int32, (count, 1), 0)
    valid = (at < lens[0] + lens[1]).astype(F32)
    starts = ((at == 0) | (at == lens[0])).astype(F32)
    return valid, starts


def mixer_forward(
    n, t, width,
    lens, layer, x_h, wi_h, wf_h, wo_h, wx_raw, wg_h, wu_h, wd_raw_h, bias_v, sgain_v, gmid_v, gin_v,
    ipre_h, fpre_h, opre_h, feff_h, states_h, gated_h, normed_h, nmid_h, mixed_h, w1_h, w2_h,
    invst, invmid, invin, consts,
    x, normed, ipre, fpre, opre, feff, states, gated, nmid, w1, prod, ssq, part, cslots, zslots, send, buf,
    wx, wd, wd_raw, s_t, s_x, s_st, s_w, s_n, s_m, cs, cr, zs, zr, s_in, s_out, r_buf, *sems,
):
    seq, tp = lax.axis_index("seq"), lax.axis_index("tp")
    load = pltpu.make_async_copy(x_h, x, s_x)
    load.start()
    load_down = pltpu.make_async_copy(wd_raw_h, wd_raw, s_t)
    load_down.start()
    sems1, sems2 = sems[:6], sems[6:]
    one = [
        grid_gather(n, seq, tp, j, src, w1.at[j], sems1)
        for j, src in enumerate((wi_h, wf_h, wo_h, wx))
    ]
    two = [
        grid_gather(n, seq, tp, j, src, w2_h.at[j], sems2)
        for j, src in enumerate((wg_h, wu_h, wd))
    ]
    START, RELAY, SHARE, ARRIVE, DRAIN = range(5)
    greet_all(n, t, seq, tp)
    one[0][START]()
    rows, depth = normed.shape
    chan = ipre.shape[1]
    tile = row_tile(rows)
    mine = pl.ds(pl.multiple_of(tp * chan, LANE), chan)
    consts[...] = jnp.zeros_like(consts)
    for k, vector in ((0, bias_v), (1, sgain_v), (3, gmid_v), (4, gin_v)):
        consts[k : k + 1, :] = vector[...].astype(F32).reshape(1, width)
    consts[2:3, :] = jnp.full((1, width), layer[0].astype(F32) / LAYERS)
    bias, sgain, bound = consts[0:1, mine], consts[1:2, mine], consts[2:3, mine]

    def stores():
        pairs = (
            (ipre, ipre_h), (fpre, fpre_h), (opre, opre_h), (feff, feff_h), (states, states_h),
            (gated, gated_h), (normed, normed_h),
        )
        return [pltpu.make_async_copy(v, o, s_st.at[i]) for i, (v, o) in enumerate(pairs)]

    def keep(j):
        return pltpu.make_async_copy(w1.at[j], w1_h.at[j], s_w.at[j])

    wx[...] = jnp.transpose(wx_raw[...])
    load.wait()

    def norm(i, c):
        at = pl.ds(pl.multiple_of(i * tile, tile), tile)
        v = x[at, :].astype(F32)
        inv = lax.rsqrt(jnp.mean(v * v, axis=-1, keepdims=True) + EPS)
        invin[at, :] = inv
        normed[at, :] = (v * inv * consts[4:5, :]).astype(BF)
        return c

    lax.fori_loop(0, rows // tile, norm, 0)
    one[0][RELAY]()
    one[1][START]()
    load_down.wait()
    turned = jnp.transpose(wd_raw[...])
    wd[:, : turned.shape[1]] = turned
    if turned.shape[1] < wd.shape[1]:
        wd[:, turned.shape[1] :] = jnp.zeros((wd.shape[0], wd.shape[1] - turned.shape[1]), BF)
    one[0][SHARE]()
    one[1][RELAY]()
    one[2][START]()
    one[0][ARRIVE]()
    keep(0).start()

    def first(i, c):
        at = pl.ds(pl.multiple_of(i * tile, tile), tile)
        ipre[at, :] = nn(normed[at, :], w1[0])
        return c

    lax.fori_loop(0, rows // tile, first, 0)
    one[1][SHARE]()
    one[2][RELAY]()
    one[3][START]()
    one[1][ARRIVE]()
    keep(1).start()

    def second(i, c):
        at = pl.ds(pl.multiple_of(i * tile, tile), tile)
        f = nn(normed[at, :], w1[1]) + bias
        fpre[at, :] = f
        valid, starts = masks(lens, seq * rows + i * tile, tile)
        gate = bound + (1.0 - bound) * jax.nn.sigmoid(f)
        put(feff, at, gate * (1.0 - starts))
        shifted = pl.ds(pl.multiple_of(i * tile + 8, 8), tile)
        v = ipre[at, :]
        put(states, shifted, v * jax.nn.sigmoid(v) * (1.0 - gate) * valid)
        return c

    lax.fori_loop(0, rows // tile, second, 0)
    put(feff, slice(rows, rows + 8), jnp.ones((8, chan), F32))

    length = rows // SEG

    def scan(i, c):
        p, h = c
        at, shifted = pl.ds(i, SEG, stride=length), pl.ds(i + 8, SEG, stride=length)
        f = get(feff, at)
        h = f * h + get(states, shifted)
        p = f * p
        put(states, shifted, h)
        put(prod, at, p)
        return p, h

    p, h = lax.fori_loop(
        0, length, scan, (jnp.ones((SEG, chan), F32), jnp.zeros((SEG, chan), F32))
    )
    block_p, block_h = p[0:1], h[0:1]
    for s in range(1, SEG):
        block_h = h[s : s + 1] + p[s : s + 1] * block_h
        block_p = p[s : s + 1] * block_p

    def travel():
        one[2][SHARE]()
        one[3][RELAY]()
        two[0][START]()

    arriving = carry_over_seq(block_p, block_h, n, seq, tp, cslots, cs, cr, False, travel)
    put(states, slice(0, 8), jnp.broadcast_to(arriving, (8, chan)))
    for s in range(SEG):
        at = slice(s * length, (s + 1) * length)
        shifted = slice(s * length + 8, (s + 1) * length + 8)
        whole = get(states, shifted) + get(prod, at) * arriving
        put(states, shifted, whole)
        ssq[at, :] = whole * whole
        arriving = h[s : s + 1] + p[s : s + 1] * arriving

    def outgate():
        one[3][SHARE]()
        one[2][ARRIVE]()
        keep(2).start()

        def third(i, c):
            at = pl.ds(pl.multiple_of(i * tile, tile), tile)
            opre[at, :] = nn(normed[at, :], w1[2])
            return c

        lax.fori_loop(0, rows // tile, third, 0)

    total = sum_over_tp(row_sums(ssq[...]), t, seq, tp, zslots, zs, zr, outgate)
    invst[...] = lax.rsqrt(total / width + EPS)

    def gating(i, c):
        at = pl.ds(pl.multiple_of(i * tile, tile), tile)
        shifted = pl.ds(pl.multiple_of(i * tile + 8, 8), tile)
        o = opre[at, :]
        gated[at, :] = (
            get(states, shifted) * invst[at, :] * sgain * (o * jax.nn.sigmoid(o))
        ).astype(BF)
        return c

    lax.fori_loop(0, rows // tile, gating, 0)
    one[3][ARRIVE]()
    keep(3).start()
    for copy in stores():
        copy.start()

    step = rows // CHUNKS
    group = part.shape[0] // step

    def partial(k):
        @pl.when(lax.rem(k, group) == 0)
        def _():
            big = pl.ds(pl.multiple_of(k * step, step), step * group)
            part[...] = nt(gated[big, :], w1[3])

        return part[pl.ds(pl.multiple_of(lax.rem(k, group) * step, step), step), :]

    def store_n(k):
        at = pl.ds(pl.multiple_of(k * step, step), step)
        return pltpu.make_async_copy(nmid.at[at], nmid_h.at[at], s_n.at[k])

    def store_m(k):
        at = pl.ds(pl.multiple_of(k * step, step), step)
        return pltpu.make_async_copy(buf.at[1, at], mixed_h.at[at], s_m.at[k])

    def finish(k):
        at = pl.ds(pl.multiple_of(k * step, step), step)
        store_m(k).start()
        resid = x[at, :].astype(F32) + buf[1, at, :].astype(F32)
        inv = lax.rsqrt(jnp.mean(resid * resid, axis=-1, keepdims=True) + EPS)
        invmid[at, :] = inv
        nmid[at, :] = (resid * inv * consts[3:4, :]).astype(BF)
        store_n(k).start()

    turns = [
        (2, lambda: (two[0][RELAY](), two[1][START]())),
        (4, lambda: two[0][SHARE]()),
        (7, lambda: (two[1][RELAY](), two[2][START]())),
        (9, lambda: two[1][SHARE]()),
        (13, lambda: two[2][RELAY]()),
        (16, lambda: two[2][SHARE]()),
    ]

    count, turn, drain = line_all_reduce(
        t, seq, tp, rows, CHUNKS, partial, send, buf, (s_in, s_out, r_buf), finish, (0, 1, 3)
    )
    loop_with(0, count, turn, turns)
    drain()
    for g in two:
        g[ARRIVE]()
    for g in one + two:
        g[DRAIN]()
    for copy in stores():
        copy.wait()
    for j in range(4):
        keep(j).wait()

    def stored(k, c):
        store_n(k).wait()
        store_m(k).wait()
        return c

    lax.fori_loop(0, CHUNKS, stored, 0)


def feed_forward(
    n, t, width,
    nmid_h, cot_h, w2_h, x_h, mixed_h, invmid, consts,
    gmix_h, gres_h, glu_h, ggain, gate_h, up_h, down_h,
    nmid, cot, pool, hid, gg, gu, glu, xs, ms, gmix, gres, wide, sums, stage, send, buf,
    s_a, s_w, s_x, s_o, s_g, s_s, s_d, m_core, ready, s_in, s_out, r_buf, *bufs,
):
    seq, tp = lax.axis_index("seq"), lax.axis_index("tp")
    core = lax.rem(seq, 2)
    sibling = (seq + 1 - 2 * core, tp)
    act_copies = [
        pltpu.make_async_copy(nmid_h, nmid, s_a.at[0]),
        pltpu.make_async_copy(cot_h, cot, s_a.at[1]),
    ]
    w_copies = [pltpu.make_async_copy(w2_h.at[j], pool.at[j], s_w.at[j]) for j in range(3)]
    act_copies[0].start()
    w_copies[0].start()
    greet_all(n, t, seq, tp)
    for copy in (w_copies[1], act_copies[1], w_copies[2]):
        copy.start()
    rows, chan = nmid.shape[0], gres.shape[2]
    step = rows // CHUNKS
    tile = rows // TILES
    ggain[...] = jnp.zeros_like(ggain)

    def fetch(k):
        at, slot = pl.ds(pl.multiple_of(k * step, step), step), lax.rem(k, 2)
        return (
            pltpu.make_async_copy(x_h.at[at], xs.at[slot], s_x.at[0, slot]),
            pltpu.make_async_copy(mixed_h.at[at], ms.at[slot], s_x.at[1, slot]),
        )

    def stored(k):
        at, slot = pl.ds(pl.multiple_of(k * step, step), step), lax.rem(k, 2)
        return (
            pltpu.make_async_copy(gmix.at[slot], gmix_h.at[at], s_o.at[0, slot]),
            pltpu.make_async_copy(gres.at[slot], gres_h.at[at], s_o.at[1, slot]),
        )

    for copy in fetch(0):
        copy.start()

    def finish(k):
        for copy in fetch(k):
            copy.wait()

        @pl.when(k + 1 < CHUNKS)
        def _():
            for copy in fetch(k + 1):
                copy.start()

        @pl.when(k >= 2)
        def _():
            for copy in stored(k - 2):
                copy.wait()

        at, slot = pl.ds(pl.multiple_of(k * step, step), step), lax.rem(k, 2)
        g = buf[1, at, :].astype(F32)
        inv = invmid[at, :]
        hat = (xs[slot].astype(F32) + ms[slot].astype(F32)) * inv
        ggain[0:1, :] += jnp.sum(g * hat, axis=0, keepdims=True)
        e = g * consts[3:4, :]
        mean = jnp.mean(e * hat, axis=-1, keepdims=True)
        result = cot[at, :].astype(F32) + inv * (e - hat * mean)
        wide[...] = result
        gmix[slot] = result.astype(BF)
        gres[slot] = wide[:, pl.ds(pl.multiple_of(tp * chan, LANE), chan)]
        for copy in stored(k):
            copy.start()

    count, turn, drain = line_all_reduce(
        t, seq, tp, rows, CHUNKS, None, send, buf, (s_in, s_out, r_buf), finish, K2_LAGS
    )

    act_copies[0].wait()
    w_copies[0].wait()

    def block(i, c):
        at = pl.ds(pl.multiple_of(i * tile, tile), tile)
        g = nn(nmid[at, :], pool[0])

        @pl.when(i == 0)
        def _():
            w_copies[1].wait()
            act_copies[1].wait()
            w_copies[2].wait()

        u = nn(nmid[at, :], pool[1])
        gh = nn(cot[at, :], pool[2])
        sig = jax.nn.sigmoid(g)
        act = g * sig
        hid[at, :] = (act * u).astype(BF)
        gg[at, :] = (gh * u * (sig * (1.0 + g * (1.0 - sig)))).astype(BF)
        gu[at, :] = (gh * act).astype(BF)

        @pl.when(i > 0)
        def _():
            turn(2 * i - 1)

        send[at, :] = (nt(gg[at, :], pool[0]) + nt(gu[at, :], pool[1])).astype(BF)
        turn(2 * i)
        return c

    lax.fori_loop(0, TILES, block, 0)
    done = 2 * TILES - 1

    ga, gb = chip_grid(n)
    chips = ga * gb
    shard = width // n
    half_pool = pl.ds(0, width // 2)
    other_half = pl.ds(width // 2, width // 2)

    def give(i):
        j, r = i // chips, lax.rem(i, chips)
        return pltpu.make_async_remote_copy(
            src_ref=stage.at[lax.rem(i, 2), 1 - core],
            dst_ref=pool.at[j, pl.ds(pl.multiple_of(width // 2 + r * shard, shard), shard)],
            send_sem=s_g.at[lax.rem(i, 2)],
            recv_sem=m_core.at[i],
            device_id=sibling,
            device_id_type=MESH,
        )

    def gradient(j, left, right, first_turn, turns):
        pl.semaphore_signal(ready, inc=1, device_id=sibling, device_id_type=MESH)
        pl.semaphore_wait(ready, 1)

        def slab(r, c):
            i = j * chips + r
            slot = lax.rem(i, 2)

            @pl.when(i >= 2)
            def _():
                give(i - 2).wait_send()

            at = pl.ds(pl.multiple_of(r * 2 * shard, 2 * shard), 2 * shard)
            values = tn(left[:, at], right[...]).astype(BF)
            for k in range(2):
                stage[slot, k] = values[k * shard : (k + 1) * shard]
            give(i).start()
            pool[j, pl.ds(pl.multiple_of(r * shard, shard), shard), :] = stage[slot, core]
            loop_with(first_turn + r * turns // chips, first_turn + (r + 1) * turns // chips, turn, ())
            return c

        lax.fori_loop(0, chips, slab, 0)

    def cores(j):
        def arrived(r, c):
            give(j * chips + r).wait_recv()
            return c

        lax.fori_loop(0, chips, arrived, 0)
        add_cores(pool.at[j, half_pool], pool.at[j, other_half])

    def summed(j):
        return pltpu.make_async_copy(sums, (gate_h, up_h)[j], s_s.at[j])

    def out(half, values):
        sums[half * (shard // 2) : (half + 1) * (shard // 2), :] = values

    reduces = [
        grid_reduce(n, seq, tp, j, pool.at[j, half_pool], bufs, out) for j in range(2)
    ]
    gradient(0, nmid, gg, done, 2)
    cores(0)
    reduces[0][0]()
    gradient(1, nmid, gu, done + 2, 2)
    cores(1)
    reduces[1][0]()

    def glu_copy(i):
        at, slot = pl.ds(pl.multiple_of(i * tile, tile), tile), lax.rem(i, 2)
        return pltpu.make_async_copy(glu.at[slot], glu_h.at[:, at], s_d.at[slot])

    def forward(i, c):
        @pl.when(i >= 2)
        def _():
            glu_copy(i - 2).wait()

        at, slot = pl.ds(pl.multiple_of(i * tile, tile), tile), lax.rem(i, 2)
        values = nt(hid[at, :], pool[2]).astype(BF)
        for q in range(t):
            glu[slot, q] = values[:, q * chan : (q + 1) * chan]
        glu_copy(i).start()

        @pl.when(lax.rem(i, 2) == 1)
        def _():
            turn(done + 4 + i // 2)

        return c

    lax.fori_loop(0, TILES, forward, 0)
    glu_copy(TILES - 2).wait()
    glu_copy(TILES - 1).wait()
    reduces[0][1]()
    gradient(2, cot, hid, done + 4 + TILES // 2, 2)
    cores(2)
    down = pltpu.make_async_copy(pool.at[2, half_pool], down_h, s_s.at[2])
    down.start()

    def second_sum():
        summed(0).wait()
        reduces[1][2]()
        summed(1).start()

    now = done + 6 + TILES // 2
    loop_with(
        now,
        count,
        turn,
        (
            (now + 1, lambda: (reduces[0][2](), summed(0).start())),
            (now + 2, lambda: reduces[1][1]()),
            (now + 5, second_sum),
        ),
    )
    drain()
    for r in reduces:
        r[3]()
    give(3 * chips - 2).wait_send()
    give(3 * chips - 1).wait_send()
    summed(1).wait()
    down.wait()
    for k in (CHUNKS - 2, CHUNKS - 1):
        for copy in stored(k):
            copy.wait()


def mixer_backward(
    n, t, width,
    lens, glu_h, x_h, mixed_h, gmix_h, normed_h, w1_h, gated_h, states_h, feff_h, ipre_h, fpre_h, opre_h,
    down_h, invst, invin, consts,
    gni_h, dw1_h, vecs, out, dot_in, sums,
    acc, gmix, normed, w1, gated, states, feff, ipre, fpre, opre,
    weighted, prod, inner, out3, cslots, zslots, zslots2, gain_sum, gsend, gtake, x, mc, own, inbox, gni, stage,
    s_f, cs, cr, zs, zr, zs2, zr2, gs_, gr_, s_x, sr, rr, sl, rl, s_o, s_d, s_acc, *bufs,
):
    seq, tp = lax.axis_index("seq"), lax.axis_index("tp")
    down = pltpu.make_async_copy(down_h, acc, s_acc)
    down.start()
    rows = gmix.shape[0]
    chan = ipre.shape[1]
    mine = pl.ds(pl.multiple_of(tp * chan, LANE), chan)
    fetches = [
        pltpu.make_async_copy(glu_h, own, s_x.at[0]),
        pltpu.make_async_copy(x_h, x, s_x.at[1]),
        pltpu.make_async_copy(mixed_h.at[:, mine], mc, s_x.at[2]),
    ]
    pairs = [
        (gmix_h, gmix),
        (w1_h.at[3], w1.at[:, pl.ds(3 * chan, chan)]),
        (states_h, states), (opre_h, opre), (feff_h, feff), (ipre_h, ipre), (fpre_h, fpre),
    ] + [(w1_h.at[j], w1.at[:, pl.ds(j * chan, chan)]) for j in range(3)] + [
        (normed_h, normed), (gated_h, gated),
    ]
    inputs = [pltpu.make_async_copy(src, dst, s_f.at[i]) for i, (src, dst) in enumerate(pairs)]
    fetches[0].start()
    for copy in inputs[:4]:
        copy.start()
    greet_all(n, t, seq, tp)
    for copy in inputs[4:] + fetches[1:]:
        copy.start()

    def down_out(half, values):
        size = sums.shape[1] // 2
        sums[:, half * size : (half + 1) * size] = jnp.transpose(values)

    far, middle, near, drain_grid = grid_reduce(n, seq, tp, 0, acc, bufs, down_out)
    tile = row_tile(rows)
    sgain, bound = consts[1:2, mine], consts[2:3, mine]
    vecs[...] = jnp.zeros_like(vecs)
    step = rows // SHARD_CHUNKS

    def finish(k, values):
        at = pl.ds(pl.multiple_of(k * step, step), step)
        ok, _ = masks(lens, seq * rows + k * step, step)
        m = mc[at, :].astype(F32)
        full = x[at, mine].astype(F32) + m + values
        out[at, :] = full.astype(BF)
        vecs[4:5, :] += jnp.sum(ok * m * m, axis=0, keepdims=True)
        vecs[5:6, :] += jnp.sum(ok * values * values, axis=0, keepdims=True)
        vecs[6:7, :] += jnp.sum(ok * full * full, axis=0, keepdims=True)

    turns, turn, last, drain = line_reduce_scatter(t, seq, tp, own, inbox, (sr, rr, sl, rl), finish)
    slots = 23

    def pump(slot):
        def one(i, c):
            turn(i)
            return c

        lax.fori_loop(slot * turns // slots, (slot + 1) * turns // slots, one, 0)

    fetches[0].wait()
    pump(0)
    pump(1)
    down.wait()
    far()
    for copy in inputs[:4]:
        copy.wait()

    def gates(i, c):
        pump(2 + i)
        at = pl.ds(pl.multiple_of(i * tile, tile), tile)
        shifted = pl.ds(pl.multiple_of(i * tile + 8, 8), tile)
        g = nn(gmix[at, :], w1[:, 3 * chan :])
        hat = get(states, shifted) * invst[at, :]
        o = opre[at, :]
        sig = jax.nn.sigmoid(o)
        q = o * sig
        vecs[2:3, :] += jnp.sum(g * hat * q, axis=0, keepdims=True)
        out3[at, 2 * chan :] = (g * hat * sgain * (sig * (1.0 + o * (1.0 - sig)))).astype(BF)
        w = g * q * sgain
        put(weighted, at, w)
        inner[at, :] = w * hat
        return c

    lax.fori_loop(0, 3, gates, 0)
    dot = sum_over_tp(row_sums(inner[...]), t, seq, tp, zslots, zs, zr, lambda: pump(5)) / width
    inner[:, 0:1] = dot

    def leaving(i, c):
        at = pl.ds(pl.multiple_of(i * tile, tile), tile)
        shifted = pl.ds(pl.multiple_of(i * tile + 8, 8), tile)
        inv = invst[at, :]
        put(weighted, at, inv * (get(weighted, at) - get(states, shifted) * inv * inner[at, 0:1]))
        return c

    lax.fori_loop(0, 3, leaving, 0)
    inputs[4].wait()
    pump(6)

    length = rows // SEG

    def scan(i, c):
        p, h = c
        r = length - 1 - i
        at = pl.ds(r, SEG, stride=length)
        f = get(feff, pl.ds(r + 1, SEG, stride=length))
        h = f * h + get(weighted, at)
        p = f * p
        put(weighted, at, h)
        put(prod, at, p)
        return p, h

    p, h = lax.fori_loop(
        0, length, scan, (jnp.ones((SEG, chan), F32), jnp.zeros((SEG, chan), F32))
    )
    block_p, block_h = p[SEG - 1 : SEG], h[SEG - 1 : SEG]
    for s in range(SEG - 2, -1, -1):
        block_h = h[s : s + 1] + p[s : s + 1] * block_h
        block_p = p[s : s + 1] * block_p
    first = get(feff, slice(0, 1))
    arriving = carry_over_seq(
        first * block_p, first * block_h, n, seq, tp, cslots, cs, cr, True, lambda: pump(7)
    )
    inputs[5].wait()
    inputs[6].wait()
    middle()
    bias_sum = jnp.zeros((1, chan), F32)
    for s in range(SEG - 1, -1, -1):
        pump(15 - s)
        at = slice(s * length, (s + 1) * length)
        gs = get(weighted, at) + get(prod, at) * arriving
        arriving = h[s : s + 1] + p[s : s + 1] * arriving
        a = ipre[at, :]
        sa = jax.nn.sigmoid(a)
        act = a * sa
        sf = jax.nn.sigmoid(fpre[at, :])
        gate = bound + (1.0 - bound) * sf
        ok, starts = masks(lens, seq * rows + s * length, length)
        out3[at, :chan] = (gs * (1.0 - gate) * ok * (sa * (1.0 + a * (1.0 - sa)))).astype(BF)
        before = get(states, slice(s * length + 7, (s + 1) * length + 7))
        gate_grad = gs * before * (1.0 - starts) - gs * act * ok
        gf = (gate_grad * (1.0 - bound) * sf * (1.0 - sf)).astype(BF)
        out3[at, chan : 2 * chan] = gf
        bias_sum = bias_sum + jnp.sum(gf.astype(F32), axis=0, keepdims=True)
    vecs[1:2, :] = bias_sum

    def gni_copy(i):
        at = pl.ds(pl.multiple_of(i * tile, tile), tile)
        return pltpu.make_async_copy(gni.at[:, at], gni_h.at[:, at], s_o.at[i])

    for copy in inputs[7:] + fetches[1:]:
        copy.wait()
    gain_sum[...] = jnp.zeros_like(gain_sum)

    def spread_in(i, c):
        at = pl.ds(pl.multiple_of(i * tile, tile), tile)
        values = nt(out3[at, :], w1[:, : 3 * chan])
        put_shards(gni, at, values.astype(BF))
        gni_copy(i).start()
        product = values * (x[at, :].astype(F32) * invin[at, :])
        gain_sum[0:1, :] += jnp.sum(product, axis=0, keepdims=True)
        product = product * consts[4:5, :]
        short = product[:, :LANE]
        for k in range(LANE, width, LANE):
            short = short + product[:, k : k + LANE]
        inner[at, :LANE] = short
        pump(16 + i)
        return c

    lax.fori_loop(0, 3, spread_in, 0)

    zslots2[tp] = row_sums(inner[:, :LANE])
    go_z, done_z = spread(t, tp, zslots2, zs2, zr2, lambda k: (seq, k))
    go_z()
    gsend[...] = jnp.zeros_like(gsend)
    for q in range(t):
        gsend[q, 0:1, :] = gain_sum[0:1, q * chan : (q + 1) * chan]

    def gain_copy(o, slot):
        to = lax.rem(tp + o, t)
        return pltpu.make_async_remote_copy(
            src_ref=gsend.at[to],
            dst_ref=gtake.at[slot],
            send_sem=gs_.at[o],
            recv_sem=gr_.at[slot],
            device_id=(seq, to),
            device_id_type=MESH,
        )

    def gain_go(o, c):
        gain_copy(o, tp).start()
        return c

    def gain_done(o, c):
        gain_copy(o, lax.rem(tp + o, t)).wait_recv()
        return c

    def gain_sent(o, c):
        gain_copy(o, tp).wait_send()
        return c

    lax.fori_loop(1, t, gain_go, 0)
    gtake[tp] = gsend[tp]
    near()
    shard = width // n
    chips = n // 2

    def d_copy(r, slot):
        at = pl.ds(pl.multiple_of(r * shard, shard), shard)
        return pltpu.make_async_copy(stage.at[slot], dw1_h.at[:, at], s_d.at[slot])

    def keep(slot, first, values):
        for k in range(2):
            stage[slot, k, :, first : first + values.shape[1]] = values[k * shard : (k + 1) * shard]

    def slab(r, c):
        slot = lax.rem(r, 2)

        @pl.when(r >= 2)
        def _():
            d_copy(r - 2, slot).wait()

        at = pl.ds(pl.multiple_of(r * 2 * shard, 2 * shard), 2 * shard)
        keep(slot, 0, tn(normed[:, at], out3[...]).astype(BF))
        keep(slot, 3 * chan, tn(gmix[:, at], gated[...]).astype(BF))
        d_copy(r, slot).start()

        @pl.when(r < 4)
        def _():
            pump(19 + r)

        return c

    lax.fori_loop(0, chips, slab, 0)
    for r in range(chips, 4):
        pump(19 + r)

    done_z()
    total = zslots2[0]
    for k in range(1, t):
        total = total + zslots2[k]
    dot_in[...] = jnp.transpose(total)[:, :1] / width
    lax.fori_loop(1, t, gain_done, 0)
    lax.fori_loop(1, t, gain_sent, 0)
    gains = gtake[0]
    for k in range(1, t):
        gains = gains + gtake[k]
    vecs[0:1, :] = gains[0:1]

    def ending(k, c):
        last(k)
        return c

    lax.fori_loop(0, SHARD_CHUNKS, ending, 0)
    for r in range(max(chips - 2, 0), chips):
        d_copy(r, r % 2).wait()

    def stored(i, c):
        gni_copy(i).wait()
        return c

    lax.fori_loop(0, 3, stored, 0)
    drain()
    drain_grid()


def closing(
    n, t, width,
    lens, gni_h, dw1_h, x_h, gres_h, invin, dot_in, consts, vecs, ggain,
    gin, vectors, rms, g_input, g_forget, g_outgate, g_output,
    acc, other, xc, gres, own, inbox, vslots, allvec,
    s_acc, m_core, s_own, s_x, sr, rr, sl, rl, vs, vr, ts, tr, *bufs,
):
    seq, tp = lax.axis_index("seq"), lax.axis_index("tp")
    rows, chan = gres.shape
    mine = pl.ds(pl.multiple_of(tp * chan, LANE), chan)
    fetch = pltpu.make_async_copy(gni_h, own, s_own)
    fetches = [
        pltpu.make_async_copy(x_h.at[:, mine], xc, s_x.at[0]),
        pltpu.make_async_copy(gres_h, gres, s_x.at[1]),
    ]
    fetch.start()
    greet_all(n, t, seq, tp)
    pieces, shard, cols = 2, g_input.shape[0], 2 * chan

    core = lax.rem(seq, 2)

    def load(j):
        return pltpu.make_async_copy(
            dw1_h.at[core, :, pl.ds(j * cols, cols)], acc.at[j], s_acc.at[j]
        )

    def swap(j):
        return pltpu.make_async_remote_copy(
            src_ref=dw1_h.at[1 - core, :, pl.ds(j * cols, cols)],
            dst_ref=other.at[j],
            send_sem=m_core.at[0, j],
            recv_sem=m_core.at[1, j],
            device_id=(seq + 1 - 2 * core, tp),
            device_id_type=MESH,
        )

    def start(j):
        load(j).start()
        swap(j).start()

    reduces = []
    for j in range(pieces):

        def out(half, values, j=j):
            at = slice(half * (shard // 2), (half + 1) * (shard // 2))
            if j == 0:
                g_input[at, :] = values[:, :chan]
                g_forget[at, :] = values[:, chan:]
            else:
                g_outgate[at, :] = values[:, :chan]
                g_output[:, at] = jnp.transpose(values[:, chan:])

        reduces.append(grid_reduce(n, seq, tp, j, acc.at[j], bufs, out))

    def stage1(j):
        load(j).wait()
        swap(j).wait_recv()
        add_cores(acc.at[j], other.at[j])
        reduces[j][0]()

    def stage2(j):
        reduces[j][1]()

    def stage3(j):
        reduces[j][2]()

    fetch.wait()
    start(0)
    for copy in fetches:
        copy.start()
    step = rows // SHARD_CHUNKS
    gain_in = consts[4:5, mine]
    vslots[seq] = vecs[...]
    vslots[seq, 3:4, :] = ggain[0:1, mine]
    go_v, done_v = spread(n, seq, vslots, vs, vr, lambda k: (k, tp))
    go_t, done_t = spread(t, tp, allvec, ts, tr, lambda k: (seq, k))
    go_v()
    for copy in fetches:
        copy.wait()

    def finish(k, values):
        at = pl.ds(pl.multiple_of(k * step, step), step)
        hat = xc[at, :].astype(F32) * invin[at, :]
        gin[at, :] = gres[at, :] + invin[at, :] * (values * gain_in - hat * dot_in[at, :])

    def vectors_on():
        done_v()
        total = vslots[0]
        for k in range(1, n):
            total = total + vslots[k]
        allvec[tp] = total
        go_t()

    turns, turn, last, drain = line_reduce_scatter(t, seq, tp, own, inbox, (sr, rr, sl, rl), finish)
    works = [
        (1, vectors_on),
        (2, lambda: (stage1(0), start(1))),
        (5, lambda: stage1(1)),
        (6, lambda: stage2(0)),
        (9, lambda: stage3(0)),
        (10, lambda: stage2(1)),
        (13, lambda: stage3(1)),
    ]
    slots = 16

    def turn_of(slot):
        def one(i, c):
            turn(i)
            return c

        lax.fori_loop(slot * turns // slots, (slot + 1) * turns // slots, one, 0)

    loop_with(0, slots, turn_of, works)
    done_t()
    squares = jnp.zeros((8, 1), F32)
    for k in range(t):
        vectors[:, k * chan : (k + 1) * chan] = allvec[k]
        squares = squares + jnp.sum(allvec[k], axis=1, keepdims=True)
    count = (lens[0] + lens[1]).astype(F32) * width
    rms[...] = jnp.broadcast_to(jnp.sqrt(squares / count), rms.shape)

    def ending(k, c):
        last(k)
        return c

    lax.fori_loop(0, SHARD_CHUNKS, ending, 0)
    drain()
    for j in range(pieces):
        swap(j).wait_send()
        reduces[j][3]()


def emit(count, *refs):
    sources, (vectors, roots) = refs[:count], refs[count : count + 2]
    targets = refs[count + 2 : 2 * count + 2]
    outs, stats = refs[2 * count + 2 : 2 * count + 6], refs[2 * count + 6]
    held, sem = refs[2 * count + 7 : 3 * count + 7], refs[3 * count + 7]
    loads = [
        pltpu.make_async_copy(src, dst, sem.at[0, i])
        for i, (src, dst) in enumerate(zip(sources, held))
    ]
    stores = [
        pltpu.make_async_copy(src, dst, sem.at[1, i])
        for i, (src, dst) in enumerate(zip(held, targets))
    ]
    for copy in loads:
        copy.start()
    for k, out in enumerate(outs):
        out[...] = vectors[k, :]
    for k in range(3):
        stats[k] = roots[4 + k, 0]
    for load, store in zip(loads, stores):
        load.wait()
        store.start()
    for copy in stores:
        copy.wait()


def params(collective=None, limit=VMEM_LIMIT):
    if collective is None:
        return pltpu.CompilerParams(vmem_limit_bytes=limit)
    return pltpu.CompilerParams(
        vmem_limit_bytes=limit, collective_id=collective, has_side_effects=True
    )


def line_sems(chunks):
    return [DMA((chunks,)), DMA((chunks,)), DMA((2, chunks))]


def on_device(
    n, t,
    hidden_in, gain_in, w_input, w_forget, forget_bias, w_outgate, state_gain, w_output,
    gain_mid, w_gate, w_up, w_down, lengths, layer_index, cotangent,
):
    rows, width = hidden_in.shape
    chan = w_input.shape[1]
    ff = w_gate.shape[1]
    ffp = -(-ff // LANE) * LANE

    def padded(w):
        return w if ffp == ff else jnp.pad(w, ((0, 0), (0, ffp - ff)))

    plane = shape((rows, chan), F32)
    plane16 = shape((rows, chan), BF)
    column = shape((rows, 1), F32)
    wide16 = shape((rows, width), BF)
    shards16 = shape((t, rows, chan), BF)

    def groups(more=0):
        return shape((chan // LANE, rows + more, LANE), F32)

    def vm(*arrays):
        return [pltpu.VMEM(a.shape, a.dtype) for a in arrays]

    SM = pl.BlockSpec(memory_space=pltpu.SMEM)
    w1s, w2s = shape((4, width, chan), BF), shape((3, width, ffp), BF)
    zslot, vslot = pltpu.VMEM((t, 8, rows), F32), pltpu.VMEM((n, 8, chan), F32)
    small = [DMA((n,)), DMA((n,)), DMA((t,)), DMA((t,))]
    saved = [plane, plane, plane, groups(8), groups(8), plane16, wide16]

    (
        ipre, fpre, opre, feff, states, gated, normed_in, nmid, mixed, w1, w2, invst, invmid, inv_in,
        consts,
    ) = pl.pallas_call(
        functools.partial(mixer_forward, n, t, width),
        out_shape=saved + [wide16, wide16, w1s, w2s, column, column, column, shape((8, width), F32)],
        in_specs=[SM] * 2 + [HB] * 4 + [VM] + [HB] * 3 + [VM] * 4,
        out_specs=[HB] * 11 + [VM] * 4,
        scratch_shapes=[
            *vm(wide16, wide16, plane, plane, plane, groups(8), groups(8), plane16, wide16, w1s),
            *vm(groups(), plane),
            pltpu.VMEM((rows // CHUNKS * 4, width), F32),
            vslot,
            zslot,
            pltpu.VMEM((rows, width), BF),
            pltpu.VMEM((2, rows, width), BF),
            pltpu.VMEM((width // n, chan), BF),
            pltpu.VMEM((width // n, ffp), BF),
            pltpu.VMEM((ff, width // n), BF),
            DMA, DMA, DMA((7,)), DMA((4,)), DMA((CHUNKS,)), DMA((CHUNKS,)),
            *small,
            *line_sems(CHUNKS),
            *gather_sems(n, 4),
            *gather_sems(n, 3),
        ],
        compiler_params=params(1),
        name="mixer_forward",
    )(
        lengths, layer_index, hidden_in, w_input, w_forget, w_outgate, w_output,
        padded(w_gate), padded(w_up), w_down, forget_bias, state_gain, gain_mid, gain_in,
    )

    shard, chips, tile, step = width // n, n // 2, rows // TILES, rows // CHUNKS
    piece = shape((shard, ffp), F32)
    ffs = shape((rows, ffp), BF)
    gmix, gres, glu_part, ggain, sum_gate, sum_up, down = pl.pallas_call(
        functools.partial(feed_forward, n, t, width),
        out_shape=[
            wide16, plane, shards16, shape((8, width), F32), piece, piece,
            shape((width // 2, ffp), BF),
        ],
        in_specs=[HB] * 5 + [VM] * 2,
        out_specs=[HB] * 3 + [VM] + [HB] * 3,
        scratch_shapes=[
            *vm(wide16, wide16, w2s, ffs, ffs, ffs),
            pltpu.VMEM((2, t, tile, chan), BF),
            pltpu.VMEM((2, step, width), BF),
            pltpu.VMEM((2, step, width), BF),
            pltpu.VMEM((2, step, width), BF),
            pltpu.VMEM((2, step, chan), F32),
            pltpu.VMEM((step, width), F32),
            *vm(piece),
            pltpu.VMEM((2, 2, shard, ffp), BF),
            *vm(wide16),
            pltpu.VMEM((2, rows, width), BF),
            DMA((2,)), DMA((3,)), DMA((2, 2)), DMA((2, 2)), DMA((2,)), DMA((3,)), DMA((2,)),
            DMA((3 * chips,)),
            pltpu.SemaphoreType.REGULAR,
            *line_sems(CHUNKS),
            *grid_buffers(n, width, 2, ffp),
        ],
        compiler_params=params(2),
        name="feed_forward",
    )(nmid, cotangent, w2, hidden_in, mixed, invmid, consts)

    shard_sems = [DMA((t, SHARD_CHUNKS))] * 4
    shard_bufs = [pltpu.VMEM((t, rows, chan), BF), pltpu.VMEM((t + 1, rows, chan), BF)]
    gni_part, dw1, vecs, block_out, dot_in, sum_down = pl.pallas_call(
        functools.partial(mixer_backward, n, t, width),
        out_shape=[
            shards16, shape((2, width // 2, 4 * chan), BF), shape((8, chan), F32), plane16, column,
            shape((ffp, shard), F32),
        ],
        in_specs=[SM] + [HB] * 13 + [VM] * 3,
        out_specs=[HB] * 2 + [VM] * 4,
        scratch_shapes=[
            pltpu.VMEM((width // 2, ffp), BF),
            *vm(wide16, wide16),
            pltpu.VMEM((width, 4 * chan), BF),
            *vm(plane16, groups(8), groups(8), plane, plane, plane),
            *vm(groups(), groups(), plane, shape((rows, 3 * chan), BF)),
            vslot,
            zslot,
            zslot,
            pltpu.VMEM((8, width), F32),
            pltpu.VMEM((t, 8, chan), F32),
            pltpu.VMEM((t, 8, chan), F32),
            *vm(wide16, plane16),
            *shard_bufs,
            *vm(shards16),
            pltpu.VMEM((2, 2, shard, 4 * chan), BF),
            DMA((12,)),
            *small,
            DMA((t,)), DMA((t,)), DMA((t,)), DMA((t,)),
            DMA((3,)),
            *shard_sems,
            DMA((3,)), DMA((2,)), DMA,
            *grid_buffers(n, width, 1, ffp),
        ],
        compiler_params=params(3),
        name="mixer_backward",
    )(
        lengths, glu_part, hidden_in, mixed, gmix, normed_in, w1, gated, states, feff, ipre, fpre, opre,
        down, invst, inv_in, consts,
    )

    square = shape((shard, chan), F32)
    grad_in, vectors, rms, g_input, g_forget, g_outgate, g_output = pl.pallas_call(
        functools.partial(closing, n, t, width),
        out_shape=[
            plane, shape((8, width), F32), shape((8, LANE), F32),
            square, square, square, shape((chan, shard), F32),
        ],
        in_specs=[SM] + [HB] * 4 + [VM] * 5,
        out_specs=[VM] * 7,
        scratch_shapes=[
            pltpu.VMEM((2, width // 2, 2 * chan), BF),
            pltpu.VMEM((2, width // 2, 2 * chan), BF),
            *vm(plane16, plane),
            *shard_bufs,
            vslot,
            pltpu.VMEM((t, 8, chan), F32),
            DMA((2,)), DMA((2, 2)), DMA, DMA((2,)),
            *shard_sems,
            DMA((n,)), DMA((n,)), DMA((t,)), DMA((t,)),
            *grid_buffers(n, width, 2, 2 * chan),
        ],
        compiler_params=params(4),
        name="closing",
    )(lengths, gni_part, dw1, hidden_in, gres, inv_in, dot_in, consts, vecs, ggain)

    arrays = (
        block_out, grad_in, g_input, g_forget, g_outgate, g_output, sum_gate[:, :ff], sum_up[:, :ff],
        sum_down[:ff],
    )
    count = len(arrays)
    *copies, gain0, bias0, gain1, gain2, rms_stats = pl.pallas_call(
        functools.partial(emit, count),
        out_shape=[shape(a.shape, a.dtype) for a in arrays] + [shape((width,), F32)] * 4 + [shape((3,), F32)],
        in_specs=[HB] * count + [VM, SM],
        out_specs=[HB] * count + [VM] * 4 + [SM],
        scratch_shapes=[pltpu.VMEM(a.shape, a.dtype) for a in arrays] + [DMA((2, count))],
        compiler_params=params(),
        name="emit",
    )(*arrays, vectors, rms)
    out, gin, g_input, g_forget, g_outgate, g_output, g_gate, g_up, g_down = copies
    return (
        out, gin, gain0, g_input, g_forget, bias0, g_outgate, gain1, g_output, gain2,
        g_gate, g_up, g_down, rms_stats,
    )


def solution(mesh):
    weight, turned = P("seq", "tp"), P("tp", "seq")
    in_specs = (
        P("seq", None), P(), weight, weight, P(), weight, P(), turned, P(), weight, weight, turned,
        P(), P(), P("seq", None),
    )
    out_specs = (
        weight, weight, P(), weight, weight, P(), weight, P(), turned, P(), weight, weight, turned, P(),
    )
    body = functools.partial(on_device, mesh.shape["seq"], mesh.shape["tp"])
    return jax.shard_map(
        body, mesh=mesh, in_specs=in_specs, out_specs=out_specs, check_vma=False
    )
```

```python
import functools

import jax
import jax.numpy as jnp
from jax import lax
from jax.experimental import pallas as pl
from jax.experimental.pallas import tpu as pltpu
from jax.sharding import PartitionSpec as P

LAYERS = 24
EPS = 1e-06
MESH = pl.DeviceIdType.MESH
DMA = pltpu.SemaphoreType.DMA
BF = jnp.bfloat16
F32 = jnp.float32
VM = pl.BlockSpec(memory_space=pltpu.VMEM)
HB = pl.BlockSpec(memory_space=pl.ANY)
LANE = 128
SEG = 8
TILES = 4
K2_LAGS = (1, 2, 3)
CHUNKS = 16
SHARD_CHUNKS = 4
HOP_LAG = 2
VMEM_LIMIT = 60 * 1024 * 1024


def nn(left, right):
    return jnp.dot(left, right, preferred_element_type=F32)


def nt(left, right):
    return lax.dot_general(left, right, (((1,), (1,)), ((), ())), preferred_element_type=F32)


def tn(left, right):
    return lax.dot_general(left, right, (((0,), (0,)), ((), ())), preferred_element_type=F32)


def shape(dims, dtype):
    return jax.ShapeDtypeStruct(dims, dtype)


def get(ref, at):
    return jnp.concatenate([ref[g, at, :] for g in range(ref.shape[0])], axis=1)


def put(ref, at, values):
    for g in range(ref.shape[0]):
        ref[g, at, :] = values[:, g * LANE : (g + 1) * LANE]


def put_shards(ref, at, values):
    k = ref.shape[2]
    for q in range(ref.shape[0]):
        ref[q, at, :] = values[:, q * k : (q + 1) * k]


def row_tile(rows):
    return rows // 3 if rows % 48 == 0 else rows


def greet_all(n, t, seq, tp):
    barrier = pltpu.get_barrier_semaphore()

    def along_seq(o, c):
        pl.semaphore_signal(barrier, inc=1, device_id=(lax.rem(seq + o, n), tp), device_id_type=MESH)
        return c

    def along_tp(o, c):
        pl.semaphore_signal(barrier, inc=1, device_id=(seq, lax.rem(tp + o, t)), device_id_type=MESH)
        return c

    lax.fori_loop(1, n, along_seq, 0)
    lax.fori_loop(1, t, along_tp, 0)
    pl.semaphore_wait(barrier, n - 1 + t - 1)


def greet_line(t, seq, tp):
    barrier = pltpu.get_barrier_semaphore()

    def along_tp(o, c):
        pl.semaphore_signal(barrier, inc=1, device_id=(seq, lax.rem(tp + o, t)), device_id_type=MESH)
        return c

    lax.fori_loop(1, t, along_tp, 0)
    pl.semaphore_wait(barrier, t - 1)


def spread(size, me, slots, send, recv, target):
    def copy(o, slot):
        return pltpu.make_async_remote_copy(
            src_ref=slots.at[slot],
            dst_ref=slots.at[slot],
            send_sem=send.at[o],
            recv_sem=recv.at[slot],
            device_id=target(lax.rem(me + o, size)),
            device_id_type=MESH,
        )

    def one(o, c):
        copy(o, me).start()
        return c

    def arrived(o, c):
        copy(o, lax.rem(me + o, size)).wait_recv()
        return c

    def sent(o, c):
        copy(o, me).wait_send()
        return c

    def go():
        lax.fori_loop(1, size, one, 0)

    def done():
        lax.fori_loop(1, size, arrived, 0)
        lax.fori_loop(1, size, sent, 0)

    return go, done


def row_sums(values):
    ones = jnp.ones((8, values.shape[1]), BF)
    high = values.astype(BF)
    rest = values - high.astype(F32)
    low = rest.astype(BF)
    return nt(ones, high) + nt(ones, low)


def sum_over_tp(part, t, seq, tp, slots, send, recv, between=None):
    slots[tp] = part
    go, done = spread(t, tp, slots, send, recv, lambda k: (seq, k))
    go()
    if between is not None:
        between()
    done()
    total = slots[0]
    for k in range(1, t):
        total = total + slots[k]
    return jnp.transpose(total)[:, :1]


def carry_over_seq(prod, state, n, seq, tp, slots, send, recv, backward, between=None):
    slots[seq] = jnp.concatenate([prod, state] + [jnp.zeros_like(prod)] * 6, axis=0)
    go, done = spread(n, seq, slots, send, recv, lambda k: (k, tp))
    go()
    if between is not None:
        between()
    done()

    def hop(i, total):
        j = n - 1 - i if backward else i
        block = slots[j]
        longer = block[1:2] + block[0:1] * total
        inside = (j > seq) if backward else (j < seq)
        return jnp.where(inside, longer, total)

    return lax.fori_loop(0, n, hop, jnp.zeros_like(prod))


def line_all_reduce(t, seq, tp, rows, chunks, partial, send, buf, sems, finish, lags):
    s_in, s_out, r_buf = sems
    step = rows // chunks
    half = t // 2
    depth = jnp.where(tp < half, tp, t - 1 - tp)
    inner = jnp.where(tp < half, tp + 1, tp - 1)
    outer = jnp.where(tp < half, tp - 1, tp + 1)
    outer = jnp.where(depth > 0, outer, inner)
    middle = (depth == half - 1).astype(jnp.int32)
    lag_in, lag_turn, lag_out = lags
    lag_first = lag_in * depth
    lag_second = lag_in * (half - 1) + lag_turn + lag_out * (half - 1 - depth)

    def part_of(k):
        return pl.ds(pl.multiple_of(k * step, step), step)

    def inward(k, slot):
        return pltpu.make_async_remote_copy(
            src_ref=send.at[part_of(k)],
            dst_ref=buf.at[slot, part_of(k)],
            send_sem=s_in.at[k],
            recv_sem=r_buf.at[slot, k],
            device_id=(seq, inner),
            device_id_type=MESH,
        )

    def outward(k):
        return pltpu.make_async_remote_copy(
            src_ref=buf.at[1, part_of(k)],
            dst_ref=buf.at[1, part_of(k)],
            send_sem=s_out.at[k],
            recv_sem=r_buf.at[1, k],
            device_id=(seq, outer),
            device_id_type=MESH,
        )

    def first(k):
        part = None if partial is None else partial(k)

        @pl.when(depth > 0)
        def _():
            inward(k, 0).wait_recv()
            mine = send[part_of(k), :].astype(F32) if part is None else part
            send[part_of(k), :] = (mine + buf[0, part_of(k), :].astype(F32)).astype(BF)

        if part is not None:

            @pl.when(depth == 0)
            def _():
                send[part_of(k), :] = part.astype(BF)

        inward(k, middle).start()

    def second(k):
        inward(k, 1).wait_recv()

        @pl.when(middle == 1)
        def _():
            both = send[part_of(k), :].astype(F32) + buf[1, part_of(k), :].astype(F32)
            buf[1, part_of(k), :] = both.astype(BF)

        @pl.when(depth > 0)
        def _():
            outward(k).start()

        finish(k)

    def turn(i):
        @pl.when((i >= lag_first) & (i - lag_first < chunks))
        def _():
            first(i - lag_first)

        @pl.when((i >= lag_second) & (i - lag_second < chunks))
        def _():
            second(i - lag_second)

    def drain():
        def sent(k, c):
            inward(k, middle).wait_send()

            @pl.when(depth > 0)
            def _():
                outward(k).wait_send()

            return c

        lax.fori_loop(0, chunks, sent, 0)

    return chunks + lag_in * (half - 1) + lag_turn + lag_out * (half - 1), turn, drain


def line_reduce_scatter(t, seq, tp, own, inbox, sems, finish, lead):
    s_r, r_r, s_l, r_l = sems
    rows = own.shape[1]
    chunks = SHARD_CHUNKS
    step = rows // chunks
    count = chunks * (t - 1)

    def part_of(k):
        return pl.ds(pl.multiple_of(k * step, step), step)

    def rightward(q, k):
        return pltpu.make_async_remote_copy(
            src_ref=own.at[q, part_of(k)],
            dst_ref=inbox.at[q + 1, part_of(k)],
            send_sem=s_r.at[q, k],
            recv_sem=r_r.at[q, k],
            device_id=(seq, lax.rem(tp + 1, t)),
            device_id_type=MESH,
        )

    def leftward(q, k):
        return pltpu.make_async_remote_copy(
            src_ref=own.at[q, part_of(k)],
            dst_ref=inbox.at[q, part_of(k)],
            send_sem=s_l.at[q, k],
            recv_sem=r_l.at[q, k],
            device_id=(seq, lax.rem(tp + t - 1, t)),
            device_id_type=MESH,
        )

    def add(q, k, slot):
        own[q, part_of(k), :] = (
            own[q, part_of(k), :].astype(F32) + inbox[slot, part_of(k), :].astype(F32)
        ).astype(BF)

    def right_turn(i):
        j, k = i // chunks, lax.rem(i, chunks)
        q = t - 1 - j

        @pl.when((i >= 0) & (i < count) & (q > tp))
        def _():
            @pl.when(tp > 0)
            def _():
                rightward(q, k).wait_recv()
                add(q, k, q + 1)

            rightward(q, k).start()

    def left_turn(i):
        q, k = i // chunks, lax.rem(i, chunks)

        @pl.when((i >= 0) & (i < count) & (q < tp))
        def _():
            @pl.when(tp < t - 1)
            def _():
                leftward(q, k).wait_recv()
                add(q, k, q)

            leftward(q, k).start()

    def begin():
        for i in range(lead):

            @pl.when(tp == 0)
            def _(i=i):
                right_turn(i)

            @pl.when(tp == t - 1)
            def _(i=i):
                left_turn(i)

    def turn(i):
        right_turn(i - jnp.where(tp == 0, -lead, HOP_LAG * tp))
        left_turn(i - jnp.where(tp == t - 1, -lead, HOP_LAG * (t - 1 - tp)))

    def last(k):
        @pl.when(tp == 0)
        def _():
            leftward(tp, k).wait_recv()
            finish(k, own[tp, part_of(k), :].astype(F32) + inbox[tp, part_of(k), :].astype(F32))

        @pl.when(tp == t - 1)
        def _():
            rightward(tp, k).wait_recv()
            finish(k, own[tp, part_of(k), :].astype(F32) + inbox[tp + 1, part_of(k), :].astype(F32))

        @pl.when((tp > 0) & (tp < t - 1))
        def _():
            leftward(tp, k).wait_recv()
            rightward(tp, k).wait_recv()
            finish(
                k,
                own[tp, part_of(k), :].astype(F32)
                + inbox[tp, part_of(k), :].astype(F32)
                + inbox[tp + 1, part_of(k), :].astype(F32),
            )

    def drain():
        def sent(i, c):
            j, k = i // chunks, lax.rem(i, chunks)

            @pl.when(t - 1 - j > tp)
            def _():
                rightward(t - 1 - j, k).wait_send()

            @pl.when(j < tp)
            def _():
                leftward(j, k).wait_send()

            return c

        lax.fori_loop(0, count, sent, 0)

    turns = max((t - 1 - p) * chunks + (HOP_LAG * p if p else -lead) for p in range(t - 1))
    return turns, begin, turn, last, drain


def chip_grid(n):
    chips = n // 2
    b = max(k for k in range(1, chips + 1) if chips % k == 0 and k * k <= chips)
    return chips // b, b


def grid_buffers(n, width, pieces, cols):
    ga, gb = chip_grid(n)
    h = width // n // 2
    pa, pb = max(ga - 1, 1), max(gb - 1, 1)
    return [
        pltpu.VMEM((pieces, pb, ga, h, cols), BF),
        pltpu.VMEM((pieces, pa, gb, h, cols), BF),
        pltpu.VMEM((pieces, pa, h, cols), BF),
        pltpu.VMEM((pieces, pb, h, cols), BF),
        DMA((2, pieces, pb, ga)), DMA((2, pieces, pa, gb)), DMA((2, pieces, pa)), DMA((2, pieces, pb)),
    ]


def add_cores(acc, first):
    part = 64

    def one(i, c):
        at = pl.ds(pl.multiple_of(i * part, part), part)
        acc[at, :] = (acc[at, :].astype(F32) + first[at, :].astype(F32)).astype(BF)
        return c

    lax.fori_loop(0, acc.shape[0] // part, one, 0)


def grid_reduce(n, seq, tp, j, acc, bufs, out):
    far_b, far_a, near_a, near_b, m_fb, m_fa, m_na, m_nb = bufs
    ga, gb = chip_grid(n)
    core = lax.rem(seq, 2)
    a, b = seq // 2 // gb, lax.rem(seq // 2, gb)
    h = near_a.shape[2]

    def device(a_, b_):
        return ((a_ * gb + b_) * 2 + core, tp)

    def block(half, x, y):
        return pl.ds(pl.multiple_of(((x * gb + y) * 2 + half) * h, h), h)

    def remote(rows, dst, sems, index, target):
        return pltpu.make_async_remote_copy(
            src_ref=acc.at[rows],
            dst_ref=dst,
            send_sem=sems.at[(0, j) + index],
            recv_sem=sems.at[(1, j) + index],
            device_id=target,
            device_id_type=MESH,
        )

    def first_way():
        copies = []
        for o in range(1, gb):
            to = lax.rem(b + o, gb)
            for x in range(ga):
                dst = far_b.at[j, o - 1, x]
                copies.append(remote(block(0, x, to), dst, m_fb, (o - 1, x), device(a, to)))
        for o in range(1, ga):
            to = lax.rem(a + o, ga)
            for y in range(gb):
                dst = far_a.at[j, o - 1, y]
                copies.append(remote(block(1, to, y), dst, m_fa, (o - 1, y), device(to, b)))
        return copies

    def second_way():
        copies = []
        for o in range(1, ga):
            to = lax.rem(a + o, ga)
            copies.append(
                remote(block(0, to, b), near_a.at[j, o - 1], m_na, (o - 1,), device(to, b))
            )
        for o in range(1, gb):
            to = lax.rem(b + o, gb)
            copies.append(
                remote(block(1, a, to), near_b.at[j, o - 1], m_nb, (o - 1,), device(a, to))
            )
        return copies

    def far():
        for copy in first_way():
            copy.start()

    def middle():
        for copy in first_way():
            copy.wait_recv()

        def along_a(x, c):
            total = acc[block(0, x, b), :].astype(F32)
            for o in range(1, gb):
                total = total + far_b[j, o - 1, x].astype(F32)
            acc[block(0, x, b), :] = total.astype(BF)
            return c

        def along_b(y, c):
            total = acc[block(1, a, y), :].astype(F32)
            for o in range(1, ga):
                total = total + far_a[j, o - 1, y].astype(F32)
            acc[block(1, a, y), :] = total.astype(BF)
            return c

        lax.fori_loop(0, ga, along_a, 0)
        lax.fori_loop(0, gb, along_b, 0)
        for copy in second_way():
            copy.start()

    def near():
        for copy in second_way():
            copy.wait_recv()
        total = acc[block(0, a, b), :].astype(F32)
        for o in range(1, ga):
            total = total + near_a[j, o - 1].astype(F32)
        out(0, total)
        total = acc[block(1, a, b), :].astype(F32)
        for o in range(1, gb):
            total = total + near_b[j, o - 1].astype(F32)
        out(1, total)

    def drain():
        for copy in first_way() + second_way():
            copy.wait_send()

    return far, middle, near, drain


def gather_sems(n, pieces):
    ga, gb = chip_grid(n)
    pa, pb = max(ga - 1, 1), max(gb - 1, 1)
    return [
        DMA((pieces,)), DMA((2, pieces, ga * gb)),
        DMA((2, pieces, pb)), DMA((2, pieces, pa)), DMA((2, pieces, gb, pa)), DMA((2, pieces, ga, pb)),
    ]


def grid_gather(n, seq, tp, j, src, dst, sems):
    s_local, m_core, m_fb, m_fa, m_na, m_nb = sems
    ga, gb = chip_grid(n)
    shard = src.shape[0]
    h = shard // 2
    core = lax.rem(seq, 2)
    a, b = seq // 2 // gb, lax.rem(seq // 2, gb)

    def device(a_, b_, core_):
        return ((a_ * gb + b_) * 2 + core_, tp)

    def block(x, y, core_, half, count):
        return pl.ds(pl.multiple_of(((x * gb + y) * 2 + core_) * shard + half * h, h), count)

    def remote(from_, rows, sem, index, target):
        return pltpu.make_async_remote_copy(
            src_ref=from_,
            dst_ref=dst.at[rows],
            send_sem=sem.at[(0, j) + index],
            recv_sem=sem.at[(1, j) + index],
            device_id=target,
            device_id_type=MESH,
        )

    def own(half):
        return src.at[pl.ds(half * h, h)]

    def far(incoming):
        copies = []
        for o in range(1, gb):
            to, of = lax.rem(b + o, gb), lax.rem(b + gb - o, gb)
            rows = block(a, of if incoming else b, core, 0, h)
            copies.append(remote(own(0), rows, m_fb, (o - 1,), device(a, to, core)))
        for o in range(1, ga):
            to, of = lax.rem(a + o, ga), lax.rem(a + ga - o, ga)
            rows = block(of if incoming else a, b, core, 1, h)
            copies.append(remote(own(1), rows, m_fa, (o - 1,), device(to, b, core)))
        return copies

    def near(incoming, first, least):
        copies = []
        for i in range(0 if first else 1, gb if least else 1):
            y = lax.rem(b + gb - i, gb)
            for o in range(1, ga):
                to, of = lax.rem(a + o, ga), lax.rem(a + ga - o, ga)
                rows = block(of if incoming else a, y, core, 0, h)
                from_ = own(0) if i == 0 or incoming else dst.at[rows]
                copies.append(remote(from_, rows, m_na, (i, o - 1), device(to, b, core)))
        for i in range(0 if first else 1, ga if least else 1):
            x = lax.rem(a + ga - i, ga)
            for o in range(1, gb):
                to, of = lax.rem(b + o, gb), lax.rem(b + gb - o, gb)
                rows = block(x, of if incoming else b, core, 1, h)
                from_ = own(1) if i == 0 or incoming else dst.at[rows]
                copies.append(remote(from_, rows, m_nb, (i, o - 1), device(a, to, core)))
        return copies

    def across(incoming, first, others):
        copies = []
        for i in range(ga):
            for k in range(gb):
                mine = i == 0 and k == 0
                if (mine and not first) or (not mine and not others):
                    continue
                x, y = lax.rem(a + i, ga), lax.rem(b + k, gb)
                rows = block(x, y, 1 - core if incoming else core, 0, shard)
                from_ = src if mine or incoming else dst.at[rows]
                copies.append(remote(from_, rows, m_core, (i * gb + k,), device(a, b, 1 - core)))
        return copies

    def local():
        return pltpu.make_async_copy(src, dst.at[block(a, b, core, 0, shard)], s_local.at[j])

    def start():
        for copy in far(False) + near(False, True, False) + across(False, True, False):
            copy.start()
        local().start()

    def relay():
        for copy in far(True):
            copy.wait_recv()
        for copy in near(False, False, True):
            copy.start()

    def share():
        for copy in near(True, True, True):
            copy.wait_recv()
        for copy in across(False, False, True):
            copy.start()

    def arrive():
        for copy in across(True, True, True):
            copy.wait_recv()
        local().wait()

    def drain():
        for copy in far(False) + near(False, True, True) + across(False, True, True):
            copy.wait_send()

    return start, relay, share, arrive, drain


def loop_with(first, last, body, works):
    def one(i, c):
        body(i)
        for when, work in works:

            @pl.when(i == when)
            def _(work=work):
                work()

        return c

    lax.fori_loop(first, last, one, 0)


def masks(lens, first, count):
    at = first + lax.broadcasted_iota(jnp.int32, (count, 1), 0)
    valid = (at < lens[0] + lens[1]).astype(F32)
    starts = ((at == 0) | (at == lens[0])).astype(F32)
    return valid, starts


def mixer_forward(
    n, t, width,
    lens, layer, x_h, wi_h, wf_h, wo_h, wx_raw, wg_h, wu_h, wd_raw_h, bias_v, sgain_v, gmid_v, gin_v,
    ipre_h, fpre_h, opre_h, feff_h, states_h, gated_h, normed_h, nmid_h, mixed_h, w1_h, w2_h,
    invst, invmid, invin, consts,
    x, normed, ipre, fpre, opre, feff, states, gated, nmid, w1, prod, ssq, part, cslots, zslots, send, buf,
    wx, wd, wd_raw, s_t, s_x, s_st, s_w, s_n, s_m, cs, cr, zs, zr, s_in, s_out, r_buf, *sems,
):
    seq, tp = lax.axis_index("seq"), lax.axis_index("tp")
    load = pltpu.make_async_copy(x_h, x, s_x)
    load.start()
    load_down = pltpu.make_async_copy(wd_raw_h, wd_raw, s_t)
    load_down.start()
    sems1, sems2 = sems[:6], sems[6:]
    one = [
        grid_gather(n, seq, tp, j, src, w1.at[j], sems1)
        for j, src in enumerate((wi_h, wf_h, wo_h, wx))
    ]
    two = [
        grid_gather(n, seq, tp, j, src, w2_h.at[j], sems2)
        for j, src in enumerate((wg_h, wu_h, wd))
    ]
    START, RELAY, SHARE, ARRIVE, DRAIN = range(5)
    greet_all(n, t, seq, tp)
    one[0][START]()
    rows, depth = normed.shape
    chan = ipre.shape[1]
    tile = row_tile(rows)
    mine = pl.ds(pl.multiple_of(tp * chan, LANE), chan)
    consts[...] = jnp.zeros_like(consts)
    for k, vector in ((0, bias_v), (1, sgain_v), (3, gmid_v), (4, gin_v)):
        consts[k : k + 1, :] = vector[...].astype(F32).reshape(1, width)
    consts[2:3, :] = jnp.full((1, width), layer[0].astype(F32) / LAYERS)
    bias, sgain, bound = consts[0:1, mine], consts[1:2, mine], consts[2:3, mine]

    def stores():
        pairs = (
            (ipre, ipre_h), (fpre, fpre_h), (opre, opre_h), (feff, feff_h), (states, states_h),
            (gated, gated_h), (normed, normed_h),
        )
        return [pltpu.make_async_copy(v, o, s_st.at[i]) for i, (v, o) in enumerate(pairs)]

    def keep(j):
        return pltpu.make_async_copy(w1.at[j], w1_h.at[j], s_w.at[j])

    wx[...] = jnp.transpose(wx_raw[...])
    load.wait()

    def norm(i, c):
        at = pl.ds(pl.multiple_of(i * tile, tile), tile)
        v = x[at, :].astype(F32)
        inv = lax.rsqrt(jnp.mean(v * v, axis=-1, keepdims=True) + EPS)
        invin[at, :] = inv
        normed[at, :] = (v * inv * consts[4:5, :]).astype(BF)
        return c

    lax.fori_loop(0, rows // tile, norm, 0)
    one[0][RELAY]()
    one[1][START]()
    load_down.wait()
    turned = jnp.transpose(wd_raw[...])
    wd[:, : turned.shape[1]] = turned
    if turned.shape[1] < wd.shape[1]:
        wd[:, turned.shape[1] :] = jnp.zeros((wd.shape[0], wd.shape[1] - turned.shape[1]), BF)
    one[0][SHARE]()
    one[1][RELAY]()
    one[2][START]()
    one[0][ARRIVE]()
    keep(0).start()

    def first(i, c):
        at = pl.ds(pl.multiple_of(i * tile, tile), tile)
        ipre[at, :] = nn(normed[at, :], w1[0])
        return c

    lax.fori_loop(0, rows // tile, first, 0)
    one[1][SHARE]()
    one[2][RELAY]()
    one[3][START]()
    one[1][ARRIVE]()
    keep(1).start()

    def second(i, c):
        at = pl.ds(pl.multiple_of(i * tile, tile), tile)
        f = nn(normed[at, :], w1[1]) + bias
        fpre[at, :] = f
        valid, starts = masks(lens, seq * rows + i * tile, tile)
        gate = bound + (1.0 - bound) * jax.nn.sigmoid(f)
        put(feff, at, gate * (1.0 - starts))
        shifted = pl.ds(pl.multiple_of(i * tile + 8, 8), tile)
        v = ipre[at, :]
        put(states, shifted, v * jax.nn.sigmoid(v) * (1.0 - gate) * valid)
        return c

    lax.fori_loop(0, rows // tile, second, 0)
    put(feff, slice(rows, rows + 8), jnp.ones((8, chan), F32))

    length = rows // SEG

    def scan(i, c):
        p, h = c
        at, shifted = pl.ds(i, SEG, stride=length), pl.ds(i + 8, SEG, stride=length)
        f = get(feff, at)
        h = f * h + get(states, shifted)
        p = f * p
        put(states, shifted, h)
        put(prod, at, p)
        return p, h

    p, h = lax.fori_loop(
        0, length, scan, (jnp.ones((SEG, chan), F32), jnp.zeros((SEG, chan), F32))
    )
    block_p, block_h = p[0:1], h[0:1]
    for s in range(1, SEG):
        block_h = h[s : s + 1] + p[s : s + 1] * block_h
        block_p = p[s : s + 1] * block_p

    def travel():
        one[2][SHARE]()
        one[3][RELAY]()
        two[0][START]()

    arriving = carry_over_seq(block_p, block_h, n, seq, tp, cslots, cs, cr, False, travel)
    put(states, slice(0, 8), jnp.broadcast_to(arriving, (8, chan)))
    for s in range(SEG):
        at = slice(s * length, (s + 1) * length)
        shifted = slice(s * length + 8, (s + 1) * length + 8)
        whole = get(states, shifted) + get(prod, at) * arriving
        put(states, shifted, whole)
        ssq[at, :] = whole * whole
        arriving = h[s : s + 1] + p[s : s + 1] * arriving

    def outgate():
        one[3][SHARE]()
        one[2][ARRIVE]()
        keep(2).start()

        def third(i, c):
            at = pl.ds(pl.multiple_of(i * tile, tile), tile)
            opre[at, :] = nn(normed[at, :], w1[2])
            return c

        lax.fori_loop(0, rows // tile, third, 0)

    total = sum_over_tp(row_sums(ssq[...]), t, seq, tp, zslots, zs, zr, outgate)
    invst[...] = lax.rsqrt(total / width + EPS)

    def gating(i, c):
        at = pl.ds(pl.multiple_of(i * tile, tile), tile)
        shifted = pl.ds(pl.multiple_of(i * tile + 8, 8), tile)
        o = opre[at, :]
        gated[at, :] = (
            get(states, shifted) * invst[at, :] * sgain * (o * jax.nn.sigmoid(o))
        ).astype(BF)
        return c

    lax.fori_loop(0, rows // tile, gating, 0)
    one[3][ARRIVE]()
    keep(3).start()
    for copy in stores():
        copy.start()

    step = rows // CHUNKS
    group = part.shape[0] // step

    def partial(k):
        @pl.when(lax.rem(k, group) == 0)
        def _():
            big = pl.ds(pl.multiple_of(k * step, step), step * group)
            part[...] = nt(gated[big, :], w1[3])

        return part[pl.ds(pl.multiple_of(lax.rem(k, group) * step, step), step), :]

    def store_n(k):
        at = pl.ds(pl.multiple_of(k * step, step), step)
        return pltpu.make_async_copy(nmid.at[at], nmid_h.at[at], s_n.at[k])

    def store_m(k):
        at = pl.ds(pl.multiple_of(k * step, step), step)
        return pltpu.make_async_copy(buf.at[1, at], mixed_h.at[at], s_m.at[k])

    def finish(k):
        at = pl.ds(pl.multiple_of(k * step, step), step)
        store_m(k).start()
        resid = x[at, :].astype(F32) + buf[1, at, :].astype(F32)
        inv = lax.rsqrt(jnp.mean(resid * resid, axis=-1, keepdims=True) + EPS)
        invmid[at, :] = inv
        nmid[at, :] = (resid * inv * consts[3:4, :]).astype(BF)
        store_n(k).start()

    turns = [
        (2, lambda: (two[0][RELAY](), two[1][START]())),
        (4, lambda: two[0][SHARE]()),
        (7, lambda: (two[1][RELAY](), two[2][START]())),
        (9, lambda: two[1][SHARE]()),
        (13, lambda: two[2][RELAY]()),
        (16, lambda: two[2][SHARE]()),
    ]

    count, turn, drain = line_all_reduce(
        t, seq, tp, rows, CHUNKS, partial, send, buf, (s_in, s_out, r_buf), finish, (0, 1, 3)
    )
    loop_with(0, count, turn, turns)
    drain()
    for g in two:
        g[ARRIVE]()
    for g in one + two:
        g[DRAIN]()
    for copy in stores():
        copy.wait()
    for j in range(4):
        keep(j).wait()

    def stored(k, c):
        store_n(k).wait()
        store_m(k).wait()
        return c

    lax.fori_loop(0, CHUNKS, stored, 0)


def feed_forward(
    n, t, width,
    nmid_h, cot_h, w2_h, x_h, mixed_h, invmid, consts,
    gmix_h, gres_h, glu_h, ggain, gate_h, up_h, down_h,
    nmid, cot, pool, hid, gg, gu, glu, xs, ms, gmix, gres, wide, sums, stage, send, buf,
    s_a, s_w, s_x, s_o, s_g, s_s, s_d, m_core, ready, s_in, s_out, r_buf, *bufs,
):
    seq, tp = lax.axis_index("seq"), lax.axis_index("tp")
    core = lax.rem(seq, 2)
    sibling = (seq + 1 - 2 * core, tp)
    act_copies = [
        pltpu.make_async_copy(nmid_h, nmid, s_a.at[0]),
        pltpu.make_async_copy(cot_h, cot, s_a.at[1]),
    ]
    w_copies = [pltpu.make_async_copy(w2_h.at[j], pool.at[j], s_w.at[j]) for j in range(3)]
    act_copies[0].start()
    w_copies[0].start()
    greet_all(n, t, seq, tp)
    for copy in (w_copies[1], act_copies[1], w_copies[2]):
        copy.start()
    rows, chan = nmid.shape[0], gres.shape[2]
    step = rows // CHUNKS
    tile = rows // TILES
    ggain[...] = jnp.zeros_like(ggain)

    def fetch(k):
        at, slot = pl.ds(pl.multiple_of(k * step, step), step), lax.rem(k, 2)
        return (
            pltpu.make_async_copy(x_h.at[at], xs.at[slot], s_x.at[0, slot]),
            pltpu.make_async_copy(mixed_h.at[at], ms.at[slot], s_x.at[1, slot]),
        )

    def stored(k):
        at, slot = pl.ds(pl.multiple_of(k * step, step), step), lax.rem(k, 2)
        return (
            pltpu.make_async_copy(gmix.at[slot], gmix_h.at[at], s_o.at[0, slot]),
            pltpu.make_async_copy(gres.at[slot], gres_h.at[at], s_o.at[1, slot]),
        )

    for copy in fetch(0):
        copy.start()

    def finish(k):
        for copy in fetch(k):
            copy.wait()

        @pl.when(k + 1 < CHUNKS)
        def _():
            for copy in fetch(k + 1):
                copy.start()

        @pl.when(k >= 2)
        def _():
            for copy in stored(k - 2):
                copy.wait()

        at, slot = pl.ds(pl.multiple_of(k * step, step), step), lax.rem(k, 2)
        g = buf[1, at, :].astype(F32)
        inv = invmid[at, :]
        hat = (xs[slot].astype(F32) + ms[slot].astype(F32)) * inv
        ggain[0:1, :] += jnp.sum(g * hat, axis=0, keepdims=True)
        e = g * consts[3:4, :]
        mean = jnp.mean(e * hat, axis=-1, keepdims=True)
        result = cot[at, :].astype(F32) + inv * (e - hat * mean)
        wide[...] = result
        gmix[slot] = result.astype(BF)
        gres[slot] = wide[:, pl.ds(pl.multiple_of(tp * chan, LANE), chan)]
        for copy in stored(k):
            copy.start()

    count, turn, drain = line_all_reduce(
        t, seq, tp, rows, CHUNKS, None, send, buf, (s_in, s_out, r_buf), finish, K2_LAGS
    )

    act_copies[0].wait()
    w_copies[0].wait()

    def block(i, c):
        at = pl.ds(pl.multiple_of(i * tile, tile), tile)
        g = nn(nmid[at, :], pool[0])

        @pl.when(i == 0)
        def _():
            w_copies[1].wait()
            act_copies[1].wait()
            w_copies[2].wait()

        u = nn(nmid[at, :], pool[1])
        gh = nn(cot[at, :], pool[2])
        sig = jax.nn.sigmoid(g)
        act = g * sig
        hid[at, :] = (act * u).astype(BF)
        gg[at, :] = (gh * u * (sig * (1.0 + g * (1.0 - sig)))).astype(BF)
        gu[at, :] = (gh * act).astype(BF)

        @pl.when(i > 0)
        def _():
            turn(2 * i - 1)

        send[at, :] = (nt(gg[at, :], pool[0]) + nt(gu[at, :], pool[1])).astype(BF)
        turn(2 * i)
        return c

    lax.fori_loop(0, TILES, block, 0)
    done = 2 * TILES - 1

    ga, gb = chip_grid(n)
    chips = ga * gb
    shard = width // n
    half_pool = pl.ds(0, width // 2)
    other_half = pl.ds(width // 2, width // 2)

    def give(i):
        j, r = i // chips, lax.rem(i, chips)
        return pltpu.make_async_remote_copy(
            src_ref=stage.at[lax.rem(i, 2), 1 - core],
            dst_ref=pool.at[j, pl.ds(pl.multiple_of(width // 2 + r * shard, shard), shard)],
            send_sem=s_g.at[lax.rem(i, 2)],
            recv_sem=m_core.at[i],
            device_id=sibling,
            device_id_type=MESH,
        )

    def gradient(j, left, right, first_turn, turns):
        pl.semaphore_signal(ready, inc=1, device_id=sibling, device_id_type=MESH)
        pl.semaphore_wait(ready, 1)

        def slab(r, c):
            i = j * chips + r
            slot = lax.rem(i, 2)

            @pl.when(i >= 2)
            def _():
                give(i - 2).wait_send()

            at = pl.ds(pl.multiple_of(r * 2 * shard, 2 * shard), 2 * shard)
            values = tn(left[:, at], right[...]).astype(BF)
            for k in range(2):
                stage[slot, k] = values[k * shard : (k + 1) * shard]
            give(i).start()
            pool[j, pl.ds(pl.multiple_of(r * shard, shard), shard), :] = stage[slot, core]
            loop_with(first_turn + r * turns // chips, first_turn + (r + 1) * turns // chips, turn, ())
            return c

        lax.fori_loop(0, chips, slab, 0)

    def cores(j):
        def arrived(r, c):
            give(j * chips + r).wait_recv()
            return c

        lax.fori_loop(0, chips, arrived, 0)
        add_cores(pool.at[j, half_pool], pool.at[j, other_half])

    def summed(j):
        return pltpu.make_async_copy(sums, (gate_h, up_h)[j], s_s.at[j])

    def out(half, values):
        sums[half * (shard // 2) : (half + 1) * (shard // 2), :] = values

    reduces = [
        grid_reduce(n, seq, tp, j, pool.at[j, half_pool], bufs, out) for j in range(2)
    ]
    gradient(0, nmid, gg, done, 2)
    cores(0)
    reduces[0][0]()
    gradient(1, nmid, gu, done + 2, 2)
    cores(1)
    reduces[1][0]()

    def glu_copy(i):
        at, slot = pl.ds(pl.multiple_of(i * tile, tile), tile), lax.rem(i, 2)
        return pltpu.make_async_copy(glu.at[slot], glu_h.at[:, at], s_d.at[slot])

    def forward(i, c):
        @pl.when(i >= 2)
        def _():
            glu_copy(i - 2).wait()

        at, slot = pl.ds(pl.multiple_of(i * tile, tile), tile), lax.rem(i, 2)
        values = nt(hid[at, :], pool[2]).astype(BF)
        for q in range(t):
            glu[slot, q] = values[:, q * chan : (q + 1) * chan]
        glu_copy(i).start()

        @pl.when(lax.rem(i, 2) == 1)
        def _():
            turn(done + 4 + i // 2)

        return c

    lax.fori_loop(0, TILES, forward, 0)
    glu_copy(TILES - 2).wait()
    glu_copy(TILES - 1).wait()
    reduces[0][1]()
    gradient(2, cot, hid, done + 4 + TILES // 2, 2)
    cores(2)
    down = pltpu.make_async_copy(pool.at[2, half_pool], down_h, s_s.at[2])
    down.start()

    def second_sum():
        summed(0).wait()
        reduces[1][2]()
        summed(1).start()

    now = done + 6 + TILES // 2
    loop_with(
        now,
        count,
        turn,
        (
            (now + 1, lambda: (reduces[0][2](), summed(0).start())),
            (now + 2, lambda: reduces[1][1]()),
            (now + 5, second_sum),
        ),
    )
    drain()
    for r in reduces:
        r[3]()
    give(3 * chips - 2).wait_send()
    give(3 * chips - 1).wait_send()
    summed(1).wait()
    down.wait()
    for k in (CHUNKS - 2, CHUNKS - 1):
        for copy in stored(k):
            copy.wait()


def mixer_backward(
    n, t, width,
    lens, glu_h, x_h, mixed_h, gmix_h, normed_h, w1_h, gated_h, states_h, feff_h, ipre_h, fpre_h, opre_h,
    down_h, invst, invin, consts,
    gni_h, dw1_h, vecs, out, dot_in, sums,
    acc, gmix, normed, w1, gated, states, feff, ipre, fpre, opre,
    weighted, prod, inner, out3, cslots, zslots, zslots2, gain_sum, gsend, gtake, x, mc, own, inbox, gni, stage,
    s_f, cs, cr, zs, zr, zs2, zr2, gs_, gr_, s_x, sr, rr, sl, rl, s_o, s_d, s_acc, *bufs,
):
    seq, tp = lax.axis_index("seq"), lax.axis_index("tp")
    down = pltpu.make_async_copy(down_h, acc, s_acc)
    down.start()
    rows = gmix.shape[0]
    chan = ipre.shape[1]
    mine = pl.ds(pl.multiple_of(tp * chan, LANE), chan)
    fetches = [
        pltpu.make_async_copy(glu_h, own, s_x.at[0]),
        pltpu.make_async_copy(x_h, x, s_x.at[1]),
        pltpu.make_async_copy(mixed_h.at[:, mine], mc, s_x.at[2]),
    ]
    pairs = [
        (gmix_h, gmix),
        (w1_h.at[3], w1.at[:, pl.ds(3 * chan, chan)]),
        (states_h, states), (opre_h, opre), (feff_h, feff), (ipre_h, ipre), (fpre_h, fpre),
    ] + [(w1_h.at[j], w1.at[:, pl.ds(j * chan, chan)]) for j in range(3)] + [
        (normed_h, normed), (gated_h, gated),
    ]
    inputs = [pltpu.make_async_copy(src, dst, s_f.at[i]) for i, (src, dst) in enumerate(pairs)]
    fetches[0].start()
    for copy in inputs[:4]:
        copy.start()
    greet_all(n, t, seq, tp)
    for copy in inputs[4:] + fetches[1:]:
        copy.start()

    def down_out(half, values):
        size = sums.shape[1] // 2
        sums[:, half * size : (half + 1) * size] = jnp.transpose(values)

    far, middle, near, drain_grid = grid_reduce(n, seq, tp, 0, acc, bufs, down_out)
    tile = row_tile(rows)
    sgain, bound = consts[1:2, mine], consts[2:3, mine]
    vecs[...] = jnp.zeros_like(vecs)
    step = rows // SHARD_CHUNKS

    def finish(k, values):
        at = pl.ds(pl.multiple_of(k * step, step), step)
        ok, _ = masks(lens, seq * rows + k * step, step)
        m = mc[at, :].astype(F32)
        full = x[at, mine].astype(F32) + m + values
        out[at, :] = full.astype(BF)
        vecs[4:5, :] += jnp.sum(ok * m * m, axis=0, keepdims=True)
        vecs[5:6, :] += jnp.sum(ok * values * values, axis=0, keepdims=True)
        vecs[6:7, :] += jnp.sum(ok * full * full, axis=0, keepdims=True)

    turns, begin, turn, last, drain = line_reduce_scatter(
        t, seq, tp, own, inbox, (sr, rr, sl, rl), finish, 0
    )
    slots = 12

    def pump(slot):
        def one(i, c):
            turn(i)
            return c

        lax.fori_loop(slot * turns // slots, (slot + 1) * turns // slots, one, 0)

    fetches[0].wait()
    pump(0)
    down.wait()
    far()
    for copy in inputs[:4]:
        copy.wait()

    def gates(i, c):
        @pl.when(i == 1)
        def _():
            pump(1)

        at = pl.ds(pl.multiple_of(i * tile, tile), tile)
        shifted = pl.ds(pl.multiple_of(i * tile + 8, 8), tile)
        g = nn(gmix[at, :], w1[:, 3 * chan :])
        hat = get(states, shifted) * invst[at, :]
        o = opre[at, :]
        sig = jax.nn.sigmoid(o)
        q = o * sig
        vecs[2:3, :] += jnp.sum(g * hat * q, axis=0, keepdims=True)
        out3[at, 2 * chan :] = (g * hat * sgain * (sig * (1.0 + o * (1.0 - sig)))).astype(BF)
        w = g * q * sgain
        put(weighted, at, w)
        inner[at, :] = w * hat
        return c

    lax.fori_loop(0, 3, gates, 0)
    dot = sum_over_tp(row_sums(inner[...]), t, seq, tp, zslots, zs, zr, lambda: (pump(2), pump(3))) / width
    inner[:, 0:1] = dot

    def leaving(i, c):
        at = pl.ds(pl.multiple_of(i * tile, tile), tile)
        shifted = pl.ds(pl.multiple_of(i * tile + 8, 8), tile)
        inv = invst[at, :]
        put(weighted, at, inv * (get(weighted, at) - get(states, shifted) * inv * inner[at, 0:1]))
        return c

    lax.fori_loop(0, 3, leaving, 0)
    inputs[4].wait()
    pump(4)

    length = rows // SEG

    def scan(i, c):
        p, h = c
        r = length - 1 - i
        at = pl.ds(r, SEG, stride=length)
        f = get(feff, pl.ds(r + 1, SEG, stride=length))
        h = f * h + get(weighted, at)
        p = f * p
        put(weighted, at, h)
        put(prod, at, p)
        return p, h

    p, h = lax.fori_loop(
        0, length, scan, (jnp.ones((SEG, chan), F32), jnp.zeros((SEG, chan), F32))
    )
    block_p, block_h = p[SEG - 1 : SEG], h[SEG - 1 : SEG]
    for s in range(SEG - 2, -1, -1):
        block_h = h[s : s + 1] + p[s : s + 1] * block_h
        block_p = p[s : s + 1] * block_p
    first = get(feff, slice(0, 1))
    arriving = carry_over_seq(
        first * block_p, first * block_h, n, seq, tp, cslots, cs, cr, True, lambda: (pump(5), pump(6))
    )
    inputs[5].wait()
    inputs[6].wait()
    middle()
    bias_sum = jnp.zeros((1, chan), F32)
    for s in range(SEG - 1, -1, -1):
        if s in (5, 1):
            pump(8 - s // 5)
        at = slice(s * length, (s + 1) * length)
        gs = get(weighted, at) + get(prod, at) * arriving
        arriving = h[s : s + 1] + p[s : s + 1] * arriving
        a = ipre[at, :]
        sa = jax.nn.sigmoid(a)
        act = a * sa
        sf = jax.nn.sigmoid(fpre[at, :])
        gate = bound + (1.0 - bound) * sf
        ok, starts = masks(lens, seq * rows + s * length, length)
        out3[at, :chan] = (gs * (1.0 - gate) * ok * (sa * (1.0 + a * (1.0 - sa)))).astype(BF)
        before = get(states, slice(s * length + 7, (s + 1) * length + 7))
        gate_grad = gs * before * (1.0 - starts) - gs * act * ok
        gf = (gate_grad * (1.0 - bound) * sf * (1.0 - sf)).astype(BF)
        out3[at, chan : 2 * chan] = gf
        bias_sum = bias_sum + jnp.sum(gf.astype(F32), axis=0, keepdims=True)
    vecs[1:2, :] = bias_sum

    def gni_copy(i):
        at = pl.ds(pl.multiple_of(i * tile, tile), tile)
        return pltpu.make_async_copy(gni.at[:, at], gni_h.at[:, at], s_o.at[i])

    for copy in inputs[7:] + fetches[1:]:
        copy.wait()
    gain_sum[...] = jnp.zeros_like(gain_sum)

    def spread_in(i, c):
        at = pl.ds(pl.multiple_of(i * tile, tile), tile)
        values = nt(out3[at, :], w1[:, : 3 * chan])
        put_shards(gni, at, values.astype(BF))
        gni_copy(i).start()
        product = values * (x[at, :].astype(F32) * invin[at, :])
        gain_sum[0:1, :] += jnp.sum(product, axis=0, keepdims=True)
        product = product * consts[4:5, :]
        short = product[:, :LANE]
        for k in range(LANE, width, LANE):
            short = short + product[:, k : k + LANE]
        inner[at, :LANE] = short
        pump(9 + i)
        return c

    lax.fori_loop(0, 3, spread_in, 0)

    zslots2[tp] = row_sums(inner[:, :LANE])
    go_z, done_z = spread(t, tp, zslots2, zs2, zr2, lambda k: (seq, k))
    go_z()
    gsend[...] = jnp.zeros_like(gsend)
    for q in range(t):
        gsend[q, 0:1, :] = gain_sum[0:1, q * chan : (q + 1) * chan]

    def gain_copy(o, slot):
        to = lax.rem(tp + o, t)
        return pltpu.make_async_remote_copy(
            src_ref=gsend.at[to],
            dst_ref=gtake.at[slot],
            send_sem=gs_.at[o],
            recv_sem=gr_.at[slot],
            device_id=(seq, to),
            device_id_type=MESH,
        )

    def gain_go(o, c):
        gain_copy(o, tp).start()
        return c

    def gain_done(o, c):
        gain_copy(o, lax.rem(tp + o, t)).wait_recv()
        return c

    def gain_sent(o, c):
        gain_copy(o, tp).wait_send()
        return c

    lax.fori_loop(1, t, gain_go, 0)
    gtake[tp] = gsend[tp]
    near()
    shard = width // n
    chips = n // 2

    def d_copy(r, slot):
        at = pl.ds(pl.multiple_of(r * shard, shard), shard)
        return pltpu.make_async_copy(stage.at[slot], dw1_h.at[:, at], s_d.at[slot])

    def keep(slot, first, values):
        for k in range(2):
            stage[slot, k, :, first : first + values.shape[1]] = values[k * shard : (k + 1) * shard]

    def slab(r, c):
        slot = lax.rem(r, 2)

        @pl.when(r >= 2)
        def _():
            d_copy(r - 2, slot).wait()

        at = pl.ds(pl.multiple_of(r * 2 * shard, 2 * shard), 2 * shard)
        keep(slot, 0, tn(normed[:, at], out3[...]).astype(BF))
        keep(slot, 3 * chan, tn(gmix[:, at], gated[...]).astype(BF))
        d_copy(r, slot).start()
        return c

    lax.fori_loop(0, chips, slab, 0)

    done_z()
    total = zslots2[0]
    for k in range(1, t):
        total = total + zslots2[k]
    dot_in[...] = jnp.transpose(total)[:, :1] / width
    lax.fori_loop(1, t, gain_done, 0)
    lax.fori_loop(1, t, gain_sent, 0)
    gains = gtake[0]
    for k in range(1, t):
        gains = gains + gtake[k]
    vecs[0:1, :] = gains[0:1]

    def ending(k, c):
        last(k)
        return c

    lax.fori_loop(0, SHARD_CHUNKS, ending, 0)
    for r in range(max(chips - 2, 0), chips):
        d_copy(r, r % 2).wait()

    def stored(i, c):
        gni_copy(i).wait()
        return c

    lax.fori_loop(0, 3, stored, 0)
    drain()
    drain_grid()


def closing(
    n, t, width,
    lens, gni_h, dw1_h, x_h, gres_h, invin, dot_in, consts, vecs, ggain,
    gin, vectors, rms, g_input, g_forget, g_outgate, g_output,
    acc, other, xc, gres, own, inbox, vslots, allvec,
    s_acc, m_core, s_own, s_x, sr, rr, sl, rl, vs, vr, ts, tr, *bufs,
):
    seq, tp = lax.axis_index("seq"), lax.axis_index("tp")
    rows, chan = gres.shape
    mine = pl.ds(pl.multiple_of(tp * chan, LANE), chan)
    fetch = pltpu.make_async_copy(gni_h, own, s_own)
    fetches = [
        pltpu.make_async_copy(x_h.at[:, mine], xc, s_x.at[0]),
        pltpu.make_async_copy(gres_h, gres, s_x.at[1]),
    ]
    fetch.start()
    greet_all(n, t, seq, tp)
    pieces, shard, cols = 2, g_input.shape[0], 2 * chan

    core = lax.rem(seq, 2)

    def load(j):
        return pltpu.make_async_copy(
            dw1_h.at[core, :, pl.ds(j * cols, cols)], acc.at[j], s_acc.at[j]
        )

    def swap(j):
        return pltpu.make_async_remote_copy(
            src_ref=dw1_h.at[1 - core, :, pl.ds(j * cols, cols)],
            dst_ref=other.at[j],
            send_sem=m_core.at[0, j],
            recv_sem=m_core.at[1, j],
            device_id=(seq + 1 - 2 * core, tp),
            device_id_type=MESH,
        )

    def start(j):
        load(j).start()
        swap(j).start()

    reduces = []
    for j in range(pieces):

        def out(half, values, j=j):
            at = slice(half * (shard // 2), (half + 1) * (shard // 2))
            if j == 0:
                g_input[at, :] = values[:, :chan]
                g_forget[at, :] = values[:, chan:]
            else:
                g_outgate[at, :] = values[:, :chan]
                g_output[:, at] = jnp.transpose(values[:, chan:])

        reduces.append(grid_reduce(n, seq, tp, j, acc.at[j], bufs, out))

    def stage1(j):
        load(j).wait()
        swap(j).wait_recv()
        add_cores(acc.at[j], other.at[j])
        reduces[j][0]()

    def stage2(j):
        reduces[j][1]()

    def stage3(j):
        reduces[j][2]()

    fetch.wait()
    start(0)
    for copy in fetches:
        copy.start()
    step = rows // SHARD_CHUNKS
    gain_in = consts[4:5, mine]
    vslots[seq] = vecs[...]
    vslots[seq, 3:4, :] = ggain[0:1, mine]
    go_v, done_v = spread(n, seq, vslots, vs, vr, lambda k: (k, tp))
    go_t, done_t = spread(t, tp, allvec, ts, tr, lambda k: (seq, k))
    go_v()
    for copy in fetches:
        copy.wait()

    def finish(k, values):
        at = pl.ds(pl.multiple_of(k * step, step), step)
        hat = xc[at, :].astype(F32) * invin[at, :]
        gin[at, :] = gres[at, :] + invin[at, :] * (values * gain_in - hat * dot_in[at, :])

    def vectors_on():
        done_v()
        total = vslots[0]
        for k in range(1, n):
            total = total + vslots[k]
        allvec[tp] = total
        go_t()

    turns, begin, turn, last, drain = line_reduce_scatter(
        t, seq, tp, own, inbox, (sr, rr, sl, rl), finish, HOP_LAG
    )
    works = [
        (0, lambda: (stage1(0), start(1), vectors_on())),
        (2, lambda: stage1(1)),
        (4, lambda: stage2(0)),
        (6, lambda: stage3(0)),
        (7, lambda: stage2(1)),
        (9, lambda: stage3(1)),
    ]
    slots = 10
    begin()

    def turn_of(slot):
        def one(i, c):
            turn(i)
            return c

        lax.fori_loop(slot * turns // slots, (slot + 1) * turns // slots, one, 0)

    loop_with(0, slots, turn_of, works)
    done_t()
    squares = jnp.zeros((8, 1), F32)
    for k in range(t):
        vectors[:, k * chan : (k + 1) * chan] = allvec[k]
        squares = squares + jnp.sum(allvec[k], axis=1, keepdims=True)
    count = (lens[0] + lens[1]).astype(F32) * width
    rms[...] = jnp.broadcast_to(jnp.sqrt(squares / count), rms.shape)

    def ending(k, c):
        last(k)
        return c

    lax.fori_loop(0, SHARD_CHUNKS, ending, 0)
    drain()
    for j in range(pieces):
        swap(j).wait_send()
        reduces[j][3]()


def emit(count, *refs):
    sources, (vectors, roots) = refs[:count], refs[count : count + 2]
    targets = refs[count + 2 : 2 * count + 2]
    outs, stats = refs[2 * count + 2 : 2 * count + 6], refs[2 * count + 6]
    held, sem = refs[2 * count + 7 : 3 * count + 7], refs[3 * count + 7]
    loads = [
        pltpu.make_async_copy(src, dst, sem.at[0, i])
        for i, (src, dst) in enumerate(zip(sources, held))
    ]
    stores = [
        pltpu.make_async_copy(src, dst, sem.at[1, i])
        for i, (src, dst) in enumerate(zip(held, targets))
    ]
    for copy in loads:
        copy.start()
    for k, out in enumerate(outs):
        out[...] = vectors[k, :]
    for k in range(3):
        stats[k] = roots[4 + k, 0]
    for load, store in zip(loads, stores):
        load.wait()
        store.start()
    for copy in stores:
        copy.wait()


def params(collective=None, limit=VMEM_LIMIT):
    if collective is None:
        return pltpu.CompilerParams(vmem_limit_bytes=limit)
    return pltpu.CompilerParams(
        vmem_limit_bytes=limit, collective_id=collective, has_side_effects=True
    )


def line_sems(chunks):
    return [DMA((chunks,)), DMA((chunks,)), DMA((2, chunks))]


def on_device(
    n, t,
    hidden_in, gain_in, w_input, w_forget, forget_bias, w_outgate, state_gain, w_output,
    gain_mid, w_gate, w_up, w_down, lengths, layer_index, cotangent,
):
    rows, width = hidden_in.shape
    chan = w_input.shape[1]
    ff = w_gate.shape[1]
    ffp = -(-ff // LANE) * LANE

    def padded(w):
        return w if ffp == ff else jnp.pad(w, ((0, 0), (0, ffp - ff)))

    plane = shape((rows, chan), F32)
    plane16 = shape((rows, chan), BF)
    column = shape((rows, 1), F32)
    wide16 = shape((rows, width), BF)
    shards16 = shape((t, rows, chan), BF)

    def groups(more=0):
        return shape((chan // LANE, rows + more, LANE), F32)

    def vm(*arrays):
        return [pltpu.VMEM(a.shape, a.dtype) for a in arrays]

    SM = pl.BlockSpec(memory_space=pltpu.SMEM)
    w1s, w2s = shape((4, width, chan), BF), shape((3, width, ffp), BF)
    zslot, vslot = pltpu.VMEM((t, 8, rows), F32), pltpu.VMEM((n, 8, chan), F32)
    small = [DMA((n,)), DMA((n,)), DMA((t,)), DMA((t,))]
    saved = [plane, plane, plane, groups(8), groups(8), plane16, wide16]

    (
        ipre, fpre, opre, feff, states, gated, normed_in, nmid, mixed, w1, w2, invst, invmid, inv_in,
        consts,
    ) = pl.pallas_call(
        functools.partial(mixer_forward, n, t, width),
        out_shape=saved + [wide16, wide16, w1s, w2s, column, column, column, shape((8, width), F32)],
        in_specs=[SM] * 2 + [HB] * 4 + [VM] + [HB] * 3 + [VM] * 4,
        out_specs=[HB] * 11 + [VM] * 4,
        scratch_shapes=[
            *vm(wide16, wide16, plane, plane, plane, groups(8), groups(8), plane16, wide16, w1s),
            *vm(groups(), plane),
            pltpu.VMEM((rows // CHUNKS * 4, width), F32),
            vslot,
            zslot,
            pltpu.VMEM((rows, width), BF),
            pltpu.VMEM((2, rows, width), BF),
            pltpu.VMEM((width // n, chan), BF),
            pltpu.VMEM((width // n, ffp), BF),
            pltpu.VMEM((ff, width // n), BF),
            DMA, DMA, DMA((7,)), DMA((4,)), DMA((CHUNKS,)), DMA((CHUNKS,)),
            *small,
            *line_sems(CHUNKS),
            *gather_sems(n, 4),
            *gather_sems(n, 3),
        ],
        compiler_params=params(1),
        name="mixer_forward",
    )(
        lengths, layer_index, hidden_in, w_input, w_forget, w_outgate, w_output,
        padded(w_gate), padded(w_up), w_down, forget_bias, state_gain, gain_mid, gain_in,
    )

    shard, chips, tile, step = width // n, n // 2, rows // TILES, rows // CHUNKS
    piece = shape((shard, ffp), F32)
    ffs = shape((rows, ffp), BF)
    gmix, gres, glu_part, ggain, sum_gate, sum_up, down = pl.pallas_call(
        functools.partial(feed_forward, n, t, width),
        out_shape=[
            wide16, plane, shards16, shape((8, width), F32), piece, piece,
            shape((width // 2, ffp), BF),
        ],
        in_specs=[HB] * 5 + [VM] * 2,
        out_specs=[HB] * 3 + [VM] + [HB] * 3,
        scratch_shapes=[
            *vm(wide16, wide16, w2s, ffs, ffs, ffs),
            pltpu.VMEM((2, t, tile, chan), BF),
            pltpu.VMEM((2, step, width), BF),
            pltpu.VMEM((2, step, width), BF),
            pltpu.VMEM((2, step, width), BF),
            pltpu.VMEM((2, step, chan), F32),
            pltpu.VMEM((step, width), F32),
            *vm(piece),
            pltpu.VMEM((2, 2, shard, ffp), BF),
            *vm(wide16),
            pltpu.VMEM((2, rows, width), BF),
            DMA((2,)), DMA((3,)), DMA((2, 2)), DMA((2, 2)), DMA((2,)), DMA((3,)), DMA((2,)),
            DMA((3 * chips,)),
            pltpu.SemaphoreType.REGULAR,
            *line_sems(CHUNKS),
            *grid_buffers(n, width, 2, ffp),
        ],
        compiler_params=params(2),
        name="feed_forward",
    )(nmid, cotangent, w2, hidden_in, mixed, invmid, consts)

    shard_sems = [DMA((t, SHARD_CHUNKS))] * 4
    shard_bufs = [pltpu.VMEM((t, rows, chan), BF), pltpu.VMEM((t + 1, rows, chan), BF)]
    gni_part, dw1, vecs, block_out, dot_in, sum_down = pl.pallas_call(
        functools.partial(mixer_backward, n, t, width),
        out_shape=[
            shards16, shape((2, width // 2, 4 * chan), BF), shape((8, chan), F32), plane16, column,
            shape((ffp, shard), F32),
        ],
        in_specs=[SM] + [HB] * 13 + [VM] * 3,
        out_specs=[HB] * 2 + [VM] * 4,
        scratch_shapes=[
            pltpu.VMEM((width // 2, ffp), BF),
            *vm(wide16, wide16),
            pltpu.VMEM((width, 4 * chan), BF),
            *vm(plane16, groups(8), groups(8), plane, plane, plane),
            *vm(groups(), groups(), plane, shape((rows, 3 * chan), BF)),
            vslot,
            zslot,
            zslot,
            pltpu.VMEM((8, width), F32),
            pltpu.VMEM((t, 8, chan), F32),
            pltpu.VMEM((t, 8, chan), F32),
            *vm(wide16, plane16),
            *shard_bufs,
            *vm(shards16),
            pltpu.VMEM((2, 2, shard, 4 * chan), BF),
            DMA((12,)),
            *small,
            DMA((t,)), DMA((t,)), DMA((t,)), DMA((t,)),
            DMA((3,)),
            *shard_sems,
            DMA((3,)), DMA((2,)), DMA,
            *grid_buffers(n, width, 1, ffp),
        ],
        compiler_params=params(3),
        name="mixer_backward",
    )(
        lengths, glu_part, hidden_in, mixed, gmix, normed_in, w1, gated, states, feff, ipre, fpre, opre,
        down, invst, inv_in, consts,
    )

    square = shape((shard, chan), F32)
    grad_in, vectors, rms, g_input, g_forget, g_outgate, g_output = pl.pallas_call(
        functools.partial(closing, n, t, width),
        out_shape=[
            plane, shape((8, width), F32), shape((8, LANE), F32),
            square, square, square, shape((chan, shard), F32),
        ],
        in_specs=[SM] + [HB] * 4 + [VM] * 5,
        out_specs=[VM] * 7,
        scratch_shapes=[
            pltpu.VMEM((2, width // 2, 2 * chan), BF),
            pltpu.VMEM((2, width // 2, 2 * chan), BF),
            *vm(plane16, plane),
            *shard_bufs,
            vslot,
            pltpu.VMEM((t, 8, chan), F32),
            DMA((2,)), DMA((2, 2)), DMA, DMA((2,)),
            *shard_sems,
            DMA((n,)), DMA((n,)), DMA((t,)), DMA((t,)),
            *grid_buffers(n, width, 2, 2 * chan),
        ],
        compiler_params=params(4),
        name="closing",
    )(lengths, gni_part, dw1, hidden_in, gres, inv_in, dot_in, consts, vecs, ggain)

    arrays = (
        block_out, grad_in, g_input, g_forget, g_outgate, g_output, sum_gate[:, :ff], sum_up[:, :ff],
        sum_down[:ff],
    )
    count = len(arrays)
    *copies, gain0, bias0, gain1, gain2, rms_stats = pl.pallas_call(
        functools.partial(emit, count),
        out_shape=[shape(a.shape, a.dtype) for a in arrays] + [shape((width,), F32)] * 4 + [shape((3,), F32)],
        in_specs=[HB] * count + [VM, SM],
        out_specs=[HB] * count + [VM] * 4 + [SM],
        scratch_shapes=[pltpu.VMEM(a.shape, a.dtype) for a in arrays] + [DMA((2, count))],
        compiler_params=params(),
        name="emit",
    )(*arrays, vectors, rms)
    out, gin, g_input, g_forget, g_outgate, g_output, g_gate, g_up, g_down = copies
    return (
        out, gin, gain0, g_input, g_forget, bias0, g_outgate, gain1, g_output, gain2,
        g_gate, g_up, g_down, rms_stats,
    )


def solution(mesh):
    weight, turned = P("seq", "tp"), P("tp", "seq")
    in_specs = (
        P("seq", None), P(), weight, weight, P(), weight, P(), turned, P(), weight, weight, turned,
        P(), P(), P("seq", None),
    )
    out_specs = (
        weight, weight, P(), weight, weight, P(), weight, P(), turned, P(), weight, weight, turned, P(),
    )
    body = functools.partial(on_device, mesh.shape["seq"], mesh.shape["tp"])
    return jax.shard_map(
        body, mesh=mesh, in_specs=in_specs, out_specs=out_specs, check_vma=False
    )
```

```python
import functools

import jax
import jax.numpy as jnp
from jax import lax
from jax.experimental import pallas as pl
from jax.experimental.pallas import tpu as pltpu
from jax.sharding import PartitionSpec as P

LAYERS = 24
EPS = 1e-06
MESH = pl.DeviceIdType.MESH
DMA = pltpu.SemaphoreType.DMA
BF = jnp.bfloat16
F32 = jnp.float32
VM = pl.BlockSpec(memory_space=pltpu.VMEM)
HB = pl.BlockSpec(memory_space=pl.ANY)
LANE = 128
SEG = 8
TILES = 4
K2_LAGS = (1, 2, 3)
CHUNKS = 16
SHARD_CHUNKS = 4
HOP_LAG = 2
VMEM_LIMIT = 60 * 1024 * 1024


def nn(left, right):
    return jnp.dot(left, right, preferred_element_type=F32)


def nt(left, right):
    return lax.dot_general(left, right, (((1,), (1,)), ((), ())), preferred_element_type=F32)


def tn(left, right):
    return lax.dot_general(left, right, (((0,), (0,)), ((), ())), preferred_element_type=F32)


def shape(dims, dtype):
    return jax.ShapeDtypeStruct(dims, dtype)


def get(ref, at):
    return jnp.concatenate([ref[g, at, :] for g in range(ref.shape[0])], axis=1)


def put(ref, at, values):
    for g in range(ref.shape[0]):
        ref[g, at, :] = values[:, g * LANE : (g + 1) * LANE]


def put_shards(ref, at, values):
    k = ref.shape[2]
    for q in range(ref.shape[0]):
        ref[q, at, :] = values[:, q * k : (q + 1) * k]


def row_tile(rows):
    return rows // 3 if rows % 48 == 0 else rows


def greet_all(n, t, seq, tp):
    barrier = pltpu.get_barrier_semaphore()

    def along_seq(o, c):
        pl.semaphore_signal(barrier, inc=1, device_id=(lax.rem(seq + o, n), tp), device_id_type=MESH)
        return c

    def along_tp(o, c):
        pl.semaphore_signal(barrier, inc=1, device_id=(seq, lax.rem(tp + o, t)), device_id_type=MESH)
        return c

    lax.fori_loop(1, n, along_seq, 0)
    lax.fori_loop(1, t, along_tp, 0)
    pl.semaphore_wait(barrier, n - 1 + t - 1)


def greet_line(t, seq, tp):
    barrier = pltpu.get_barrier_semaphore()

    def along_tp(o, c):
        pl.semaphore_signal(barrier, inc=1, device_id=(seq, lax.rem(tp + o, t)), device_id_type=MESH)
        return c

    lax.fori_loop(1, t, along_tp, 0)
    pl.semaphore_wait(barrier, t - 1)


def spread(size, me, slots, send, recv, target):
    def copy(o, slot):
        return pltpu.make_async_remote_copy(
            src_ref=slots.at[slot],
            dst_ref=slots.at[slot],
            send_sem=send.at[o],
            recv_sem=recv.at[slot],
            device_id=target(lax.rem(me + o, size)),
            device_id_type=MESH,
        )

    def one(o, c):
        copy(o, me).start()
        return c

    def arrived(o, c):
        copy(o, lax.rem(me + o, size)).wait_recv()
        return c

    def sent(o, c):
        copy(o, me).wait_send()
        return c

    def go():
        lax.fori_loop(1, size, one, 0)

    def done():
        lax.fori_loop(1, size, arrived, 0)
        lax.fori_loop(1, size, sent, 0)

    return go, done


def row_sums(values):
    ones = jnp.ones((8, values.shape[1]), BF)
    high = values.astype(BF)
    rest = values - high.astype(F32)
    low = rest.astype(BF)
    return nt(ones, high) + nt(ones, low)


def sum_over_tp(part, t, seq, tp, slots, send, recv, between=None):
    slots[tp] = part
    go, done = spread(t, tp, slots, send, recv, lambda k: (seq, k))
    go()
    if between is not None:
        between()
    done()
    total = slots[0]
    for k in range(1, t):
        total = total + slots[k]
    return jnp.transpose(total)[:, :1]


def carry_over_seq(prod, state, n, seq, tp, slots, send, recv, backward, between=None):
    slots[seq] = jnp.concatenate([prod, state] + [jnp.zeros_like(prod)] * 6, axis=0)
    go, done = spread(n, seq, slots, send, recv, lambda k: (k, tp))
    go()
    if between is not None:
        between()
    done()

    def hop(i, total):
        j = n - 1 - i if backward else i
        block = slots[j]
        longer = block[1:2] + block[0:1] * total
        inside = (j > seq) if backward else (j < seq)
        return jnp.where(inside, longer, total)

    return lax.fori_loop(0, n, hop, jnp.zeros_like(prod))


def line_all_reduce(t, seq, tp, rows, chunks, partial, send, buf, sems, finish, lags):
    s_in, s_out, r_buf = sems
    step = rows // chunks
    half = t // 2
    depth = jnp.where(tp < half, tp, t - 1 - tp)
    inner = jnp.where(tp < half, tp + 1, tp - 1)
    outer = jnp.where(tp < half, tp - 1, tp + 1)
    outer = jnp.where(depth > 0, outer, inner)
    middle = (depth == half - 1).astype(jnp.int32)
    lag_in, lag_turn, lag_out = lags
    lag_first = lag_in * depth
    lag_second = lag_in * (half - 1) + lag_turn + lag_out * (half - 1 - depth)

    def part_of(k):
        return pl.ds(pl.multiple_of(k * step, step), step)

    def inward(k, slot):
        return pltpu.make_async_remote_copy(
            src_ref=send.at[part_of(k)],
            dst_ref=buf.at[slot, part_of(k)],
            send_sem=s_in.at[k],
            recv_sem=r_buf.at[slot, k],
            device_id=(seq, inner),
            device_id_type=MESH,
        )

    def outward(k):
        return pltpu.make_async_remote_copy(
            src_ref=buf.at[1, part_of(k)],
            dst_ref=buf.at[1, part_of(k)],
            send_sem=s_out.at[k],
            recv_sem=r_buf.at[1, k],
            device_id=(seq, outer),
            device_id_type=MESH,
        )

    def first(k):
        part = None if partial is None else partial(k)

        @pl.when(depth > 0)
        def _():
            inward(k, 0).wait_recv()
            mine = send[part_of(k), :].astype(F32) if part is None else part
            send[part_of(k), :] = (mine + buf[0, part_of(k), :].astype(F32)).astype(BF)

        if part is not None:

            @pl.when(depth == 0)
            def _():
                send[part_of(k), :] = part.astype(BF)

        inward(k, middle).start()

    def second(k):
        inward(k, 1).wait_recv()

        @pl.when(middle == 1)
        def _():
            both = send[part_of(k), :].astype(F32) + buf[1, part_of(k), :].astype(F32)
            buf[1, part_of(k), :] = both.astype(BF)

        @pl.when(depth > 0)
        def _():
            outward(k).start()

        finish(k)

    def turn(i):
        @pl.when((i >= lag_first) & (i - lag_first < chunks))
        def _():
            first(i - lag_first)

        @pl.when((i >= lag_second) & (i - lag_second < chunks))
        def _():
            second(i - lag_second)

    def drain():
        def sent(k, c):
            inward(k, middle).wait_send()

            @pl.when(depth > 0)
            def _():
                outward(k).wait_send()

            return c

        lax.fori_loop(0, chunks, sent, 0)

    return chunks + lag_in * (half - 1) + lag_turn + lag_out * (half - 1), turn, drain


def line_reduce_scatter(t, seq, tp, own, inbox, sems, finish, lead):
    s_r, r_r, s_l, r_l = sems
    rows = own.shape[1]
    chunks = SHARD_CHUNKS
    step = rows // chunks
    count = chunks * (t - 1)

    def part_of(k):
        return pl.ds(pl.multiple_of(k * step, step), step)

    def rightward(q, k):
        return pltpu.make_async_remote_copy(
            src_ref=own.at[q, part_of(k)],
            dst_ref=inbox.at[q + 1, part_of(k)],
            send_sem=s_r.at[q, k],
            recv_sem=r_r.at[q, k],
            device_id=(seq, lax.rem(tp + 1, t)),
            device_id_type=MESH,
        )

    def leftward(q, k):
        return pltpu.make_async_remote_copy(
            src_ref=own.at[q, part_of(k)],
            dst_ref=inbox.at[q, part_of(k)],
            send_sem=s_l.at[q, k],
            recv_sem=r_l.at[q, k],
            device_id=(seq, lax.rem(tp + t - 1, t)),
            device_id_type=MESH,
        )

    def add(q, k, slot):
        own[q, part_of(k), :] = (
            own[q, part_of(k), :].astype(F32) + inbox[slot, part_of(k), :].astype(F32)
        ).astype(BF)

    def right_turn(i):
        j, k = i // chunks, lax.rem(i, chunks)
        q = t - 1 - j

        @pl.when((i >= 0) & (i < count) & (q > tp))
        def _():
            @pl.when(tp > 0)
            def _():
                rightward(q, k).wait_recv()
                add(q, k, q + 1)

            rightward(q, k).start()

    def left_turn(i):
        q, k = i // chunks, lax.rem(i, chunks)

        @pl.when((i >= 0) & (i < count) & (q < tp))
        def _():
            @pl.when(tp < t - 1)
            def _():
                leftward(q, k).wait_recv()
                add(q, k, q)

            leftward(q, k).start()

    def begin():
        for i in range(lead):

            @pl.when(tp == 0)
            def _(i=i):
                right_turn(i)

            @pl.when(tp == t - 1)
            def _(i=i):
                left_turn(i)

    def turn(i):
        right_turn(i - jnp.where(tp == 0, -lead, HOP_LAG * tp))
        left_turn(i - jnp.where(tp == t - 1, -lead, HOP_LAG * (t - 1 - tp)))

    def last(k):
        @pl.when(tp == 0)
        def _():
            leftward(tp, k).wait_recv()
            finish(k, own[tp, part_of(k), :].astype(F32) + inbox[tp, part_of(k), :].astype(F32))

        @pl.when(tp == t - 1)
        def _():
            rightward(tp, k).wait_recv()
            finish(k, own[tp, part_of(k), :].astype(F32) + inbox[tp + 1, part_of(k), :].astype(F32))

        @pl.when((tp > 0) & (tp < t - 1))
        def _():
            leftward(tp, k).wait_recv()
            rightward(tp, k).wait_recv()
            finish(
                k,
                own[tp, part_of(k), :].astype(F32)
                + inbox[tp, part_of(k), :].astype(F32)
                + inbox[tp + 1, part_of(k), :].astype(F32),
            )

    def drain():
        def sent(i, c):
            j, k = i // chunks, lax.rem(i, chunks)

            @pl.when(t - 1 - j > tp)
            def _():
                rightward(t - 1 - j, k).wait_send()

            @pl.when(j < tp)
            def _():
                leftward(j, k).wait_send()

            return c

        lax.fori_loop(0, count, sent, 0)

    turns = max((t - 1 - p) * chunks + (HOP_LAG * p if p else -lead) for p in range(t - 1))
    return turns, begin, turn, last, drain


def chip_grid(n):
    chips = n // 2
    b = max(k for k in range(1, chips + 1) if chips % k == 0 and k * k <= chips)
    return chips // b, b


def grid_buffers(n, width, pieces, cols):
    ga, gb = chip_grid(n)
    h = width // n // 2
    pa, pb = max(ga - 1, 1), max(gb - 1, 1)
    return [
        pltpu.VMEM((pieces, pb, ga, h, cols), BF),
        pltpu.VMEM((pieces, pa, gb, h, cols), BF),
        pltpu.VMEM((pieces, pa, h, cols), BF),
        pltpu.VMEM((pieces, pb, h, cols), BF),
        DMA((2, pieces, pb, ga)), DMA((2, pieces, pa, gb)), DMA((2, pieces, pa)), DMA((2, pieces, pb)),
    ]


def add_cores(acc, first):
    part = 64

    def one(i, c):
        at = pl.ds(pl.multiple_of(i * part, part), part)
        acc[at, :] = (acc[at, :].astype(F32) + first[at, :].astype(F32)).astype(BF)
        return c

    lax.fori_loop(0, acc.shape[0] // part, one, 0)


def grid_reduce(n, seq, tp, j, acc, bufs, out):
    far_b, far_a, near_a, near_b, m_fb, m_fa, m_na, m_nb = bufs
    ga, gb = chip_grid(n)
    core = lax.rem(seq, 2)
    a, b = seq // 2 // gb, lax.rem(seq // 2, gb)
    h = near_a.shape[2]

    def device(a_, b_):
        return ((a_ * gb + b_) * 2 + core, tp)

    def block(half, x, y):
        return pl.ds(pl.multiple_of(((x * gb + y) * 2 + half) * h, h), h)

    def remote(rows, dst, sems, index, target):
        return pltpu.make_async_remote_copy(
            src_ref=acc.at[rows],
            dst_ref=dst,
            send_sem=sems.at[(0, j) + index],
            recv_sem=sems.at[(1, j) + index],
            device_id=target,
            device_id_type=MESH,
        )

    def first_way():
        copies = []
        for o in range(1, gb):
            to = lax.rem(b + o, gb)
            for x in range(ga):
                dst = far_b.at[j, o - 1, x]
                copies.append(remote(block(0, x, to), dst, m_fb, (o - 1, x), device(a, to)))
        for o in range(1, ga):
            to = lax.rem(a + o, ga)
            for y in range(gb):
                dst = far_a.at[j, o - 1, y]
                copies.append(remote(block(1, to, y), dst, m_fa, (o - 1, y), device(to, b)))
        return copies

    def second_way():
        copies = []
        for o in range(1, ga):
            to = lax.rem(a + o, ga)
            copies.append(
                remote(block(0, to, b), near_a.at[j, o - 1], m_na, (o - 1,), device(to, b))
            )
        for o in range(1, gb):
            to = lax.rem(b + o, gb)
            copies.append(
                remote(block(1, a, to), near_b.at[j, o - 1], m_nb, (o - 1,), device(a, to))
            )
        return copies

    def far():
        for copy in first_way():
            copy.start()

    def middle():
        for copy in first_way():
            copy.wait_recv()

        def along_a(x, c):
            total = acc[block(0, x, b), :].astype(F32)
            for o in range(1, gb):
                total = total + far_b[j, o - 1, x].astype(F32)
            acc[block(0, x, b), :] = total.astype(BF)
            return c

        def along_b(y, c):
            total = acc[block(1, a, y), :].astype(F32)
            for o in range(1, ga):
                total = total + far_a[j, o - 1, y].astype(F32)
            acc[block(1, a, y), :] = total.astype(BF)
            return c

        lax.fori_loop(0, ga, along_a, 0)
        lax.fori_loop(0, gb, along_b, 0)
        for copy in second_way():
            copy.start()

    def near():
        for copy in second_way():
            copy.wait_recv()
        total = acc[block(0, a, b), :].astype(F32)
        for o in range(1, ga):
            total = total + near_a[j, o - 1].astype(F32)
        out(0, total)
        total = acc[block(1, a, b), :].astype(F32)
        for o in range(1, gb):
            total = total + near_b[j, o - 1].astype(F32)
        out(1, total)

    def drain():
        for copy in first_way() + second_way():
            copy.wait_send()

    return far, middle, near, drain


def gather_sems(n, pieces):
    ga, gb = chip_grid(n)
    pa, pb = max(ga - 1, 1), max(gb - 1, 1)
    return [
        DMA((pieces,)), DMA((2, pieces, ga * gb)),
        DMA((2, pieces, pb)), DMA((2, pieces, pa)), DMA((2, pieces, gb, pa)), DMA((2, pieces, ga, pb)),
    ]


def grid_gather(n, seq, tp, j, src, dst, sems):
    s_local, m_core, m_fb, m_fa, m_na, m_nb = sems
    ga, gb = chip_grid(n)
    shard = src.shape[0]
    h = shard // 2
    core = lax.rem(seq, 2)
    a, b = seq // 2 // gb, lax.rem(seq // 2, gb)

    def device(a_, b_, core_):
        return ((a_ * gb + b_) * 2 + core_, tp)

    def block(x, y, core_, half, count):
        return pl.ds(pl.multiple_of(((x * gb + y) * 2 + core_) * shard + half * h, h), count)

    def remote(from_, rows, sem, index, target):
        return pltpu.make_async_remote_copy(
            src_ref=from_,
            dst_ref=dst.at[rows],
            send_sem=sem.at[(0, j) + index],
            recv_sem=sem.at[(1, j) + index],
            device_id=target,
            device_id_type=MESH,
        )

    def own(half):
        return src.at[pl.ds(half * h, h)]

    def far(incoming):
        copies = []
        for o in range(1, gb):
            to, of = lax.rem(b + o, gb), lax.rem(b + gb - o, gb)
            rows = block(a, of if incoming else b, core, 0, h)
            copies.append(remote(own(0), rows, m_fb, (o - 1,), device(a, to, core)))
        for o in range(1, ga):
            to, of = lax.rem(a + o, ga), lax.rem(a + ga - o, ga)
            rows = block(of if incoming else a, b, core, 1, h)
            copies.append(remote(own(1), rows, m_fa, (o - 1,), device(to, b, core)))
        return copies

    def near(incoming, first, least):
        copies = []
        for i in range(0 if first else 1, gb if least else 1):
            y = lax.rem(b + gb - i, gb)
            for o in range(1, ga):
                to, of = lax.rem(a + o, ga), lax.rem(a + ga - o, ga)
                rows = block(of if incoming else a, y, core, 0, h)
                from_ = own(0) if i == 0 or incoming else dst.at[rows]
                copies.append(remote(from_, rows, m_na, (i, o - 1), device(to, b, core)))
        for i in range(0 if first else 1, ga if least else 1):
            x = lax.rem(a + ga - i, ga)
            for o in range(1, gb):
                to, of = lax.rem(b + o, gb), lax.rem(b + gb - o, gb)
                rows = block(x, of if incoming else b, core, 1, h)
                from_ = own(1) if i == 0 or incoming else dst.at[rows]
                copies.append(remote(from_, rows, m_nb, (i, o - 1), device(a, to, core)))
        return copies

    def across(incoming, first, others):
        copies = []
        for i in range(ga):
            for k in range(gb):
                mine = i == 0 and k == 0
                if (mine and not first) or (not mine and not others):
                    continue
                x, y = lax.rem(a + i, ga), lax.rem(b + k, gb)
                rows = block(x, y, 1 - core if incoming else core, 0, shard)
                from_ = src if mine or incoming else dst.at[rows]
                copies.append(remote(from_, rows, m_core, (i * gb + k,), device(a, b, 1 - core)))
        return copies

    def local():
        return pltpu.make_async_copy(src, dst.at[block(a, b, core, 0, shard)], s_local.at[j])

    def start():
        for copy in far(False) + near(False, True, False) + across(False, True, False):
            copy.start()
        local().start()

    def relay():
        for copy in far(True):
            copy.wait_recv()
        for copy in near(False, False, True):
            copy.start()

    def share():
        for copy in near(True, True, True):
            copy.wait_recv()
        for copy in across(False, False, True):
            copy.start()

    def arrive():
        for copy in across(True, True, True):
            copy.wait_recv()
        local().wait()

    def drain():
        for copy in far(False) + near(False, True, True) + across(False, True, True):
            copy.wait_send()

    return start, relay, share, arrive, drain


def loop_with(first, last, body, works):
    def one(i, c):
        body(i)
        for when, work in works:

            @pl.when(i == when)
            def _(work=work):
                work()

        return c

    lax.fori_loop(first, last, one, 0)


def masks(lens, first, count):
    at = first + lax.broadcasted_iota(jnp.int32, (count, 1), 0)
    valid = (at < lens[0] + lens[1]).astype(F32)
    starts = ((at == 0) | (at == lens[0])).astype(F32)
    return valid, starts


def mixer_forward(
    n, t, width,
    lens, layer, x_h, wi_h, wf_h, wo_h, wx_raw, wg_h, wu_h, wd_raw_h, bias_v, sgain_v, gmid_v, gin_v,
    ipre_h, fpre_h, opre_h, feff_h, states_h, gated_h, normed_h, nmid_h, mixed_h, w1_h, w2_h,
    invst, invmid, invin, consts,
    x, normed, ipre, fpre, opre, feff, states, gated, nmid, w1, prod, ssq, part, cslots, zslots, send, buf,
    wx, wd, wd_raw, s_t, s_x, s_st, s_w, s_n, s_m, cs, cr, zs, zr, s_in, s_out, r_buf, *sems,
):
    seq, tp = lax.axis_index("seq"), lax.axis_index("tp")
    load = pltpu.make_async_copy(x_h, x, s_x)
    load.start()
    load_down = pltpu.make_async_copy(wd_raw_h, wd_raw, s_t)
    load_down.start()
    sems1, sems2 = sems[:6], sems[6:]
    one = [
        grid_gather(n, seq, tp, j, src, w1.at[j], sems1)
        for j, src in enumerate((wi_h, wf_h, wo_h, wx))
    ]
    two = [
        grid_gather(n, seq, tp, j, src, w2_h.at[j], sems2)
        for j, src in enumerate((wg_h, wu_h, wd))
    ]
    START, RELAY, SHARE, ARRIVE, DRAIN = range(5)
    greet_all(n, t, seq, tp)
    one[0][START]()
    rows, depth = normed.shape
    chan = ipre.shape[1]
    tile = row_tile(rows)
    mine = pl.ds(pl.multiple_of(tp * chan, LANE), chan)
    consts[...] = jnp.zeros_like(consts)
    for k, vector in ((0, bias_v), (1, sgain_v), (3, gmid_v), (4, gin_v)):
        consts[k : k + 1, :] = vector[...].astype(F32).reshape(1, width)
    consts[2:3, :] = jnp.full((1, width), layer[0].astype(F32) / LAYERS)
    bias, sgain, bound = consts[0:1, mine], consts[1:2, mine], consts[2:3, mine]

    def stores():
        pairs = (
            (ipre, ipre_h), (fpre, fpre_h), (opre, opre_h), (feff, feff_h), (states, states_h),
            (gated, gated_h), (normed, normed_h),
        )
        return [pltpu.make_async_copy(v, o, s_st.at[i]) for i, (v, o) in enumerate(pairs)]

    def keep(j):
        return pltpu.make_async_copy(w1.at[j], w1_h.at[j], s_w.at[j])

    wx[...] = jnp.transpose(wx_raw[...])
    load.wait()

    def norm(i, c):
        at = pl.ds(pl.multiple_of(i * tile, tile), tile)
        v = x[at, :].astype(F32)
        inv = lax.rsqrt(jnp.mean(v * v, axis=-1, keepdims=True) + EPS)
        invin[at, :] = inv
        normed[at, :] = (v * inv * consts[4:5, :]).astype(BF)
        return c

    lax.fori_loop(0, rows // tile, norm, 0)
    one[0][RELAY]()
    one[1][START]()
    load_down.wait()
    turned = jnp.transpose(wd_raw[...])
    wd[:, : turned.shape[1]] = turned
    if turned.shape[1] < wd.shape[1]:
        wd[:, turned.shape[1] :] = jnp.zeros((wd.shape[0], wd.shape[1] - turned.shape[1]), BF)
    one[0][SHARE]()
    one[1][RELAY]()
    one[2][START]()
    one[0][ARRIVE]()
    keep(0).start()

    def first(i, c):
        at = pl.ds(pl.multiple_of(i * tile, tile), tile)
        ipre[at, :] = nn(normed[at, :], w1[0])
        return c

    lax.fori_loop(0, rows // tile, first, 0)
    one[1][SHARE]()
    one[2][RELAY]()
    one[3][START]()
    one[1][ARRIVE]()
    keep(1).start()

    def second(i, c):
        at = pl.ds(pl.multiple_of(i * tile, tile), tile)
        f = nn(normed[at, :], w1[1]) + bias
        fpre[at, :] = f
        valid, starts = masks(lens, seq * rows + i * tile, tile)
        gate = bound + (1.0 - bound) * jax.nn.sigmoid(f)
        put(feff, at, gate * (1.0 - starts))
        shifted = pl.ds(pl.multiple_of(i * tile + 8, 8), tile)
        v = ipre[at, :]
        put(states, shifted, v * jax.nn.sigmoid(v) * (1.0 - gate) * valid)
        return c

    lax.fori_loop(0, rows // tile, second, 0)
    put(feff, slice(rows, rows + 8), jnp.ones((8, chan), F32))

    length = rows // SEG

    def scan(i, c):
        p, h = c
        at, shifted = pl.ds(i, SEG, stride=length), pl.ds(i + 8, SEG, stride=length)
        f = get(feff, at)
        h = f * h + get(states, shifted)
        p = f * p
        put(states, shifted, h)
        put(prod, at, p)
        return p, h

    p, h = lax.fori_loop(
        0, length, scan, (jnp.ones((SEG, chan), F32), jnp.zeros((SEG, chan), F32))
    )
    block_p, block_h = p[0:1], h[0:1]
    for s in range(1, SEG):
        block_h = h[s : s + 1] + p[s : s + 1] * block_h
        block_p = p[s : s + 1] * block_p

    def travel():
        one[2][SHARE]()
        one[3][RELAY]()
        two[0][START]()

    arriving = carry_over_seq(block_p, block_h, n, seq, tp, cslots, cs, cr, False, travel)
    put(states, slice(0, 8), jnp.broadcast_to(arriving, (8, chan)))
    for s in range(SEG):
        at = slice(s * length, (s + 1) * length)
        shifted = slice(s * length + 8, (s + 1) * length + 8)
        whole = get(states, shifted) + get(prod, at) * arriving
        put(states, shifted, whole)
        ssq[at, :] = whole * whole
        arriving = h[s : s + 1] + p[s : s + 1] * arriving

    def outgate():
        one[3][SHARE]()
        one[2][ARRIVE]()
        keep(2).start()

        def third(i, c):
            at = pl.ds(pl.multiple_of(i * tile, tile), tile)
            opre[at, :] = nn(normed[at, :], w1[2])
            return c

        lax.fori_loop(0, rows // tile, third, 0)

    total = sum_over_tp(row_sums(ssq[...]), t, seq, tp, zslots, zs, zr, outgate)
    invst[...] = lax.rsqrt(total / width + EPS)

    def gating(i, c):
        at = pl.ds(pl.multiple_of(i * tile, tile), tile)
        shifted = pl.ds(pl.multiple_of(i * tile + 8, 8), tile)
        o = opre[at, :]
        gated[at, :] = (
            get(states, shifted) * invst[at, :] * sgain * (o * jax.nn.sigmoid(o))
        ).astype(BF)
        return c

    lax.fori_loop(0, rows // tile, gating, 0)
    one[3][ARRIVE]()
    keep(3).start()
    for copy in stores():
        copy.start()

    step = rows // CHUNKS
    group = part.shape[0] // step

    def partial(k):
        @pl.when(lax.rem(k, group) == 0)
        def _():
            big = pl.ds(pl.multiple_of(k * step, step), step * group)
            part[...] = nt(gated[big, :], w1[3])

        return part[pl.ds(pl.multiple_of(lax.rem(k, group) * step, step), step), :]

    def store_n(k):
        at = pl.ds(pl.multiple_of(k * step, step), step)
        return pltpu.make_async_copy(nmid.at[at], nmid_h.at[at], s_n.at[k])

    def store_m(k):
        at = pl.ds(pl.multiple_of(k * step, step), step)
        return pltpu.make_async_copy(buf.at[1, at], mixed_h.at[at], s_m.at[k])

    def finish(k):
        at = pl.ds(pl.multiple_of(k * step, step), step)
        store_m(k).start()
        resid = x[at, :].astype(F32) + buf[1, at, :].astype(F32)
        inv = lax.rsqrt(jnp.mean(resid * resid, axis=-1, keepdims=True) + EPS)
        invmid[at, :] = inv
        nmid[at, :] = (resid * inv * consts[3:4, :]).astype(BF)
        store_n(k).start()

    turns = [
        (2, lambda: (two[0][RELAY](), two[1][START]())),
        (4, lambda: two[0][SHARE]()),
        (7, lambda: (two[1][RELAY](), two[2][START]())),
        (9, lambda: two[1][SHARE]()),
        (13, lambda: two[2][RELAY]()),
        (16, lambda: two[2][SHARE]()),
    ]

    count, turn, drain = line_all_reduce(
        t, seq, tp, rows, CHUNKS, partial, send, buf, (s_in, s_out, r_buf), finish, (0, 1, 4)
    )
    loop_with(0, count, turn, turns)
    drain()
    for g in two:
        g[ARRIVE]()
    for g in one + two:
        g[DRAIN]()
    for copy in stores():
        copy.wait()
    for j in range(4):
        keep(j).wait()

    def stored(k, c):
        store_n(k).wait()
        store_m(k).wait()
        return c

    lax.fori_loop(0, CHUNKS, stored, 0)


def feed_forward(
    n, t, width,
    nmid_h, cot_h, w2_h, x_h, mixed_h, invmid, consts,
    gmix_h, gres_h, glu_h, ggain, gate_h, up_h, down_h,
    nmid, cot, pool, hid, gg, gu, glu, xs, ms, gmix, gres, wide, sums, stage, send, buf,
    s_a, s_w, s_x, s_o, s_g, s_s, s_d, m_core, ready, s_in, s_out, r_buf, *bufs,
):
    seq, tp = lax.axis_index("seq"), lax.axis_index("tp")
    core = lax.rem(seq, 2)
    sibling = (seq + 1 - 2 * core, tp)
    act_copies = [
        pltpu.make_async_copy(nmid_h, nmid, s_a.at[0]),
        pltpu.make_async_copy(cot_h, cot, s_a.at[1]),
    ]
    w_copies = [pltpu.make_async_copy(w2_h.at[j], pool.at[j], s_w.at[j]) for j in range(3)]
    w_copies[0].start()
    act_copies[0].start()
    greet_all(n, t, seq, tp)
    for copy in (w_copies[1], act_copies[1], w_copies[2]):
        copy.start()
    rows, chan = nmid.shape[0], gres.shape[2]
    step = rows // CHUNKS
    tile = rows // TILES
    ggain[...] = jnp.zeros_like(ggain)

    def fetch(k):
        at, slot = pl.ds(pl.multiple_of(k * step, step), step), lax.rem(k, 2)
        return (
            pltpu.make_async_copy(x_h.at[at], xs.at[slot], s_x.at[0, slot]),
            pltpu.make_async_copy(mixed_h.at[at], ms.at[slot], s_x.at[1, slot]),
        )

    def stored(k):
        at, slot = pl.ds(pl.multiple_of(k * step, step), step), lax.rem(k, 2)
        return (
            pltpu.make_async_copy(gmix.at[slot], gmix_h.at[at], s_o.at[0, slot]),
            pltpu.make_async_copy(gres.at[slot], gres_h.at[at], s_o.at[1, slot]),
        )

    for copy in fetch(0):
        copy.start()

    def finish(k):
        for copy in fetch(k):
            copy.wait()

        @pl.when(k + 1 < CHUNKS)
        def _():
            for copy in fetch(k + 1):
                copy.start()

        @pl.when(k >= 2)
        def _():
            for copy in stored(k - 2):
                copy.wait()

        at, slot = pl.ds(pl.multiple_of(k * step, step), step), lax.rem(k, 2)
        g = buf[1, at, :].astype(F32)
        inv = invmid[at, :]
        hat = (xs[slot].astype(F32) + ms[slot].astype(F32)) * inv
        ggain[0:1, :] += jnp.sum(g * hat, axis=0, keepdims=True)
        e = g * consts[3:4, :]
        mean = jnp.mean(e * hat, axis=-1, keepdims=True)
        result = cot[at, :].astype(F32) + inv * (e - hat * mean)
        wide[...] = result
        gmix[slot] = result.astype(BF)
        gres[slot] = wide[:, pl.ds(pl.multiple_of(tp * chan, LANE), chan)]
        for copy in stored(k):
            copy.start()

    count, turn, drain = line_all_reduce(
        t, seq, tp, rows, CHUNKS, None, send, buf, (s_in, s_out, r_buf), finish, K2_LAGS
    )

    act_copies[0].wait()
    w_copies[0].wait()

    def block(i, c):
        at = pl.ds(pl.multiple_of(i * tile, tile), tile)
        g = nn(nmid[at, :], pool[0])

        @pl.when(i == 0)
        def _():
            w_copies[1].wait()
            act_copies[1].wait()
            w_copies[2].wait()

        u = nn(nmid[at, :], pool[1])
        gh = nn(cot[at, :], pool[2])
        sig = jax.nn.sigmoid(g)
        act = g * sig
        hid[at, :] = (act * u).astype(BF)
        gg[at, :] = (gh * u * (sig * (1.0 + g * (1.0 - sig)))).astype(BF)
        gu[at, :] = (gh * act).astype(BF)

        @pl.when(i > 0)
        def _():
            turn(2 * i - 1)

        send[at, :] = (nt(gg[at, :], pool[0]) + nt(gu[at, :], pool[1])).astype(BF)
        turn(2 * i)
        return c

    lax.fori_loop(0, TILES, block, 0)
    done = 2 * TILES - 1

    ga, gb = chip_grid(n)
    chips = ga * gb
    shard = width // n
    half_pool = pl.ds(0, width // 2)
    other_half = pl.ds(width // 2, width // 2)

    def give(i):
        j, r = i // chips, lax.rem(i, chips)
        return pltpu.make_async_remote_copy(
            src_ref=stage.at[lax.rem(i, 2), 1 - core],
            dst_ref=pool.at[j, pl.ds(pl.multiple_of(width // 2 + r * shard, shard), shard)],
            send_sem=s_g.at[lax.rem(i, 2)],
            recv_sem=m_core.at[i],
            device_id=sibling,
            device_id_type=MESH,
        )

    def gradient(j, left, right, first_turn, turns):
        pl.semaphore_signal(ready, inc=1, device_id=sibling, device_id_type=MESH)
        pl.semaphore_wait(ready, 1)

        def slab(r, c):
            i = j * chips + r
            slot = lax.rem(i, 2)

            @pl.when(i >= 2)
            def _():
                give(i - 2).wait_send()

            at = pl.ds(pl.multiple_of(r * 2 * shard, 2 * shard), 2 * shard)
            values = tn(left[:, at], right[...]).astype(BF)
            for k in range(2):
                stage[slot, k] = values[k * shard : (k + 1) * shard]
            give(i).start()
            pool[j, pl.ds(pl.multiple_of(r * shard, shard), shard), :] = stage[slot, core]
            loop_with(first_turn + r * turns // chips, first_turn + (r + 1) * turns // chips, turn, ())
            return c

        lax.fori_loop(0, chips, slab, 0)

    def cores(j):
        def arrived(r, c):
            give(j * chips + r).wait_recv()
            return c

        lax.fori_loop(0, chips, arrived, 0)
        add_cores(pool.at[j, half_pool], pool.at[j, other_half])

    def summed(j):
        return pltpu.make_async_copy(sums, (gate_h, up_h)[j], s_s.at[j])

    def out(half, values):
        sums[half * (shard // 2) : (half + 1) * (shard // 2), :] = values

    reduces = [
        grid_reduce(n, seq, tp, j, pool.at[j, half_pool], bufs, out) for j in range(2)
    ]
    gradient(0, nmid, gg, done, 2)
    cores(0)
    reduces[0][0]()
    gradient(1, nmid, gu, done + 2, 2)
    cores(1)
    reduces[1][0]()

    def glu_copy(i):
        at, slot = pl.ds(pl.multiple_of(i * tile, tile), tile), lax.rem(i, 2)
        return pltpu.make_async_copy(glu.at[slot], glu_h.at[:, at], s_d.at[slot])

    def forward(i, c):
        @pl.when(i >= 2)
        def _():
            glu_copy(i - 2).wait()

        at, slot = pl.ds(pl.multiple_of(i * tile, tile), tile), lax.rem(i, 2)
        values = nt(hid[at, :], pool[2]).astype(BF)
        for q in range(t):
            glu[slot, q] = values[:, q * chan : (q + 1) * chan]
        glu_copy(i).start()

        @pl.when(lax.rem(i, 2) == 1)
        def _():
            turn(done + 4 + i // 2)

        return c

    lax.fori_loop(0, TILES, forward, 0)
    glu_copy(TILES - 2).wait()
    glu_copy(TILES - 1).wait()
    reduces[0][1]()
    gradient(2, cot, hid, done + 4 + TILES // 2, 2)
    cores(2)
    down = pltpu.make_async_copy(pool.at[2, half_pool], down_h, s_s.at[2])
    down.start()

    def second_sum():
        summed(0).wait()
        reduces[1][2]()
        summed(1).start()

    now = done + 6 + TILES // 2
    loop_with(
        now,
        count,
        turn,
        (
            (now + 1, lambda: (reduces[0][2](), summed(0).start())),
            (now + 2, lambda: reduces[1][1]()),
            (now + 5, second_sum),
        ),
    )
    drain()
    for r in reduces:
        r[3]()
    give(3 * chips - 2).wait_send()
    give(3 * chips - 1).wait_send()
    summed(1).wait()
    down.wait()
    for k in (CHUNKS - 2, CHUNKS - 1):
        for copy in stored(k):
            copy.wait()


def mixer_backward(
    n, t, width,
    lens, glu_h, x_h, mixed_h, gmix_h, normed_h, w1_h, gated_h, states_h, feff_h, ipre_h, fpre_h, opre_h,
    down_h, invst, invin, consts,
    gni_h, dw1_h, vecs, out, dot_in, sums,
    acc, gmix, normed, w1, gated, states, feff, ipre, fpre, opre,
    weighted, prod, inner, out3, cslots, zslots, zslots2, gain_sum, gsend, gtake, x, mc, own, inbox, gni, stage,
    s_f, cs, cr, zs, zr, zs2, zr2, gs_, gr_, s_x, sr, rr, sl, rl, s_o, s_d, s_acc, *bufs,
):
    seq, tp = lax.axis_index("seq"), lax.axis_index("tp")
    down = pltpu.make_async_copy(down_h, acc, s_acc)
    down.start()
    rows = gmix.shape[0]
    chan = ipre.shape[1]
    mine = pl.ds(pl.multiple_of(tp * chan, LANE), chan)
    fetches = [
        pltpu.make_async_copy(glu_h, own, s_x.at[0]),
        pltpu.make_async_copy(x_h, x, s_x.at[1]),
        pltpu.make_async_copy(mixed_h.at[:, mine], mc, s_x.at[2]),
    ]
    pairs = [
        (gmix_h, gmix),
        (w1_h.at[3], w1.at[:, pl.ds(3 * chan, chan)]),
        (states_h, states), (opre_h, opre), (feff_h, feff), (ipre_h, ipre), (fpre_h, fpre),
    ] + [(w1_h.at[j], w1.at[:, pl.ds(j * chan, chan)]) for j in range(3)] + [
        (normed_h, normed), (gated_h, gated),
    ]
    inputs = [pltpu.make_async_copy(src, dst, s_f.at[i]) for i, (src, dst) in enumerate(pairs)]
    fetches[0].start()
    for copy in inputs[:4]:
        copy.start()
    greet_all(n, t, seq, tp)
    for copy in inputs[4:] + fetches[1:]:
        copy.start()

    def down_out(half, values):
        size = sums.shape[1] // 2
        sums[:, half * size : (half + 1) * size] = jnp.transpose(values)

    far, middle, near, drain_grid = grid_reduce(n, seq, tp, 0, acc, bufs, down_out)
    tile = row_tile(rows)
    sgain, bound = consts[1:2, mine], consts[2:3, mine]
    vecs[...] = jnp.zeros_like(vecs)
    step = rows // SHARD_CHUNKS

    def finish(k, values):
        at = pl.ds(pl.multiple_of(k * step, step), step)
        ok, _ = masks(lens, seq * rows + k * step, step)
        m = mc[at, :].astype(F32)
        full = x[at, mine].astype(F32) + m + values
        out[at, :] = full.astype(BF)
        vecs[4:5, :] += jnp.sum(ok * m * m, axis=0, keepdims=True)
        vecs[5:6, :] += jnp.sum(ok * values * values, axis=0, keepdims=True)
        vecs[6:7, :] += jnp.sum(ok * full * full, axis=0, keepdims=True)

    turns, begin, turn, last, drain = line_reduce_scatter(
        t, seq, tp, own, inbox, (sr, rr, sl, rl), finish, 0
    )
    slots = 12

    def pump(slot):
        def one(i, c):
            turn(i)
            return c

        lax.fori_loop(slot * turns // slots, (slot + 1) * turns // slots, one, 0)

    fetches[0].wait()
    pump(0)
    down.wait()
    far()
    for copy in inputs[:4]:
        copy.wait()

    def gates(i, c):
        @pl.when(i == 1)
        def _():
            pump(1)

        at = pl.ds(pl.multiple_of(i * tile, tile), tile)
        shifted = pl.ds(pl.multiple_of(i * tile + 8, 8), tile)
        g = nn(gmix[at, :], w1[:, 3 * chan :])
        hat = get(states, shifted) * invst[at, :]
        o = opre[at, :]
        sig = jax.nn.sigmoid(o)
        q = o * sig
        vecs[2:3, :] += jnp.sum(g * hat * q, axis=0, keepdims=True)
        out3[at, 2 * chan :] = (g * hat * sgain * (sig * (1.0 + o * (1.0 - sig)))).astype(BF)
        w = g * q * sgain
        put(weighted, at, w)
        inner[at, :] = w * hat
        return c

    lax.fori_loop(0, 3, gates, 0)
    dot = sum_over_tp(row_sums(inner[...]), t, seq, tp, zslots, zs, zr, lambda: (pump(2), pump(3))) / width
    inner[:, 0:1] = dot

    def leaving(i, c):
        at = pl.ds(pl.multiple_of(i * tile, tile), tile)
        shifted = pl.ds(pl.multiple_of(i * tile + 8, 8), tile)
        inv = invst[at, :]
        put(weighted, at, inv * (get(weighted, at) - get(states, shifted) * inv * inner[at, 0:1]))
        return c

    lax.fori_loop(0, 3, leaving, 0)
    inputs[4].wait()
    pump(4)

    length = rows // SEG

    def scan(i, c):
        p, h = c
        r = length - 1 - i
        at = pl.ds(r, SEG, stride=length)
        f = get(feff, pl.ds(r + 1, SEG, stride=length))
        h = f * h + get(weighted, at)
        p = f * p
        put(weighted, at, h)
        put(prod, at, p)
        return p, h

    p, h = lax.fori_loop(
        0, length, scan, (jnp.ones((SEG, chan), F32), jnp.zeros((SEG, chan), F32))
    )
    block_p, block_h = p[SEG - 1 : SEG], h[SEG - 1 : SEG]
    for s in range(SEG - 2, -1, -1):
        block_h = h[s : s + 1] + p[s : s + 1] * block_h
        block_p = p[s : s + 1] * block_p
    first = get(feff, slice(0, 1))
    arriving = carry_over_seq(
        first * block_p, first * block_h, n, seq, tp, cslots, cs, cr, True, lambda: (pump(5), pump(6))
    )
    inputs[5].wait()
    inputs[6].wait()
    middle()
    bias_sum = jnp.zeros((1, chan), F32)
    for s in range(SEG - 1, -1, -1):
        if s in (5, 1):
            pump(8 - s // 5)
        at = slice(s * length, (s + 1) * length)
        gs = get(weighted, at) + get(prod, at) * arriving
        arriving = h[s : s + 1] + p[s : s + 1] * arriving
        a = ipre[at, :]
        sa = jax.nn.sigmoid(a)
        act = a * sa
        sf = jax.nn.sigmoid(fpre[at, :])
        gate = bound + (1.0 - bound) * sf
        ok, starts = masks(lens, seq * rows + s * length, length)
        out3[at, :chan] = (gs * (1.0 - gate) * ok * (sa * (1.0 + a * (1.0 - sa)))).astype(BF)
        before = get(states, slice(s * length + 7, (s + 1) * length + 7))
        gate_grad = gs * before * (1.0 - starts) - gs * act * ok
        gf = (gate_grad * (1.0 - bound) * sf * (1.0 - sf)).astype(BF)
        out3[at, chan : 2 * chan] = gf
        bias_sum = bias_sum + jnp.sum(gf.astype(F32), axis=0, keepdims=True)
    vecs[1:2, :] = bias_sum

    def gni_copy(i):
        at = pl.ds(pl.multiple_of(i * tile, tile), tile)
        return pltpu.make_async_copy(gni.at[:, at], gni_h.at[:, at], s_o.at[i])

    for copy in inputs[7:] + fetches[1:]:
        copy.wait()
    gain_sum[...] = jnp.zeros_like(gain_sum)

    def spread_in(i, c):
        at = pl.ds(pl.multiple_of(i * tile, tile), tile)
        values = nt(out3[at, :], w1[:, : 3 * chan])
        put_shards(gni, at, values.astype(BF))
        gni_copy(i).start()
        product = values * (x[at, :].astype(F32) * invin[at, :])
        gain_sum[0:1, :] += jnp.sum(product, axis=0, keepdims=True)
        product = product * consts[4:5, :]
        short = product[:, :LANE]
        for k in range(LANE, width, LANE):
            short = short + product[:, k : k + LANE]
        inner[at, :LANE] = short
        pump(9 + i)
        return c

    lax.fori_loop(0, 3, spread_in, 0)

    zslots2[tp] = row_sums(inner[:, :LANE])
    go_z, done_z = spread(t, tp, zslots2, zs2, zr2, lambda k: (seq, k))
    go_z()
    gsend[...] = jnp.zeros_like(gsend)
    for q in range(t):
        gsend[q, 0:1, :] = gain_sum[0:1, q * chan : (q + 1) * chan]

    def gain_copy(o, slot):
        to = lax.rem(tp + o, t)
        return pltpu.make_async_remote_copy(
            src_ref=gsend.at[to],
            dst_ref=gtake.at[slot],
            send_sem=gs_.at[o],
            recv_sem=gr_.at[slot],
            device_id=(seq, to),
            device_id_type=MESH,
        )

    def gain_go(o, c):
        gain_copy(o, tp).start()
        return c

    def gain_done(o, c):
        gain_copy(o, lax.rem(tp + o, t)).wait_recv()
        return c

    def gain_sent(o, c):
        gain_copy(o, tp).wait_send()
        return c

    lax.fori_loop(1, t, gain_go, 0)
    gtake[tp] = gsend[tp]
    near()
    shard = width // n
    chips = n // 2

    def d_copy(r, slot):
        at = pl.ds(pl.multiple_of(r * shard, shard), shard)
        return pltpu.make_async_copy(stage.at[slot], dw1_h.at[:, at], s_d.at[slot])

    def keep(slot, first, values):
        for k in range(2):
            stage[slot, k, :, first : first + values.shape[1]] = values[k * shard : (k + 1) * shard]

    def slab(r, c):
        slot = lax.rem(r, 2)

        @pl.when(r >= 2)
        def _():
            d_copy(r - 2, slot).wait()

        at = pl.ds(pl.multiple_of(r * 2 * shard, 2 * shard), 2 * shard)
        keep(slot, 0, tn(normed[:, at], out3[...]).astype(BF))
        keep(slot, 3 * chan, tn(gmix[:, at], gated[...]).astype(BF))
        d_copy(r, slot).start()
        return c

    lax.fori_loop(0, chips, slab, 0)

    done_z()
    total = zslots2[0]
    for k in range(1, t):
        total = total + zslots2[k]
    dot_in[...] = jnp.transpose(total)[:, :1] / width
    lax.fori_loop(1, t, gain_done, 0)
    lax.fori_loop(1, t, gain_sent, 0)
    gains = gtake[0]
    for k in range(1, t):
        gains = gains + gtake[k]
    vecs[0:1, :] = gains[0:1]

    def ending(k, c):
        last(k)
        return c

    lax.fori_loop(0, SHARD_CHUNKS, ending, 0)
    for r in range(max(chips - 2, 0), chips):
        d_copy(r, r % 2).wait()

    def stored(i, c):
        gni_copy(i).wait()
        return c

    lax.fori_loop(0, 3, stored, 0)
    drain()
    drain_grid()


def closing(
    n, t, width,
    lens, gni_h, dw1_h, x_h, gres_h, invin, dot_in, consts, vecs, ggain,
    gin, vectors, rms, g_input, g_forget, g_outgate, g_output,
    acc, other, xc, gres, own, inbox, vslots, allvec,
    s_acc, m_core, s_own, s_x, sr, rr, sl, rl, vs, vr, ts, tr, *bufs,
):
    seq, tp = lax.axis_index("seq"), lax.axis_index("tp")
    rows, chan = gres.shape
    mine = pl.ds(pl.multiple_of(tp * chan, LANE), chan)
    fetch = pltpu.make_async_copy(gni_h, own, s_own)
    fetches = [
        pltpu.make_async_copy(x_h.at[:, mine], xc, s_x.at[0]),
        pltpu.make_async_copy(gres_h, gres, s_x.at[1]),
    ]
    fetch.start()
    greet_all(n, t, seq, tp)
    pieces, shard, cols = 2, g_input.shape[0], 2 * chan

    core = lax.rem(seq, 2)

    def load(j):
        return pltpu.make_async_copy(
            dw1_h.at[core, :, pl.ds(j * cols, cols)], acc.at[j], s_acc.at[j]
        )

    def swap(j):
        return pltpu.make_async_remote_copy(
            src_ref=dw1_h.at[1 - core, :, pl.ds(j * cols, cols)],
            dst_ref=other.at[j],
            send_sem=m_core.at[0, j],
            recv_sem=m_core.at[1, j],
            device_id=(seq + 1 - 2 * core, tp),
            device_id_type=MESH,
        )

    def start(j):
        load(j).start()
        swap(j).start()

    reduces = []
    for j in range(pieces):

        def out(half, values, j=j):
            at = slice(half * (shard // 2), (half + 1) * (shard // 2))
            if j == 0:
                g_input[at, :] = values[:, :chan]
                g_forget[at, :] = values[:, chan:]
            else:
                g_outgate[at, :] = values[:, :chan]
                g_output[:, at] = jnp.transpose(values[:, chan:])

        reduces.append(grid_reduce(n, seq, tp, j, acc.at[j], bufs, out))

    def stage1(j):
        load(j).wait()
        swap(j).wait_recv()
        add_cores(acc.at[j], other.at[j])
        reduces[j][0]()

    def stage2(j):
        reduces[j][1]()

    def stage3(j):
        reduces[j][2]()

    fetch.wait()
    start(0)
    for copy in fetches:
        copy.start()
    step = rows // SHARD_CHUNKS
    gain_in = consts[4:5, mine]
    vslots[seq] = vecs[...]
    vslots[seq, 3:4, :] = ggain[0:1, mine]
    go_v, done_v = spread(n, seq, vslots, vs, vr, lambda k: (k, tp))
    go_t, done_t = spread(t, tp, allvec, ts, tr, lambda k: (seq, k))
    go_v()
    for copy in fetches:
        copy.wait()

    def finish(k, values):
        at = pl.ds(pl.multiple_of(k * step, step), step)
        hat = xc[at, :].astype(F32) * invin[at, :]
        gin[at, :] = gres[at, :] + invin[at, :] * (values * gain_in - hat * dot_in[at, :])

    def vectors_on():
        done_v()
        total = vslots[0]
        for k in range(1, n):
            total = total + vslots[k]
        allvec[tp] = total
        go_t()

    turns, begin, turn, last, drain = line_reduce_scatter(
        t, seq, tp, own, inbox, (sr, rr, sl, rl), finish, HOP_LAG
    )
    works = [
        (0, lambda: (stage1(0), start(1), vectors_on())),
        (2, lambda: stage1(1)),
        (4, lambda: stage2(0)),
        (6, lambda: stage3(0)),
        (7, lambda: stage2(1)),
        (9, lambda: stage3(1)),
    ]
    slots = 10
    begin()

    def turn_of(slot):
        def one(i, c):
            turn(i)
            return c

        lax.fori_loop(slot * turns // slots, (slot + 1) * turns // slots, one, 0)

    loop_with(0, slots, turn_of, works)
    done_t()
    squares = jnp.zeros((8, 1), F32)
    for k in range(t):
        vectors[:, k * chan : (k + 1) * chan] = allvec[k]
        squares = squares + jnp.sum(allvec[k], axis=1, keepdims=True)
    count = (lens[0] + lens[1]).astype(F32) * width
    rms[...] = jnp.broadcast_to(jnp.sqrt(squares / count), rms.shape)

    def ending(k, c):
        last(k)
        return c

    lax.fori_loop(0, SHARD_CHUNKS, ending, 0)
    drain()
    for j in range(pieces):
        swap(j).wait_send()
        reduces[j][3]()


def emit(count, *refs):
    sources, (vectors, roots) = refs[:count], refs[count : count + 2]
    targets = refs[count + 2 : 2 * count + 2]
    outs, stats = refs[2 * count + 2 : 2 * count + 6], refs[2 * count + 6]
    held, sem = refs[2 * count + 7 : 3 * count + 7], refs[3 * count + 7]
    loads = [
        pltpu.make_async_copy(src, dst, sem.at[0, i])
        for i, (src, dst) in enumerate(zip(sources, held))
    ]
    stores = [
        pltpu.make_async_copy(src, dst, sem.at[1, i])
        for i, (src, dst) in enumerate(zip(held, targets))
    ]
    for copy in loads:
        copy.start()
    for k, out in enumerate(outs):
        out[...] = vectors[k, :]
    for k in range(3):
        stats[k] = roots[4 + k, 0]
    for load, store in zip(loads, stores):
        load.wait()
        store.start()
    for copy in stores:
        copy.wait()


def params(collective=None, limit=VMEM_LIMIT):
    if collective is None:
        return pltpu.CompilerParams(vmem_limit_bytes=limit)
    return pltpu.CompilerParams(
        vmem_limit_bytes=limit, collective_id=collective, has_side_effects=True
    )


def line_sems(chunks):
    return [DMA((chunks,)), DMA((chunks,)), DMA((2, chunks))]


def on_device(
    n, t,
    hidden_in, gain_in, w_input, w_forget, forget_bias, w_outgate, state_gain, w_output,
    gain_mid, w_gate, w_up, w_down, lengths, layer_index, cotangent,
):
    rows, width = hidden_in.shape
    chan = w_input.shape[1]
    ff = w_gate.shape[1]
    ffp = -(-ff // LANE) * LANE

    def padded(w):
        return w if ffp == ff else jnp.pad(w, ((0, 0), (0, ffp - ff)))

    plane = shape((rows, chan), F32)
    plane16 = shape((rows, chan), BF)
    column = shape((rows, 1), F32)
    wide16 = shape((rows, width), BF)
    shards16 = shape((t, rows, chan), BF)

    def groups(more=0):
        return shape((chan // LANE, rows + more, LANE), F32)

    def vm(*arrays):
        return [pltpu.VMEM(a.shape, a.dtype) for a in arrays]

    SM = pl.BlockSpec(memory_space=pltpu.SMEM)
    w1s, w2s = shape((4, width, chan), BF), shape((3, width, ffp), BF)
    zslot, vslot = pltpu.VMEM((t, 8, rows), F32), pltpu.VMEM((n, 8, chan), F32)
    small = [DMA((n,)), DMA((n,)), DMA((t,)), DMA((t,))]
    saved = [plane, plane, plane, groups(8), groups(8), plane16, wide16]

    (
        ipre, fpre, opre, feff, states, gated, normed_in, nmid, mixed, w1, w2, invst, invmid, inv_in,
        consts,
    ) = pl.pallas_call(
        functools.partial(mixer_forward, n, t, width),
        out_shape=saved + [wide16, wide16, w1s, w2s, column, column, column, shape((8, width), F32)],
        in_specs=[SM] * 2 + [HB] * 4 + [VM] + [HB] * 3 + [VM] * 4,
        out_specs=[HB] * 11 + [VM] * 4,
        scratch_shapes=[
            *vm(wide16, wide16, plane, plane, plane, groups(8), groups(8), plane16, wide16, w1s),
            *vm(groups(), plane),
            pltpu.VMEM((rows // CHUNKS * 4, width), F32),
            vslot,
            zslot,
            pltpu.VMEM((rows, width), BF),
            pltpu.VMEM((2, rows, width), BF),
            pltpu.VMEM((width // n, chan), BF),
            pltpu.VMEM((width // n, ffp), BF),
            pltpu.VMEM((ff, width // n), BF),
            DMA, DMA, DMA((7,)), DMA((4,)), DMA((CHUNKS,)), DMA((CHUNKS,)),
            *small,
            *line_sems(CHUNKS),
            *gather_sems(n, 4),
            *gather_sems(n, 3),
        ],
        compiler_params=params(1),
        name="mixer_forward",
    )(
        lengths, layer_index, hidden_in, w_input, w_forget, w_outgate, w_output,
        padded(w_gate), padded(w_up), w_down, forget_bias, state_gain, gain_mid, gain_in,
    )

    shard, chips, tile, step = width // n, n // 2, rows // TILES, rows // CHUNKS
    piece = shape((shard, ffp), F32)
    ffs = shape((rows, ffp), BF)
    gmix, gres, glu_part, ggain, sum_gate, sum_up, down = pl.pallas_call(
        functools.partial(feed_forward, n, t, width),
        out_shape=[
            wide16, plane, shards16, shape((8, width), F32), piece, piece,
            shape((width // 2, ffp), BF),
        ],
        in_specs=[HB] * 5 + [VM] * 2,
        out_specs=[HB] * 3 + [VM] + [HB] * 3,
        scratch_shapes=[
            *vm(wide16, wide16, w2s, ffs, ffs, ffs),
            pltpu.VMEM((2, t, tile, chan), BF),
            pltpu.VMEM((2, step, width), BF),
            pltpu.VMEM((2, step, width), BF),
            pltpu.VMEM((2, step, width), BF),
            pltpu.VMEM((2, step, chan), F32),
            pltpu.VMEM((step, width), F32),
            *vm(piece),
            pltpu.VMEM((2, 2, shard, ffp), BF),
            *vm(wide16),
            pltpu.VMEM((2, rows, width), BF),
            DMA((2,)), DMA((3,)), DMA((2, 2)), DMA((2, 2)), DMA((2,)), DMA((3,)), DMA((2,)),
            DMA((3 * chips,)),
            pltpu.SemaphoreType.REGULAR,
            *line_sems(CHUNKS),
            *grid_buffers(n, width, 2, ffp),
        ],
        compiler_params=params(2),
        name="feed_forward",
    )(nmid, cotangent, w2, hidden_in, mixed, invmid, consts)

    shard_sems = [DMA((t, SHARD_CHUNKS))] * 4
    shard_bufs = [pltpu.VMEM((t, rows, chan), BF), pltpu.VMEM((t + 1, rows, chan), BF)]
    gni_part, dw1, vecs, block_out, dot_in, sum_down = pl.pallas_call(
        functools.partial(mixer_backward, n, t, width),
        out_shape=[
            shards16, shape((2, width // 2, 4 * chan), BF), shape((8, chan), F32), plane16, column,
            shape((ffp, shard), F32),
        ],
        in_specs=[SM] + [HB] * 13 + [VM] * 3,
        out_specs=[HB] * 2 + [VM] * 4,
        scratch_shapes=[
            pltpu.VMEM((width // 2, ffp), BF),
            *vm(wide16, wide16),
            pltpu.VMEM((width, 4 * chan), BF),
            *vm(plane16, groups(8), groups(8), plane, plane, plane),
            *vm(groups(), groups(), plane, shape((rows, 3 * chan), BF)),
            vslot,
            zslot,
            zslot,
            pltpu.VMEM((8, width), F32),
            pltpu.VMEM((t, 8, chan), F32),
            pltpu.VMEM((t, 8, chan), F32),
            *vm(wide16, plane16),
            *shard_bufs,
            *vm(shards16),
            pltpu.VMEM((2, 2, shard, 4 * chan), BF),
            DMA((12,)),
            *small,
            DMA((t,)), DMA((t,)), DMA((t,)), DMA((t,)),
            DMA((3,)),
            *shard_sems,
            DMA((3,)), DMA((2,)), DMA,
            *grid_buffers(n, width, 1, ffp),
        ],
        compiler_params=params(3),
        name="mixer_backward",
    )(
        lengths, glu_part, hidden_in, mixed, gmix, normed_in, w1, gated, states, feff, ipre, fpre, opre,
        down, invst, inv_in, consts,
    )

    square = shape((shard, chan), F32)
    grad_in, vectors, rms, g_input, g_forget, g_outgate, g_output = pl.pallas_call(
        functools.partial(closing, n, t, width),
        out_shape=[
            plane, shape((8, width), F32), shape((8, LANE), F32),
            square, square, square, shape((chan, shard), F32),
        ],
        in_specs=[SM] + [HB] * 4 + [VM] * 5,
        out_specs=[VM] * 7,
        scratch_shapes=[
            pltpu.VMEM((2, width // 2, 2 * chan), BF),
            pltpu.VMEM((2, width // 2, 2 * chan), BF),
            *vm(plane16, plane),
            *shard_bufs,
            vslot,
            pltpu.VMEM((t, 8, chan), F32),
            DMA((2,)), DMA((2, 2)), DMA, DMA((2,)),
            *shard_sems,
            DMA((n,)), DMA((n,)), DMA((t,)), DMA((t,)),
            *grid_buffers(n, width, 2, 2 * chan),
        ],
        compiler_params=params(4),
        name="closing",
    )(lengths, gni_part, dw1, hidden_in, gres, inv_in, dot_in, consts, vecs, ggain)

    arrays = (
        block_out, grad_in, g_input, g_forget, g_outgate, g_output, sum_gate[:, :ff], sum_up[:, :ff],
        sum_down[:ff],
    )
    count = len(arrays)
    *copies, gain0, bias0, gain1, gain2, rms_stats = pl.pallas_call(
        functools.partial(emit, count),
        out_shape=[shape(a.shape, a.dtype) for a in arrays] + [shape((width,), F32)] * 4 + [shape((3,), F32)],
        in_specs=[HB] * count + [VM, SM],
        out_specs=[HB] * count + [VM] * 4 + [SM],
        scratch_shapes=[pltpu.VMEM(a.shape, a.dtype) for a in arrays] + [DMA((2, count))],
        compiler_params=params(),
        name="emit",
    )(*arrays, vectors, rms)
    out, gin, g_input, g_forget, g_outgate, g_output, g_gate, g_up, g_down = copies
    return (
        out, gin, gain0, g_input, g_forget, bias0, g_outgate, gain1, g_output, gain2,
        g_gate, g_up, g_down, rms_stats,
    )


def solution(mesh):
    weight, turned = P("seq", "tp"), P("tp", "seq")
    in_specs = (
        P("seq", None), P(), weight, weight, P(), weight, P(), turned, P(), weight, weight, turned,
        P(), P(), P("seq", None),
    )
    out_specs = (
        weight, weight, P(), weight, weight, P(), weight, P(), turned, P(), weight, weight, turned, P(),
    )
    body = functools.partial(on_device, mesh.shape["seq"], mesh.shape["tp"])
    return jax.shard_map(
        body, mesh=mesh, in_specs=in_specs, out_specs=out_specs, check_vma=False
    )
```

```python
import functools

import jax
import jax.numpy as jnp
from jax import lax
from jax.experimental import pallas as pl
from jax.experimental.pallas import tpu as pltpu
from jax.sharding import PartitionSpec as P

LAYERS = 24
EPS = 1e-06
MESH = pl.DeviceIdType.MESH
DMA = pltpu.SemaphoreType.DMA
BF = jnp.bfloat16
F32 = jnp.float32
VM = pl.BlockSpec(memory_space=pltpu.VMEM)
HB = pl.BlockSpec(memory_space=pl.ANY)
LANE = 128
SEG = 8
TILES = 4
K2_LAGS = (1, 2, 3)
CHUNKS = 16
SHARD_CHUNKS = 4
HOP_LAG = 2
VMEM_LIMIT = 60 * 1024 * 1024


def nn(left, right):
    return jnp.dot(left, right, preferred_element_type=F32)


def nt(left, right):
    return lax.dot_general(left, right, (((1,), (1,)), ((), ())), preferred_element_type=F32)


def tn(left, right):
    return lax.dot_general(left, right, (((0,), (0,)), ((), ())), preferred_element_type=F32)


def shape(dims, dtype):
    return jax.ShapeDtypeStruct(dims, dtype)


def get(ref, at):
    return jnp.concatenate([ref[g, at, :] for g in range(ref.shape[0])], axis=1)


def put(ref, at, values):
    for g in range(ref.shape[0]):
        ref[g, at, :] = values[:, g * LANE : (g + 1) * LANE]


def put_shards(ref, at, values):
    k = ref.shape[2]
    for q in range(ref.shape[0]):
        ref[q, at, :] = values[:, q * k : (q + 1) * k]


def row_tile(rows):
    return rows // 3 if rows % 48 == 0 else rows


def greet_all(n, t, seq, tp):
    barrier = pltpu.get_barrier_semaphore()

    def along_seq(o, c):
        pl.semaphore_signal(barrier, inc=1, device_id=(lax.rem(seq + o, n), tp), device_id_type=MESH)
        return c

    def along_tp(o, c):
        pl.semaphore_signal(barrier, inc=1, device_id=(seq, lax.rem(tp + o, t)), device_id_type=MESH)
        return c

    lax.fori_loop(1, n, along_seq, 0)
    lax.fori_loop(1, t, along_tp, 0)
    pl.semaphore_wait(barrier, n - 1 + t - 1)


def greet_line(t, seq, tp):
    barrier = pltpu.get_barrier_semaphore()

    def along_tp(o, c):
        pl.semaphore_signal(barrier, inc=1, device_id=(seq, lax.rem(tp + o, t)), device_id_type=MESH)
        return c

    lax.fori_loop(1, t, along_tp, 0)
    pl.semaphore_wait(barrier, t - 1)


def spread(size, me, slots, send, recv, target):
    def copy(o, slot):
        return pltpu.make_async_remote_copy(
            src_ref=slots.at[slot],
            dst_ref=slots.at[slot],
            send_sem=send.at[o],
            recv_sem=recv.at[slot],
            device_id=target(lax.rem(me + o, size)),
            device_id_type=MESH,
        )

    def one(o, c):
        copy(o, me).start()
        return c

    def arrived(o, c):
        copy(o, lax.rem(me + o, size)).wait_recv()
        return c

    def sent(o, c):
        copy(o, me).wait_send()
        return c

    def go():
        lax.fori_loop(1, size, one, 0)

    def done():
        lax.fori_loop(1, size, arrived, 0)
        lax.fori_loop(1, size, sent, 0)

    return go, done


def row_sums(values):
    ones = jnp.ones((8, values.shape[1]), BF)
    high = values.astype(BF)
    rest = values - high.astype(F32)
    low = rest.astype(BF)
    return nt(ones, high) + nt(ones, low)


def sum_over_tp(part, t, seq, tp, slots, send, recv, between=None):
    slots[tp] = part
    go, done = spread(t, tp, slots, send, recv, lambda k: (seq, k))
    go()
    if between is not None:
        between()
    done()
    total = slots[0]
    for k in range(1, t):
        total = total + slots[k]
    return jnp.transpose(total)[:, :1]


def carry_over_seq(prod, state, n, seq, tp, slots, send, recv, backward, between=None):
    slots[seq] = jnp.concatenate([prod, state] + [jnp.zeros_like(prod)] * 6, axis=0)
    go, done = spread(n, seq, slots, send, recv, lambda k: (k, tp))
    go()
    if between is not None:
        between()
    done()

    def hop(i, total):
        j = n - 1 - i if backward else i
        block = slots[j]
        longer = block[1:2] + block[0:1] * total
        inside = (j > seq) if backward else (j < seq)
        return jnp.where(inside, longer, total)

    return lax.fori_loop(0, n, hop, jnp.zeros_like(prod))


def line_all_reduce(t, seq, tp, rows, chunks, partial, send, buf, sems, finish, lags):
    s_in, s_out, r_buf = sems
    step = rows // chunks
    half = t // 2
    depth = jnp.where(tp < half, tp, t - 1 - tp)
    inner = jnp.where(tp < half, tp + 1, tp - 1)
    outer = jnp.where(tp < half, tp - 1, tp + 1)
    outer = jnp.where(depth > 0, outer, inner)
    middle = (depth == half - 1).astype(jnp.int32)
    lag_in, lag_turn, lag_out = lags
    lag_first = lag_in * depth
    lag_second = lag_in * (half - 1) + lag_turn + lag_out * (half - 1 - depth)

    def part_of(k):
        return pl.ds(pl.multiple_of(k * step, step), step)

    def inward(k, slot):
        return pltpu.make_async_remote_copy(
            src_ref=send.at[part_of(k)],
            dst_ref=buf.at[slot, part_of(k)],
            send_sem=s_in.at[k],
            recv_sem=r_buf.at[slot, k],
            device_id=(seq, inner),
            device_id_type=MESH,
        )

    def outward(k):
        return pltpu.make_async_remote_copy(
            src_ref=buf.at[1, part_of(k)],
            dst_ref=buf.at[1, part_of(k)],
            send_sem=s_out.at[k],
            recv_sem=r_buf.at[1, k],
            device_id=(seq, outer),
            device_id_type=MESH,
        )

    def first(k):
        part = None if partial is None else partial(k)

        @pl.when(depth > 0)
        def _():
            inward(k, 0).wait_recv()
            mine = send[part_of(k), :].astype(F32) if part is None else part
            send[part_of(k), :] = (mine + buf[0, part_of(k), :].astype(F32)).astype(BF)

        if part is not None:

            @pl.when(depth == 0)
            def _():
                send[part_of(k), :] = part.astype(BF)

        inward(k, middle).start()

    def second(k):
        inward(k, 1).wait_recv()

        @pl.when(middle == 1)
        def _():
            both = send[part_of(k), :].astype(F32) + buf[1, part_of(k), :].astype(F32)
            buf[1, part_of(k), :] = both.astype(BF)

        @pl.when(depth > 0)
        def _():
            outward(k).start()

        finish(k)

    def turn(i):
        @pl.when((i >= lag_first) & (i - lag_first < chunks))
        def _():
            first(i - lag_first)

        @pl.when((i >= lag_second) & (i - lag_second < chunks))
        def _():
            second(i - lag_second)

    def drain():
        def sent(k, c):
            inward(k, middle).wait_send()

            @pl.when(depth > 0)
            def _():
                outward(k).wait_send()

            return c

        lax.fori_loop(0, chunks, sent, 0)

    return chunks + lag_in * (half - 1) + lag_turn + lag_out * (half - 1), turn, drain


def line_reduce_scatter(t, seq, tp, own, inbox, sems, finish, lead):
    s_r, r_r, s_l, r_l = sems
    rows = own.shape[1]
    chunks = SHARD_CHUNKS
    step = rows // chunks
    count = chunks * (t - 1)

    def part_of(k):
        return pl.ds(pl.multiple_of(k * step, step), step)

    def rightward(q, k):
        return pltpu.make_async_remote_copy(
            src_ref=own.at[q, part_of(k)],
            dst_ref=inbox.at[q + 1, part_of(k)],
            send_sem=s_r.at[q, k],
            recv_sem=r_r.at[q, k],
            device_id=(seq, lax.rem(tp + 1, t)),
            device_id_type=MESH,
        )

    def leftward(q, k):
        return pltpu.make_async_remote_copy(
            src_ref=own.at[q, part_of(k)],
            dst_ref=inbox.at[q, part_of(k)],
            send_sem=s_l.at[q, k],
            recv_sem=r_l.at[q, k],
            device_id=(seq, lax.rem(tp + t - 1, t)),
            device_id_type=MESH,
        )

    def add(q, k, slot):
        own[q, part_of(k), :] = (
            own[q, part_of(k), :].astype(F32) + inbox[slot, part_of(k), :].astype(F32)
        ).astype(BF)

    def right_turn(i):
        j, k = i // chunks, lax.rem(i, chunks)
        q = t - 1 - j

        @pl.when((i >= 0) & (i < count) & (q > tp))
        def _():
            @pl.when(tp > 0)
            def _():
                rightward(q, k).wait_recv()
                add(q, k, q + 1)

            rightward(q, k).start()

    def left_turn(i):
        q, k = i // chunks, lax.rem(i, chunks)

        @pl.when((i >= 0) & (i < count) & (q < tp))
        def _():
            @pl.when(tp < t - 1)
            def _():
                leftward(q, k).wait_recv()
                add(q, k, q)

            leftward(q, k).start()

    def begin():
        for i in range(lead):

            @pl.when(tp == 0)
            def _(i=i):
                right_turn(i)

            @pl.when(tp == t - 1)
            def _(i=i):
                left_turn(i)

    def turn(i):
        right_turn(i - jnp.where(tp == 0, -lead, HOP_LAG * tp))
        left_turn(i - jnp.where(tp == t - 1, -lead, HOP_LAG * (t - 1 - tp)))

    def last(k):
        @pl.when(tp == 0)
        def _():
            leftward(tp, k).wait_recv()
            finish(k, own[tp, part_of(k), :].astype(F32) + inbox[tp, part_of(k), :].astype(F32))

        @pl.when(tp == t - 1)
        def _():
            rightward(tp, k).wait_recv()
            finish(k, own[tp, part_of(k), :].astype(F32) + inbox[tp + 1, part_of(k), :].astype(F32))

        @pl.when((tp > 0) & (tp < t - 1))
        def _():
            leftward(tp, k).wait_recv()
            rightward(tp, k).wait_recv()
            finish(
                k,
                own[tp, part_of(k), :].astype(F32)
                + inbox[tp, part_of(k), :].astype(F32)
                + inbox[tp + 1, part_of(k), :].astype(F32),
            )

    def drain():
        def sent(i, c):
            j, k = i // chunks, lax.rem(i, chunks)

            @pl.when(t - 1 - j > tp)
            def _():
                rightward(t - 1 - j, k).wait_send()

            @pl.when(j < tp)
            def _():
                leftward(j, k).wait_send()

            return c

        lax.fori_loop(0, count, sent, 0)

    turns = max((t - 1 - p) * chunks + (HOP_LAG * p if p else -lead) for p in range(t - 1))
    return turns, begin, turn, last, drain


def chip_grid(n):
    chips = n // 2
    b = max(k for k in range(1, chips + 1) if chips % k == 0 and k * k <= chips)
    return chips // b, b


def grid_buffers(n, width, pieces, cols):
    ga, gb = chip_grid(n)
    h = width // n // 2
    pa, pb = max(ga - 1, 1), max(gb - 1, 1)
    return [
        pltpu.VMEM((pieces, pb, ga, h, cols), BF),
        pltpu.VMEM((pieces, pa, gb, h, cols), BF),
        pltpu.VMEM((pieces, pa, h, cols), BF),
        pltpu.VMEM((pieces, pb, h, cols), BF),
        DMA((2, pieces, pb, ga)), DMA((2, pieces, pa, gb)), DMA((2, pieces, pa)), DMA((2, pieces, pb)),
    ]


def add_cores(acc, first):
    part = 64

    def one(i, c):
        at = pl.ds(pl.multiple_of(i * part, part), part)
        acc[at, :] = (acc[at, :].astype(F32) + first[at, :].astype(F32)).astype(BF)
        return c

    lax.fori_loop(0, acc.shape[0] // part, one, 0)


def grid_reduce(n, seq, tp, j, acc, bufs, out):
    far_b, far_a, near_a, near_b, m_fb, m_fa, m_na, m_nb = bufs
    ga, gb = chip_grid(n)
    core = lax.rem(seq, 2)
    a, b = seq // 2 // gb, lax.rem(seq // 2, gb)
    h = near_a.shape[2]

    def device(a_, b_):
        return ((a_ * gb + b_) * 2 + core, tp)

    def block(half, x, y):
        return pl.ds(pl.multiple_of(((x * gb + y) * 2 + half) * h, h), h)

    def remote(rows, dst, sems, index, target):
        return pltpu.make_async_remote_copy(
            src_ref=acc.at[rows],
            dst_ref=dst,
            send_sem=sems.at[(0, j) + index],
            recv_sem=sems.at[(1, j) + index],
            device_id=target,
            device_id_type=MESH,
        )

    def first_way():
        copies = []
        for o in range(1, gb):
            to = lax.rem(b + o, gb)
            for x in range(ga):
                dst = far_b.at[j, o - 1, x]
                copies.append(remote(block(0, x, to), dst, m_fb, (o - 1, x), device(a, to)))
        for o in range(1, ga):
            to = lax.rem(a + o, ga)
            for y in range(gb):
                dst = far_a.at[j, o - 1, y]
                copies.append(remote(block(1, to, y), dst, m_fa, (o - 1, y), device(to, b)))
        return copies

    def second_way():
        copies = []
        for o in range(1, ga):
            to = lax.rem(a + o, ga)
            copies.append(
                remote(block(0, to, b), near_a.at[j, o - 1], m_na, (o - 1,), device(to, b))
            )
        for o in range(1, gb):
            to = lax.rem(b + o, gb)
            copies.append(
                remote(block(1, a, to), near_b.at[j, o - 1], m_nb, (o - 1,), device(a, to))
            )
        return copies

    def far():
        for copy in first_way():
            copy.start()

    def middle():
        for copy in first_way():
            copy.wait_recv()

        def along_a(x, c):
            total = acc[block(0, x, b), :].astype(F32)
            for o in range(1, gb):
                total = total + far_b[j, o - 1, x].astype(F32)
            acc[block(0, x, b), :] = total.astype(BF)
            return c

        def along_b(y, c):
            total = acc[block(1, a, y), :].astype(F32)
            for o in range(1, ga):
                total = total + far_a[j, o - 1, y].astype(F32)
            acc[block(1, a, y), :] = total.astype(BF)
            return c

        lax.fori_loop(0, ga, along_a, 0)
        lax.fori_loop(0, gb, along_b, 0)
        for copy in second_way():
            copy.start()

    def near():
        for copy in second_way():
            copy.wait_recv()
        total = acc[block(0, a, b), :].astype(F32)
        for o in range(1, ga):
            total = total + near_a[j, o - 1].astype(F32)
        out(0, total)
        total = acc[block(1, a, b), :].astype(F32)
        for o in range(1, gb):
            total = total + near_b[j, o - 1].astype(F32)
        out(1, total)

    def drain():
        for copy in first_way() + second_way():
            copy.wait_send()

    return far, middle, near, drain


def gather_sems(n, pieces):
    ga, gb = chip_grid(n)
    pa, pb = max(ga - 1, 1), max(gb - 1, 1)
    return [
        DMA((pieces,)), DMA((2, pieces, ga * gb)),
        DMA((2, pieces, pb)), DMA((2, pieces, pa)), DMA((2, pieces, gb, pa)), DMA((2, pieces, ga, pb)),
    ]


def grid_gather(n, seq, tp, j, src, dst, sems):
    s_local, m_core, m_fb, m_fa, m_na, m_nb = sems
    ga, gb = chip_grid(n)
    shard = src.shape[0]
    h = shard // 2
    core = lax.rem(seq, 2)
    a, b = seq // 2 // gb, lax.rem(seq // 2, gb)

    def device(a_, b_, core_):
        return ((a_ * gb + b_) * 2 + core_, tp)

    def block(x, y, core_, half, count):
        return pl.ds(pl.multiple_of(((x * gb + y) * 2 + core_) * shard + half * h, h), count)

    def remote(from_, rows, sem, index, target):
        return pltpu.make_async_remote_copy(
            src_ref=from_,
            dst_ref=dst.at[rows],
            send_sem=sem.at[(0, j) + index],
            recv_sem=sem.at[(1, j) + index],
            device_id=target,
            device_id_type=MESH,
        )

    def own(half):
        return src.at[pl.ds(half * h, h)]

    def far(incoming):
        copies = []
        for o in range(1, gb):
            to, of = lax.rem(b + o, gb), lax.rem(b + gb - o, gb)
            rows = block(a, of if incoming else b, core, 0, h)
            copies.append(remote(own(0), rows, m_fb, (o - 1,), device(a, to, core)))
        for o in range(1, ga):
            to, of = lax.rem(a + o, ga), lax.rem(a + ga - o, ga)
            rows = block(of if incoming else a, b, core, 1, h)
            copies.append(remote(own(1), rows, m_fa, (o - 1,), device(to, b, core)))
        return copies

    def near(incoming, first, least):
        copies = []
        for i in range(0 if first else 1, gb if least else 1):
            y = lax.rem(b + gb - i, gb)
            for o in range(1, ga):
                to, of = lax.rem(a + o, ga), lax.rem(a + ga - o, ga)
                rows = block(of if incoming else a, y, core, 0, h)
                from_ = own(0) if i == 0 or incoming else dst.at[rows]
                copies.append(remote(from_, rows, m_na, (i, o - 1), device(to, b, core)))
        for i in range(0 if first else 1, ga if least else 1):
            x = lax.rem(a + ga - i, ga)
            for o in range(1, gb):
                to, of = lax.rem(b + o, gb), lax.rem(b + gb - o, gb)
                rows = block(x, of if incoming else b, core, 1, h)
                from_ = own(1) if i == 0 or incoming else dst.at[rows]
                copies.append(remote(from_, rows, m_nb, (i, o - 1), device(a, to, core)))
        return copies

    def across(incoming, first, others):
        copies = []
        for i in range(ga):
            for k in range(gb):
                mine = i == 0 and k == 0
                if (mine and not first) or (not mine and not others):
                    continue
                x, y = lax.rem(a + i, ga), lax.rem(b + k, gb)
                rows = block(x, y, 1 - core if incoming else core, 0, shard)
                from_ = src if mine or incoming else dst.at[rows]
                copies.append(remote(from_, rows, m_core, (i * gb + k,), device(a, b, 1 - core)))
        return copies

    def local():
        return pltpu.make_async_copy(src, dst.at[block(a, b, core, 0, shard)], s_local.at[j])

    def start():
        for copy in far(False) + near(False, True, False) + across(False, True, False):
            copy.start()
        local().start()

    def relay():
        for copy in far(True):
            copy.wait_recv()
        for copy in near(False, False, True):
            copy.start()

    def share():
        for copy in near(True, True, True):
            copy.wait_recv()
        for copy in across(False, False, True):
            copy.start()

    def arrive():
        for copy in across(True, True, True):
            copy.wait_recv()
        local().wait()

    def drain():
        for copy in far(False) + near(False, True, True) + across(False, True, True):
            copy.wait_send()

    return start, relay, share, arrive, drain


def loop_with(first, last, body, works):
    def one(i, c):
        body(i)
        for when, work in works:

            @pl.when(i == when)
            def _(work=work):
                work()

        return c

    lax.fori_loop(first, last, one, 0)


def masks(lens, first, count):
    at = first + lax.broadcasted_iota(jnp.int32, (count, 1), 0)
    valid = (at < lens[0] + lens[1]).astype(F32)
    starts = ((at == 0) | (at == lens[0])).astype(F32)
    return valid, starts


def mixer_forward(
    n, t, width,
    lens, layer, x_h, wi_h, wf_h, wo_h, wx_raw, wg_h, wu_h, wd_raw_h, bias_v, sgain_v, gmid_v, gin_v,
    ipre_h, fpre_h, opre_h, feff_h, states_h, gated_h, normed_h, nmid_h, mixed_h, w1_h, w2_h,
    invst, invmid, invin, consts,
    x, normed, ipre, fpre, opre, feff, states, gated, nmid, w1, prod, ssq, part, cslots, zslots, send, buf,
    wx, wd, wd_raw, s_t, s_x, s_st, s_w, s_n, s_m, cs, cr, zs, zr, s_in, s_out, r_buf, *sems,
):
    seq, tp = lax.axis_index("seq"), lax.axis_index("tp")
    load = pltpu.make_async_copy(x_h, x, s_x)
    load.start()
    load_down = pltpu.make_async_copy(wd_raw_h, wd_raw, s_t)
    load_down.start()
    sems1, sems2 = sems[:6], sems[6:]
    one = [
        grid_gather(n, seq, tp, j, src, w1.at[j], sems1)
        for j, src in enumerate((wi_h, wf_h, wo_h, wx))
    ]
    two = [
        grid_gather(n, seq, tp, j, src, w2_h.at[j], sems2)
        for j, src in enumerate((wg_h, wu_h, wd))
    ]
    START, RELAY, SHARE, ARRIVE, DRAIN = range(5)
    greet_all(n, t, seq, tp)
    one[0][START]()
    rows, depth = normed.shape
    chan = ipre.shape[1]
    tile = row_tile(rows)
    mine = pl.ds(pl.multiple_of(tp * chan, LANE), chan)
    consts[...] = jnp.zeros_like(consts)
    for k, vector in ((0, bias_v), (1, sgain_v), (3, gmid_v), (4, gin_v)):
        consts[k : k + 1, :] = vector[...].astype(F32).reshape(1, width)
    consts[2:3, :] = jnp.full((1, width), layer[0].astype(F32) / LAYERS)
    bias, sgain, bound = consts[0:1, mine], consts[1:2, mine], consts[2:3, mine]

    def stores():
        pairs = (
            (ipre, ipre_h), (fpre, fpre_h), (opre, opre_h), (feff, feff_h), (states, states_h),
            (gated, gated_h), (normed, normed_h),
        )
        return [pltpu.make_async_copy(v, o, s_st.at[i]) for i, (v, o) in enumerate(pairs)]

    def keep(j):
        return pltpu.make_async_copy(w1.at[j], w1_h.at[j], s_w.at[j])

    wx[...] = jnp.transpose(wx_raw[...])
    load.wait()

    def norm(i, c):
        at = pl.ds(pl.multiple_of(i * tile, tile), tile)
        v = x[at, :].astype(F32)
        inv = lax.rsqrt(jnp.mean(v * v, axis=-1, keepdims=True) + EPS)
        invin[at, :] = inv
        normed[at, :] = (v * inv * consts[4:5, :]).astype(BF)
        return c

    lax.fori_loop(0, rows // tile, norm, 0)
    one[0][RELAY]()
    one[1][START]()
    load_down.wait()
    turned = jnp.transpose(wd_raw[...])
    wd[:, : turned.shape[1]] = turned
    if turned.shape[1] < wd.shape[1]:
        wd[:, turned.shape[1] :] = jnp.zeros((wd.shape[0], wd.shape[1] - turned.shape[1]), BF)
    one[0][SHARE]()
    one[1][RELAY]()
    one[2][START]()
    one[0][ARRIVE]()
    keep(0).start()

    def first(i, c):
        at = pl.ds(pl.multiple_of(i * tile, tile), tile)
        ipre[at, :] = nn(normed[at, :], w1[0])
        return c

    lax.fori_loop(0, rows // tile, first, 0)
    one[1][SHARE]()
    one[2][RELAY]()
    one[3][START]()
    one[1][ARRIVE]()
    keep(1).start()

    def second(i, c):
        at = pl.ds(pl.multiple_of(i * tile, tile), tile)
        f = nn(normed[at, :], w1[1]) + bias
        fpre[at, :] = f
        valid, starts = masks(lens, seq * rows + i * tile, tile)
        gate = bound + (1.0 - bound) * jax.nn.sigmoid(f)
        put(feff, at, gate * (1.0 - starts))
        shifted = pl.ds(pl.multiple_of(i * tile + 8, 8), tile)
        v = ipre[at, :]
        put(states, shifted, v * jax.nn.sigmoid(v) * (1.0 - gate) * valid)
        return c

    lax.fori_loop(0, rows // tile, second, 0)
    put(feff, slice(rows, rows + 8), jnp.ones((8, chan), F32))

    length = rows // SEG

    def scan(i, c):
        p, h = c
        at, shifted = pl.ds(i, SEG, stride=length), pl.ds(i + 8, SEG, stride=length)
        f = get(feff, at)
        h = f * h + get(states, shifted)
        p = f * p
        put(states, shifted, h)
        put(prod, at, p)
        return p, h

    p, h = lax.fori_loop(
        0, length, scan, (jnp.ones((SEG, chan), F32), jnp.zeros((SEG, chan), F32))
    )
    block_p, block_h = p[0:1], h[0:1]
    for s in range(1, SEG):
        block_h = h[s : s + 1] + p[s : s + 1] * block_h
        block_p = p[s : s + 1] * block_p

    def travel():
        one[2][SHARE]()
        one[3][RELAY]()
        two[0][START]()

    arriving = carry_over_seq(block_p, block_h, n, seq, tp, cslots, cs, cr, False, travel)
    put(states, slice(0, 8), jnp.broadcast_to(arriving, (8, chan)))
    for s in range(SEG):
        at = slice(s * length, (s + 1) * length)
        shifted = slice(s * length + 8, (s + 1) * length + 8)
        whole = get(states, shifted) + get(prod, at) * arriving
        put(states, shifted, whole)
        ssq[at, :] = whole * whole
        arriving = h[s : s + 1] + p[s : s + 1] * arriving

    def outgate():
        one[3][SHARE]()
        one[2][ARRIVE]()
        keep(2).start()

        def third(i, c):
            at = pl.ds(pl.multiple_of(i * tile, tile), tile)
            opre[at, :] = nn(normed[at, :], w1[2])
            return c

        lax.fori_loop(0, rows // tile, third, 0)

    total = sum_over_tp(row_sums(ssq[...]), t, seq, tp, zslots, zs, zr, outgate)
    invst[...] = lax.rsqrt(total / width + EPS)

    def gating(i, c):
        at = pl.ds(pl.multiple_of(i * tile, tile), tile)
        shifted = pl.ds(pl.multiple_of(i * tile + 8, 8), tile)
        o = opre[at, :]
        gated[at, :] = (
            get(states, shifted) * invst[at, :] * sgain * (o * jax.nn.sigmoid(o))
        ).astype(BF)
        return c

    lax.fori_loop(0, rows // tile, gating, 0)
    one[3][ARRIVE]()
    keep(3).start()
    for copy in stores():
        copy.start()

    step = rows // CHUNKS
    group = part.shape[0] // step

    def partial(k):
        @pl.when(lax.rem(k, group) == 0)
        def _():
            big = pl.ds(pl.multiple_of(k * step, step), step * group)
            part[...] = nt(gated[big, :], w1[3])

        return part[pl.ds(pl.multiple_of(lax.rem(k, group) * step, step), step), :]

    def store_n(k):
        at = pl.ds(pl.multiple_of(k * step, step), step)
        return pltpu.make_async_copy(nmid.at[at], nmid_h.at[at], s_n.at[k])

    def store_m(k):
        at = pl.ds(pl.multiple_of(k * step, step), step)
        return pltpu.make_async_copy(buf.at[1, at], mixed_h.at[at], s_m.at[k])

    def finish(k):
        at = pl.ds(pl.multiple_of(k * step, step), step)
        store_m(k).start()
        resid = x[at, :].astype(F32) + buf[1, at, :].astype(F32)
        inv = lax.rsqrt(jnp.mean(resid * resid, axis=-1, keepdims=True) + EPS)
        invmid[at, :] = inv
        nmid[at, :] = (resid * inv * consts[3:4, :]).astype(BF)
        store_n(k).start()

    turns = [
        (2, lambda: (two[0][RELAY](), two[1][START]())),
        (4, lambda: two[0][SHARE]()),
        (7, lambda: (two[1][RELAY](), two[2][START]())),
        (9, lambda: two[1][SHARE]()),
        (13, lambda: two[2][RELAY]()),
        (16, lambda: two[2][SHARE]()),
    ]

    count, turn, drain = line_all_reduce(
        t, seq, tp, rows, CHUNKS, partial, send, buf, (s_in, s_out, r_buf), finish, (0, 1, 3)
    )
    loop_with(0, count, turn, turns)
    drain()
    for g in two:
        g[ARRIVE]()
    for g in one + two:
        g[DRAIN]()
    for copy in stores():
        copy.wait()
    for j in range(4):
        keep(j).wait()

    def stored(k, c):
        store_n(k).wait()
        store_m(k).wait()
        return c

    lax.fori_loop(0, CHUNKS, stored, 0)


def feed_forward(
    n, t, width,
    nmid_h, cot_h, w2_h, x_h, mixed_h, invmid, consts,
    gmix_h, gres_h, glu_h, ggain, gate_h, up_h, down_h,
    nmid, cot, pool, hid, gg, gu, glu, xs, ms, gmix, gres, wide, sums, stage, send, buf,
    s_a, s_w, s_x, s_o, s_g, s_s, s_d, m_core, ready, s_in, s_out, r_buf, *bufs,
):
    seq, tp = lax.axis_index("seq"), lax.axis_index("tp")
    core = lax.rem(seq, 2)
    sibling = (seq + 1 - 2 * core, tp)
    act_copies = [
        pltpu.make_async_copy(nmid_h, nmid, s_a.at[0]),
        pltpu.make_async_copy(cot_h, cot, s_a.at[1]),
    ]
    w_copies = [pltpu.make_async_copy(w2_h.at[j], pool.at[j], s_w.at[j]) for j in range(3)]
    act_copies[0].start()
    w_copies[0].start()
    greet_all(n, t, seq, tp)
    for copy in (w_copies[1], act_copies[1], w_copies[2]):
        copy.start()
    rows, chan = nmid.shape[0], gres.shape[2]
    step = rows // CHUNKS
    tile = rows // TILES
    ggain[...] = jnp.zeros_like(ggain)

    def fetch(k):
        at, slot = pl.ds(pl.multiple_of(k * step, step), step), lax.rem(k, 2)
        return (
            pltpu.make_async_copy(x_h.at[at], xs.at[slot], s_x.at[0, slot]),
            pltpu.make_async_copy(mixed_h.at[at], ms.at[slot], s_x.at[1, slot]),
        )

    def stored(k):
        at, slot = pl.ds(pl.multiple_of(k * step, step), step), lax.rem(k, 2)
        return (
            pltpu.make_async_copy(gmix.at[slot], gmix_h.at[at], s_o.at[0, slot]),
            pltpu.make_async_copy(gres.at[slot], gres_h.at[at], s_o.at[1, slot]),
        )

    for copy in fetch(0):
        copy.start()

    def finish(k):
        for copy in fetch(k):
            copy.wait()

        @pl.when(k + 1 < CHUNKS)
        def _():
            for copy in fetch(k + 1):
                copy.start()

        @pl.when(k >= 2)
        def _():
            for copy in stored(k - 2):
                copy.wait()

        at, slot = pl.ds(pl.multiple_of(k * step, step), step), lax.rem(k, 2)
        g = buf[1, at, :].astype(F32)
        inv = invmid[at, :]
        hat = (xs[slot].astype(F32) + ms[slot].astype(F32)) * inv
        ggain[0:1, :] += jnp.sum(g * hat, axis=0, keepdims=True)
        e = g * consts[3:4, :]
        mean = jnp.mean(e * hat, axis=-1, keepdims=True)
        result = cot[at, :].astype(F32) + inv * (e - hat * mean)
        wide[...] = result
        gmix[slot] = result.astype(BF)
        gres[slot] = wide[:, pl.ds(pl.multiple_of(tp * chan, LANE), chan)]
        for copy in stored(k):
            copy.start()

    count, turn, drain = line_all_reduce(
        t, seq, tp, rows, CHUNKS, None, send, buf, (s_in, s_out, r_buf), finish, K2_LAGS
    )

    act_copies[0].wait()
    w_copies[0].wait()

    def block(i, c):
        at = pl.ds(pl.multiple_of(i * tile, tile), tile)
        g = nn(nmid[at, :], pool[0])

        @pl.when(i == 0)
        def _():
            w_copies[1].wait()
            act_copies[1].wait()
            w_copies[2].wait()

        u = nn(nmid[at, :], pool[1])
        gh = nn(cot[at, :], pool[2])
        sig = jax.nn.sigmoid(g)
        act = g * sig
        hid[at, :] = (act * u).astype(BF)
        gg[at, :] = (gh * u * (sig * (1.0 + g * (1.0 - sig)))).astype(BF)
        gu[at, :] = (gh * act).astype(BF)

        @pl.when(i > 0)
        def _():
            turn(2 * i - 1)

        send[at, :] = (nt(gg[at, :], pool[0]) + nt(gu[at, :], pool[1])).astype(BF)
        turn(2 * i)
        return c

    lax.fori_loop(0, TILES, block, 0)
    done = 2 * TILES - 1

    ga, gb = chip_grid(n)
    chips = ga * gb
    shard = width // n
    half_pool = pl.ds(0, width // 2)
    other_half = pl.ds(width // 2, width // 2)

    def give(i):
        j, r = i // chips, lax.rem(i, chips)
        return pltpu.make_async_remote_copy(
            src_ref=stage.at[lax.rem(i, 2), 1 - core],
            dst_ref=pool.at[j, pl.ds(pl.multiple_of(width // 2 + r * shard, shard), shard)],
            send_sem=s_g.at[lax.rem(i, 2)],
            recv_sem=m_core.at[i],
            device_id=sibling,
            device_id_type=MESH,
        )

    def gradient(j, left, right, first_turn, turns):
        pl.semaphore_signal(ready, inc=1, device_id=sibling, device_id_type=MESH)
        pl.semaphore_wait(ready, 1)

        def slab(r, c):
            i = j * chips + r
            slot = lax.rem(i, 2)

            @pl.when(i >= 2)
            def _():
                give(i - 2).wait_send()

            at = pl.ds(pl.multiple_of(r * 2 * shard, 2 * shard), 2 * shard)
            values = tn(left[:, at], right[...]).astype(BF)
            for k in range(2):
                stage[slot, k] = values[k * shard : (k + 1) * shard]
            give(i).start()
            pool[j, pl.ds(pl.multiple_of(r * shard, shard), shard), :] = stage[slot, core]
            loop_with(first_turn + r * turns // chips, first_turn + (r + 1) * turns // chips, turn, ())
            return c

        lax.fori_loop(0, chips, slab, 0)

    def cores(j):
        def arrived(r, c):
            give(j * chips + r).wait_recv()
            return c

        lax.fori_loop(0, chips, arrived, 0)
        add_cores(pool.at[j, half_pool], pool.at[j, other_half])

    def summed(j):
        return pltpu.make_async_copy(sums, (gate_h, up_h)[j], s_s.at[j])

    def out(half, values):
        sums[half * (shard // 2) : (half + 1) * (shard // 2), :] = values

    reduces = [
        grid_reduce(n, seq, tp, j, pool.at[j, half_pool], bufs, out) for j in range(2)
    ]
    gradient(0, nmid, gg, done, 2)
    cores(0)
    reduces[0][0]()
    gradient(1, nmid, gu, done + 2, 2)
    cores(1)
    reduces[1][0]()

    def glu_copy(i):
        at, slot = pl.ds(pl.multiple_of(i * tile, tile), tile), lax.rem(i, 2)
        return pltpu.make_async_copy(glu.at[slot], glu_h.at[:, at], s_d.at[slot])

    def forward(i, c):
        @pl.when(i >= 2)
        def _():
            glu_copy(i - 2).wait()

        at, slot = pl.ds(pl.multiple_of(i * tile, tile), tile), lax.rem(i, 2)
        values = nt(hid[at, :], pool[2]).astype(BF)
        for q in range(t):
            glu[slot, q] = values[:, q * chan : (q + 1) * chan]
        glu_copy(i).start()

        @pl.when(lax.rem(i, 2) == 1)
        def _():
            turn(done + 4 + i // 2)

        return c

    lax.fori_loop(0, TILES, forward, 0)
    glu_copy(TILES - 2).wait()
    glu_copy(TILES - 1).wait()
    reduces[0][1]()
    gradient(2, cot, hid, done + 4 + TILES // 2, 2)
    cores(2)
    down = pltpu.make_async_copy(pool.at[2, half_pool], down_h, s_s.at[2])
    down.start()

    def second_sum():
        summed(0).wait()
        reduces[1][2]()
        summed(1).start()

    now = done + 6 + TILES // 2
    loop_with(
        now,
        count,
        turn,
        (
            (now + 1, lambda: (reduces[0][2](), summed(0).start())),
            (now + 2, lambda: reduces[1][1]()),
            (now + 5, second_sum),
        ),
    )
    drain()
    for r in reduces:
        r[3]()
    give(3 * chips - 2).wait_send()
    give(3 * chips - 1).wait_send()
    summed(1).wait()
    down.wait()
    for k in (CHUNKS - 2, CHUNKS - 1):
        for copy in stored(k):
            copy.wait()


def mixer_backward(
    n, t, width,
    lens, glu_h, x_h, mixed_h, gmix_h, normed_h, w1_h, gated_h, states_h, feff_h, ipre_h, fpre_h, opre_h,
    down_h, invst, invin, consts,
    gni_h, dw1_h, vecs, out, dot_in, sums,
    acc, gmix, normed, w1, gated, states, feff, ipre, fpre, opre,
    weighted, prod, inner, out3, cslots, zslots, zslots2, gain_sum, gsend, gtake, x, mc, own, inbox, gni, stage,
    s_f, cs, cr, zs, zr, zs2, zr2, gs_, gr_, s_x, sr, rr, sl, rl, s_o, s_d, s_acc, *bufs,
):
    seq, tp = lax.axis_index("seq"), lax.axis_index("tp")
    down = pltpu.make_async_copy(down_h, acc, s_acc)
    down.start()
    rows = gmix.shape[0]
    chan = ipre.shape[1]
    mine = pl.ds(pl.multiple_of(tp * chan, LANE), chan)
    fetches = [
        pltpu.make_async_copy(glu_h, own, s_x.at[0]),
        pltpu.make_async_copy(x_h, x, s_x.at[1]),
        pltpu.make_async_copy(mixed_h.at[:, mine], mc, s_x.at[2]),
    ]
    pairs = [
        (gmix_h, gmix),
        (w1_h.at[3], w1.at[:, pl.ds(3 * chan, chan)]),
        (states_h, states), (opre_h, opre), (feff_h, feff), (ipre_h, ipre), (fpre_h, fpre),
    ] + [(w1_h.at[j], w1.at[:, pl.ds(j * chan, chan)]) for j in range(3)] + [
        (normed_h, normed), (gated_h, gated),
    ]
    inputs = [pltpu.make_async_copy(src, dst, s_f.at[i]) for i, (src, dst) in enumerate(pairs)]
    fetches[0].start()
    for copy in inputs[:4]:
        copy.start()
    greet_all(n, t, seq, tp)
    for copy in inputs[4:] + fetches[1:]:
        copy.start()

    def down_out(half, values):
        size = sums.shape[1] // 2
        sums[:, half * size : (half + 1) * size] = jnp.transpose(values)

    far, middle, near, drain_grid = grid_reduce(n, seq, tp, 0, acc, bufs, down_out)
    tile = row_tile(rows)
    sgain, bound = consts[1:2, mine], consts[2:3, mine]
    vecs[...] = jnp.zeros_like(vecs)
    step = rows // SHARD_CHUNKS

    def finish(k, values):
        at = pl.ds(pl.multiple_of(k * step, step), step)
        ok, _ = masks(lens, seq * rows + k * step, step)
        m = mc[at, :].astype(F32)
        full = x[at, mine].astype(F32) + m + values
        out[at, :] = full.astype(BF)
        vecs[4:5, :] += jnp.sum(ok * m * m, axis=0, keepdims=True)
        vecs[5:6, :] += jnp.sum(ok * values * values, axis=0, keepdims=True)
        vecs[6:7, :] += jnp.sum(ok * full * full, axis=0, keepdims=True)

    turns, begin, turn, last, drain = line_reduce_scatter(
        t, seq, tp, own, inbox, (sr, rr, sl, rl), finish, 1
    )
    slots = 12

    def pump(slot):
        def one(i, c):
            turn(i)
            return c

        lax.fori_loop(slot * turns // slots, (slot + 1) * turns // slots, one, 0)

    fetches[0].wait()
    begin()
    pump(0)
    down.wait()
    far()
    for copy in inputs[:4]:
        copy.wait()

    def gates(i, c):
        @pl.when(i == 1)
        def _():
            pump(1)

        at = pl.ds(pl.multiple_of(i * tile, tile), tile)
        shifted = pl.ds(pl.multiple_of(i * tile + 8, 8), tile)
        g = nn(gmix[at, :], w1[:, 3 * chan :])
        hat = get(states, shifted) * invst[at, :]
        o = opre[at, :]
        sig = jax.nn.sigmoid(o)
        q = o * sig
        vecs[2:3, :] += jnp.sum(g * hat * q, axis=0, keepdims=True)
        out3[at, 2 * chan :] = (g * hat * sgain * (sig * (1.0 + o * (1.0 - sig)))).astype(BF)
        w = g * q * sgain
        put(weighted, at, w)
        inner[at, :] = w * hat
        return c

    lax.fori_loop(0, 3, gates, 0)
    dot = sum_over_tp(row_sums(inner[...]), t, seq, tp, zslots, zs, zr, lambda: (pump(2), pump(3))) / width
    inner[:, 0:1] = dot

    def leaving(i, c):
        at = pl.ds(pl.multiple_of(i * tile, tile), tile)
        shifted = pl.ds(pl.multiple_of(i * tile + 8, 8), tile)
        inv = invst[at, :]
        put(weighted, at, inv * (get(weighted, at) - get(states, shifted) * inv * inner[at, 0:1]))
        return c

    lax.fori_loop(0, 3, leaving, 0)
    inputs[4].wait()
    pump(4)

    length = rows // SEG

    def scan(i, c):
        p, h = c
        r = length - 1 - i
        at = pl.ds(r, SEG, stride=length)
        f = get(feff, pl.ds(r + 1, SEG, stride=length))
        h = f * h + get(weighted, at)
        p = f * p
        put(weighted, at, h)
        put(prod, at, p)
        return p, h

    p, h = lax.fori_loop(
        0, length, scan, (jnp.ones((SEG, chan), F32), jnp.zeros((SEG, chan), F32))
    )
    block_p, block_h = p[SEG - 1 : SEG], h[SEG - 1 : SEG]
    for s in range(SEG - 2, -1, -1):
        block_h = h[s : s + 1] + p[s : s + 1] * block_h
        block_p = p[s : s + 1] * block_p
    first = get(feff, slice(0, 1))
    arriving = carry_over_seq(
        first * block_p, first * block_h, n, seq, tp, cslots, cs, cr, True, lambda: (pump(5), pump(6))
    )
    inputs[5].wait()
    inputs[6].wait()
    middle()
    bias_sum = jnp.zeros((1, chan), F32)
    for s in range(SEG - 1, -1, -1):
        if s in (5, 1):
            pump(8 - s // 5)
        at = slice(s * length, (s + 1) * length)
        gs = get(weighted, at) + get(prod, at) * arriving
        arriving = h[s : s + 1] + p[s : s + 1] * arriving
        a = ipre[at, :]
        sa = jax.nn.sigmoid(a)
        act = a * sa
        sf = jax.nn.sigmoid(fpre[at, :])
        gate = bound + (1.0 - bound) * sf
        ok, starts = masks(lens, seq * rows + s * length, length)
        out3[at, :chan] = (gs * (1.0 - gate) * ok * (sa * (1.0 + a * (1.0 - sa)))).astype(BF)
        before = get(states, slice(s * length + 7, (s + 1) * length + 7))
        gate_grad = gs * before * (1.0 - starts) - gs * act * ok
        gf = (gate_grad * (1.0 - bound) * sf * (1.0 - sf)).astype(BF)
        out3[at, chan : 2 * chan] = gf
        bias_sum = bias_sum + jnp.sum(gf.astype(F32), axis=0, keepdims=True)
    vecs[1:2, :] = bias_sum

    def gni_copy(i):
        at = pl.ds(pl.multiple_of(i * tile, tile), tile)
        return pltpu.make_async_copy(gni.at[:, at], gni_h.at[:, at], s_o.at[i])

    for copy in inputs[7:] + fetches[1:]:
        copy.wait()
    gain_sum[...] = jnp.zeros_like(gain_sum)

    def spread_in(i, c):
        at = pl.ds(pl.multiple_of(i * tile, tile), tile)
        values = nt(out3[at, :], w1[:, : 3 * chan])
        put_shards(gni, at, values.astype(BF))
        gni_copy(i).start()
        product = values * (x[at, :].astype(F32) * invin[at, :])
        gain_sum[0:1, :] += jnp.sum(product, axis=0, keepdims=True)
        product = product * consts[4:5, :]
        short = product[:, :LANE]
        for k in range(LANE, width, LANE):
            short = short + product[:, k : k + LANE]
        inner[at, :LANE] = short
        pump(9 + i)
        return c

    lax.fori_loop(0, 3, spread_in, 0)

    zslots2[tp] = row_sums(inner[:, :LANE])
    go_z, done_z = spread(t, tp, zslots2, zs2, zr2, lambda k: (seq, k))
    go_z()
    gsend[...] = jnp.zeros_like(gsend)
    for q in range(t):
        gsend[q, 0:1, :] = gain_sum[0:1, q * chan : (q + 1) * chan]

    def gain_copy(o, slot):
        to = lax.rem(tp + o, t)
        return pltpu.make_async_remote_copy(
            src_ref=gsend.at[to],
            dst_ref=gtake.at[slot],
            send_sem=gs_.at[o],
            recv_sem=gr_.at[slot],
            device_id=(seq, to),
            device_id_type=MESH,
        )

    def gain_go(o, c):
        gain_copy(o, tp).start()
        return c

    def gain_done(o, c):
        gain_copy(o, lax.rem(tp + o, t)).wait_recv()
        return c

    def gain_sent(o, c):
        gain_copy(o, tp).wait_send()
        return c

    lax.fori_loop(1, t, gain_go, 0)
    gtake[tp] = gsend[tp]
    near()
    shard = width // n
    chips = n // 2

    def d_copy(r, slot):
        at = pl.ds(pl.multiple_of(r * shard, shard), shard)
        return pltpu.make_async_copy(stage.at[slot], dw1_h.at[:, at], s_d.at[slot])

    def keep(slot, first, values):
        for k in range(2):
            stage[slot, k, :, first : first + values.shape[1]] = values[k * shard : (k + 1) * shard]

    def slab(r, c):
        slot = lax.rem(r, 2)

        @pl.when(r >= 2)
        def _():
            d_copy(r - 2, slot).wait()

        at = pl.ds(pl.multiple_of(r * 2 * shard, 2 * shard), 2 * shard)
        keep(slot, 0, tn(normed[:, at], out3[...]).astype(BF))
        keep(slot, 3 * chan, tn(gmix[:, at], gated[...]).astype(BF))
        d_copy(r, slot).start()
        return c

    lax.fori_loop(0, chips, slab, 0)

    done_z()
    total = zslots2[0]
    for k in range(1, t):
        total = total + zslots2[k]
    dot_in[...] = jnp.transpose(total)[:, :1] / width
    lax.fori_loop(1, t, gain_done, 0)
    lax.fori_loop(1, t, gain_sent, 0)
    gains = gtake[0]
    for k in range(1, t):
        gains = gains + gtake[k]
    vecs[0:1, :] = gains[0:1]

    def ending(k, c):
        last(k)
        return c

    lax.fori_loop(0, SHARD_CHUNKS, ending, 0)
    for r in range(max(chips - 2, 0), chips):
        d_copy(r, r % 2).wait()

    def stored(i, c):
        gni_copy(i).wait()
        return c

    lax.fori_loop(0, 3, stored, 0)
    drain()
    drain_grid()


def closing(
    n, t, width,
    lens, gni_h, dw1_h, x_h, gres_h, invin, dot_in, consts, vecs, ggain,
    gin, vectors, rms, g_input, g_forget, g_outgate, g_output,
    acc, other, xc, gres, own, inbox, vslots, allvec,
    s_acc, m_core, s_own, s_x, sr, rr, sl, rl, vs, vr, ts, tr, *bufs,
):
    seq, tp = lax.axis_index("seq"), lax.axis_index("tp")
    rows, chan = gres.shape
    mine = pl.ds(pl.multiple_of(tp * chan, LANE), chan)
    fetch = pltpu.make_async_copy(gni_h, own, s_own)
    fetches = [
        pltpu.make_async_copy(x_h.at[:, mine], xc, s_x.at[0]),
        pltpu.make_async_copy(gres_h, gres, s_x.at[1]),
    ]
    fetch.start()
    greet_all(n, t, seq, tp)
    pieces, shard, cols = 2, g_input.shape[0], 2 * chan

    core = lax.rem(seq, 2)

    def load(j):
        return pltpu.make_async_copy(
            dw1_h.at[core, :, pl.ds(j * cols, cols)], acc.at[j], s_acc.at[j]
        )

    def swap(j):
        return pltpu.make_async_remote_copy(
            src_ref=dw1_h.at[1 - core, :, pl.ds(j * cols, cols)],
            dst_ref=other.at[j],
            send_sem=m_core.at[0, j],
            recv_sem=m_core.at[1, j],
            device_id=(seq + 1 - 2 * core, tp),
            device_id_type=MESH,
        )

    def start(j):
        load(j).start()
        swap(j).start()

    reduces = []
    for j in range(pieces):

        def out(half, values, j=j):
            at = slice(half * (shard // 2), (half + 1) * (shard // 2))
            if j == 0:
                g_input[at, :] = values[:, :chan]
                g_forget[at, :] = values[:, chan:]
            else:
                g_outgate[at, :] = values[:, :chan]
                g_output[:, at] = jnp.transpose(values[:, chan:])

        reduces.append(grid_reduce(n, seq, tp, j, acc.at[j], bufs, out))

    def stage1(j):
        load(j).wait()
        swap(j).wait_recv()
        add_cores(acc.at[j], other.at[j])
        reduces[j][0]()

    def stage2(j):
        reduces[j][1]()

    def stage3(j):
        reduces[j][2]()

    fetch.wait()
    start(0)
    for copy in fetches:
        copy.start()
    step = rows // SHARD_CHUNKS
    gain_in = consts[4:5, mine]
    vslots[seq] = vecs[...]
    vslots[seq, 3:4, :] = ggain[0:1, mine]
    go_v, done_v = spread(n, seq, vslots, vs, vr, lambda k: (k, tp))
    go_t, done_t = spread(t, tp, allvec, ts, tr, lambda k: (seq, k))
    go_v()
    for copy in fetches:
        copy.wait()

    def finish(k, values):
        at = pl.ds(pl.multiple_of(k * step, step), step)
        hat = xc[at, :].astype(F32) * invin[at, :]
        gin[at, :] = gres[at, :] + invin[at, :] * (values * gain_in - hat * dot_in[at, :])

    def vectors_on():
        done_v()
        total = vslots[0]
        for k in range(1, n):
            total = total + vslots[k]
        allvec[tp] = total
        go_t()

    turns, begin, turn, last, drain = line_reduce_scatter(
        t, seq, tp, own, inbox, (sr, rr, sl, rl), finish, HOP_LAG
    )
    works = [
        (0, lambda: (stage1(0), start(1), vectors_on())),
        (2, lambda: stage1(1)),
        (4, lambda: stage2(0)),
        (6, lambda: stage3(0)),
        (7, lambda: stage2(1)),
        (9, lambda: stage3(1)),
    ]
    slots = 10
    begin()

    def turn_of(slot):
        def one(i, c):
            turn(i)
            return c

        lax.fori_loop(slot * turns // slots, (slot + 1) * turns // slots, one, 0)

    loop_with(0, slots, turn_of, works)
    done_t()
    squares = jnp.zeros((8, 1), F32)
    for k in range(t):
        vectors[:, k * chan : (k + 1) * chan] = allvec[k]
        squares = squares + jnp.sum(allvec[k], axis=1, keepdims=True)
    count = (lens[0] + lens[1]).astype(F32) * width
    rms[...] = jnp.broadcast_to(jnp.sqrt(squares / count), rms.shape)

    def ending(k, c):
        last(k)
        return c

    lax.fori_loop(0, SHARD_CHUNKS, ending, 0)
    drain()
    for j in range(pieces):
        swap(j).wait_send()
        reduces[j][3]()


def emit(count, *refs):
    sources, (vectors, roots) = refs[:count], refs[count : count + 2]
    targets = refs[count + 2 : 2 * count + 2]
    outs, stats = refs[2 * count + 2 : 2 * count + 6], refs[2 * count + 6]
    held, sem = refs[2 * count + 7 : 3 * count + 7], refs[3 * count + 7]
    loads = [
        pltpu.make_async_copy(src, dst, sem.at[0, i])
        for i, (src, dst) in enumerate(zip(sources, held))
    ]
    stores = [
        pltpu.make_async_copy(src, dst, sem.at[1, i])
        for i, (src, dst) in enumerate(zip(held, targets))
    ]
    for copy in loads:
        copy.start()
    for k, out in enumerate(outs):
        out[...] = vectors[k, :]
    for k in range(3):
        stats[k] = roots[4 + k, 0]
    for load, store in zip(loads, stores):
        load.wait()
        store.start()
    for copy in stores:
        copy.wait()


def params(collective=None, limit=VMEM_LIMIT):
    if collective is None:
        return pltpu.CompilerParams(vmem_limit_bytes=limit)
    return pltpu.CompilerParams(
        vmem_limit_bytes=limit, collective_id=collective, has_side_effects=True
    )


def line_sems(chunks):
    return [DMA((chunks,)), DMA((chunks,)), DMA((2, chunks))]


def on_device(
    n, t,
    hidden_in, gain_in, w_input, w_forget, forget_bias, w_outgate, state_gain, w_output,
    gain_mid, w_gate, w_up, w_down, lengths, layer_index, cotangent,
):
    rows, width = hidden_in.shape
    chan = w_input.shape[1]
    ff = w_gate.shape[1]
    ffp = -(-ff // LANE) * LANE

    def padded(w):
        return w if ffp == ff else jnp.pad(w, ((0, 0), (0, ffp - ff)))

    plane = shape((rows, chan), F32)
    plane16 = shape((rows, chan), BF)
    column = shape((rows, 1), F32)
    wide16 = shape((rows, width), BF)
    shards16 = shape((t, rows, chan), BF)

    def groups(more=0):
        return shape((chan // LANE, rows + more, LANE), F32)

    def vm(*arrays):
        return [pltpu.VMEM(a.shape, a.dtype) for a in arrays]

    SM = pl.BlockSpec(memory_space=pltpu.SMEM)
    w1s, w2s = shape((4, width, chan), BF), shape((3, width, ffp), BF)
    zslot, vslot = pltpu.VMEM((t, 8, rows), F32), pltpu.VMEM((n, 8, chan), F32)
    small = [DMA((n,)), DMA((n,)), DMA((t,)), DMA((t,))]
    saved = [plane, plane, plane, groups(8), groups(8), plane16, wide16]

    (
        ipre, fpre, opre, feff, states, gated, normed_in, nmid, mixed, w1, w2, invst, invmid, inv_in,
        consts,
    ) = pl.pallas_call(
        functools.partial(mixer_forward, n, t, width),
        out_shape=saved + [wide16, wide16, w1s, w2s, column, column, column, shape((8, width), F32)],
        in_specs=[SM] * 2 + [HB] * 4 + [VM] + [HB] * 3 + [VM] * 4,
        out_specs=[HB] * 11 + [VM] * 4,
        scratch_shapes=[
            *vm(wide16, wide16, plane, plane, plane, groups(8), groups(8), plane16, wide16, w1s),
            *vm(groups(), plane),
            pltpu.VMEM((rows // CHUNKS * 4, width), F32),
            vslot,
            zslot,
            pltpu.VMEM((rows, width), BF),
            pltpu.VMEM((2, rows, width), BF),
            pltpu.VMEM((width // n, chan), BF),
            pltpu.VMEM((width // n, ffp), BF),
            pltpu.VMEM((ff, width // n), BF),
            DMA, DMA, DMA((7,)), DMA((4,)), DMA((CHUNKS,)), DMA((CHUNKS,)),
            *small,
            *line_sems(CHUNKS),
            *gather_sems(n, 4),
            *gather_sems(n, 3),
        ],
        compiler_params=params(1),
        name="mixer_forward",
    )(
        lengths, layer_index, hidden_in, w_input, w_forget, w_outgate, w_output,
        padded(w_gate), padded(w_up), w_down, forget_bias, state_gain, gain_mid, gain_in,
    )

    shard, chips, tile, step = width // n, n // 2, rows // TILES, rows // CHUNKS
    piece = shape((shard, ffp), F32)
    ffs = shape((rows, ffp), BF)
    gmix, gres, glu_part, ggain, sum_gate, sum_up, down = pl.pallas_call(
        functools.partial(feed_forward, n, t, width),
        out_shape=[
            wide16, plane, shards16, shape((8, width), F32), piece, piece,
            shape((width // 2, ffp), BF),
        ],
        in_specs=[HB] * 5 + [VM] * 2,
        out_specs=[HB] * 3 + [VM] + [HB] * 3,
        scratch_shapes=[
            *vm(wide16, wide16, w2s, ffs, ffs, ffs),
            pltpu.VMEM((2, t, tile, chan), BF),
            pltpu.VMEM((2, step, width), BF),
            pltpu.VMEM((2, step, width), BF),
            pltpu.VMEM((2, step, width), BF),
            pltpu.VMEM((2, step, chan), F32),
            pltpu.VMEM((step, width), F32),
            *vm(piece),
            pltpu.VMEM((2, 2, shard, ffp), BF),
            *vm(wide16),
            pltpu.VMEM((2, rows, width), BF),
            DMA((2,)), DMA((3,)), DMA((2, 2)), DMA((2, 2)), DMA((2,)), DMA((3,)), DMA((2,)),
            DMA((3 * chips,)),
            pltpu.SemaphoreType.REGULAR,
            *line_sems(CHUNKS),
            *grid_buffers(n, width, 2, ffp),
        ],
        compiler_params=params(2),
        name="feed_forward",
    )(nmid, cotangent, w2, hidden_in, mixed, invmid, consts)

    shard_sems = [DMA((t, SHARD_CHUNKS))] * 4
    shard_bufs = [pltpu.VMEM((t, rows, chan), BF), pltpu.VMEM((t + 1, rows, chan), BF)]
    gni_part, dw1, vecs, block_out, dot_in, sum_down = pl.pallas_call(
        functools.partial(mixer_backward, n, t, width),
        out_shape=[
            shards16, shape((2, width // 2, 4 * chan), BF), shape((8, chan), F32), plane16, column,
            shape((ffp, shard), F32),
        ],
        in_specs=[SM] + [HB] * 13 + [VM] * 3,
        out_specs=[HB] * 2 + [VM] * 4,
        scratch_shapes=[
            pltpu.VMEM((width // 2, ffp), BF),
            *vm(wide16, wide16),
            pltpu.VMEM((width, 4 * chan), BF),
            *vm(plane16, groups(8), groups(8), plane, plane, plane),
            *vm(groups(), groups(), plane, shape((rows, 3 * chan), BF)),
            vslot,
            zslot,
            zslot,
            pltpu.VMEM((8, width), F32),
            pltpu.VMEM((t, 8, chan), F32),
            pltpu.VMEM((t, 8, chan), F32),
            *vm(wide16, plane16),
            *shard_bufs,
            *vm(shards16),
            pltpu.VMEM((2, 2, shard, 4 * chan), BF),
            DMA((12,)),
            *small,
            DMA((t,)), DMA((t,)), DMA((t,)), DMA((t,)),
            DMA((3,)),
            *shard_sems,
            DMA((3,)), DMA((2,)), DMA,
            *grid_buffers(n, width, 1, ffp),
        ],
        compiler_params=params(3),
        name="mixer_backward",
    )(
        lengths, glu_part, hidden_in, mixed, gmix, normed_in, w1, gated, states, feff, ipre, fpre, opre,
        down, invst, inv_in, consts,
    )

    square = shape((shard, chan), F32)
    grad_in, vectors, rms, g_input, g_forget, g_outgate, g_output = pl.pallas_call(
        functools.partial(closing, n, t, width),
        out_shape=[
            plane, shape((8, width), F32), shape((8, LANE), F32),
            square, square, square, shape((chan, shard), F32),
        ],
        in_specs=[SM] + [HB] * 4 + [VM] * 5,
        out_specs=[VM] * 7,
        scratch_shapes=[
            pltpu.VMEM((2, width // 2, 2 * chan), BF),
            pltpu.VMEM((2, width // 2, 2 * chan), BF),
            *vm(plane16, plane),
            *shard_bufs,
            vslot,
            pltpu.VMEM((t, 8, chan), F32),
            DMA((2,)), DMA((2, 2)), DMA, DMA((2,)),
            *shard_sems,
            DMA((n,)), DMA((n,)), DMA((t,)), DMA((t,)),
            *grid_buffers(n, width, 2, 2 * chan),
        ],
        compiler_params=params(4),
        name="closing",
    )(lengths, gni_part, dw1, hidden_in, gres, inv_in, dot_in, consts, vecs, ggain)

    arrays = (
        block_out, grad_in, g_input, g_forget, g_outgate, g_output, sum_gate[:, :ff], sum_up[:, :ff],
        sum_down[:ff],
    )
    count = len(arrays)
    *copies, gain0, bias0, gain1, gain2, rms_stats = pl.pallas_call(
        functools.partial(emit, count),
        out_shape=[shape(a.shape, a.dtype) for a in arrays] + [shape((width,), F32)] * 4 + [shape((3,), F32)],
        in_specs=[HB] * count + [VM, SM],
        out_specs=[HB] * count + [VM] * 4 + [SM],
        scratch_shapes=[pltpu.VMEM(a.shape, a.dtype) for a in arrays] + [DMA((2, count))],
        compiler_params=params(),
        name="emit",
    )(*arrays, vectors, rms)
    out, gin, g_input, g_forget, g_outgate, g_output, g_gate, g_up, g_down = copies
    return (
        out, gin, gain0, g_input, g_forget, bias0, g_outgate, gain1, g_output, gain2,
        g_gate, g_up, g_down, rms_stats,
    )


def solution(mesh):
    weight, turned = P("seq", "tp"), P("tp", "seq")
    in_specs = (
        P("seq", None), P(), weight, weight, P(), weight, P(), turned, P(), weight, weight, turned,
        P(), P(), P("seq", None),
    )
    out_specs = (
        weight, weight, P(), weight, weight, P(), weight, P(), turned, P(), weight, weight, turned, P(),
    )
    body = functools.partial(on_device, mesh.shape["seq"], mesh.shape["tp"])
    return jax.shard_map(
        body, mesh=mesh, in_specs=in_specs, out_specs=out_specs, check_vma=False
    )
```
